32 devices in a mesh: dom: 8 (over y, x, core), feat: 4 (over z).
Axes of the slice: x: 2, y: 2, z: 4, core: 2. Of those that a mesh axis runs over, the one named last changes fastest.
Arguments:
- node_state: bfloat16 [49152, 128], P(('dom', 'feat')), may hold values from -6 to 6
- w_msg: bfloat16 [128, 128], replicated, may hold values from -0.5 to 0.5
- w_first: bfloat16 [256, 128], replicated, may hold values from -0.375 to 0.375
- b_first: float32 [128], replicated, may hold values from -3 to 3
- w_second: bfloat16 [128, 128], replicated, may hold values from -0.5 to 0.5
- b_second: float32 [128], replicated, may hold values from -3 to 3
- ln_gain: float32 [128], replicated, may hold values from 0.5 to 1.5
- col_index: int32 [384, 4], P(('dom', 'feat')), may hold values from 0 to 383, as said below
- edge_counts: int32 [384, 4, 128, 128], P(('dom', 'feat')), may hold values from 0 to 3, as said below
- cotangent: bfloat16 [49152, 128], P(('dom', 'feat')), may hold values from -14 to 14
Outputs:
- updated: bfloat16 [49152, 128], P(('dom', 'feat'))
- grad_state: bfloat16 [49152, 128], P(('dom', 'feat'))
- grad_w_msg: float32 [128, 128], replicated
- grad_w_first: float32 [256, 128], replicated
- grad_b_first: float32 [128], replicated
- grad_w_second: float32 [128, 128], replicated
- grad_b_second: float32 [128], replicated
- grad_gain: float32 [128], replicated
The draws below stay inside these ranges and needn't reach their ends.
Inputs may be any that keep to these rules, and one draw needn't show every extreme that they name: `col_index`: tile 0 of block row b is block b itself; every other tile's column lies within 2 blocks of b, reflected at the two ends of the curve; columns of one block row may repeat. `edge_counts`: most entries are zero.
All inputs are finite; a program needn't handle non-finite values.
Results may differ from the reference program's by a relative error of at most 0.0093.
Values may be sent and summed in bfloat16 or wider, within the bound.
No kernel may reach another device: no remote copies, remote signals or barrier semaphores. Data moves between devices by JAX's collectives and lax.ppermute only.
A program may use at most 64 MiB of HBM per device.

```python
import jax
import jax.numpy as jnp
from jax import lax

HID = 128
BLK = 128
TILES = 4
WIN = 2
NB_DEV = 12
NBLKS = 384
NODES = 49152


def draw_col_index(key, part):
    block_rows = jnp.arange(NBLKS, dtype=jnp.int32)
    offsets = jax.random.randint(key, (NBLKS, TILES - 1), -WIN, WIN + 1, dtype=jnp.int32)
    offsets = jnp.concatenate([jnp.zeros((NBLKS, 1), jnp.int32), offsets], axis=1)
    columns = block_rows[:, None] + offsets
    columns = jnp.where(columns < 0, -columns, columns)
    columns = jnp.where(columns > NBLKS - 1, 2 * (NBLKS - 1) - columns, columns)
    return columns.astype(jnp.int32)


def draw_edge_counts(key, part):
    key_live = jax.random.fold_in(key, 11)
    key_value = jax.random.fold_in(key, 23)
    shape_all = (NBLKS, TILES, BLK, BLK)
    live = jax.random.randint(key_live, shape_all, 0, BLK, dtype=jnp.int32) < 2
    values = jax.random.randint(key_value, shape_all, 1, 4, dtype=jnp.int32)
    return jnp.where(live, values, 0).astype(jnp.int32)


def draw_cotangent(key, part):
    key_base = jax.random.fold_in(key, 5)
    positions = jnp.arange(NODES, dtype=jnp.float32) / NODES
    row_scale = jnp.power(10.0, positions - 0.5)
    base = jnp.clip(jax.random.normal(key_base, (NODES, HID), jnp.float32), -4.0, 4.0)
    return (base * row_scale[:, None]).astype(jnp.bfloat16)


def level_of(own_key, extent, split, least, high):
    def one(dim, shards_of):
        heights = jax.random.uniform(jax.random.fold_in(jax.random.fold_in(own_key, 6), dim), (shards_of,), jnp.float32, least / len(split), high / len(split))
        return jnp.repeat(jnp.exp(heights), extent[dim] // shards_of).reshape((-1,) + (1,) * (len(extent) - dim - 1))

    level = one(*split[0])
    for cut in split[1:]:
        level = level * one(*cut)
    return level


def normal_values(own_key, shape, scale, limit, pieces=(), held_as=jnp.bfloat16):
    result = jax.random.normal(own_key, shape, jnp.float32) * scale
    if len(pieces) > 0:
        result = level_of(own_key, shape, pieces, -0.22, 0.18) * result
    return jnp.clip(result, min=-limit, max=limit).astype(held_as)


def setup_inputs(seed: int = 0) -> dict:
    arg_keys = jax.random.split(jax.random.key(seed), 11)
    return {
        "node_state": normal_values(arg_keys[0], (NODES, HID), 1.0, 6.0, ((0, 32),)),
        "w_msg": normal_values(arg_keys[1], (HID, HID), HID ** -0.5, 0.5),
        "w_first": normal_values(arg_keys[2], (2 * HID, HID), (2 * HID) ** -0.5, 0.375),
        "b_first": normal_values(arg_keys[3], (HID,), 0.5, 3.0, (), jnp.float32),
        "w_second": normal_values(arg_keys[4], (HID, HID), HID ** -0.5, 0.5),
        "b_second": normal_values(arg_keys[5], (HID,), 0.5, 3.0, (), jnp.float32),
        "ln_gain": jnp.clip(jax.random.uniform(arg_keys[6], (HID,), jnp.float32, 0.5, 1.5), 0.5, 1.5),
        "col_index": draw_col_index(jax.random.fold_in(arg_keys[10], 71), 0),
        "edge_counts": draw_edge_counts(jax.random.fold_in(arg_keys[10], 71), 0),
        "cotangent": draw_cotangent(jax.random.fold_in(arg_keys[10], 71), 0),
    }


epsilon = 1e-05

def inner_rows(left, right):
    return lax.dot_general(left, right, (((0,), (0,)), ((), ())), preferred_element_type=jnp.float32)

def times_transposed(left, right):
    return lax.dot_general(left, right, (((1,), (1,)), ((), ())), preferred_element_type=jnp.float32)

def reference(node_state, w_msg, w_first, b_first, w_second, b_second, ln_gain, col_index, edge_counts, cotangent):
    node_total = node_state.shape[0]
    groups = NBLKS // NB_DEV
    messages = jnp.dot(node_state, w_msg, preferred_element_type=jnp.float32).astype(jnp.bfloat16)
    msg_blocks = messages.reshape(NBLKS, BLK, HID)

    def forward_group(group_index):
        start = group_index * NB_DEV
        col_slice = lax.dynamic_slice_in_dim(col_index, start, NB_DEV, 0)
        count_slice = lax.dynamic_slice_in_dim(edge_counts, start, NB_DEV, 0).astype(jnp.float32)
        picked = msg_blocks[col_slice].astype(jnp.float32)
        return jnp.einsum('btij,btjh->bih', count_slice, picked)
    aggregate = lax.map(forward_group, jnp.arange(groups, dtype=jnp.int32))
    aggregate = aggregate.reshape(node_total, HID).astype(jnp.bfloat16)
    joined = jnp.concatenate([node_state, aggregate], axis=1)
    pre_hidden = jnp.dot(joined, w_first, preferred_element_type=jnp.float32) + b_first
    activated = jax.nn.silu(pre_hidden).astype(jnp.bfloat16)
    pre_norm = jnp.dot(activated, w_second, preferred_element_type=jnp.float32) + b_second
    row_mean = lax.optimization_barrier(jnp.mean(pre_norm, axis=-1, keepdims=True))
    centred = pre_norm - row_mean
    inv_std = lax.rsqrt(lax.optimization_barrier(jnp.mean(centred * centred, axis=-1, keepdims=True)) + epsilon)
    normed = centred * inv_std
    updated = (node_state.astype(jnp.float32) + ln_gain * normed).astype(jnp.bfloat16)
    cot_f32 = cotangent.astype(jnp.float32)
    d_normed = cot_f32 * ln_gain
    d_pre_norm = (inv_std * (d_normed - lax.optimization_barrier(jnp.mean(d_normed, axis=-1, keepdims=True)) - normed * lax.optimization_barrier(jnp.mean(d_normed * normed, axis=-1, keepdims=True)))).astype(jnp.bfloat16)
    sigmoid_z = jax.nn.sigmoid(pre_hidden)
    d_pre_hidden = (times_transposed(d_pre_norm, w_second) * sigmoid_z * (1.0 + pre_hidden * (1.0 - sigmoid_z))).astype(jnp.bfloat16)
    d_joined = times_transposed(d_pre_hidden, w_first)
    d_aggregate = d_joined[:, HID:].astype(jnp.bfloat16).reshape(NBLKS, BLK, HID)
    span_blocks = NB_DEV + 2 * WIN

    def backward_group(group_index):
        start = jnp.clip(group_index * NB_DEV - WIN, 0, NBLKS - span_blocks).astype(jnp.int32)
        col_slice = lax.dynamic_slice_in_dim(col_index, start, span_blocks, 0)
        count_slice = lax.dynamic_slice_in_dim(edge_counts, start, span_blocks, 0).astype(jnp.float32)
        grad_slice = lax.dynamic_slice_in_dim(d_aggregate, start, span_blocks, 0).astype(jnp.float32)
        contribution = jnp.einsum('btij,bih->btjh', count_slice, grad_slice)
        one_hot = ((col_slice - group_index * NB_DEV)[:, :, None] == jnp.arange(NB_DEV, dtype=jnp.int32)[None, None, :]).astype(jnp.float32)
        return jnp.einsum('btc,btjh->cjh', one_hot, contribution, precision=lax.Precision.HIGHEST)
    d_messages = lax.map(backward_group, jnp.arange(groups, dtype=jnp.int32))
    d_messages = d_messages.reshape(node_total, HID).astype(jnp.bfloat16)
    grad_state = (cot_f32 + d_joined[:, :HID] + times_transposed(d_messages, w_msg)).astype(jnp.bfloat16)
    grad_scale = 1.0 / jnp.sqrt(jnp.float32(NODES))
    grad_w_msg = inner_rows(node_state, d_messages) * grad_scale
    grad_w_first = inner_rows(joined, d_pre_hidden) * grad_scale
    grad_b_first = lax.optimization_barrier(jnp.sum(d_pre_hidden.astype(jnp.float32), axis=0)) * grad_scale
    grad_w_second = inner_rows(activated, d_pre_norm) * grad_scale
    grad_b_second = lax.optimization_barrier(jnp.sum(d_pre_norm.astype(jnp.float32), axis=0)) * grad_scale
    grad_gain = lax.optimization_barrier(jnp.sum(cot_f32 * normed, axis=0)) * grad_scale
    return (updated, grad_state, grad_w_msg, grad_w_first, grad_b_first, grad_w_second, grad_b_second, grad_gain)
```

```python
import math

import jax
import jax.numpy as jnp
from jax import lax
from jax.sharding import PartitionSpec as P

WIN = 2


epsilon = 1e-05


def with_halo(cells, sides, width):
    for axis, dim in sides:
        count = lax.axis_size(axis)
        ends = count - 1
        head = lax.slice_in_dim(cells, 0, width, axis=dim)
        tail = lax.slice_in_dim(cells, cells.shape[dim] - width, cells.shape[dim], axis=dim)
        cells = jnp.concatenate(
            [
                lax.ppermute(tail, axis, [(i, (i + 1) % count) for i in range(ends)]),
                cells,
                lax.ppermute(head, axis, [((i + 1) % count, i) for i in range(ends)]),
            ],
            axis=dim,
        )
    return cells


def passed_along(block, axis, distance):
    devices = range(lax.axis_size(axis))
    route = [(i - distance, i) for i in devices if i - distance in devices]
    return lax.ppermute(block, axis, route)


def inner_rows(left, right):
    return lax.dot_general(
        left, right, (((0,), (0,)), ((), ())), preferred_element_type=jnp.float32
    )


def times_transposed(left, right):
    return lax.dot_general(
        left, right, (((1,), (1,)), ((), ())), preferred_element_type=jnp.float32
    )


def summed_over_devices(terms, axes):
    devices = lax.axis_size(axes)
    sizes = [math.prod(term.shape) for term in terms]
    total = sum(sizes)
    rows = -(-total // (devices * 128))
    flat = jnp.concatenate([term.reshape(-1) for term in terms])
    flat = jnp.pad(flat, (0, rows * devices * 128 - total))
    parts = lax.all_to_all(flat.reshape(devices, rows, 128), axes, 0, 0, tiled=True)
    own = jnp.sum(parts, axis=0)
    spread = jnp.broadcast_to(own[None], (devices, rows, 128))
    whole = lax.all_to_all(spread, axes, 0, 0, tiled=True).reshape(-1)
    results, start = [], 0
    for term, size in zip(terms, sizes):
        results.append(whole[start : start + size].reshape(term.shape))
        start += size
    return results


def shards(
    node_state,
    w_msg,
    w_first,
    b_first,
    w_second,
    b_second,
    ln_gain,
    col_index,
    edge_counts,
    cotangent,
):
    node_rows, features = node_state.shape
    block_count, tile_count, block_size, _ = edge_counts.shape
    span_blocks = WIN
    devices = lax.axis_size("dom") * lax.axis_size("feat")
    grad_scale = 1.0 / math.sqrt(node_rows * devices)
    messages = jnp.dot(node_state, w_msg, preferred_element_type=jnp.float32).astype(jnp.bfloat16)
    extended = with_halo(messages, ((("dom", "feat"), 0),), span_blocks * block_size)
    ext_blocks = extended.reshape(block_count + 2 * span_blocks, block_size, features)
    first_block = lax.axis_index(("dom", "feat")) * block_count
    local_col = col_index - first_block + span_blocks
    gathered = ext_blocks[local_col]
    tile_weights = edge_counts.astype(jnp.bfloat16)
    aggregate = jnp.einsum(
        "btij,btjh->bih", tile_weights, gathered, preferred_element_type=jnp.float32
    )
    aggregate = aggregate.reshape(node_rows, features).astype(jnp.bfloat16)
    joined = jnp.concatenate([node_state, aggregate], axis=1)
    pre_hidden = jnp.dot(joined, w_first, preferred_element_type=jnp.float32) + b_first
    activated = jax.nn.silu(pre_hidden).astype(jnp.bfloat16)
    pre_norm = jnp.dot(activated, w_second, preferred_element_type=jnp.float32) + b_second
    row_mean = jnp.mean(pre_norm, axis=-1, keepdims=True)
    centred = pre_norm - row_mean
    inv_std = lax.rsqrt(jnp.mean(centred * centred, axis=-1, keepdims=True) + epsilon)
    normed = centred * inv_std
    updated = (node_state.astype(jnp.float32) + ln_gain * normed).astype(jnp.bfloat16)
    cot_f32 = cotangent.astype(jnp.float32)
    d_normed = cot_f32 * ln_gain
    d_pre_norm = (
        inv_std
        * (
            d_normed
            - jnp.mean(d_normed, axis=-1, keepdims=True)
            - normed * jnp.mean(d_normed * normed, axis=-1, keepdims=True)
        )
    ).astype(jnp.bfloat16)
    sigmoid_z = jax.nn.sigmoid(pre_hidden)
    d_pre_hidden = (
        times_transposed(d_pre_norm, w_second) * sigmoid_z * (1.0 + pre_hidden * (1.0 - sigmoid_z))
    ).astype(jnp.bfloat16)
    d_joined = times_transposed(d_pre_hidden, w_first)
    d_aggregate = (
        d_joined[:, features:].astype(jnp.bfloat16).reshape(block_count, block_size, features)
    )
    contribution = jnp.einsum(
        "btij,bih->btjh", tile_weights, d_aggregate, preferred_element_type=jnp.float32
    )
    slot_ids = jnp.arange(block_count + 2 * span_blocks, dtype=jnp.int32)
    one_hot = (local_col[:, :, None] == slot_ids[None, None, :]).astype(jnp.float32)
    ext_grad = jnp.einsum("btc,btjh->cjh", one_hot, contribution, precision=lax.Precision.HIGHEST)
    lower_part = ext_grad[:span_blocks]
    upper_part = ext_grad[block_count + span_blocks :]
    own_part = ext_grad[span_blocks : block_count + span_blocks]
    from_below = passed_along(upper_part.astype(jnp.bfloat16), ("dom", "feat"), 1).astype(
        upper_part.dtype
    )
    from_above = passed_along(lower_part.astype(jnp.bfloat16), ("dom", "feat"), -1).astype(
        lower_part.dtype
    )
    summed_grad = own_part.at[:span_blocks].add(from_below)
    summed_grad = summed_grad.at[block_count - span_blocks :].add(from_above)
    d_messages = summed_grad.reshape(node_rows, features).astype(jnp.bfloat16)
    grad_state = (cot_f32 + d_joined[:, :features] + times_transposed(d_messages, w_msg)).astype(
        jnp.bfloat16
    )
    terms = (
        inner_rows(node_state, d_messages) * grad_scale,
        inner_rows(joined, d_pre_hidden) * grad_scale,
        jnp.sum(d_pre_hidden, axis=0, dtype=jnp.float32) * grad_scale,
        inner_rows(activated, d_pre_norm) * grad_scale,
        jnp.sum(d_pre_norm, axis=0, dtype=jnp.float32) * grad_scale,
        jnp.sum(cot_f32 * normed, axis=0) * grad_scale,
    )
    totals = summed_over_devices(terms, ("dom", "feat"))
    return (updated, grad_state, totals[0], totals[1], totals[2], totals[3], totals[4], totals[5])


def solution(mesh):
    return jax.shard_map(
        shards,
        mesh=mesh,
        in_specs=(
            P(("dom", "feat"), None),
            P(),
            P(),
            P(),
            P(),
            P(),
            P(),
            P(("dom", "feat"), None),
            P(("dom", "feat"), None, None, None),
            P(("dom", "feat"), None),
        ),
        out_specs=(
            P(("dom", "feat"), None),
            P(("dom", "feat"), None),
            P(),
            P(),
            P(),
            P(),
            P(),
            P(),
        ),
        check_vma=False,
    )
```

```python
import functools
import math

import jax
import jax.numpy as jnp
from jax import lax
from jax.experimental import pallas as pl
from jax.experimental.pallas import tpu as pltpu
from jax.sharding import PartitionSpec as P

WIN = 2
epsilon = 1e-05
AXES = ("dom", "feat")
SENT = jnp.bfloat16
BIAS_ROWS = 16


def dot(left, right):
    return jnp.dot(left, right, preferred_element_type=jnp.float32)


def dot_nt(left, right):
    return lax.dot_general(
        left, right, (((1,), (1,)), ((), ())), preferred_element_type=jnp.float32
    )


def column(row_ref, width):
    features = row_ref.shape[1]
    return jnp.broadcast_to(row_ref[...], (width, features)).T


def layer_kernel(
    grad_scale,
    chunk,
    col_ref,
    state_ref,
    below_ref,
    above_ref,
    cot_ref,
    counts_ref,
    w_msg_ref,
    w_first_ref,
    b_first_ref,
    w_second_ref,
    b_second_ref,
    gain_ref,
    updated_ref,
    grad_state_ref,
    grads_ref,
    to_below_ref,
    to_above_ref,
    edge_msg_ref,
    edge_state_ref,
    states,
    messages,
    counts,
    ext_grad,
    direct,
    joined,
    d_hidden,
    active,
    d_norm,
):
    blocks, tiles, size, _ = counts_ref.shape
    features = state_ref.shape[1]
    ext = blocks + 2 * WIN
    group = 2
    width = group * size

    w_msg = w_msg_ref[...]
    w_msg_t = w_msg.T
    w_first = w_first_ref[...]
    w_first_t = jnp.concatenate([w_first[:features].T, w_first[features:].T], axis=1)
    w_second = w_second_ref[...]
    w_second_t = w_second.T
    b_first = column(b_first_ref, width)
    b_second = column(b_second_ref, width)
    gain = column(gain_ref, width)

    for slot in range(ext):
        if slot < WIN:
            block = below_ref[pl.ds(slot * size, size), :]
        elif slot < blocks + WIN:
            block = state_ref[pl.ds((slot - WIN) * size, size), :]
        else:
            block = above_ref[pl.ds((slot - WIN - blocks) * size, size), :]
        state_t = block.T
        states[:, pl.ds(slot * size, size)] = state_t
        messages[slot] = dot(w_msg_t, state_t).astype(jnp.bfloat16)
    ext_grad[...] = jnp.zeros_like(ext_grad)
    joined[pl.ds(2 * features, BIAS_ROWS), :] = jnp.ones((BIAS_ROWS, blocks * size), jnp.bfloat16)
    active[pl.ds(features, BIAS_ROWS), :] = jnp.ones((BIAS_ROWS, blocks * size), jnp.bfloat16)

    gain_terms = jnp.zeros((features, size), jnp.float32)
    for first in range(0, blocks, group):
        rows = range(first, first + group)
        place = pl.ds(first * size, width)
        slots = {}
        parts = []
        for b in rows:
            own = col_ref[b, 0]
            slots[b] = [b + WIN] + [col_ref[b, t] - own + (b + WIN) for t in range(1, tiles)]
            tile_row = jnp.concatenate(
                [counts_ref[b, t].astype(jnp.float32).astype(jnp.bfloat16) for t in range(tiles)],
                axis=1,
            )
            counts[b] = tile_row
            picked = jnp.concatenate([messages[slot] for slot in slots[b]], axis=1)
            parts.append(dot_nt(picked, tile_row).astype(jnp.bfloat16))
        state_t = states[:, pl.ds((first + WIN) * size, width)]
        joined_t = jnp.concatenate([state_t, jnp.concatenate(parts, axis=1)], axis=0)
        joined[pl.ds(0, 2 * features), place] = joined_t
        pre_hidden = dot(w_first_t, joined_t) + b_first
        sigmoid = 1.0 / (1.0 + jnp.exp(-pre_hidden))
        active_t = (pre_hidden * sigmoid).astype(jnp.bfloat16)
        active[pl.ds(0, features), place] = active_t
        slope = sigmoid * (1.0 + pre_hidden * (1.0 - sigmoid))
        pre_norm = dot(w_second_t, active_t) + b_second
        centred = pre_norm - jnp.mean(pre_norm, axis=0, keepdims=True)
        inv_std = lax.rsqrt(jnp.mean(centred * centred, axis=0, keepdims=True) + epsilon)
        normed = centred * inv_std
        updated_t = (state_t.astype(jnp.float32) + gain * normed).astype(jnp.bfloat16)
        cot_t = jnp.concatenate(
            [cot_ref[pl.ds(b * size, size), :].T for b in rows], axis=1
        ).astype(jnp.float32)
        terms = cot_t * normed
        q = cot_t * gain
        mean_q = jnp.mean(q, axis=0, keepdims=True)
        mean_qn = jnp.mean(q * normed, axis=0, keepdims=True)
        d_norm_t = (inv_std * (q - mean_q - normed * mean_qn)).astype(jnp.bfloat16)
        d_norm[:, place] = d_norm_t
        d_hidden_t = (dot(w_second, d_norm_t) * slope).astype(jnp.bfloat16)
        d_hidden[:, place] = d_hidden_t
        d_joined = dot(w_first, d_hidden_t)
        direct[:, place] = cot_t + d_joined[:features]
        d_aggregate = d_joined[features:].astype(jnp.bfloat16)
        for k, b in enumerate(rows):
            lanes = slice(k * size, (k + 1) * size)
            updated_ref[pl.ds(b * size, size), :] = updated_t[:, lanes].T
            gain_terms = gain_terms + terms[:, lanes]
            owed = dot(d_aggregate[:, lanes], counts[b])
            for t, slot in enumerate(slots[b]):
                ext_grad[slot] += owed[:, t * size : (t + 1) * size]

    d_msg = [ext_grad[slot].astype(jnp.bfloat16) for slot in range(ext)]
    for k in range(WIN):
        to_below_ref[k] = d_msg[k]
        to_above_ref[k] = d_msg[blocks + WIN + k]
        for e, b in ((k, k), (WIN + k, blocks - WIN + k)):
            edge_msg_ref[e] = ext_grad[b + WIN]
            edge_state_ref[e] = direct[:, pl.ds(b * size, size)]
    for b in range(WIN, blocks - WIN):
        total = direct[:, pl.ds(b * size, size)] + dot(w_msg, d_msg[b + WIN])
        grad_state_ref[pl.ds(b * size, size), :] = total.astype(jnp.bfloat16).T

    sent = grads_ref.dtype
    first_sums = dot_nt(joined[...], d_hidden[...]) * grad_scale
    second_sums = dot_nt(active[...], d_norm[...]) * grad_scale
    msg_sums = dot_nt(states[...], jnp.concatenate(d_msg, axis=1)) * grad_scale
    gain_sum = jnp.sum(gain_terms.T, axis=0, keepdims=True) * grad_scale
    bias = jnp.concatenate(
        [
            first_sums[2 * features : 2 * features + 1],
            second_sums[features : features + 1],
            gain_sum,
            jnp.zeros((BIAS_ROWS - 3, features), jnp.float32),
        ],
        axis=0,
    )
    sums = jnp.concatenate(
        [first_sums[: 2 * features], second_sums[:features], msg_sums], axis=0
    ).astype(sent)
    for k in range(grads_ref.shape[0]):
        have = max(0, min(chunk, sums.shape[0] - k * chunk))
        if have > 0:
            grads_ref[k, pl.ds(0, have), :] = sums[k * chunk : k * chunk + have]
        if have < chunk:
            grads_ref[k, pl.ds(have, chunk - have), :] = jnp.zeros((chunk - have, features), sent)
        tail = bias if k == 0 else jnp.zeros_like(bias)
        grads_ref[k, pl.ds(chunk, BIAS_ROWS), :] = tail.astype(sent)


def edge_kernel(
    grad_state_ref, msg_ref, state_ref, below_ref, above_ref, w_msg_ref, out_ref
):
    del grad_state_ref
    size = msg_ref.shape[2]
    side = pl.program_id(0)
    w_msg = w_msg_ref[...]
    for k in range(WIN):
        arrived = jnp.where(side == 0, below_ref[k], above_ref[k]).astype(jnp.float32)
        d_msg = (msg_ref[k] + arrived).astype(jnp.bfloat16)
        total = state_ref[k] + dot(w_msg, d_msg)
        out_ref[pl.ds(k * size, size), :] = total.astype(jnp.bfloat16).T


def sum_kernel(parts_ref, spread_ref):
    total = parts_ref[0].astype(jnp.float32)
    for k in range(1, parts_ref.shape[0]):
        total = total + parts_ref[k].astype(jnp.float32)
    total = total.astype(spread_ref.dtype)
    for k in range(spread_ref.shape[0]):
        spread_ref[k] = total


def unpack_kernel(chunk, parts_ref, msg_ref, first_ref, b_first_ref, second_ref, b_second_ref, gain_ref):
    place = 0
    for ref in (first_ref, second_ref, msg_ref):
        done = 0
        while done < ref.shape[0]:
            k, row = divmod(place, chunk)
            count = min(chunk - row, ref.shape[0] - done)
            ref[pl.ds(done, count), :] = parts_ref[k, pl.ds(row, count), :].astype(jnp.float32)
            done += count
            place += count
    bias = parts_ref[0, pl.ds(chunk, BIAS_ROWS), :].astype(jnp.float32)
    b_first_ref[...] = bias[0:1]
    b_second_ref[...] = bias[1:2]
    gain_ref[...] = bias[2:3]


def passed_along(block, distance):
    devices = range(lax.axis_size(AXES))
    route = [(i - distance, i) for i in devices if i - distance in devices]
    return lax.ppermute(block, AXES, route)


def in_vmem():
    return pl.BlockSpec(memory_space=pltpu.VMEM)


def shards(
    node_state,
    w_msg,
    w_first,
    b_first,
    w_second,
    b_second,
    ln_gain,
    col_index,
    edge_counts,
    cotangent,
):
    nodes, features = node_state.shape
    blocks, tiles, size, _ = edge_counts.shape
    ext = blocks + 2 * WIN
    devices = lax.axis_size(AXES)
    dom, feat = lax.axis_size("dom"), lax.axis_size("feat")
    grad_scale = 1.0 / math.sqrt(nodes * devices)
    chunk = -(-4 * features // (dom * 16)) * 16
    bf16, f32 = jnp.bfloat16, jnp.float32
    shape = jax.ShapeDtypeStruct

    from_below = passed_along(node_state[nodes - WIN * size :], 1)
    from_above = passed_along(node_state[: WIN * size], -1)
    row = lambda vector: vector.reshape(1, features)

    updated, grad_state, grads, to_below, to_above, edge_msg, edge_state = pl.pallas_call(
        functools.partial(layer_kernel, grad_scale, chunk),
        out_shape=(
            shape((nodes, features), bf16),
            shape((nodes, features), bf16),
            shape((dom, chunk + BIAS_ROWS, features), SENT),
            shape((WIN, features, size), bf16),
            shape((WIN, features, size), bf16),
            shape((2 * WIN, features, size), f32),
            shape((2 * WIN, features, size), f32),
        ),
        in_specs=[pl.BlockSpec(memory_space=pltpu.SMEM)] + [in_vmem()] * 11,
        out_specs=(in_vmem(),) * 7,
        scratch_shapes=[
            pltpu.VMEM((features, ext * size), bf16),
            pltpu.VMEM((ext, features, size), bf16),
            pltpu.VMEM((blocks, size, tiles * size), bf16),
            pltpu.VMEM((ext, features, size), f32),
            pltpu.VMEM((features, nodes), f32),
            pltpu.VMEM((2 * features + BIAS_ROWS, nodes), bf16),
            pltpu.VMEM((features, nodes), bf16),
            pltpu.VMEM((features + BIAS_ROWS, nodes), bf16),
            pltpu.VMEM((features, nodes), bf16),
        ],
        compiler_params=pltpu.CompilerParams(vmem_limit_bytes=32 * 1024 * 1024),
        cost_estimate=pl.CostEstimate(
            flops=1_000_000_000, bytes_accessed=5_000_000, transcendentals=200_000
        ),
        name="layer",
    )(
        col_index,
        node_state,
        from_below,
        from_above,
        cotangent,
        edge_counts,
        w_msg,
        w_first,
        row(b_first),
        w_second,
        row(b_second),
        row(ln_gain),
    )

    def summed(parts, count, name):
        return pl.pallas_call(
            sum_kernel,
            out_shape=shape((count,) + parts.shape[1:], parts.dtype),
            in_specs=[in_vmem()],
            out_specs=in_vmem(),
            name=name,
        )(parts)

    plane = lax.all_to_all(grads, "dom", 0, 0, tiled=True)
    owed_above = passed_along(to_above, 1)
    owed_below = passed_along(to_below, -1)
    line = lax.all_to_all(summed(plane, feat, "sum_dom"), "feat", 0, 0, tiled=True)

    edge_rows = WIN * size
    grad_state = pl.pallas_call(
        edge_kernel,
        grid=(2,),
        out_shape=shape((nodes, features), bf16),
        in_specs=[
            pl.BlockSpec(memory_space=pl.ANY),
            pl.BlockSpec((WIN, features, size), lambda side: (side, 0, 0)),
            pl.BlockSpec((WIN, features, size), lambda side: (side, 0, 0)),
            pl.BlockSpec((WIN, features, size), lambda side: (0, 0, 0)),
            pl.BlockSpec((WIN, features, size), lambda side: (0, 0, 0)),
            pl.BlockSpec((features, features), lambda side: (0, 0)),
        ],
        out_specs=pl.BlockSpec(
            (edge_rows, features), lambda side: (side * (nodes // edge_rows - 1), 0)
        ),
        input_output_aliases={0: 0},
        name="edge_state",
    )(grad_state, edge_msg, edge_state, owed_above, owed_below, w_msg)

    whole = lax.all_to_all(summed(line, dom, "sum_feat"), "dom", 0, 0, tiled=True)
    g_msg, g_first, g_b_first, g_second, g_b_second, g_gain = pl.pallas_call(
        functools.partial(unpack_kernel, chunk),
        out_shape=(
            shape((features, features), f32),
            shape((2 * features, features), f32),
            shape((1, features), f32),
            shape((features, features), f32),
            shape((1, features), f32),
            shape((1, features), f32),
        ),
        in_specs=[in_vmem()],
        out_specs=(in_vmem(),) * 6,
        name="unpack",
    )(whole)
    flat = lambda vector: vector.reshape(features)
    return (
        updated,
        grad_state,
        g_msg,
        g_first,
        flat(g_b_first),
        g_second,
        flat(g_b_second),
        flat(g_gain),
    )


def solution(mesh):
    split = P(AXES, None)
    return jax.shard_map(
        shards,
        mesh=mesh,
        in_specs=(split, P(), P(), P(), P(), P(), P(), split, P(AXES, None, None, None), split),
        out_specs=(split, split, P(), P(), P(), P(), P(), P()),
        check_vma=False,
    )
```

```python
import functools
import math

import jax
import jax.numpy as jnp
from jax import lax
from jax.experimental import pallas as pl
from jax.experimental.pallas import tpu as pltpu
from jax.sharding import PartitionSpec as P

WIN = 2
epsilon = 1e-05
AXES = ("dom", "feat")
SENT = jnp.bfloat16
ONES_ROWS = 16
BIAS_ROWS = 8


def dot(left, right):
    return jnp.dot(left, right, preferred_element_type=jnp.float32)


def dot_nt(left, right):
    return lax.dot_general(
        left, right, (((1,), (1,)), ((), ())), preferred_element_type=jnp.float32
    )


def column(row_ref, width):
    features = row_ref.shape[1]
    return jnp.broadcast_to(row_ref[...], (width, features)).T


def layer_kernel(
    grad_scale,
    chunk,
    place_ref,
    got_even_ref,
    got_odd_ref,
    state_hbm,
    cot_hbm,
    counts_hbm,
    w_msg_hbm,
    w_first_hbm,
    b_first_hbm,
    w_second_hbm,
    b_second_hbm,
    gain_hbm,
    updated_hbm,
    grad_state_hbm,
    grads_ref,
    send_even_ref,
    send_odd_ref,
    edge_msg_ref,
    edge_state_ref,
    state_ref,
    cot_ref,
    counts_ref,
    w_msg_ref,
    w_first_ref,
    b_first_ref,
    w_second_ref,
    b_second_ref,
    gain_ref,
    updated_ref,
    grad_state_ref,
    states,
    messages,
    counts,
    ext_grad,
    direct,
    joined,
    d_hidden,
    active,
    d_norm,
    arrived,
    left,
):
    blocks, tiles, size, _ = counts_ref.shape
    features = state_ref.shape[1]
    ext = blocks + 2 * WIN
    group = 2
    width = group * size

    smalls = (
        (w_msg_hbm, w_msg_ref),
        (w_first_hbm, w_first_ref),
        (b_first_hbm, b_first_ref),
        (w_second_hbm, w_second_ref),
        (b_second_hbm, b_second_ref),
        (gain_hbm, gain_ref),
    )
    state_copy = pltpu.make_async_copy(state_hbm, state_ref, arrived.at[0])
    cot_copy = pltpu.make_async_copy(cot_hbm, cot_ref, arrived.at[1])
    small_copies = [
        pltpu.make_async_copy(source, target, arrived.at[2 + k])
        for k, (source, target) in enumerate(smalls)
    ]
    count_copies = [
        pltpu.make_async_copy(
            counts_hbm.at[pl.ds(b, group)],
            counts_ref.at[pl.ds(b, group)],
            arrived.at[2 + len(smalls) + b // group],
        )
        for b in range(0, blocks, group)
    ]
    for copy in [state_copy] + small_copies + count_copies[:1] + [cot_copy] + count_copies[1:]:
        copy.start()
    odd = place_ref[blocks * tiles] == 1
    got_even, got_odd = got_even_ref[...], got_odd_ref[...]
    below = jnp.where(odd, got_even, got_odd)
    above = jnp.where(odd, got_odd, got_even)
    state_copy.wait()
    for copy in small_copies:
        copy.wait()

    w_msg = w_msg_ref[...]
    w_msg_t = w_msg.T
    w_first = w_first_ref[...]
    w_first_t = jnp.concatenate([w_first[:features].T, w_first[features:].T], axis=1)
    w_second = w_second_ref[...]
    w_second_t = w_second.T
    b_first = column(b_first_ref, width)
    b_second = column(b_second_ref, width)
    gain = column(gain_ref, width)

    for slot in range(ext):
        if slot < WIN:
            block = below[slot * size : (slot + 1) * size]
        elif slot < blocks + WIN:
            block = state_ref[pl.ds((slot - WIN) * size, size), :]
        else:
            block = above[(slot - WIN - blocks) * size : (slot - WIN - blocks + 1) * size]
        state_t = block.T
        states[:, pl.ds(slot * size, size)] = state_t
        messages[slot] = dot(w_msg_t, state_t).astype(jnp.bfloat16)
    ext_grad[...] = jnp.zeros_like(ext_grad)
    joined[pl.ds(2 * features, ONES_ROWS), :] = jnp.ones((ONES_ROWS, blocks * size), jnp.bfloat16)
    active[pl.ds(features, ONES_ROWS), :] = jnp.ones((ONES_ROWS, blocks * size), jnp.bfloat16)

    gain_terms = jnp.zeros((features, size), jnp.float32)
    for first in range(0, blocks, group):
        rows = range(first, first + group)
        place = pl.ds(first * size, width)
        count_copies[first // group].wait()
        if first == 0:
            cot_copy.wait()
        slots = {}
        parts = []
        for b in rows:
            own = place_ref[b * tiles]
            slots[b] = [b + WIN] + [
                place_ref[b * tiles + t] - own + (b + WIN) for t in range(1, tiles)
            ]
            tile_row = jnp.concatenate(
                [counts_ref[b, t].astype(jnp.float32).astype(jnp.bfloat16) for t in range(tiles)],
                axis=1,
            )
            counts[b] = tile_row
            picked = jnp.concatenate([messages[slot] for slot in slots[b]], axis=1)
            parts.append(dot_nt(picked, tile_row).astype(jnp.bfloat16))
        state_t = states[:, pl.ds((first + WIN) * size, width)]
        joined_t = jnp.concatenate([state_t, jnp.concatenate(parts, axis=1)], axis=0)
        joined[pl.ds(0, 2 * features), place] = joined_t
        pre_hidden = dot(w_first_t, joined_t) + b_first
        sigmoid = 1.0 / (1.0 + jnp.exp(-pre_hidden))
        active_t = (pre_hidden * sigmoid).astype(jnp.bfloat16)
        active[pl.ds(0, features), place] = active_t
        slope = sigmoid * (1.0 + pre_hidden * (1.0 - sigmoid))
        pre_norm = dot(w_second_t, active_t) + b_second
        centred = pre_norm - jnp.mean(pre_norm, axis=0, keepdims=True)
        inv_std = lax.rsqrt(jnp.mean(centred * centred, axis=0, keepdims=True) + epsilon)
        normed = centred * inv_std
        updated_t = (state_t.astype(jnp.float32) + gain * normed).astype(jnp.bfloat16)
        cot_t = jnp.concatenate(
            [cot_ref[pl.ds(b * size, size), :].T for b in rows], axis=1
        ).astype(jnp.float32)
        terms = cot_t * normed
        q = cot_t * gain
        mean_q = jnp.mean(q, axis=0, keepdims=True)
        mean_qn = jnp.mean(q * normed, axis=0, keepdims=True)
        d_norm_t = (inv_std * (q - mean_q - normed * mean_qn)).astype(jnp.bfloat16)
        d_norm[:, place] = d_norm_t
        d_hidden_t = (dot(w_second, d_norm_t) * slope).astype(jnp.bfloat16)
        d_hidden[:, place] = d_hidden_t
        d_joined = dot(w_first, d_hidden_t)
        direct[:, place] = cot_t + d_joined[:features]
        d_aggregate = d_joined[features:].astype(jnp.bfloat16)
        for k, b in enumerate(rows):
            lanes = slice(k * size, (k + 1) * size)
            updated_ref[pl.ds(b * size, size), :] = updated_t[:, lanes].T
            gain_terms = gain_terms + terms[:, lanes]
            owed = dot(d_aggregate[:, lanes], counts[b])
            for t, slot in enumerate(slots[b]):
                ext_grad[slot] += owed[:, t * size : (t + 1) * size]

    updated_copy = pltpu.make_async_copy(updated_ref, updated_hbm, left.at[0])
    updated_copy.start()
    d_msg = [ext_grad[slot].astype(jnp.bfloat16) for slot in range(ext)]
    for k in range(WIN):
        to_below, to_above = d_msg[k], d_msg[blocks + WIN + k]
        send_even_ref[k] = jnp.where(odd, to_below, to_above)
        send_odd_ref[k] = jnp.where(odd, to_above, to_below)
        for e, b in ((k, k), (WIN + k, blocks - WIN + k)):
            edge_msg_ref[e] = ext_grad[b + WIN]
            edge_state_ref[e] = direct[:, pl.ds(b * size, size)]
    inner = pl.ds(WIN * size, (blocks - 2 * WIN) * size)
    for b in range(WIN, blocks - WIN):
        total = direct[:, pl.ds(b * size, size)] + dot(w_msg, d_msg[b + WIN])
        grad_state_ref[pl.ds(b * size, size), :] = total.astype(jnp.bfloat16).T
    grad_state_copy = pltpu.make_async_copy(
        grad_state_ref.at[inner], grad_state_hbm.at[inner], left.at[1]
    )
    grad_state_copy.start()

    sent = grads_ref.dtype
    first_sums = dot_nt(joined[...], d_hidden[...]) * grad_scale
    second_sums = dot_nt(active[...], d_norm[...]) * grad_scale
    msg_sums = dot_nt(states[...], jnp.concatenate(d_msg, axis=1)) * grad_scale
    gain_sum = jnp.sum(gain_terms.T, axis=0, keepdims=True) * grad_scale
    bias = jnp.concatenate(
        [
            first_sums[2 * features : 2 * features + 1],
            second_sums[features : features + 1],
            gain_sum,
            jnp.zeros((BIAS_ROWS - 3, features), jnp.float32),
        ],
        axis=0,
    )
    sums = jnp.concatenate(
        [first_sums[: 2 * features], second_sums[:features], msg_sums], axis=0
    ).astype(sent)
    bias = bias.astype(sent)
    nothing = jnp.zeros((chunk, features), sent)
    for k in range(grads_ref.shape[0]):
        part = sums[k * chunk : (k + 1) * chunk] if k * chunk < sums.shape[0] else nothing
        tail = bias if k == 0 else nothing[:BIAS_ROWS]
        grads_ref[k] = jnp.concatenate([part, tail], axis=0)
    updated_copy.wait()
    grad_state_copy.wait()


def edge_kernel(
    odd_ref, grad_state_ref, msg_ref, state_ref, even_ref, odd_part_ref, w_msg_ref, out_ref
):
    del grad_state_ref
    size = msg_ref.shape[2]
    from_odd_pair = (pl.program_id(0) == 0) != (odd_ref[0] == 1)
    w_msg = w_msg_ref[...]
    for k in range(WIN):
        arrived = jnp.where(from_odd_pair, odd_part_ref[k], even_ref[k]).astype(jnp.float32)
        d_msg = (msg_ref[k] + arrived).astype(jnp.bfloat16)
        total = state_ref[k] + dot(w_msg, d_msg)
        out_ref[pl.ds(k * size, size), :] = total.astype(jnp.bfloat16).T


def unpack_kernel(chunk, parts_ref, msg_ref, first_ref, b_first_ref, second_ref, b_second_ref, gain_ref):
    place = 0
    for ref in (first_ref, second_ref, msg_ref):
        done = 0
        while done < ref.shape[0]:
            k, row = divmod(place, chunk)
            count = min(chunk - row, ref.shape[0] - done)
            ref[pl.ds(done, count), :] = parts_ref[k, pl.ds(row, count), :].astype(jnp.float32)
            done += count
            place += count
    bias = parts_ref[0, pl.ds(chunk, BIAS_ROWS), :].astype(jnp.float32)
    b_first_ref[...] = bias[0:1]
    b_second_ref[...] = bias[1:2]
    gain_ref[...] = bias[2:3]


def swapped(block, parity):
    last = lax.axis_size(AXES) - 1
    lower = range(parity, last, 2)
    return lax.ppermute(block, AXES, [(i, i + 1) for i in lower] + [(i + 1, i) for i in lower])


kept = pltpu.with_memory_space_constraint


def in_vmem():
    return pl.BlockSpec(memory_space=pltpu.VMEM)


def shards(
    node_state,
    w_msg,
    w_first,
    b_first,
    w_second,
    b_second,
    ln_gain,
    col_index,
    edge_counts,
    cotangent,
):
    nodes, features = node_state.shape
    blocks, tiles, size, _ = edge_counts.shape
    ext = blocks + 2 * WIN
    devices = lax.axis_size(AXES)
    grad_scale = 1.0 / math.sqrt(nodes * devices)
    chunk = -(-4 * features // (devices * 8)) * 8
    bf16, f32 = jnp.bfloat16, jnp.float32
    shape = jax.ShapeDtypeStruct
    in_hbm = pl.BlockSpec(memory_space=pltpu.HBM)
    in_smem = pl.BlockSpec(memory_space=pltpu.SMEM)

    edge_rows = WIN * size
    odd = lax.axis_index(AXES) % 2
    side = lambda upper: lax.dynamic_slice_in_dim(
        node_state, upper * (nodes - edge_rows), edge_rows, 0
    )
    got_odd = swapped(side(odd), 1)
    got_even = swapped(side(1 - odd), 0)
    odd = odd.astype(jnp.int32).reshape(1)
    place = jnp.concatenate([col_index.reshape(-1), odd])
    row = lambda vector: vector.reshape(1, features)

    updated, grad_state, grads, send_even, send_odd, edge_msg, edge_state = pl.pallas_call(
        functools.partial(layer_kernel, grad_scale, chunk),
        out_shape=(
            pltpu.HBM((nodes, features), bf16),
            pltpu.HBM((nodes, features), bf16),
            pltpu.VMEM((devices, chunk + BIAS_ROWS, features), SENT),
            pltpu.VMEM((WIN, features, size), bf16),
            pltpu.VMEM((WIN, features, size), bf16),
            pltpu.VMEM((2 * WIN, features, size), f32),
            pltpu.VMEM((2 * WIN, features, size), f32),
        ),
        in_specs=[in_smem] + [in_vmem()] * 2 + [in_hbm] * 9,
        out_specs=(in_hbm,) * 2 + (in_vmem(),) * 5,
        scratch_shapes=[
            pltpu.VMEM((nodes, features), bf16),
            pltpu.VMEM((nodes, features), bf16),
            pltpu.VMEM(edge_counts.shape, jnp.int32),
            pltpu.VMEM((features, features), bf16),
            pltpu.VMEM((2 * features, features), bf16),
            pltpu.VMEM((1, features), f32),
            pltpu.VMEM((features, features), bf16),
            pltpu.VMEM((1, features), f32),
            pltpu.VMEM((1, features), f32),
            pltpu.VMEM((nodes, features), bf16),
            pltpu.VMEM((nodes, features), bf16),
            pltpu.VMEM((features, ext * size), bf16),
            pltpu.VMEM((ext, features, size), bf16),
            pltpu.VMEM((blocks, size, tiles * size), bf16),
            pltpu.VMEM((ext, features, size), f32),
            pltpu.VMEM((features, nodes), f32),
            pltpu.VMEM((2 * features + ONES_ROWS, nodes), bf16),
            pltpu.VMEM((features, nodes), bf16),
            pltpu.VMEM((features + ONES_ROWS, nodes), bf16),
            pltpu.VMEM((features, nodes), bf16),
            pltpu.SemaphoreType.DMA((8 + blocks // 2,)),
            pltpu.SemaphoreType.DMA((2,)),
        ],
        compiler_params=pltpu.CompilerParams(vmem_limit_bytes=24 * 1024 * 1024),
        cost_estimate=pl.CostEstimate(
            flops=1_000_000_000, bytes_accessed=5_000_000, transcendentals=200_000
        ),
        name="layer",
    )(
        place,
        kept(got_even, pltpu.VMEM),
        kept(got_odd, pltpu.VMEM),
        kept(node_state, pltpu.HBM),
        kept(cotangent, pltpu.HBM),
        kept(edge_counts, pltpu.HBM),
        kept(w_msg, pltpu.HBM),
        kept(w_first, pltpu.HBM),
        kept(row(b_first), pltpu.HBM),
        kept(w_second, pltpu.HBM),
        kept(row(b_second), pltpu.HBM),
        kept(row(ln_gain), pltpu.HBM),
    )

    parts = lax.all_to_all(grads, AXES, 0, 0, tiled=True)
    owed_odd = swapped(send_odd, 1)
    owed_even = swapped(send_even, 0)
    own_sum = jnp.sum(parts.astype(f32), axis=0)
    own_sum, owed_odd, owed_even = lax.optimization_barrier((own_sum, owed_odd, owed_even))
    spread = jnp.broadcast_to(own_sum.astype(SENT)[None], parts.shape)

    whole_block = lambda k: (0, 0, 0)
    grad_state = pl.pallas_call(
        edge_kernel,
        grid=(2,),
        out_shape=shape((nodes, features), bf16),
        in_specs=[
            in_smem,
            pl.BlockSpec(memory_space=pl.ANY),
            pl.BlockSpec((WIN, features, size), lambda k: (k, 0, 0)),
            pl.BlockSpec((WIN, features, size), lambda k: (k, 0, 0)),
            pl.BlockSpec((WIN, features, size), whole_block),
            pl.BlockSpec((WIN, features, size), whole_block),
            pl.BlockSpec((features, features), lambda k: (0, 0)),
        ],
        out_specs=pl.BlockSpec(
            (edge_rows, features), lambda k: (k * (nodes // edge_rows - 1), 0)
        ),
        input_output_aliases={1: 0},
        name="edge_state",
    )(odd, grad_state, edge_msg, edge_state, owed_even, owed_odd, w_msg)

    whole = lax.all_to_all(spread, AXES, 0, 0, tiled=True)
    g_msg, g_first, g_b_first, g_second, g_b_second, g_gain = pl.pallas_call(
        functools.partial(unpack_kernel, chunk),
        out_shape=(
            shape((features, features), f32),
            shape((2 * features, features), f32),
            shape((1, features), f32),
            shape((features, features), f32),
            shape((1, features), f32),
            shape((1, features), f32),
        ),
        in_specs=[in_vmem()],
        out_specs=(in_vmem(),) * 6,
        name="unpack",
    )(whole)
    flat = lambda vector: vector.reshape(features)
    return (
        updated,
        grad_state,
        g_msg,
        g_first,
        flat(g_b_first),
        g_second,
        flat(g_b_second),
        flat(g_gain),
    )


def solution(mesh):
    split = P(AXES, None)
    return jax.shard_map(
        shards,
        mesh=mesh,
        in_specs=(split, P(), P(), P(), P(), P(), P(), split, P(AXES, None, None, None), split),
        out_specs=(split, split, P(), P(), P(), P(), P(), P()),
        check_vma=False,
    )
```

```python
import functools
import math

import jax
import jax.numpy as jnp
from jax import lax
from jax.experimental import pallas as pl
from jax.experimental.pallas import tpu as pltpu
from jax.sharding import PartitionSpec as P

WIN = 2
epsilon = 1e-05
AXES = ("dom", "feat")
SENT = jnp.bfloat16
ONES_ROWS = 16
BIAS_ROWS = 8


def dot(left, right):
    return jnp.dot(left, right, preferred_element_type=jnp.float32)


def dot_nt(left, right):
    return lax.dot_general(
        left, right, (((1,), (1,)), ((), ())), preferred_element_type=jnp.float32
    )


def column(row_ref, width):
    features = row_ref.shape[1]
    return jnp.broadcast_to(row_ref[...], (width, features)).T


def layer_kernel(
    grad_scale,
    chunk,
    place_ref,
    got_even_ref,
    got_odd_ref,
    state_hbm,
    cot_hbm,
    counts_hbm,
    w_msg_hbm,
    w_first_hbm,
    b_first_hbm,
    w_second_hbm,
    b_second_hbm,
    gain_hbm,
    updated_hbm,
    grad_state_hbm,
    grads_ref,
    send_even_ref,
    send_odd_ref,
    edge_msg_ref,
    edge_state_ref,
    state_ref,
    cot_ref,
    counts_ref,
    w_msg_ref,
    w_first_ref,
    b_first_ref,
    w_second_ref,
    b_second_ref,
    gain_ref,
    updated_ref,
    grad_state_ref,
    states,
    messages,
    counts,
    ext_grad,
    direct,
    joined,
    d_hidden,
    active,
    d_norm,
    arrived,
    left,
):
    blocks, tiles, size, _ = counts_ref.shape
    features = state_ref.shape[1]
    ext = blocks + 2 * WIN
    group = 2
    width = group * size

    smalls = (
        (w_msg_hbm, w_msg_ref),
        (w_first_hbm, w_first_ref),
        (b_first_hbm, b_first_ref),
        (w_second_hbm, w_second_ref),
        (b_second_hbm, b_second_ref),
        (gain_hbm, gain_ref),
    )
    state_copy = pltpu.make_async_copy(state_hbm, state_ref, arrived.at[0])
    cot_copy = pltpu.make_async_copy(cot_hbm, cot_ref, arrived.at[1])
    small_copies = [
        pltpu.make_async_copy(source, target, arrived.at[2 + k])
        for k, (source, target) in enumerate(smalls)
    ]
    count_copies = [
        pltpu.make_async_copy(
            counts_hbm.at[pl.ds(b, group)],
            counts_ref.at[pl.ds(b, group)],
            arrived.at[2 + len(smalls) + b // group],
        )
        for b in range(0, blocks, group)
    ]
    for copy in [state_copy] + small_copies + count_copies[:1] + [cot_copy] + count_copies[1:]:
        copy.start()
    odd = place_ref[blocks * tiles] == 1
    got_even, got_odd = got_even_ref[...], got_odd_ref[...]
    below = jnp.where(odd, got_even, got_odd)
    above = jnp.where(odd, got_odd, got_even)
    state_copy.wait()
    for copy in small_copies:
        copy.wait()

    w_msg = w_msg_ref[...]
    w_msg_t = w_msg.T
    w_first = w_first_ref[...]
    w_first_t = jnp.concatenate([w_first[:features].T, w_first[features:].T], axis=1)
    w_second = w_second_ref[...]
    w_second_t = w_second.T
    b_first = column(b_first_ref, width)
    b_second = column(b_second_ref, width)
    gain = column(gain_ref, width)

    for slot in range(ext):
        if slot < WIN:
            block = below[slot * size : (slot + 1) * size]
        elif slot < blocks + WIN:
            block = state_ref[pl.ds((slot - WIN) * size, size), :]
        else:
            block = above[(slot - WIN - blocks) * size : (slot - WIN - blocks + 1) * size]
        state_t = block.T
        states[:, pl.ds(slot * size, size)] = state_t
        messages[slot] = dot(w_msg_t, state_t).astype(jnp.bfloat16)
    ext_grad[...] = jnp.zeros_like(ext_grad)
    joined[pl.ds(2 * features, ONES_ROWS), :] = jnp.ones((ONES_ROWS, blocks * size), jnp.bfloat16)
    active[pl.ds(features, ONES_ROWS), :] = jnp.ones((ONES_ROWS, blocks * size), jnp.bfloat16)

    gain_terms = jnp.zeros((features, size), jnp.float32)
    for first in range(0, blocks, group):
        rows = range(first, first + group)
        place = pl.ds(first * size, width)
        count_copies[first // group].wait()
        if first == 0:
            cot_copy.wait()
        slots = {}
        parts = []
        for b in rows:
            own = place_ref[b * tiles]
            slots[b] = [b + WIN] + [
                place_ref[b * tiles + t] - own + (b + WIN) for t in range(1, tiles)
            ]
            tile_row = jnp.concatenate(
                [counts_ref[b, t].astype(jnp.float32).astype(jnp.bfloat16) for t in range(tiles)],
                axis=1,
            )
            counts[b] = tile_row
            picked = jnp.concatenate([messages[slot] for slot in slots[b]], axis=1)
            parts.append(dot_nt(picked, tile_row).astype(jnp.bfloat16))
        state_t = states[:, pl.ds((first + WIN) * size, width)]
        joined_t = jnp.concatenate([state_t, jnp.concatenate(parts, axis=1)], axis=0)
        joined[pl.ds(0, 2 * features), place] = joined_t
        pre_hidden = dot(w_first_t, joined_t) + b_first
        sigmoid = 1.0 / (1.0 + jnp.exp(-pre_hidden))
        active_t = (pre_hidden * sigmoid).astype(jnp.bfloat16)
        active[pl.ds(0, features), place] = active_t
        slope = sigmoid * (1.0 + pre_hidden * (1.0 - sigmoid))
        pre_norm = dot(w_second_t, active_t) + b_second
        centred = pre_norm - jnp.mean(pre_norm, axis=0, keepdims=True)
        inv_std = lax.rsqrt(jnp.mean(centred * centred, axis=0, keepdims=True) + epsilon)
        normed = centred * inv_std
        updated_t = (state_t.astype(jnp.float32) + gain * normed).astype(jnp.bfloat16)
        cot_t = jnp.concatenate(
            [cot_ref[pl.ds(b * size, size), :].T for b in rows], axis=1
        ).astype(jnp.float32)
        terms = cot_t * normed
        q = cot_t * gain
        mean_q = jnp.mean(q, axis=0, keepdims=True)
        mean_qn = jnp.mean(q * normed, axis=0, keepdims=True)
        d_norm_t = (inv_std * (q - mean_q - normed * mean_qn)).astype(jnp.bfloat16)
        d_norm[:, place] = d_norm_t
        d_hidden_t = (dot(w_second, d_norm_t) * slope).astype(jnp.bfloat16)
        d_hidden[:, place] = d_hidden_t
        d_joined = dot(w_first, d_hidden_t)
        direct[:, place] = cot_t + d_joined[:features]
        d_aggregate = d_joined[features:].astype(jnp.bfloat16)
        for k, b in enumerate(rows):
            lanes = slice(k * size, (k + 1) * size)
            updated_ref[pl.ds(b * size, size), :] = updated_t[:, lanes].T
            gain_terms = gain_terms + terms[:, lanes]
            owed = dot(d_aggregate[:, lanes], counts[b])
            for t, slot in enumerate(slots[b]):
                ext_grad[slot] += owed[:, t * size : (t + 1) * size]

    updated_copy = pltpu.make_async_copy(updated_ref, updated_hbm, left.at[0])
    updated_copy.start()
    d_msg = [ext_grad[slot].astype(jnp.bfloat16) for slot in range(ext)]
    for k in range(WIN):
        to_below, to_above = d_msg[k], d_msg[blocks + WIN + k]
        send_even_ref[k] = jnp.where(odd, to_below, to_above)
        send_odd_ref[k] = jnp.where(odd, to_above, to_below)
        for e, b in ((k, k), (WIN + k, blocks - WIN + k)):
            edge_msg_ref[e] = ext_grad[b + WIN]
            edge_state_ref[e] = direct[:, pl.ds(b * size, size)]
    inner = pl.ds(WIN * size, (blocks - 2 * WIN) * size)
    for b in range(WIN, blocks - WIN):
        total = direct[:, pl.ds(b * size, size)] + dot(w_msg, d_msg[b + WIN])
        grad_state_ref[pl.ds(b * size, size), :] = total.astype(jnp.bfloat16).T
    grad_state_copy = pltpu.make_async_copy(
        grad_state_ref.at[inner], grad_state_hbm.at[inner], left.at[1]
    )
    grad_state_copy.start()

    sent = grads_ref.dtype
    first_sums = dot_nt(joined[...], d_hidden[...]) * grad_scale
    second_sums = dot_nt(active[...], d_norm[...]) * grad_scale
    msg_sums = dot_nt(states[...], jnp.concatenate(d_msg, axis=1)) * grad_scale
    gain_sum = jnp.sum(gain_terms.T, axis=0, keepdims=True) * grad_scale
    bias = jnp.concatenate(
        [
            first_sums[2 * features : 2 * features + 1],
            second_sums[features : features + 1],
            gain_sum,
        ],
        axis=0,
    )
    bias_high = bias.astype(sent)
    bias_low = (bias - bias_high.astype(jnp.float32)).astype(sent)
    bias = jnp.concatenate(
        [bias_high, bias_low, jnp.zeros((BIAS_ROWS - 6, features), sent)], axis=0
    )
    sums = jnp.concatenate(
        [first_sums[: 2 * features], second_sums[:features], msg_sums], axis=0
    ).astype(sent)
    nothing = jnp.zeros((chunk, features), sent)
    for k in range(grads_ref.shape[0]):
        part = sums[k * chunk : (k + 1) * chunk] if k * chunk < sums.shape[0] else nothing
        grads_ref[k] = jnp.concatenate([part, bias], axis=0)
    updated_copy.wait()
    grad_state_copy.wait()


def edge_kernel(
    odd_ref,
    grad_state_ref,
    msg_ref,
    state_ref,
    even_ref,
    odd_part_ref,
    w_msg_ref,
    bias_ref,
    out_ref,
    b_first_ref,
    b_second_ref,
    gain_ref,
):
    del grad_state_ref
    size = msg_ref.shape[2]
    from_odd_pair = (pl.program_id(0) == 0) != (odd_ref[0] == 1)
    w_msg = w_msg_ref[...]
    for k in range(WIN):
        arrived = jnp.where(from_odd_pair, odd_part_ref[k], even_ref[k]).astype(jnp.float32)
        d_msg = (msg_ref[k] + arrived).astype(jnp.bfloat16)
        total = state_ref[k] + dot(w_msg, d_msg)
        out_ref[pl.ds(k * size, size), :] = total.astype(jnp.bfloat16).T
    for k, ref in enumerate((b_first_ref, b_second_ref, gain_ref)):
        ref[...] = bias_ref[pl.ds(k, 1), :] + bias_ref[pl.ds(k + 3, 1), :]


def sum_kernel(parts_ref, spread_ref, bias_ref):
    total = parts_ref[0].astype(jnp.float32)
    for k in range(1, parts_ref.shape[0]):
        total = total + parts_ref[k].astype(jnp.float32)
    chunk = spread_ref.shape[1]
    weights = total[:chunk].astype(spread_ref.dtype)
    for k in range(spread_ref.shape[0]):
        spread_ref[k] = weights
    bias_ref[...] = total[chunk:]


def unpack_kernel(rows_ref, msg_ref, first_ref, second_ref):
    place = 0
    for ref in (first_ref, second_ref, msg_ref):
        count = ref.shape[0]
        ref[...] = rows_ref[pl.ds(place, count), :].astype(jnp.float32)
        place += count


def swapped(block, parity):
    last = lax.axis_size(AXES) - 1
    lower = range(parity, last, 2)
    return lax.ppermute(block, AXES, [(i, i + 1) for i in lower] + [(i + 1, i) for i in lower])


kept = pltpu.with_memory_space_constraint


def in_vmem():
    return pl.BlockSpec(memory_space=pltpu.VMEM)


def shards(
    node_state,
    w_msg,
    w_first,
    b_first,
    w_second,
    b_second,
    ln_gain,
    col_index,
    edge_counts,
    cotangent,
):
    nodes, features = node_state.shape
    blocks, tiles, size, _ = edge_counts.shape
    ext = blocks + 2 * WIN
    devices = lax.axis_size(AXES)
    grad_scale = 1.0 / math.sqrt(nodes * devices)
    chunk = -(-4 * features // (devices * 8)) * 8
    bf16, f32 = jnp.bfloat16, jnp.float32
    shape = jax.ShapeDtypeStruct
    in_hbm = pl.BlockSpec(memory_space=pltpu.HBM)
    in_smem = pl.BlockSpec(memory_space=pltpu.SMEM)

    edge_rows = WIN * size
    odd = lax.axis_index(AXES) % 2
    side = lambda upper: lax.dynamic_slice_in_dim(
        node_state, upper * (nodes - edge_rows), edge_rows, 0
    )
    got_odd = swapped(side(odd), 1)
    got_even = swapped(side(1 - odd), 0)
    odd = odd.astype(jnp.int32).reshape(1)
    place = jnp.concatenate([col_index.reshape(-1), odd])
    row = lambda vector: vector.reshape(1, features)

    updated, grad_state, grads, send_even, send_odd, edge_msg, edge_state = pl.pallas_call(
        functools.partial(layer_kernel, grad_scale, chunk),
        out_shape=(
            pltpu.HBM((nodes, features), bf16),
            pltpu.HBM((nodes, features), bf16),
            pltpu.VMEM((devices, chunk + BIAS_ROWS, features), SENT),
            pltpu.VMEM((WIN, features, size), bf16),
            pltpu.VMEM((WIN, features, size), bf16),
            pltpu.VMEM((2 * WIN, features, size), f32),
            pltpu.VMEM((2 * WIN, features, size), f32),
        ),
        in_specs=[in_smem] + [in_vmem()] * 2 + [in_hbm] * 9,
        out_specs=(in_hbm,) * 2 + (in_vmem(),) * 5,
        scratch_shapes=[
            pltpu.VMEM((nodes, features), bf16),
            pltpu.VMEM((nodes, features), bf16),
            pltpu.VMEM(edge_counts.shape, jnp.int32),
            pltpu.VMEM((features, features), bf16),
            pltpu.VMEM((2 * features, features), bf16),
            pltpu.VMEM((1, features), f32),
            pltpu.VMEM((features, features), bf16),
            pltpu.VMEM((1, features), f32),
            pltpu.VMEM((1, features), f32),
            pltpu.VMEM((nodes, features), bf16),
            pltpu.VMEM((nodes, features), bf16),
            pltpu.VMEM((features, ext * size), bf16),
            pltpu.VMEM((ext, features, size), bf16),
            pltpu.VMEM((blocks, size, tiles * size), bf16),
            pltpu.VMEM((ext, features, size), f32),
            pltpu.VMEM((features, nodes), f32),
            pltpu.VMEM((2 * features + ONES_ROWS, nodes), bf16),
            pltpu.VMEM((features, nodes), bf16),
            pltpu.VMEM((features + ONES_ROWS, nodes), bf16),
            pltpu.VMEM((features, nodes), bf16),
            pltpu.SemaphoreType.DMA((8 + blocks // 2,)),
            pltpu.SemaphoreType.DMA((2,)),
        ],
        compiler_params=pltpu.CompilerParams(vmem_limit_bytes=24 * 1024 * 1024),
        cost_estimate=pl.CostEstimate(
            flops=1_000_000_000, bytes_accessed=5_000_000, transcendentals=200_000
        ),
        name="layer",
    )(
        place,
        kept(got_even, pltpu.VMEM),
        kept(got_odd, pltpu.VMEM),
        kept(node_state, pltpu.HBM),
        kept(cotangent, pltpu.HBM),
        kept(edge_counts, pltpu.HBM),
        kept(w_msg, pltpu.HBM),
        kept(w_first, pltpu.HBM),
        kept(row(b_first), pltpu.HBM),
        kept(w_second, pltpu.HBM),
        kept(row(b_second), pltpu.HBM),
        kept(row(ln_gain), pltpu.HBM),
    )

    parts = lax.all_to_all(grads, AXES, 0, 0, tiled=True)
    owed_odd = swapped(send_odd, 1)
    owed_even = swapped(send_even, 0)
    small_limit = pltpu.CompilerParams(vmem_limit_bytes=16 * 1024 * 1024)
    spread, bias = pl.pallas_call(
        sum_kernel,
        out_shape=(
            pltpu.VMEM((devices, chunk, features), SENT),
            pltpu.VMEM((BIAS_ROWS, features), f32),
        ),
        in_specs=[in_vmem()],
        out_specs=(in_vmem(),) * 2,
        compiler_params=small_limit,
        name="sum",
    )(kept(parts, pltpu.VMEM))
    spread, owed_odd, owed_even = lax.optimization_barrier((spread, owed_odd, owed_even))

    whole_block = lambda k: (0, 0, 0)
    one_row = pl.BlockSpec((1, features), lambda k: (0, 0))
    grad_state, g_b_first, g_b_second, g_gain = pl.pallas_call(
        edge_kernel,
        grid=(2,),
        out_shape=(
            shape((nodes, features), bf16),
            shape((1, features), f32),
            shape((1, features), f32),
            shape((1, features), f32),
        ),
        in_specs=[
            in_smem,
            pl.BlockSpec(memory_space=pl.ANY),
            pl.BlockSpec((WIN, features, size), lambda k: (k, 0, 0)),
            pl.BlockSpec((WIN, features, size), lambda k: (k, 0, 0)),
            pl.BlockSpec((WIN, features, size), whole_block),
            pl.BlockSpec((WIN, features, size), whole_block),
            pl.BlockSpec((features, features), lambda k: (0, 0)),
            pl.BlockSpec((BIAS_ROWS, features), lambda k: (0, 0)),
        ],
        out_specs=(
            pl.BlockSpec((edge_rows, features), lambda k: (k * (nodes // edge_rows - 1), 0)),
            one_row,
            one_row,
            one_row,
        ),
        input_output_aliases={1: 0},
        compiler_params=small_limit,
        name="edge_state",
    )(
        odd,
        grad_state,
        kept(edge_msg, pltpu.VMEM),
        kept(edge_state, pltpu.VMEM),
        kept(owed_even, pltpu.VMEM),
        kept(owed_odd, pltpu.VMEM),
        w_msg,
        kept(bias, pltpu.VMEM),
    )

    whole = lax.all_to_all(spread, AXES, 0, 0, tiled=True)
    rows = whole.reshape(devices * chunk, features)
    g_msg, g_first, g_second = pl.pallas_call(
        unpack_kernel,
        out_shape=(
            shape((features, features), f32),
            shape((2 * features, features), f32),
            shape((features, features), f32),
        ),
        in_specs=[in_vmem()],
        out_specs=(in_vmem(),) * 3,
        compiler_params=small_limit,
        name="unpack",
    )(kept(rows, pltpu.VMEM))
    flat = lambda vector: vector.reshape(features)
    return (
        updated,
        grad_state,
        g_msg,
        g_first,
        flat(g_b_first),
        g_second,
        flat(g_b_second),
        flat(g_gain),
    )


def solution(mesh):
    split = P(AXES, None)
    return jax.shard_map(
        shards,
        mesh=mesh,
        in_specs=(split, P(), P(), P(), P(), P(), P(), split, P(AXES, None, None, None), split),
        out_specs=(split, split, P(), P(), P(), P(), P(), P()),
        check_vma=False,
    )
```

```python
import functools
import math

import jax
import jax.numpy as jnp
from jax import lax
from jax.experimental import pallas as pl
from jax.experimental.pallas import tpu as pltpu
from jax.sharding import PartitionSpec as P

WIN = 2
BAND = 2 * WIN + 1
GROUP = 4
epsilon = 1e-05
AXES = ("dom", "feat")
BF16, F32 = jnp.bfloat16, jnp.float32
SENT = BF16
ONES = 128
BIAS_ROWS = 8

kept = pltpu.with_memory_space_constraint


def dot(left, right):
    return jnp.dot(left, right, preferred_element_type=F32)


def dot_nt(left, right):
    return lax.dot_general(left, right, (((1,), (1,)), ((), ())), preferred_element_type=F32)


def joined_lanes(parts):
    return jnp.concatenate(parts, axis=1)


def device_is_odd():
    index = lax.axis_index("dom") * lax.axis_size("feat") + lax.axis_index("feat")
    return index % 2 == 1


def column(row_ref, width):
    return jnp.broadcast_to(row_ref[...], (width, row_ref.shape[1])).T


def node_layer(state_t, aggregate_t, cot_t, first_t, second_t, w_first, w_second, columns):
    features, width = state_t.shape
    b_first, b_second, gain = (
        joined_lanes([c] * (width // c.shape[1])) for c in columns
    )
    pre_hidden = dot(first_t, jnp.concatenate([state_t, aggregate_t], axis=0)) + b_first
    sigmoid = 1.0 / (1.0 + jnp.exp(-pre_hidden))
    active_t = (pre_hidden * sigmoid).astype(BF16)
    slope = sigmoid * (1.0 + pre_hidden * (1.0 - sigmoid))
    pre_norm = dot(second_t, active_t) + b_second
    centred = pre_norm - jnp.mean(pre_norm, axis=0, keepdims=True)
    inv_std = lax.rsqrt(jnp.mean(centred * centred, axis=0, keepdims=True) + epsilon)
    normed = centred * inv_std
    updated_t = (state_t.astype(F32) + gain * normed).astype(BF16)
    cot = cot_t.astype(F32)
    terms = cot * normed
    q = cot * gain
    mean_q = jnp.mean(q, axis=0, keepdims=True)
    mean_qn = jnp.mean(q * normed, axis=0, keepdims=True)
    d_norm_t = (inv_std * (q - mean_q - normed * mean_qn)).astype(BF16)
    d_hidden_t = (dot(w_second, d_norm_t) * slope).astype(BF16)
    d_joined = dot(w_first, d_hidden_t)
    direct = cot + d_joined[:features]
    d_aggregate_t = d_joined[features:].astype(BF16)
    return updated_t, terms, active_t, d_norm_t, d_hidden_t, direct, d_aggregate_t


def first_products(d_hidden_t, state, aggregate):
    ones = jnp.ones((state.shape[0], ONES), BF16)
    return dot(d_hidden_t, joined_lanes([state, aggregate, ones]))


def second_products(active_t, d_norm_t):
    ones = jnp.ones((16, active_t.shape[1]), BF16)
    return dot_nt(jnp.concatenate([active_t, ones], axis=0), d_norm_t)


def inner_kernel(
    col_ref,
    state_hbm,
    cot_hbm,
    counts_hbm,
    w_msg_hbm,
    w_first_hbm,
    b_first_hbm,
    w_second_hbm,
    b_second_hbm,
    gain_hbm,
    state_ref,
    w_msg_ref,
    w_first_ref,
    w_second_ref,
    first_t_ref,
    second_t_ref,
    columns_ref,
    edge_state_ref,
    edge_cot_ref,
    edge_band_ref,
    edge_msg_ref,
    updated_ref,
    direct_ref,
    owed_ref,
    first_sums_ref,
    second_sums_ref,
    msg_sums_ref,
    gain_sums_ref,
    cot_ref,
    counts_ref,
    b_first_ref,
    b_second_ref,
    gain_ref,
    messages,
    band,
    arrived,
):
    blocks, tiles, size, _ = counts_ref.shape
    features = state_ref.shape[1]
    edge_rows = [*range(WIN), *range(blocks - WIN, blocks)]
    inner_rows = range(WIN, blocks - WIN)
    part = blocks // 4

    copies = [
        (state_hbm, state_ref),
        (w_msg_hbm, w_msg_ref),
        (w_first_hbm, w_first_ref),
        (b_first_hbm, b_first_ref),
        (w_second_hbm, w_second_ref),
        (b_second_hbm, b_second_ref),
        (gain_hbm, gain_ref),
    ]
    early = len(copies)
    copies += [
        (counts_hbm.at[pl.ds(b, part)], counts_ref.at[pl.ds(b, part)])
        for b in range(0, blocks, part)
    ]
    copies.append((cot_hbm, cot_ref))
    copies = [
        pltpu.make_async_copy(source, target, arrived.at[k])
        for k, (source, target) in enumerate(copies)
    ]
    for copy in copies:
        copy.start()
    for copy in copies[:early]:
        copy.wait()

    def rows(block, count=1):
        return pl.ds(block * size, count * size)

    w_msg, w_first, w_second = w_msg_ref[...], w_first_ref[...], w_second_ref[...]
    first_t = joined_lanes([w_first[:features].T, w_first[features:].T])
    second_t = w_second.T
    columns = [column(ref, size) for ref in (b_first_ref, b_second_ref, gain_ref)]
    first_t_ref[...] = first_t
    second_t_ref[...] = second_t
    for k in range(3):
        columns_ref[k] = columns[k]
    messages[...] = dot(state_ref[...], w_msg).astype(BF16)
    edge_msg_ref[0] = messages[rows(0, 2 * WIN), :]
    edge_msg_ref[1] = messages[rows(blocks - 2 * WIN, 2 * WIN), :]
    state_t = [state_ref[rows(b), :].T for b in range(blocks)]
    for k, b in enumerate(edge_rows):
        edge_state_ref[:, rows(k)] = state_t[b]

    for copy in copies[early:]:
        copy.wait()
    for k, b in enumerate(edge_rows):
        edge_cot_ref[:, rows(k)] = cot_ref[rows(b), :].T
    nothing = jnp.zeros((size, size), BF16)
    places = [(band, k, b) for k, b in enumerate(inner_rows)]
    places += [(edge_band_ref, k, b) for k, b in enumerate(edge_rows)]
    for ref, k, b in places:
        for place in range(BAND):
            if place != WIN:
                ref[k, place] = nothing
        ref[k, WIN] = counts_ref[b, 0].astype(F32).astype(BF16)
        own = col_ref[0, b]
        for t in range(1, tiles):
            ref[k, col_ref[t, b] - own + WIN] += counts_ref[b, t].astype(F32).astype(BF16)

    gain_sums = jnp.zeros((features, size), F32)
    first_sums = second_sums = 0.0
    reached = set()
    for start in range(0, len(inner_rows), GROUP):
        group = inner_rows[start : start + GROUP]
        lanes = pl.ds(start * size, len(group) * size)
        aggregate = [
            dot(
                joined_lanes([band[b - WIN, place] for place in range(BAND)]),
                messages[rows(b - WIN, BAND), :],
            ).astype(BF16)
            for b in group
        ]
        updated_t, terms, active_t, d_norm_t, d_hidden_t, direct, d_aggregate_t = node_layer(
            joined_lanes([state_t[b] for b in group]),
            joined_lanes([block.T for block in aggregate]),
            joined_lanes([cot_ref[rows(b), :].T for b in group]),
            first_t,
            second_t,
            w_first,
            w_second,
            columns,
        )
        updated_ref[:, lanes] = updated_t
        direct_ref[:, lanes] = direct
        first_sums += first_products(
            d_hidden_t, state_ref[rows(group[0], len(group)), :], jnp.concatenate(aggregate, axis=0)
        )
        second_sums += second_products(active_t, d_norm_t)
        for k, b in enumerate(group):
            own = slice(k * size, (k + 1) * size)
            gain_sums += terms[:, own]
            owed = dot(
                d_aggregate_t[:, own],
                joined_lanes([band[b - WIN, place] for place in range(BAND)]),
            )
            for place in range(BAND):
                block = b - WIN + place
                value = owed[:, place * size : (place + 1) * size]
                if block in reached:
                    owed_ref[block] += value
                else:
                    owed_ref[block] = value
                reached.add(block)
    first_sums_ref[...] = first_sums
    second_sums_ref[...] = second_sums
    gain_sums_ref[...] = gain_sums
    done = range(2 * WIN, blocks - 2 * WIN)
    msg_sums_ref[...] = dot(
        joined_lanes([owed_ref[b].astype(BF16) for b in done]), state_ref[rows(2 * WIN, len(done)), :]
    )


def outer_kernel(
    grad_scale,
    got_even_ref,
    got_odd_ref,
    state_ref,
    w_msg_ref,
    w_first_ref,
    w_second_ref,
    first_t_ref,
    second_t_ref,
    columns_ref,
    edge_state_ref,
    edge_cot_ref,
    edge_band_ref,
    edge_msg_ref,
    owed_ref,
    first_sums_ref,
    second_sums_ref,
    msg_sums_ref,
    gain_sums_ref,
    grads_ref,
    send_even_ref,
    send_odd_ref,
    updated_ref,
    direct_ref,
    edge_owed_ref,
):
    blocks, features, size = owed_ref.shape
    width = WIN * size

    def rows(block, count=1):
        return pl.ds(block * size, count * size)

    odd = device_is_odd()
    got_even, got_odd = got_even_ref[...], got_odd_ref[...]
    halo = (jnp.where(odd, got_even, got_odd), jnp.where(odd, got_odd, got_even))
    w_msg = w_msg_ref[...]
    below, above = (dot(block, w_msg).astype(BF16) for block in halo)
    messages = (
        jnp.concatenate([below, edge_msg_ref[0]], axis=0),
        jnp.concatenate([edge_msg_ref[1], above], axis=0),
    )

    bands = [
        joined_lanes([edge_band_ref[k, place] for place in range(BAND)]) for k in range(2 * WIN)
    ]
    aggregate = [
        dot(bands[k], messages[k // WIN][(k % WIN) * size : (k % WIN + BAND) * size]).astype(BF16)
        for k in range(2 * WIN)
    ]
    updated_t, terms, active_t, d_norm_t, d_hidden_t, direct, d_aggregate_t = node_layer(
        edge_state_ref[...],
        joined_lanes([block.T for block in aggregate]),
        edge_cot_ref[...],
        first_t_ref[...],
        second_t_ref[...],
        w_first_ref[...],
        w_second_ref[...],
        [columns_ref[k] for k in range(3)],
    )
    updated_ref[...] = updated_t
    direct_ref[...] = direct

    ends = []
    for end in range(2):
        owed = [None] * (3 * WIN)
        for k in range(WIN):
            own = slice((end * WIN + k) * size, (end * WIN + k + 1) * size)
            value = dot(d_aggregate_t[:, own], bands[end * WIN + k])
            for place in range(BAND):
                term = value[:, place * size : (place + 1) * size]
                owed[k + place] = term if owed[k + place] is None else owed[k + place] + term
        ends.append(owed)
    to_below = [block.astype(BF16) for block in ends[0][:WIN]]
    to_above = [block.astype(BF16) for block in ends[1][2 * WIN :]]
    for k in range(WIN):
        send_even_ref[k] = jnp.where(odd, to_below[k], to_above[k])
        send_odd_ref[k] = jnp.where(odd, to_above[k], to_below[k])
    inside = []
    for k in range(2 * WIN):
        inside.append(owed_ref[k] + ends[0][WIN + k])
    for k in range(2 * WIN):
        inside.append(owed_ref[blocks - 2 * WIN + k] + ends[1][k])
    for k, block in enumerate(inside):
        edge_owed_ref[k] = block
    inside = [block.astype(BF16) for block in inside]

    state = state_ref[...]
    low, high = state[:width], state[(blocks - WIN) * size :]
    first_sums = first_sums_ref[...] + first_products(
        d_hidden_t, jnp.concatenate([low, high], axis=0), jnp.concatenate(aggregate, axis=0)
    )
    second_sums = second_sums_ref[...] + second_products(active_t, d_norm_t)
    msg_sums = msg_sums_ref[...] + dot(
        joined_lanes(to_below + inside + to_above),
        jnp.concatenate(
            [halo[0], state[: 2 * width], state[(blocks - 2 * WIN) * size :], halo[1]], axis=0
        ),
    )
    gain_sums = gain_sums_ref[...]
    for k in range(2 * WIN):
        gain_sums = gain_sums + terms[:, k * size : (k + 1) * size]

    chunk = grads_ref.shape[1] - BIAS_ROWS
    turned = [first_sums[:, k * size : (k + 1) * size].T for k in range(3)]
    sums = (
        jnp.concatenate([turned[0], turned[1], second_sums[:features], msg_sums.T], axis=0)
        * grad_scale
    ).astype(SENT)
    bias = (
        jnp.concatenate(
            [
                turned[2][:1],
                second_sums[features : features + 1],
                jnp.sum(gain_sums.T, axis=0, keepdims=True),
            ],
            axis=0,
        )
        * grad_scale
    )
    bias_high = bias.astype(SENT)
    bias_low = (bias - bias_high.astype(F32)).astype(SENT)
    bias = jnp.concatenate(
        [bias_high, bias_low, jnp.zeros((BIAS_ROWS - 6, features), SENT)], axis=0
    )
    nothing = jnp.zeros((chunk, features), SENT)
    for k in range(grads_ref.shape[0]):
        block = sums[k * chunk : (k + 1) * chunk] if k * chunk < sums.shape[0] else nothing
        grads_ref[k] = jnp.concatenate([block, bias], axis=0)


def sum_kernel(parts_ref, spread_ref, bias_ref):
    total = parts_ref[0].astype(F32)
    for k in range(1, parts_ref.shape[0]):
        total = total + parts_ref[k].astype(F32)
    chunk = spread_ref.shape[1]
    weights = total[:chunk].astype(spread_ref.dtype)
    for k in range(spread_ref.shape[0]):
        spread_ref[k] = weights
    bias_ref[...] = total[chunk:]


def result_kernel(
    even_ref,
    odd_ref,
    w_msg_ref,
    inner_updated_ref,
    outer_updated_ref,
    inner_direct_ref,
    outer_direct_ref,
    owed_ref,
    edge_owed_ref,
    bias_ref,
    updated_ref,
    grad_state_ref,
    b_first_ref,
    b_second_ref,
    gain_ref,
):
    blocks, _, size = owed_ref.shape
    odd = device_is_odd()
    even_part, odd_part = even_ref[...].astype(F32), odd_ref[...].astype(F32)
    from_below = jnp.where(odd, even_part, odd_part)
    from_above = jnp.where(odd, odd_part, even_part)
    w_msg = w_msg_ref[...]
    for b in range(blocks):
        if b < 2 * WIN:
            owed = edge_owed_ref[b]
        elif b < blocks - 2 * WIN:
            owed = owed_ref[b]
        else:
            owed = edge_owed_ref[b - blocks + 4 * WIN]
        if b < WIN:
            owed = owed + from_below[b]
        elif b >= blocks - WIN:
            owed = owed + from_above[b - blocks + WIN]
        if WIN <= b < blocks - WIN:
            k, updated, direct = b - WIN, inner_updated_ref, inner_direct_ref
        else:
            k = b if b < WIN else b - blocks + 2 * WIN
            updated, direct = outer_updated_ref, outer_direct_ref
        lanes, rows = pl.ds(k * size, size), pl.ds(b * size, size)
        total = direct[:, lanes] + dot(w_msg, owed.astype(BF16))
        grad_state_ref[rows, :] = total.astype(BF16).T
        updated_ref[rows, :] = updated[:, lanes].T
    for k, ref in enumerate((b_first_ref, b_second_ref, gain_ref)):
        ref[...] = bias_ref[pl.ds(k, 1), :] + bias_ref[pl.ds(k + 3, 1), :]


def unpack_kernel(rows_ref, msg_ref, first_ref, second_ref):
    place = 0
    for ref in (first_ref, second_ref, msg_ref):
        count = ref.shape[0]
        ref[...] = rows_ref[pl.ds(place, count), :].astype(F32)
        place += count


def swapped(block, parity):
    last = lax.axis_size(AXES) - 1
    lower = range(parity, last, 2)
    return lax.ppermute(block, AXES, [(i, i + 1) for i in lower] + [(i + 1, i) for i in lower])


def call(kernel, name, outs, operands, scratch=(), limit=16, smem=0, flops=0):
    specs = [pl.BlockSpec(memory_space=pltpu.SMEM)] * smem
    specs += [pl.BlockSpec(memory_space=space) for _, space in operands[smem:]]
    arrays = list(operands[:smem]) + [kept(array, space) for array, space in operands[smem:]]
    return pl.pallas_call(
        kernel,
        out_shape=tuple(outs),
        in_specs=specs,
        out_specs=tuple(pl.BlockSpec(memory_space=pltpu.VMEM) for _ in outs),
        scratch_shapes=list(scratch),
        compiler_params=pltpu.CompilerParams(vmem_limit_bytes=limit * 1024 * 1024),
        cost_estimate=pl.CostEstimate(
            flops=flops, bytes_accessed=1_000_000, transcendentals=0
        ),
        name=name,
    )(*arrays)


def shards(
    node_state,
    w_msg,
    w_first,
    b_first,
    w_second,
    b_second,
    ln_gain,
    col_index,
    edge_counts,
    cotangent,
):
    nodes, features = node_state.shape
    blocks, tiles, size, _ = edge_counts.shape
    devices = lax.axis_size(AXES)
    grad_scale = 1.0 / math.sqrt(nodes * devices)
    chunk = -(-4 * features // (devices * 8)) * 8
    inner = blocks - 2 * WIN
    edge = 2 * WIN
    vmem, hbm = pltpu.VMEM, pltpu.HBM
    result = jax.ShapeDtypeStruct

    edge_rows = WIN * size
    odd = lax.axis_index(AXES) % 2
    side = lambda upper: lax.dynamic_slice_in_dim(
        node_state, upper * (nodes - edge_rows), edge_rows, 0
    )
    got_odd = swapped(side(odd), 1)
    got_even = swapped(side(1 - odd), 0)
    row = lambda vector: vector.reshape(1, features)

    (
        state,
        w_msg_here,
        w_first_here,
        w_second_here,
        first_t,
        second_t,
        columns,
        edge_state,
        edge_cot,
        edge_band,
        edge_msg,
        inner_updated,
        inner_direct,
        owed,
        first_sums,
        second_sums,
        msg_sums,
        gain_sums,
    ) = call(
        inner_kernel,
        "inner_rows",
        (
            vmem((nodes, features), BF16),
            vmem((features, features), BF16),
            vmem((2 * features, features), BF16),
            vmem((features, features), BF16),
            vmem((features, 2 * features), BF16),
            vmem((features, features), BF16),
            vmem((3, features, size), F32),
            vmem((features, edge * size), BF16),
            vmem((features, edge * size), BF16),
            vmem((edge, BAND, size, size), BF16),
            vmem((2, edge * size, features), BF16),
            vmem((features, inner * size), BF16),
            vmem((features, inner * size), F32),
            vmem((blocks, features, size), F32),
            vmem((features, 2 * features + ONES), F32),
            vmem((features + 16, features), F32),
            vmem((features, features), F32),
            vmem((features, size), F32),
        ),
        (
            col_index.T,
            (node_state, hbm),
            (cotangent, hbm),
            (edge_counts, hbm),
            (w_msg, hbm),
            (w_first, hbm),
            (row(b_first), hbm),
            (w_second, hbm),
            (row(b_second), hbm),
            (row(ln_gain), hbm),
        ),
        scratch=(
            vmem((nodes, features), BF16),
            vmem(edge_counts.shape, jnp.int32),
            vmem((1, features), F32),
            vmem((1, features), F32),
            vmem((1, features), F32),
            vmem((nodes, features), BF16),
            vmem((inner, BAND, size, size), BF16),
            pltpu.SemaphoreType.DMA((12,)),
        ),
        limit=32,
        smem=1,
        flops=700_000_000,
    )

    grads, send_even, send_odd, outer_updated, outer_direct, edge_owed = call(
        functools.partial(outer_kernel, grad_scale),
        "outer_rows",
        (
            vmem((devices, chunk + BIAS_ROWS, features), SENT),
            vmem((WIN, features, size), BF16),
            vmem((WIN, features, size), BF16),
            vmem((features, edge * size), BF16),
            vmem((features, edge * size), F32),
            vmem((2 * edge, features, size), F32),
        ),
        [
            (array, vmem)
            for array in (
                got_even,
                got_odd,
                state,
                w_msg_here,
                w_first_here,
                w_second_here,
                first_t,
                second_t,
                columns,
                edge_state,
                edge_cot,
                edge_band,
                edge_msg,
                owed,
                first_sums,
                second_sums,
                msg_sums,
                gain_sums,
            )
        ],
        flops=300_000_000,
    )

    parts = lax.all_to_all(grads, AXES, 0, 0, tiled=True)
    owed_odd = swapped(send_odd, 1)
    owed_even = swapped(send_even, 0)
    spread, bias = call(
        sum_kernel,
        "sum",
        (vmem((devices, chunk, features), SENT), vmem((BIAS_ROWS, features), F32)),
        [(parts, vmem)],
    )
    spread, owed_odd, owed_even = lax.optimization_barrier((spread, owed_odd, owed_even))

    updated, grad_state, g_b_first, g_b_second, g_gain = call(
        result_kernel,
        "results",
        (
            result((nodes, features), BF16),
            result((nodes, features), BF16),
            result((1, features), F32),
            result((1, features), F32),
            result((1, features), F32),
        ),
        [
            (array, vmem)
            for array in (
                owed_even,
                owed_odd,
                w_msg_here,
                inner_updated,
                outer_updated,
                inner_direct,
                outer_direct,
                owed,
                edge_owed,
                bias,
            )
        ],
        flops=100_000_000,
    )

    whole = lax.all_to_all(spread, AXES, 0, 0, tiled=True)
    g_msg, g_first, g_second = call(
        unpack_kernel,
        "unpack",
        (
            result((features, features), F32),
            result((2 * features, features), F32),
            result((features, features), F32),
        ),
        [(whole.reshape(devices * chunk, features), vmem)],
    )
    flat = lambda vector: vector.reshape(features)
    return (
        updated,
        grad_state,
        g_msg,
        g_first,
        flat(g_b_first),
        g_second,
        flat(g_b_second),
        flat(g_gain),
    )


def solution(mesh):
    split = P(AXES, None)
    return jax.shard_map(
        shards,
        mesh=mesh,
        in_specs=(split, P(), P(), P(), P(), P(), P(), split, P(AXES, None, None, None), split),
        out_specs=(split, split, P(), P(), P(), P(), P(), P()),
        check_vma=False,
    )
```

```python
import functools
import math

import jax
import jax.numpy as jnp
from jax import lax
from jax.experimental import pallas as pl
from jax.experimental.pallas import tpu as pltpu
from jax.sharding import PartitionSpec as P

WIN = 2
BAND = 2 * WIN + 1
GROUP = 2
epsilon = 1e-05
AXES = ("dom", "feat")
BF16, F32 = jnp.bfloat16, jnp.float32
SENT = BF16
ONES = 128
BIAS_ROWS = 8

kept = pltpu.with_memory_space_constraint


def dot(left, right):
    return jnp.dot(left, right, preferred_element_type=F32)


def dot_nt(left, right):
    return lax.dot_general(left, right, (((1,), (1,)), ((), ())), preferred_element_type=F32)


def joined_lanes(parts):
    return jnp.concatenate(parts, axis=1)


def device_is_odd():
    index = lax.axis_index("dom") * lax.axis_size("feat") + lax.axis_index("feat")
    return index % 2 == 1


def column(row_ref, width):
    return jnp.broadcast_to(row_ref[...], (width, row_ref.shape[1])).T


def node_layer(state_t, aggregate_t, cot_t, first_t, second_t, w_first, w_second, columns):
    features, width = state_t.shape
    b_first, b_second, gain = (
        joined_lanes([c] * (width // c.shape[1])) for c in columns
    )
    pre_hidden = dot(first_t, jnp.concatenate([state_t, aggregate_t], axis=0)) + b_first
    sigmoid = 1.0 / (1.0 + jnp.exp(-pre_hidden))
    active_t = (pre_hidden * sigmoid).astype(BF16)
    slope = sigmoid * (1.0 + pre_hidden * (1.0 - sigmoid))
    pre_norm = dot(second_t, active_t) + b_second
    centred = pre_norm - jnp.mean(pre_norm, axis=0, keepdims=True)
    inv_std = lax.rsqrt(jnp.mean(centred * centred, axis=0, keepdims=True) + epsilon)
    normed = centred * inv_std
    updated_t = (state_t.astype(F32) + gain * normed).astype(BF16)
    cot = cot_t.astype(F32)
    terms = cot * normed
    q = cot * gain
    mean_q = jnp.mean(q, axis=0, keepdims=True)
    mean_qn = jnp.mean(q * normed, axis=0, keepdims=True)
    d_norm_t = (inv_std * (q - mean_q - normed * mean_qn)).astype(BF16)
    d_hidden_t = (dot(w_second, d_norm_t) * slope).astype(BF16)
    d_joined = dot(w_first, d_hidden_t)
    direct = cot + d_joined[:features]
    d_aggregate_t = d_joined[features:].astype(BF16)
    return updated_t, terms, active_t, d_norm_t, d_hidden_t, direct, d_aggregate_t


def first_products(d_hidden_t, state, aggregate):
    ones = jnp.ones((state.shape[0], ONES), BF16)
    return dot(d_hidden_t, joined_lanes([state, aggregate, ones]))


def second_products(active_t, d_norm_t):
    ones = jnp.ones((16, active_t.shape[1]), BF16)
    return dot_nt(jnp.concatenate([active_t, ones], axis=0), d_norm_t)


def fetch_kernel(*refs):
    count = (len(refs) - 3) // 2
    sources, targets = refs[:count], refs[count : 2 * count]
    even_side_ref, odd_side_ref, arrived = refs[2 * count :]
    copies = [
        pltpu.make_async_copy(source, target, arrived.at[k])
        for k, (source, target) in enumerate(zip(sources, targets))
    ]
    for copy in copies:
        copy.start()
    copies[0].wait()
    state, edge = targets[0], even_side_ref.shape[0]
    odd = device_is_odd()
    head, tail = state[pl.ds(0, edge), :], state[pl.ds(state.shape[0] - edge, edge), :]
    even_side_ref[...] = jnp.where(odd, head, tail)
    odd_side_ref[...] = jnp.where(odd, tail, head)
    for copy in copies[1:]:
        copy.wait()


def inner_kernel(
    col_hbm,
    counts_hbm,
    state_ref,
    cot_ref,
    w_msg_ref,
    w_first_ref,
    w_second_ref,
    b_first_ref,
    b_second_ref,
    gain_ref,
    first_t_ref,
    second_t_ref,
    columns_ref,
    edge_state_ref,
    edge_cot_ref,
    edge_band_ref,
    edge_msg_ref,
    updated_ref,
    direct_ref,
    owed_ref,
    first_sums_ref,
    second_sums_ref,
    msg_sums_ref,
    gain_sums_ref,
    col_ref,
    counts_ref,
    messages,
    band,
    arrived,
):
    blocks, tiles, size, _ = counts_ref.shape
    features = state_ref.shape[1]
    edge_rows = [*range(WIN), *range(blocks - WIN, blocks)]
    inner_rows = range(WIN, blocks - WIN)
    part = blocks // 4

    copies = [(col_hbm, col_ref)]
    copies += [
        (counts_hbm.at[pl.ds(b, part)], counts_ref.at[pl.ds(b, part)])
        for b in range(0, blocks, part)
    ]
    copies = [
        pltpu.make_async_copy(source, target, arrived.at[k])
        for k, (source, target) in enumerate(copies)
    ]
    for copy in copies:
        copy.start()

    def rows(block, count=1):
        return pl.ds(block * size, count * size)

    w_msg, w_first, w_second = w_msg_ref[...], w_first_ref[...], w_second_ref[...]
    first_t = joined_lanes([w_first[:features].T, w_first[features:].T])
    second_t = w_second.T
    columns = [column(ref, size) for ref in (b_first_ref, b_second_ref, gain_ref)]
    first_t_ref[...] = first_t
    second_t_ref[...] = second_t
    for k in range(3):
        columns_ref[k] = columns[k]
    messages[...] = dot(state_ref[...], w_msg).astype(BF16)
    edge_msg_ref[0] = messages[rows(0, 2 * WIN), :]
    edge_msg_ref[1] = messages[rows(blocks - 2 * WIN, 2 * WIN), :]
    state_t = [state_ref[rows(b), :].T for b in range(blocks)]
    for k, b in enumerate(edge_rows):
        edge_state_ref[:, rows(k)] = state_t[b]

    for k, b in enumerate(edge_rows):
        edge_cot_ref[:, rows(k)] = cot_ref[rows(b), :].T
    for copy in copies:
        copy.wait()
    nothing = jnp.zeros((size, size), BF16)
    places = [(band, k, b) for k, b in enumerate(inner_rows)]
    places += [(edge_band_ref, k, b) for k, b in enumerate(edge_rows)]
    for ref, k, b in places:
        for place in range(BAND):
            if place != WIN:
                ref[k, place] = nothing
        ref[k, WIN] = counts_ref[b, 0].astype(F32).astype(BF16)
        own = col_ref[0, b]
        for t in range(1, tiles):
            ref[k, col_ref[t, b] - own + WIN] += counts_ref[b, t].astype(F32).astype(BF16)

    gain_sums = jnp.zeros((features, size), F32)
    first_sums = second_sums = 0.0
    reached = set()
    for start in range(0, len(inner_rows), GROUP):
        group = inner_rows[start : start + GROUP]
        lanes = pl.ds(start * size, len(group) * size)
        aggregate = [
            dot(
                joined_lanes([band[b - WIN, place] for place in range(BAND)]),
                messages[rows(b - WIN, BAND), :],
            ).astype(BF16)
            for b in group
        ]
        updated_t, terms, active_t, d_norm_t, d_hidden_t, direct, d_aggregate_t = node_layer(
            joined_lanes([state_t[b] for b in group]),
            joined_lanes([block.T for block in aggregate]),
            joined_lanes([cot_ref[rows(b), :].T for b in group]),
            first_t,
            second_t,
            w_first,
            w_second,
            columns,
        )
        updated_ref[:, lanes] = updated_t
        direct_ref[:, lanes] = direct
        first_sums += first_products(
            d_hidden_t, state_ref[rows(group[0], len(group)), :], jnp.concatenate(aggregate, axis=0)
        )
        second_sums += second_products(active_t, d_norm_t)
        for k, b in enumerate(group):
            own = slice(k * size, (k + 1) * size)
            gain_sums += terms[:, own]
            owed = dot(
                d_aggregate_t[:, own],
                joined_lanes([band[b - WIN, place] for place in range(BAND)]),
            )
            for place in range(BAND):
                block = b - WIN + place
                value = owed[:, place * size : (place + 1) * size]
                if block in reached:
                    owed_ref[block] += value
                else:
                    owed_ref[block] = value
                reached.add(block)
    first_sums_ref[...] = first_sums
    second_sums_ref[...] = second_sums
    gain_sums_ref[...] = gain_sums
    done = range(2 * WIN, blocks - 2 * WIN)
    msg_sums_ref[...] = dot(
        joined_lanes([owed_ref[b].astype(BF16) for b in done]), state_ref[rows(2 * WIN, len(done)), :]
    )


def outer_kernel(
    grad_scale,
    got_even_ref,
    got_odd_ref,
    state_ref,
    w_msg_ref,
    w_first_ref,
    w_second_ref,
    first_t_ref,
    second_t_ref,
    columns_ref,
    edge_state_ref,
    edge_cot_ref,
    edge_band_ref,
    edge_msg_ref,
    owed_ref,
    first_sums_ref,
    second_sums_ref,
    msg_sums_ref,
    gain_sums_ref,
    grads_ref,
    send_even_ref,
    send_odd_ref,
    updated_ref,
    direct_ref,
    edge_owed_ref,
):
    blocks, features, size = owed_ref.shape
    width = WIN * size

    def rows(block, count=1):
        return pl.ds(block * size, count * size)

    odd = device_is_odd()
    got_even, got_odd = got_even_ref[...], got_odd_ref[...]
    halo = (jnp.where(odd, got_even, got_odd), jnp.where(odd, got_odd, got_even))
    w_msg = w_msg_ref[...]
    below, above = (dot(block, w_msg).astype(BF16) for block in halo)
    messages = (
        jnp.concatenate([below, edge_msg_ref[0]], axis=0),
        jnp.concatenate([edge_msg_ref[1], above], axis=0),
    )

    bands = [
        joined_lanes([edge_band_ref[k, place] for place in range(BAND)]) for k in range(2 * WIN)
    ]
    aggregate = [
        dot(bands[k], messages[k // WIN][(k % WIN) * size : (k % WIN + BAND) * size]).astype(BF16)
        for k in range(2 * WIN)
    ]
    updated_t, terms, active_t, d_norm_t, d_hidden_t, direct, d_aggregate_t = node_layer(
        edge_state_ref[...],
        joined_lanes([block.T for block in aggregate]),
        edge_cot_ref[...],
        first_t_ref[...],
        second_t_ref[...],
        w_first_ref[...],
        w_second_ref[...],
        [columns_ref[k] for k in range(3)],
    )
    updated_ref[...] = updated_t
    direct_ref[...] = direct

    ends = []
    for end in range(2):
        owed = [None] * (3 * WIN)
        for k in range(WIN):
            own = slice((end * WIN + k) * size, (end * WIN + k + 1) * size)
            value = dot(d_aggregate_t[:, own], bands[end * WIN + k])
            for place in range(BAND):
                term = value[:, place * size : (place + 1) * size]
                owed[k + place] = term if owed[k + place] is None else owed[k + place] + term
        ends.append(owed)
    to_below = [block.astype(BF16) for block in ends[0][:WIN]]
    to_above = [block.astype(BF16) for block in ends[1][2 * WIN :]]
    for k in range(WIN):
        send_even_ref[k] = jnp.where(odd, to_below[k], to_above[k])
        send_odd_ref[k] = jnp.where(odd, to_above[k], to_below[k])
    inside = []
    for k in range(2 * WIN):
        inside.append(owed_ref[k] + ends[0][WIN + k])
    for k in range(2 * WIN):
        inside.append(owed_ref[blocks - 2 * WIN + k] + ends[1][k])
    for k, block in enumerate(inside):
        edge_owed_ref[k] = block
    inside = [block.astype(BF16) for block in inside]

    state = state_ref[...]
    low, high = state[:width], state[(blocks - WIN) * size :]
    first_sums = first_sums_ref[...] + first_products(
        d_hidden_t, jnp.concatenate([low, high], axis=0), jnp.concatenate(aggregate, axis=0)
    )
    second_sums = second_sums_ref[...] + second_products(active_t, d_norm_t)
    msg_sums = msg_sums_ref[...] + dot(
        joined_lanes(to_below + inside + to_above),
        jnp.concatenate(
            [halo[0], state[: 2 * width], state[(blocks - 2 * WIN) * size :], halo[1]], axis=0
        ),
    )
    gain_sums = gain_sums_ref[...]
    for k in range(2 * WIN):
        gain_sums = gain_sums + terms[:, k * size : (k + 1) * size]

    chunk = grads_ref.shape[1] - BIAS_ROWS
    turned = [first_sums[:, k * size : (k + 1) * size].T for k in range(3)]
    sums = (
        jnp.concatenate([turned[0], turned[1], second_sums[:features], msg_sums.T], axis=0)
        * grad_scale
    ).astype(SENT)
    bias = (
        jnp.concatenate(
            [
                turned[2][:1],
                second_sums[features : features + 1],
                jnp.sum(gain_sums.T, axis=0, keepdims=True),
            ],
            axis=0,
        )
        * grad_scale
    )
    bias_high = bias.astype(SENT)
    bias_low = (bias - bias_high.astype(F32)).astype(SENT)
    bias = jnp.concatenate(
        [bias_high, bias_low, jnp.zeros((BIAS_ROWS - 6, features), SENT)], axis=0
    )
    nothing = jnp.zeros((chunk, features), SENT)
    for k in range(grads_ref.shape[0]):
        block = sums[k * chunk : (k + 1) * chunk] if k * chunk < sums.shape[0] else nothing
        grads_ref[k] = jnp.concatenate([block, bias], axis=0)


def sum_kernel(parts_ref, spread_ref, bias_ref):
    total = parts_ref[0].astype(F32)
    for k in range(1, parts_ref.shape[0]):
        total = total + parts_ref[k].astype(F32)
    chunk = spread_ref.shape[1]
    weights = total[:chunk].astype(spread_ref.dtype)
    for k in range(spread_ref.shape[0]):
        spread_ref[k] = weights
    bias_ref[...] = total[chunk:]


def result_kernel(
    even_ref,
    odd_ref,
    w_msg_ref,
    inner_updated_ref,
    outer_updated_ref,
    inner_direct_ref,
    outer_direct_ref,
    owed_ref,
    edge_owed_ref,
    bias_ref,
    updated_ref,
    grad_state_ref,
    b_first_ref,
    b_second_ref,
    gain_ref,
):
    blocks, _, size = owed_ref.shape
    odd = device_is_odd()
    even_part, odd_part = even_ref[...].astype(F32), odd_ref[...].astype(F32)
    from_below = jnp.where(odd, even_part, odd_part)
    from_above = jnp.where(odd, odd_part, even_part)
    w_msg = w_msg_ref[...]
    for b in range(blocks):
        if b < 2 * WIN:
            owed = edge_owed_ref[b]
        elif b < blocks - 2 * WIN:
            owed = owed_ref[b]
        else:
            owed = edge_owed_ref[b - blocks + 4 * WIN]
        if b < WIN:
            owed = owed + from_below[b]
        elif b >= blocks - WIN:
            owed = owed + from_above[b - blocks + WIN]
        if WIN <= b < blocks - WIN:
            k, updated, direct = b - WIN, inner_updated_ref, inner_direct_ref
        else:
            k = b if b < WIN else b - blocks + 2 * WIN
            updated, direct = outer_updated_ref, outer_direct_ref
        lanes, rows = pl.ds(k * size, size), pl.ds(b * size, size)
        total = direct[:, lanes] + dot(w_msg, owed.astype(BF16))
        grad_state_ref[rows, :] = total.astype(BF16).T
        updated_ref[rows, :] = updated[:, lanes].T
    for k, ref in enumerate((b_first_ref, b_second_ref, gain_ref)):
        ref[...] = bias_ref[pl.ds(k, 1), :] + bias_ref[pl.ds(k + 3, 1), :]


def unpack_kernel(rows_ref, msg_ref, first_ref, second_ref):
    place = 0
    for ref in (first_ref, second_ref, msg_ref):
        count = ref.shape[0]
        ref[...] = rows_ref[pl.ds(place, count), :].astype(F32)
        place += count


def swapped(block, parity):
    last = lax.axis_size(AXES) - 1
    lower = range(parity, last, 2)
    return lax.ppermute(block, AXES, [(i, i + 1) for i in lower] + [(i + 1, i) for i in lower])


def call(kernel, name, outs, operands, scratch=(), limit=16, flops=0):
    specs = [pl.BlockSpec(memory_space=space) for _, space in operands]
    arrays = [kept(array, space) for array, space in operands]
    return pl.pallas_call(
        kernel,
        out_shape=tuple(outs),
        in_specs=specs,
        out_specs=tuple(pl.BlockSpec(memory_space=pltpu.VMEM) for _ in outs),
        scratch_shapes=list(scratch),
        compiler_params=pltpu.CompilerParams(vmem_limit_bytes=limit * 1024 * 1024),
        cost_estimate=pl.CostEstimate(
            flops=flops, bytes_accessed=1_000_000, transcendentals=0
        ),
        name=name,
    )(*arrays)


def shards(
    node_state,
    w_msg,
    w_first,
    b_first,
    w_second,
    b_second,
    ln_gain,
    col_index,
    edge_counts,
    cotangent,
):
    nodes, features = node_state.shape
    blocks, tiles, size, _ = edge_counts.shape
    devices = lax.axis_size(AXES)
    grad_scale = 1.0 / math.sqrt(nodes * devices)
    chunk = -(-4 * features // (devices * 8)) * 8
    inner = blocks - 2 * WIN
    edge = 2 * WIN
    vmem, hbm = pltpu.VMEM, pltpu.HBM
    result = jax.ShapeDtypeStruct

    row = lambda vector: vector.reshape(1, features)
    sources = (
        node_state,
        cotangent,
        w_msg,
        w_first,
        w_second,
        row(b_first),
        row(b_second),
        row(ln_gain),
    )
    *fetched, even_side, odd_side = call(
        fetch_kernel,
        "fetch",
        [vmem(array.shape, array.dtype) for array in sources]
        + [vmem((WIN * size, features), BF16)] * 2,
        [(array, hbm) for array in sources],
        scratch=(pltpu.SemaphoreType.DMA((len(sources),)),),
    )
    state, cot_here, w_msg_here, w_first_here, w_second_here, *vectors = fetched
    got_even = swapped(even_side, 0)
    got_odd = swapped(odd_side, 1)

    (
        first_t,
        second_t,
        columns,
        edge_state,
        edge_cot,
        edge_band,
        edge_msg,
        inner_updated,
        inner_direct,
        owed,
        first_sums,
        second_sums,
        msg_sums,
        gain_sums,
    ) = call(
        inner_kernel,
        "inner_rows",
        (
            vmem((features, 2 * features), BF16),
            vmem((features, features), BF16),
            vmem((3, features, size), F32),
            vmem((features, edge * size), BF16),
            vmem((features, edge * size), BF16),
            vmem((edge, BAND, size, size), BF16),
            vmem((2, edge * size, features), BF16),
            vmem((features, inner * size), BF16),
            vmem((features, inner * size), F32),
            vmem((blocks, features, size), F32),
            vmem((features, 2 * features + ONES), F32),
            vmem((features + 16, features), F32),
            vmem((features, features), F32),
            vmem((features, size), F32),
        ),
        [(col_index.T, hbm), (edge_counts, hbm)]
        + [
            (array, vmem)
            for array in (state, cot_here, w_msg_here, w_first_here, w_second_here, *vectors)
        ],
        scratch=(
            pltpu.SMEM((tiles, blocks), jnp.int32),
            vmem(edge_counts.shape, jnp.int32),
            vmem((nodes, features), BF16),
            vmem((inner, BAND, size, size), BF16),
            pltpu.SemaphoreType.DMA((5,)),
        ),
        limit=32,
        flops=700_000_000,
    )

    grads, send_even, send_odd, outer_updated, outer_direct, edge_owed = call(
        functools.partial(outer_kernel, grad_scale),
        "outer_rows",
        (
            vmem((devices, chunk + BIAS_ROWS, features), SENT),
            vmem((WIN, features, size), BF16),
            vmem((WIN, features, size), BF16),
            vmem((features, edge * size), BF16),
            vmem((features, edge * size), F32),
            vmem((2 * edge, features, size), F32),
        ),
        [
            (array, vmem)
            for array in (
                got_even,
                got_odd,
                state,
                w_msg_here,
                w_first_here,
                w_second_here,
                first_t,
                second_t,
                columns,
                edge_state,
                edge_cot,
                edge_band,
                edge_msg,
                owed,
                first_sums,
                second_sums,
                msg_sums,
                gain_sums,
            )
        ],
        flops=300_000_000,
    )

    parts = lax.all_to_all(grads, AXES, 0, 0, tiled=True)
    owed_even = swapped(send_even, 0)
    owed_odd = swapped(send_odd, 1)
    spread, bias = call(
        sum_kernel,
        "sum",
        (vmem((devices, chunk, features), SENT), vmem((BIAS_ROWS, features), F32)),
        [(parts, vmem)],
        flops=10_000_000_000,
    )
    updated, grad_state, g_b_first, g_b_second, g_gain = call(
        result_kernel,
        "results",
        (
            result((nodes, features), BF16),
            result((nodes, features), BF16),
            result((1, features), F32),
            result((1, features), F32),
            result((1, features), F32),
        ),
        [
            (array, vmem)
            for array in (
                owed_even,
                owed_odd,
                w_msg_here,
                inner_updated,
                outer_updated,
                inner_direct,
                outer_direct,
                owed,
                edge_owed,
                bias,
            )
        ],
        flops=50_000_000_000,
    )

    whole = lax.all_to_all(spread, AXES, 0, 0, tiled=True)
    g_msg, g_first, g_second = call(
        unpack_kernel,
        "unpack",
        (
            result((features, features), F32),
            result((2 * features, features), F32),
            result((features, features), F32),
        ),
        [(whole.reshape(devices * chunk, features), vmem)],
    )
    flat = lambda vector: vector.reshape(features)
    return (
        updated,
        grad_state,
        g_msg,
        g_first,
        flat(g_b_first),
        g_second,
        flat(g_b_second),
        flat(g_gain),
    )


def solution(mesh):
    split = P(AXES, None)
    return jax.shard_map(
        shards,
        mesh=mesh,
        in_specs=(split, P(), P(), P(), P(), P(), P(), split, P(AXES, None, None, None), split),
        out_specs=(split, split, P(), P(), P(), P(), P(), P()),
        check_vma=False,
    )
```

```python
import functools
import math

import jax
import jax.numpy as jnp
from jax import lax
from jax.experimental import pallas as pl
from jax.experimental.pallas import tpu as pltpu
from jax.sharding import PartitionSpec as P

WIN = 2
BAND = 2 * WIN + 1
GROUP = 8
epsilon = 1e-05
AXES = ("dom", "feat")
BF16, F32 = jnp.bfloat16, jnp.float32
SENT = BF16
ONES = 128
BIAS_ROWS = 8

kept = pltpu.with_memory_space_constraint


def dot(left, right):
    return jnp.dot(left, right, preferred_element_type=F32)


def dot_nt(left, right):
    return lax.dot_general(left, right, (((1,), (1,)), ((), ())), preferred_element_type=F32)


def joined_lanes(parts):
    return jnp.concatenate(parts, axis=1)


def device_is_odd():
    index = lax.axis_index("dom") * lax.axis_size("feat") + lax.axis_index("feat")
    return index % 2 == 1


def column(row_ref, width):
    return jnp.broadcast_to(row_ref[...], (width, row_ref.shape[1])).T


def node_layer(state_t, aggregate_t, cot_t, first_t, second_t, w_first, w_second, columns):
    features, width = state_t.shape
    b_first, b_second, gain = (
        joined_lanes([c] * (width // c.shape[1])) for c in columns
    )
    pre_hidden = dot(first_t, jnp.concatenate([state_t, aggregate_t], axis=0)) + b_first
    sigmoid = 1.0 / (1.0 + jnp.exp(-pre_hidden))
    active_t = (pre_hidden * sigmoid).astype(BF16)
    slope = sigmoid * (1.0 + pre_hidden * (1.0 - sigmoid))
    pre_norm = dot(second_t, active_t) + b_second
    centred = pre_norm - jnp.mean(pre_norm, axis=0, keepdims=True)
    inv_std = lax.rsqrt(jnp.mean(centred * centred, axis=0, keepdims=True) + epsilon)
    normed = centred * inv_std
    updated_t = (state_t.astype(F32) + gain * normed).astype(BF16)
    cot = cot_t.astype(F32)
    terms = cot * normed
    q = cot * gain
    mean_q = jnp.mean(q, axis=0, keepdims=True)
    mean_qn = jnp.mean(q * normed, axis=0, keepdims=True)
    d_norm_t = (inv_std * (q - mean_q - normed * mean_qn)).astype(BF16)
    d_hidden_t = (dot(w_second, d_norm_t) * slope).astype(BF16)
    d_joined = dot(w_first, d_hidden_t)
    direct = cot + d_joined[:features]
    d_aggregate_t = d_joined[features:].astype(BF16)
    return updated_t, terms, active_t, d_norm_t, d_hidden_t, direct, d_aggregate_t


def first_products(d_hidden_t, state, aggregate):
    ones = jnp.ones((state.shape[0], ONES), BF16)
    return dot(d_hidden_t, joined_lanes([state, aggregate, ones]))


def second_products(active_t, d_norm_t):
    ones = jnp.ones((16, active_t.shape[1]), BF16)
    return dot_nt(jnp.concatenate([active_t, ones], axis=0), d_norm_t)


def fetch_kernel(*refs):
    count = (len(refs) - 3) // 2
    sources, targets = refs[:count], refs[count : 2 * count]
    even_side_ref, odd_side_ref, arrived = refs[2 * count :]
    copies = [
        pltpu.make_async_copy(source, target, arrived.at[k])
        for k, (source, target) in enumerate(zip(sources, targets))
    ]
    for copy in copies:
        copy.start()
    copies[0].wait()
    state, edge = targets[0], even_side_ref.shape[0]
    odd = device_is_odd()
    head, tail = state[pl.ds(0, edge), :], state[pl.ds(state.shape[0] - edge, edge), :]
    even_side_ref[...] = jnp.where(odd, head, tail)
    odd_side_ref[...] = jnp.where(odd, tail, head)
    for copy in copies[1:]:
        copy.wait()


def inner_kernel(
    col_hbm,
    counts_hbm,
    cot_hbm,
    state_ref,
    w_msg_ref,
    w_first_ref,
    w_second_ref,
    b_first_ref,
    b_second_ref,
    gain_ref,
    first_t_ref,
    second_t_ref,
    columns_ref,
    edge_state_ref,
    edge_cot_ref,
    edge_band_ref,
    edge_msg_ref,
    updated_ref,
    direct_ref,
    owed_ref,
    first_sums_ref,
    second_sums_ref,
    msg_sums_ref,
    gain_sums_ref,
    col_ref,
    counts_ref,
    cot_ref,
    messages,
    band,
    arrived,
):
    blocks, tiles, size, _ = counts_ref.shape
    features = state_ref.shape[1]
    edge_rows = [*range(WIN), *range(blocks - WIN, blocks)]
    inner_rows = range(WIN, blocks - WIN)
    part = blocks // 4

    copies = [(col_hbm, col_ref)]
    copies += [
        (counts_hbm.at[pl.ds(b, part)], counts_ref.at[pl.ds(b, part)])
        for b in range(0, blocks, part)
    ]
    copies.append((cot_hbm, cot_ref))
    copies = [
        pltpu.make_async_copy(source, target, arrived.at[k])
        for k, (source, target) in enumerate(copies)
    ]
    for copy in copies:
        copy.start()

    def rows(block, count=1):
        return pl.ds(block * size, count * size)

    w_msg, w_first, w_second = w_msg_ref[...], w_first_ref[...], w_second_ref[...]
    first_t = joined_lanes([w_first[:features].T, w_first[features:].T])
    second_t = w_second.T
    columns = [column(ref, size) for ref in (b_first_ref, b_second_ref, gain_ref)]
    first_t_ref[...] = first_t
    second_t_ref[...] = second_t
    for k in range(3):
        columns_ref[k] = columns[k]
    messages[...] = dot(state_ref[...], w_msg).astype(BF16)
    edge_msg_ref[0] = messages[rows(0, 2 * WIN), :]
    edge_msg_ref[1] = messages[rows(blocks - 2 * WIN, 2 * WIN), :]
    state_t = [state_ref[rows(b), :].T for b in range(blocks)]
    for k, b in enumerate(edge_rows):
        edge_state_ref[:, rows(k)] = state_t[b]

    for copy in copies:
        copy.wait()
    for k, b in enumerate(edge_rows):
        edge_cot_ref[:, rows(k)] = cot_ref[rows(b), :].T
    nothing = jnp.zeros((size, size), BF16)
    places = [(band, k, b) for k, b in enumerate(inner_rows)]
    places += [(edge_band_ref, k, b) for k, b in enumerate(edge_rows)]
    for ref, k, b in places:
        for place in range(BAND):
            if place != WIN:
                ref[k, place] = nothing
        ref[k, WIN] = counts_ref[b, 0].astype(F32).astype(BF16)
        own = col_ref[0, b]
        for t in range(1, tiles):
            ref[k, col_ref[t, b] - own + WIN] += counts_ref[b, t].astype(F32).astype(BF16)

    gain_sums = jnp.zeros((features, size), F32)
    first_sums = second_sums = 0.0
    reached = set()
    for start in range(0, len(inner_rows), GROUP):
        group = inner_rows[start : start + GROUP]
        lanes = pl.ds(start * size, len(group) * size)
        aggregate = [
            dot(
                joined_lanes([band[b - WIN, place] for place in range(BAND)]),
                messages[rows(b - WIN, BAND), :],
            ).astype(BF16)
            for b in group
        ]
        updated_t, terms, active_t, d_norm_t, d_hidden_t, direct, d_aggregate_t = node_layer(
            joined_lanes([state_t[b] for b in group]),
            joined_lanes([block.T for block in aggregate]),
            joined_lanes([cot_ref[rows(b), :].T for b in group]),
            first_t,
            second_t,
            w_first,
            w_second,
            columns,
        )
        updated_ref[:, lanes] = updated_t
        direct_ref[:, lanes] = direct
        first_sums += first_products(
            d_hidden_t, state_ref[rows(group[0], len(group)), :], jnp.concatenate(aggregate, axis=0)
        )
        second_sums += second_products(active_t, d_norm_t)
        for k, b in enumerate(group):
            own = slice(k * size, (k + 1) * size)
            gain_sums += terms[:, own]
            owed = dot(
                d_aggregate_t[:, own],
                joined_lanes([band[b - WIN, place] for place in range(BAND)]),
            )
            for place in range(BAND):
                block = b - WIN + place
                value = owed[:, place * size : (place + 1) * size]
                if block in reached:
                    owed_ref[block] += value
                else:
                    owed_ref[block] = value
                reached.add(block)
    first_sums_ref[...] = first_sums
    second_sums_ref[...] = second_sums
    gain_sums_ref[...] = gain_sums
    done = range(2 * WIN, blocks - 2 * WIN)
    msg_sums_ref[...] = dot(
        joined_lanes([owed_ref[b].astype(BF16) for b in done]), state_ref[rows(2 * WIN, len(done)), :]
    )


def outer_kernel(
    grad_scale,
    got_even_ref,
    got_odd_ref,
    state_ref,
    w_msg_ref,
    w_first_ref,
    w_second_ref,
    first_t_ref,
    second_t_ref,
    columns_ref,
    edge_state_ref,
    edge_cot_ref,
    edge_band_ref,
    edge_msg_ref,
    owed_ref,
    first_sums_ref,
    second_sums_ref,
    msg_sums_ref,
    gain_sums_ref,
    grads_ref,
    send_even_ref,
    send_odd_ref,
    updated_ref,
    direct_ref,
    edge_owed_ref,
):
    blocks, features, size = owed_ref.shape
    width = WIN * size

    def rows(block, count=1):
        return pl.ds(block * size, count * size)

    odd = device_is_odd()
    got_even, got_odd = got_even_ref[...], got_odd_ref[...]
    halo = (jnp.where(odd, got_even, got_odd), jnp.where(odd, got_odd, got_even))
    w_msg = w_msg_ref[...]
    below, above = (dot(block, w_msg).astype(BF16) for block in halo)
    messages = (
        jnp.concatenate([below, edge_msg_ref[0]], axis=0),
        jnp.concatenate([edge_msg_ref[1], above], axis=0),
    )

    bands = [
        joined_lanes([edge_band_ref[k, place] for place in range(BAND)]) for k in range(2 * WIN)
    ]
    aggregate = [
        dot(bands[k], messages[k // WIN][(k % WIN) * size : (k % WIN + BAND) * size]).astype(BF16)
        for k in range(2 * WIN)
    ]
    updated_t, terms, active_t, d_norm_t, d_hidden_t, direct, d_aggregate_t = node_layer(
        edge_state_ref[...],
        joined_lanes([block.T for block in aggregate]),
        edge_cot_ref[...],
        first_t_ref[...],
        second_t_ref[...],
        w_first_ref[...],
        w_second_ref[...],
        [columns_ref[k] for k in range(3)],
    )
    updated_ref[...] = updated_t
    direct_ref[...] = direct

    ends = []
    for end in range(2):
        owed = [None] * (3 * WIN)
        for k in range(WIN):
            own = slice((end * WIN + k) * size, (end * WIN + k + 1) * size)
            value = dot(d_aggregate_t[:, own], bands[end * WIN + k])
            for place in range(BAND):
                term = value[:, place * size : (place + 1) * size]
                owed[k + place] = term if owed[k + place] is None else owed[k + place] + term
        ends.append(owed)
    to_below = [block.astype(BF16) for block in ends[0][:WIN]]
    to_above = [block.astype(BF16) for block in ends[1][2 * WIN :]]
    for k in range(WIN):
        send_even_ref[k] = jnp.where(odd, to_below[k], to_above[k])
        send_odd_ref[k] = jnp.where(odd, to_above[k], to_below[k])
    inside = []
    for k in range(2 * WIN):
        inside.append(owed_ref[k] + ends[0][WIN + k])
    for k in range(2 * WIN):
        inside.append(owed_ref[blocks - 2 * WIN + k] + ends[1][k])
    for k, block in enumerate(inside):
        edge_owed_ref[k] = block
    inside = [block.astype(BF16) for block in inside]

    state = state_ref[...]
    low, high = state[:width], state[(blocks - WIN) * size :]
    first_sums = first_sums_ref[...] + first_products(
        d_hidden_t, jnp.concatenate([low, high], axis=0), jnp.concatenate(aggregate, axis=0)
    )
    second_sums = second_sums_ref[...] + second_products(active_t, d_norm_t)
    msg_sums = msg_sums_ref[...] + dot(
        joined_lanes(to_below + inside + to_above),
        jnp.concatenate(
            [halo[0], state[: 2 * width], state[(blocks - 2 * WIN) * size :], halo[1]], axis=0
        ),
    )
    gain_sums = gain_sums_ref[...]
    for k in range(2 * WIN):
        gain_sums = gain_sums + terms[:, k * size : (k + 1) * size]

    chunk = grads_ref.shape[1] - BIAS_ROWS
    turned = [first_sums[:, k * size : (k + 1) * size].T for k in range(3)]
    sums = (
        jnp.concatenate([turned[0], turned[1], second_sums[:features], msg_sums.T], axis=0)
        * grad_scale
    ).astype(SENT)
    bias = (
        jnp.concatenate(
            [
                turned[2][:1],
                second_sums[features : features + 1],
                jnp.sum(gain_sums.T, axis=0, keepdims=True),
            ],
            axis=0,
        )
        * grad_scale
    )
    bias_high = bias.astype(SENT)
    bias_low = (bias - bias_high.astype(F32)).astype(SENT)
    bias = jnp.concatenate(
        [bias_high, bias_low, jnp.zeros((BIAS_ROWS - 6, features), SENT)], axis=0
    )
    nothing = jnp.zeros((chunk, features), SENT)
    for k in range(grads_ref.shape[0]):
        block = sums[k * chunk : (k + 1) * chunk] if k * chunk < sums.shape[0] else nothing
        grads_ref[k] = jnp.concatenate([block, bias], axis=0)


def sum_kernel(parts_ref, spread_ref, bias_ref):
    total = parts_ref[0].astype(F32)
    for k in range(1, parts_ref.shape[0]):
        total = total + parts_ref[k].astype(F32)
    chunk = spread_ref.shape[1]
    weights = total[:chunk].astype(spread_ref.dtype)
    for k in range(spread_ref.shape[0]):
        spread_ref[k] = weights
    bias_ref[...] = total[chunk:]


def result_kernel(
    even_ref,
    odd_ref,
    w_msg_ref,
    inner_updated_ref,
    outer_updated_ref,
    inner_direct_ref,
    outer_direct_ref,
    owed_ref,
    edge_owed_ref,
    bias_ref,
    updated_ref,
    grad_state_ref,
    b_first_ref,
    b_second_ref,
    gain_ref,
):
    blocks, _, size = owed_ref.shape
    odd = device_is_odd()
    even_part, odd_part = even_ref[...].astype(F32), odd_ref[...].astype(F32)
    from_below = jnp.where(odd, even_part, odd_part)
    from_above = jnp.where(odd, odd_part, even_part)
    w_msg = w_msg_ref[...]
    for b in range(blocks):
        if b < 2 * WIN:
            owed = edge_owed_ref[b]
        elif b < blocks - 2 * WIN:
            owed = owed_ref[b]
        else:
            owed = edge_owed_ref[b - blocks + 4 * WIN]
        if b < WIN:
            owed = owed + from_below[b]
        elif b >= blocks - WIN:
            owed = owed + from_above[b - blocks + WIN]
        if WIN <= b < blocks - WIN:
            k, updated, direct = b - WIN, inner_updated_ref, inner_direct_ref
        else:
            k = b if b < WIN else b - blocks + 2 * WIN
            updated, direct = outer_updated_ref, outer_direct_ref
        lanes, rows = pl.ds(k * size, size), pl.ds(b * size, size)
        total = direct[:, lanes] + dot(w_msg, owed.astype(BF16))
        grad_state_ref[rows, :] = total.astype(BF16).T
        updated_ref[rows, :] = updated[:, lanes].T
    for k, ref in enumerate((b_first_ref, b_second_ref, gain_ref)):
        ref[...] = bias_ref[pl.ds(k, 1), :] + bias_ref[pl.ds(k + 3, 1), :]


def unpack_kernel(rows_ref, msg_ref, first_ref, second_ref):
    place = 0
    for ref in (first_ref, second_ref, msg_ref):
        count = ref.shape[0]
        ref[...] = rows_ref[pl.ds(place, count), :].astype(F32)
        place += count


def swapped(block, parity):
    last = lax.axis_size(AXES) - 1
    lower = range(parity, last, 2)
    return lax.ppermute(block, AXES, [(i, i + 1) for i in lower] + [(i + 1, i) for i in lower])


def call(kernel, name, outs, operands, scratch=(), limit=16, flops=0):
    specs = [pl.BlockSpec(memory_space=space) for _, space in operands]
    arrays = [kept(array, space) for array, space in operands]
    return pl.pallas_call(
        kernel,
        out_shape=tuple(outs),
        in_specs=specs,
        out_specs=tuple(pl.BlockSpec(memory_space=pltpu.VMEM) for _ in outs),
        scratch_shapes=list(scratch),
        compiler_params=pltpu.CompilerParams(vmem_limit_bytes=limit * 1024 * 1024),
        cost_estimate=pl.CostEstimate(
            flops=flops, bytes_accessed=1_000_000, transcendentals=0
        ),
        name=name,
    )(*arrays)


def shards(
    node_state,
    w_msg,
    w_first,
    b_first,
    w_second,
    b_second,
    ln_gain,
    col_index,
    edge_counts,
    cotangent,
):
    nodes, features = node_state.shape
    blocks, tiles, size, _ = edge_counts.shape
    devices = lax.axis_size(AXES)
    grad_scale = 1.0 / math.sqrt(nodes * devices)
    chunk = -(-4 * features // (devices * 8)) * 8
    inner = blocks - 2 * WIN
    edge = 2 * WIN
    vmem, hbm = pltpu.VMEM, pltpu.HBM
    result = jax.ShapeDtypeStruct

    row = lambda vector: vector.reshape(1, features)
    sources = (
        node_state,
        w_msg,
        w_first,
        w_second,
        row(b_first),
        row(b_second),
        row(ln_gain),
    )
    *fetched, even_side, odd_side = call(
        fetch_kernel,
        "fetch",
        [vmem(array.shape, array.dtype) for array in sources]
        + [vmem((WIN * size, features), BF16)] * 2,
        [(array, hbm) for array in sources],
        scratch=(pltpu.SemaphoreType.DMA((len(sources),)),),
    )
    state, w_msg_here, w_first_here, w_second_here, *vectors = fetched
    got_even = swapped(even_side, 0)
    got_odd = swapped(odd_side, 1)

    (
        first_t,
        second_t,
        columns,
        edge_state,
        edge_cot,
        edge_band,
        edge_msg,
        inner_updated,
        inner_direct,
        owed,
        first_sums,
        second_sums,
        msg_sums,
        gain_sums,
    ) = call(
        inner_kernel,
        "inner_rows",
        (
            vmem((features, 2 * features), BF16),
            vmem((features, features), BF16),
            vmem((3, features, size), F32),
            vmem((features, edge * size), BF16),
            vmem((features, edge * size), BF16),
            vmem((edge, BAND, size, size), BF16),
            vmem((2, edge * size, features), BF16),
            vmem((features, inner * size), BF16),
            vmem((features, inner * size), F32),
            vmem((blocks, features, size), F32),
            vmem((features, 2 * features + ONES), F32),
            vmem((features + 16, features), F32),
            vmem((features, features), F32),
            vmem((features, size), F32),
        ),
        [(col_index.T, hbm), (edge_counts, hbm), (cotangent, hbm)]
        + [
            (array, vmem)
            for array in (state, w_msg_here, w_first_here, w_second_here, *vectors)
        ],
        scratch=(
            pltpu.SMEM((tiles, blocks), jnp.int32),
            vmem(edge_counts.shape, jnp.int32),
            vmem((nodes, features), BF16),
            vmem((nodes, features), BF16),
            vmem((inner, BAND, size, size), BF16),
            pltpu.SemaphoreType.DMA((6,)),
        ),
        limit=32,
        flops=700_000_000,
    )

    grads, send_even, send_odd, outer_updated, outer_direct, edge_owed = call(
        functools.partial(outer_kernel, grad_scale),
        "outer_rows",
        (
            vmem((devices, chunk + BIAS_ROWS, features), SENT),
            vmem((WIN, features, size), BF16),
            vmem((WIN, features, size), BF16),
            vmem((features, edge * size), BF16),
            vmem((features, edge * size), F32),
            vmem((2 * edge, features, size), F32),
        ),
        [
            (array, vmem)
            for array in (
                got_even,
                got_odd,
                state,
                w_msg_here,
                w_first_here,
                w_second_here,
                first_t,
                second_t,
                columns,
                edge_state,
                edge_cot,
                edge_band,
                edge_msg,
                owed,
                first_sums,
                second_sums,
                msg_sums,
                gain_sums,
            )
        ],
        flops=300_000_000,
    )

    parts = lax.all_to_all(grads, AXES, 0, 0, tiled=True)
    owed_even = swapped(send_even, 0)
    owed_odd = swapped(send_odd, 1)
    spread, bias = call(
        sum_kernel,
        "sum",
        (vmem((devices, chunk, features), SENT), vmem((BIAS_ROWS, features), F32)),
        [(parts, vmem)],
        flops=10_000_000_000,
    )
    updated, grad_state, g_b_first, g_b_second, g_gain = call(
        result_kernel,
        "results",
        (
            result((nodes, features), BF16),
            result((nodes, features), BF16),
            result((1, features), F32),
            result((1, features), F32),
            result((1, features), F32),
        ),
        [
            (array, vmem)
            for array in (
                owed_even,
                owed_odd,
                w_msg_here,
                inner_updated,
                outer_updated,
                inner_direct,
                outer_direct,
                owed,
                edge_owed,
                bias,
            )
        ],
        flops=50_000_000_000,
    )

    whole = lax.all_to_all(spread, AXES, 0, 0, tiled=True)
    g_msg, g_first, g_second = call(
        unpack_kernel,
        "unpack",
        (
            result((features, features), F32),
            result((2 * features, features), F32),
            result((features, features), F32),
        ),
        [(whole.reshape(devices * chunk, features), vmem)],
    )
    flat = lambda vector: vector.reshape(features)
    return (
        updated,
        grad_state,
        g_msg,
        g_first,
        flat(g_b_first),
        g_second,
        flat(g_b_second),
        flat(g_gain),
    )


def solution(mesh):
    split = P(AXES, None)
    return jax.shard_map(
        shards,
        mesh=mesh,
        in_specs=(split, P(), P(), P(), P(), P(), P(), split, P(AXES, None, None, None), split),
        out_specs=(split, split, P(), P(), P(), P(), P(), P()),
        check_vma=False,
    )
```

```python
import functools
import math

import jax
import jax.numpy as jnp
from jax import lax
from jax.experimental import pallas as pl
from jax.experimental.pallas import tpu as pltpu
from jax.sharding import PartitionSpec as P

WIN = 2
BAND = 2 * WIN + 1
epsilon = 1e-05
AXES = ("dom", "feat")
BF16, F32 = jnp.bfloat16, jnp.float32
SENT = BF16
ONES = 128
BIAS_ROWS = 8

kept = pltpu.with_memory_space_constraint


def dot(left, right):
    return jnp.dot(left, right, preferred_element_type=F32)


def dot_nt(left, right):
    return lax.dot_general(left, right, (((1,), (1,)), ((), ())), preferred_element_type=F32)


def joined_lanes(parts):
    return jnp.concatenate(parts, axis=1)


def device_is_odd():
    index = lax.axis_index("dom") * lax.axis_size("feat") + lax.axis_index("feat")
    return index % 2 == 1


def column(row_ref, width):
    return jnp.broadcast_to(row_ref[...], (width, row_ref.shape[1])).T


def blocks_turned(array):
    size = array.shape[1]
    return [array[k : k + size].T for k in range(0, array.shape[0], size)]


def node_layer(state_t, aggregate_t, cot_t, first_t, second_t, w_first, w_second, columns):
    features, width = state_t.shape
    b_first, b_second, gain = (
        joined_lanes([c] * (width // c.shape[1])) for c in columns
    )
    pre_hidden = dot(first_t, jnp.concatenate([state_t, aggregate_t], axis=0)) + b_first
    sigmoid = 0.5 * jnp.tanh(0.5 * pre_hidden) + 0.5
    silu = pre_hidden * sigmoid
    active_t = silu.astype(BF16)
    slope = sigmoid + silu * (1.0 - sigmoid)
    pre_norm = dot(second_t, active_t) + b_second
    centred = pre_norm - jnp.mean(pre_norm, axis=0, keepdims=True)
    inv_std = lax.rsqrt(jnp.mean(centred * centred, axis=0, keepdims=True) + epsilon)
    normed = centred * inv_std
    updated_t = (state_t.astype(F32) + gain * normed).astype(BF16)
    cot = cot_t.astype(F32)
    terms = cot * normed
    q = cot * gain
    mean_q = jnp.mean(q, axis=0, keepdims=True)
    mean_qn = jnp.mean(q * normed, axis=0, keepdims=True)
    d_norm_t = (inv_std * (q - mean_q - normed * mean_qn)).astype(BF16)
    d_hidden_t = (dot(w_second, d_norm_t) * slope).astype(BF16)
    d_joined = dot(w_first, d_hidden_t)
    direct = cot + d_joined[:features]
    d_aggregate_t = d_joined[features:].astype(BF16)
    return updated_t, terms, active_t, d_norm_t, d_hidden_t, direct, d_aggregate_t


def first_products(d_hidden_t, state, aggregate):
    ones = jnp.ones((state.shape[0], ONES), BF16)
    return dot(d_hidden_t, joined_lanes([state, aggregate, ones]))


def second_products(active_t, d_norm_t):
    ones = jnp.ones((16, active_t.shape[1]), BF16)
    return dot_nt(jnp.concatenate([active_t, ones], axis=0), d_norm_t)


def fetch_kernel(*refs):
    count = (len(refs) - 3) // 2
    sources, targets = refs[:count], refs[count : 2 * count]
    even_side_ref, odd_side_ref, arrived = refs[2 * count :]
    copies = [
        pltpu.make_async_copy(source, target, arrived.at[k])
        for k, (source, target) in enumerate(zip(sources, targets))
    ]
    for copy in copies:
        copy.start()
    copies[0].wait()
    state, edge = targets[0], even_side_ref.shape[0]
    odd = device_is_odd()
    head, tail = state[pl.ds(0, edge), :], state[pl.ds(state.shape[0] - edge, edge), :]
    even_side_ref[...] = jnp.where(odd, head, tail)
    odd_side_ref[...] = jnp.where(odd, tail, head)
    for copy in copies[1:]:
        copy.wait()


def inner_kernel(
    col_hbm,
    counts_hbm,
    cot_hbm,
    state_ref,
    w_msg_ref,
    w_first_ref,
    w_second_ref,
    b_first_ref,
    b_second_ref,
    gain_ref,
    first_t_ref,
    second_t_ref,
    columns_ref,
    edge_state_ref,
    edge_cot_ref,
    edge_sum_ref,
    band_ref,
    updated_ref,
    direct_ref,
    d_aggregate_ref,
    first_sums_ref,
    second_sums_ref,
    msg_sums_ref,
    gain_sums_ref,
    col_ref,
    counts_ref,
    cot_ref,
    arrived,
):
    blocks, tiles, size, _ = counts_ref.shape
    features = state_ref.shape[1]
    edge_rows = [*range(WIN), *range(blocks - WIN, blocks)]
    inner_rows = range(WIN, blocks - WIN)
    part = blocks // 4

    copies = [(col_hbm, col_ref)]
    copies += [
        (counts_hbm.at[pl.ds(b, part)], counts_ref.at[pl.ds(b, part)])
        for b in range(0, blocks, part)
    ]
    copies.append((cot_hbm, cot_ref))
    copies = [
        pltpu.make_async_copy(source, target, arrived.at[k])
        for k, (source, target) in enumerate(copies)
    ]
    for copy in copies:
        copy.start()

    def rows(block, count=1):
        return pl.ds(block * size, count * size)

    w_msg, w_first, w_second = w_msg_ref[...], w_first_ref[...], w_second_ref[...]
    first_t = joined_lanes([w_first[:features].T, w_first[features:].T])
    second_t = w_second.T
    columns = [column(ref, size) for ref in (b_first_ref, b_second_ref, gain_ref)]
    first_t_ref[...] = first_t
    second_t_ref[...] = second_t
    for k in range(3):
        columns_ref[k] = columns[k]
    state_t = [state_ref[rows(b), :].T for b in range(blocks)]
    for k, b in enumerate(edge_rows):
        edge_state_ref[:, rows(k)] = state_t[b]

    for copy in copies:
        copy.wait()
    for k, b in enumerate(edge_rows):
        edge_cot_ref[:, rows(k)] = cot_ref[rows(b), :].T
    nothing = jnp.zeros((size, size), BF16)
    for b in [*inner_rows, *edge_rows]:
        for place in range(BAND):
            if place != WIN:
                band_ref[b, place] = nothing
        band_ref[b, WIN] = counts_ref[b, 0].astype(F32).astype(BF16)
        own = col_ref[0, b]
        for t in range(1, tiles):
            band_ref[b, col_ref[t, b] - own + WIN] += counts_ref[b, t].astype(F32).astype(BF16)

    def neighbour_sum(b):
        first, last = max(b - WIN, 0), min(b + WIN, blocks - 1)
        tiles_of = [band_ref[b, block - b + WIN] for block in range(first, last + 1)]
        return dot(joined_lanes(tiles_of), state_ref[rows(first, last + 1 - first), :])

    for k, b in enumerate(edge_rows):
        edge_sum_ref[k] = neighbour_sum(b)
    summed = jnp.concatenate([neighbour_sum(b).astype(BF16) for b in inner_rows], axis=0)
    aggregate = dot(summed, w_msg).astype(BF16)
    updated_t, terms, active_t, d_norm_t, d_hidden_t, direct, d_aggregate_t = node_layer(
        joined_lanes([state_t[b] for b in inner_rows]),
        joined_lanes(blocks_turned(aggregate)),
        joined_lanes([cot_ref[rows(b), :].T for b in inner_rows]),
        first_t,
        second_t,
        w_first,
        w_second,
        columns,
    )
    updated_ref[...] = updated_t
    direct_ref[...] = direct
    d_aggregate_ref[...] = d_aggregate_t
    first_sums_ref[...] = first_products(
        d_hidden_t, state_ref[rows(WIN, len(inner_rows)), :], aggregate
    )
    second_sums_ref[...] = second_products(active_t, d_norm_t)
    msg_sums_ref[...] = dot(d_aggregate_t, summed)
    gain_sums_ref[...] = sum(
        terms[:, k * size : (k + 1) * size] for k in range(len(inner_rows))
    )


def outer_kernel(
    grad_scale,
    got_even_ref,
    got_odd_ref,
    state_ref,
    w_msg_ref,
    w_first_ref,
    w_second_ref,
    first_t_ref,
    second_t_ref,
    columns_ref,
    edge_state_ref,
    edge_cot_ref,
    edge_sum_ref,
    band_ref,
    first_sums_ref,
    second_sums_ref,
    msg_sums_ref,
    gain_sums_ref,
    grads_ref,
    updated_ref,
    direct_ref,
    d_aggregate_ref,
):
    blocks, _, size, _ = band_ref.shape
    features = w_msg_ref.shape[0]
    odd = device_is_odd()
    got_even, got_odd = got_even_ref[...], got_odd_ref[...]
    below, above = jnp.where(odd, got_even, got_odd), jnp.where(odd, got_odd, got_even)

    summed = []
    for k in range(WIN):
        far = joined_lanes([band_ref[k, place] for place in range(WIN - k)])
        summed.append(edge_sum_ref[k] + dot(far, below[k * size :]))
    for k in range(WIN):
        far = [band_ref[blocks - WIN + k, place] for place in range(2 * WIN - k, BAND)]
        summed.append(edge_sum_ref[WIN + k] + dot(joined_lanes(far), above[: (k + 1) * size]))
    summed = jnp.concatenate(summed, axis=0).astype(BF16)
    aggregate = dot(summed, w_msg_ref[...]).astype(BF16)
    updated_t, terms, active_t, d_norm_t, d_hidden_t, direct, d_aggregate_t = node_layer(
        edge_state_ref[...],
        joined_lanes(blocks_turned(aggregate)),
        edge_cot_ref[...],
        first_t_ref[...],
        second_t_ref[...],
        w_first_ref[...],
        w_second_ref[...],
        [columns_ref[k] for k in range(3)],
    )
    updated_ref[...] = updated_t
    direct_ref[...] = direct
    d_aggregate_ref[...] = d_aggregate_t

    width = WIN * size
    ends = [state_ref[pl.ds(0, width), :], state_ref[pl.ds((blocks - WIN) * size, width), :]]
    first_sums = first_sums_ref[...] + first_products(
        d_hidden_t, jnp.concatenate(ends, axis=0), aggregate
    )
    second_sums = second_sums_ref[...] + second_products(active_t, d_norm_t)
    msg_sums = msg_sums_ref[...] + dot(d_aggregate_t, summed)
    gain_sums = gain_sums_ref[...]
    for k in range(2 * WIN):
        gain_sums = gain_sums + terms[:, k * size : (k + 1) * size]

    chunk = grads_ref.shape[1] - BIAS_ROWS
    turned = [first_sums[:, k * size : (k + 1) * size].T for k in range(3)]
    sums = (
        jnp.concatenate([turned[0], turned[1], second_sums[:features], msg_sums.T], axis=0)
        * grad_scale
    ).astype(SENT)
    bias = (
        jnp.concatenate(
            [
                turned[2][:1],
                second_sums[features : features + 1],
                jnp.sum(gain_sums.T, axis=0, keepdims=True),
            ],
            axis=0,
        )
        * grad_scale
    )
    bias_high = bias.astype(SENT)
    bias_low = (bias - bias_high.astype(F32)).astype(SENT)
    bias = jnp.concatenate(
        [bias_high, bias_low, jnp.zeros((BIAS_ROWS - 6, features), SENT)], axis=0
    )
    nothing = jnp.zeros((chunk, features), SENT)
    for k in range(grads_ref.shape[0]):
        block = sums[k * chunk : (k + 1) * chunk] if k * chunk < sums.shape[0] else nothing
        grads_ref[k] = jnp.concatenate([block, bias], axis=0)


def owed_kernel(
    band_ref, inner_ref, outer_ref, owed_ref, send_even_ref, send_odd_ref
):
    blocks, _, size, _ = band_ref.shape
    odd = device_is_odd()

    def d_aggregate(b):
        if WIN <= b < blocks - WIN:
            return inner_ref[:, pl.ds((b - WIN) * size, size)]
        k = b if b < WIN else b - blocks + 2 * WIN
        return outer_ref[:, pl.ds(k * size, size)]

    def owed(block):
        near = range(max(block - WIN, 0), min(block + WIN, blocks - 1) + 1)
        tiles_of = [band_ref[b, block - b + WIN] for b in near]
        return dot(
            joined_lanes([d_aggregate(b) for b in near]), jnp.concatenate(tiles_of, axis=0)
        )

    for k in range(WIN):
        to_below = owed(k - WIN).astype(BF16)
        to_above = owed(blocks + k).astype(BF16)
        send_even_ref[k] = jnp.where(odd, to_below, to_above)
        send_odd_ref[k] = jnp.where(odd, to_above, to_below)
    for b in range(blocks):
        owed_ref[b] = owed(b)


def sum_kernel(parts_ref, spread_ref, bias_ref):
    total = parts_ref[0].astype(F32)
    for k in range(1, parts_ref.shape[0]):
        total = total + parts_ref[k].astype(F32)
    chunk = spread_ref.shape[1]
    weights = total[:chunk].astype(spread_ref.dtype)
    for k in range(spread_ref.shape[0]):
        spread_ref[k] = weights
    bias_ref[...] = total[chunk:]


def result_kernel(
    even_ref,
    odd_ref,
    w_msg_ref,
    inner_updated_ref,
    outer_updated_ref,
    inner_direct_ref,
    outer_direct_ref,
    owed_ref,
    bias_ref,
    updated_ref,
    grad_state_ref,
    b_first_ref,
    b_second_ref,
    gain_ref,
):
    blocks, _, size = owed_ref.shape
    odd = device_is_odd()
    even_part, odd_part = even_ref[...].astype(F32), odd_ref[...].astype(F32)
    from_below = jnp.where(odd, even_part, odd_part)
    from_above = jnp.where(odd, odd_part, even_part)
    w_msg = w_msg_ref[...]
    for b in range(blocks):
        owed = owed_ref[b]
        if b < WIN:
            owed = owed + from_below[b]
        elif b >= blocks - WIN:
            owed = owed + from_above[b - blocks + WIN]
        if WIN <= b < blocks - WIN:
            k, updated, direct = b - WIN, inner_updated_ref, inner_direct_ref
        else:
            k = b if b < WIN else b - blocks + 2 * WIN
            updated, direct = outer_updated_ref, outer_direct_ref
        lanes, rows = pl.ds(k * size, size), pl.ds(b * size, size)
        total = direct[:, lanes] + dot(w_msg, owed.astype(BF16))
        grad_state_ref[rows, :] = total.astype(BF16).T
        updated_ref[rows, :] = updated[:, lanes].T
    for k, ref in enumerate((b_first_ref, b_second_ref, gain_ref)):
        ref[...] = bias_ref[pl.ds(k, 1), :] + bias_ref[pl.ds(k + 3, 1), :]


def unpack_kernel(rows_ref, msg_ref, first_ref, second_ref):
    place = 0
    for ref in (first_ref, second_ref, msg_ref):
        count = ref.shape[0]
        ref[...] = rows_ref[pl.ds(place, count), :].astype(F32)
        place += count


def swapped(block, parity):
    last = lax.axis_size(AXES) - 1
    lower = range(parity, last, 2)
    return lax.ppermute(block, AXES, [(i, i + 1) for i in lower] + [(i + 1, i) for i in lower])


def call(kernel, name, outs, operands, scratch=(), limit=16, flops=0):
    specs = [pl.BlockSpec(memory_space=space) for _, space in operands]
    arrays = [kept(array, space) for array, space in operands]
    return pl.pallas_call(
        kernel,
        out_shape=tuple(outs),
        in_specs=specs,
        out_specs=tuple(pl.BlockSpec(memory_space=pltpu.VMEM) for _ in outs),
        scratch_shapes=list(scratch),
        compiler_params=pltpu.CompilerParams(vmem_limit_bytes=limit * 1024 * 1024),
        cost_estimate=pl.CostEstimate(
            flops=flops, bytes_accessed=1_000_000, transcendentals=0
        ),
        name=name,
    )(*arrays)


def shards(
    node_state,
    w_msg,
    w_first,
    b_first,
    w_second,
    b_second,
    ln_gain,
    col_index,
    edge_counts,
    cotangent,
):
    nodes, features = node_state.shape
    blocks, tiles, size, _ = edge_counts.shape
    devices = lax.axis_size(AXES)
    grad_scale = 1.0 / math.sqrt(nodes * devices)
    chunk = -(-4 * features // (devices * 8)) * 8
    inner = blocks - 2 * WIN
    edge = 2 * WIN
    vmem, hbm = pltpu.VMEM, pltpu.HBM
    result = jax.ShapeDtypeStruct

    row = lambda vector: vector.reshape(1, features)
    sources = (
        node_state,
        w_msg,
        w_first,
        w_second,
        row(b_first),
        row(b_second),
        row(ln_gain),
    )
    *fetched, even_side, odd_side = call(
        fetch_kernel,
        "fetch",
        [vmem(array.shape, array.dtype) for array in sources]
        + [vmem((WIN * size, features), BF16)] * 2,
        [(array, hbm) for array in sources],
        scratch=(pltpu.SemaphoreType.DMA((len(sources),)),),
    )
    state, w_msg_here, w_first_here, w_second_here, *vectors = fetched
    got_even = swapped(even_side, 0)
    got_odd = swapped(odd_side, 1)

    (
        first_t,
        second_t,
        columns,
        edge_state,
        edge_cot,
        edge_sum,
        band,
        inner_updated,
        inner_direct,
        inner_d_aggregate,
        first_sums,
        second_sums,
        msg_sums,
        gain_sums,
    ) = call(
        inner_kernel,
        "inner_rows",
        (
            vmem((features, 2 * features), BF16),
            vmem((features, features), BF16),
            vmem((3, features, size), F32),
            vmem((features, edge * size), BF16),
            vmem((features, edge * size), BF16),
            vmem((edge, size, features), F32),
            vmem((blocks, BAND, size, size), BF16),
            vmem((features, inner * size), BF16),
            vmem((features, inner * size), F32),
            vmem((features, inner * size), BF16),
            vmem((features, 2 * features + ONES), F32),
            vmem((features + 16, features), F32),
            vmem((features, features), F32),
            vmem((features, size), F32),
        ),
        [(col_index.T, hbm), (edge_counts, hbm), (cotangent, hbm)]
        + [
            (array, vmem)
            for array in (state, w_msg_here, w_first_here, w_second_here, *vectors)
        ],
        scratch=(
            pltpu.SMEM((tiles, blocks), jnp.int32),
            vmem(edge_counts.shape, jnp.int32),
            vmem((nodes, features), BF16),
            pltpu.SemaphoreType.DMA((6,)),
        ),
        limit=32,
        flops=700_000_000,
    )

    grads, outer_updated, outer_direct, outer_d_aggregate = call(
        functools.partial(outer_kernel, grad_scale),
        "outer_rows",
        (
            vmem((devices, chunk + BIAS_ROWS, features), SENT),
            vmem((features, edge * size), BF16),
            vmem((features, edge * size), F32),
            vmem((features, edge * size), BF16),
        ),
        [
            (array, vmem)
            for array in (
                got_even,
                got_odd,
                state,
                w_msg_here,
                w_first_here,
                w_second_here,
                first_t,
                second_t,
                columns,
                edge_state,
                edge_cot,
                edge_sum,
                band,
                first_sums,
                second_sums,
                msg_sums,
                gain_sums,
            )
        ],
        flops=300_000_000,
    )

    parts = lax.all_to_all(grads, AXES, 0, 0, tiled=True)
    owed, send_even, send_odd = call(
        owed_kernel,
        "owed",
        (
            vmem((blocks, features, size), F32),
            vmem((WIN, features, size), BF16),
            vmem((WIN, features, size), BF16),
        ),
        [(band, vmem), (inner_d_aggregate, vmem), (outer_d_aggregate, vmem)],
        flops=200_000_000,
    )
    owed_even = swapped(send_even, 0)
    owed_odd = swapped(send_odd, 1)
    spread, bias = call(
        sum_kernel,
        "sum",
        (vmem((devices, chunk, features), SENT), vmem((BIAS_ROWS, features), F32)),
        [(parts, vmem)],
        flops=10_000_000_000,
    )
    updated, grad_state, g_b_first, g_b_second, g_gain = call(
        result_kernel,
        "results",
        (
            result((nodes, features), BF16),
            result((nodes, features), BF16),
            result((1, features), F32),
            result((1, features), F32),
            result((1, features), F32),
        ),
        [
            (array, vmem)
            for array in (
                owed_even,
                owed_odd,
                w_msg_here,
                inner_updated,
                outer_updated,
                inner_direct,
                outer_direct,
                owed,
                bias,
            )
        ],
        flops=50_000_000_000,
    )

    whole = lax.all_to_all(spread, AXES, 0, 0, tiled=True)
    g_msg, g_first, g_second = call(
        unpack_kernel,
        "unpack",
        (
            result((features, features), F32),
            result((2 * features, features), F32),
            result((features, features), F32),
        ),
        [(whole.reshape(devices * chunk, features), vmem)],
    )
    flat = lambda vector: vector.reshape(features)
    return (
        updated,
        grad_state,
        g_msg,
        g_first,
        flat(g_b_first),
        g_second,
        flat(g_b_second),
        flat(g_gain),
    )


def solution(mesh):
    split = P(AXES, None)
    return jax.shard_map(
        shards,
        mesh=mesh,
        in_specs=(split, P(), P(), P(), P(), P(), P(), split, P(AXES, None, None, None), split),
        out_specs=(split, split, P(), P(), P(), P(), P(), P()),
        check_vma=False,
    )
```

```python
import functools
import math

import jax
import jax.numpy as jnp
from jax import lax
from jax.experimental import pallas as pl
from jax.experimental.pallas import tpu as pltpu
from jax.sharding import PartitionSpec as P

WIN = 2
BAND = 2 * WIN + 1
epsilon = 1e-05
AXES = ("dom", "feat")
BF16, F32 = jnp.bfloat16, jnp.float32
SENT = BF16
ONES = 128
BIAS_ROWS = 8

kept = pltpu.with_memory_space_constraint


def dot(left, right):
    return jnp.dot(left, right, preferred_element_type=F32)


def dot_nt(left, right):
    return lax.dot_general(left, right, (((1,), (1,)), ((), ())), preferred_element_type=F32)


def joined_lanes(parts):
    return jnp.concatenate(parts, axis=1)


def device_is_odd():
    index = lax.axis_index("dom") * lax.axis_size("feat") + lax.axis_index("feat")
    return index % 2 == 1


def column(row_ref, width):
    return jnp.broadcast_to(row_ref[...], (width, row_ref.shape[1])).T


def blocks_turned(array):
    size = array.shape[1]
    return [array[k : k + size].T for k in range(0, array.shape[0], size)]


def node_layer(state_t, aggregate_t, cot_t, first_t, second_t, w_second, columns):
    features, width = state_t.shape
    b_first, b_second, gain = (
        joined_lanes([c] * (width // c.shape[1])) for c in columns
    )
    pre_hidden = dot(first_t, jnp.concatenate([state_t, aggregate_t], axis=0)) + b_first
    sigmoid = 0.5 * jnp.tanh(0.5 * pre_hidden) + 0.5
    silu = pre_hidden * sigmoid
    active_t = silu.astype(BF16)
    slope = sigmoid + silu * (1.0 - sigmoid)
    pre_norm = dot(second_t, active_t) + b_second
    centred = pre_norm - jnp.mean(pre_norm, axis=0, keepdims=True)
    inv_std = lax.rsqrt(jnp.mean(centred * centred, axis=0, keepdims=True) + epsilon)
    normed = centred * inv_std
    updated_t = (state_t.astype(F32) + gain * normed).astype(BF16)
    cot = cot_t.astype(F32)
    terms = cot * normed
    q = cot * gain
    mean_q = jnp.mean(q, axis=0, keepdims=True)
    mean_qn = jnp.mean(q * normed, axis=0, keepdims=True)
    d_norm_t = (inv_std * (q - mean_q - normed * mean_qn)).astype(BF16)
    d_hidden_t = (dot(w_second, d_norm_t) * slope).astype(BF16)
    return updated_t, terms, active_t, d_norm_t, d_hidden_t


def d_aggregate_of(w_first, d_hidden_t):
    return dot(w_first[w_first.shape[1] :], d_hidden_t).astype(BF16)


def first_products(d_hidden_t, state, aggregate):
    ones = jnp.ones((state.shape[0], ONES), BF16)
    return dot(d_hidden_t, joined_lanes([state, aggregate, ones]))


def second_products(active_t, d_norm_t):
    ones = jnp.ones((16, active_t.shape[1]), BF16)
    return dot_nt(jnp.concatenate([active_t, ones], axis=0), d_norm_t)


def fetch_kernel(*refs):
    count = (len(refs) - 3) // 2
    sources, targets = refs[:count], refs[count : 2 * count]
    even_side_ref, odd_side_ref, arrived = refs[2 * count :]
    copies = [
        pltpu.make_async_copy(source, target, arrived.at[k])
        for k, (source, target) in enumerate(zip(sources, targets))
    ]
    for copy in copies:
        copy.start()
    copies[0].wait()
    state, edge = targets[0], even_side_ref.shape[0]
    odd = device_is_odd()
    head, tail = state[pl.ds(0, edge), :], state[pl.ds(state.shape[0] - edge, edge), :]
    even_side_ref[...] = jnp.where(odd, head, tail)
    odd_side_ref[...] = jnp.where(odd, tail, head)
    for copy in copies[1:]:
        copy.wait()


def inner_kernel(
    col_hbm,
    counts_hbm,
    cot_hbm,
    state_ref,
    w_msg_ref,
    w_first_ref,
    w_second_ref,
    b_first_ref,
    b_second_ref,
    gain_ref,
    first_t_ref,
    second_t_ref,
    columns_ref,
    edge_state_ref,
    edge_cot_ref,
    edge_sum_ref,
    band_ref,
    updated_ref,
    d_hidden_ref,
    first_sums_ref,
    second_sums_ref,
    msg_sums_ref,
    gain_sums_ref,
    col_ref,
    counts_ref,
    cot_ref,
    arrived,
):
    blocks, tiles, size, _ = counts_ref.shape
    features = state_ref.shape[1]
    edge_rows = [*range(WIN), *range(blocks - WIN, blocks)]
    inner_rows = range(WIN, blocks - WIN)
    part = blocks // 4

    copies = [(col_hbm, col_ref)]
    copies += [
        (counts_hbm.at[pl.ds(b, part)], counts_ref.at[pl.ds(b, part)])
        for b in range(0, blocks, part)
    ]
    copies.append((cot_hbm, cot_ref))
    copies = [
        pltpu.make_async_copy(source, target, arrived.at[k])
        for k, (source, target) in enumerate(copies)
    ]
    for copy in copies:
        copy.start()

    def rows(block, count=1):
        return pl.ds(block * size, count * size)

    w_msg, w_first, w_second = w_msg_ref[...], w_first_ref[...], w_second_ref[...]
    first_t = joined_lanes([w_first[:features].T, w_first[features:].T])
    second_t = w_second.T
    columns = [column(ref, size) for ref in (b_first_ref, b_second_ref, gain_ref)]
    first_t_ref[...] = first_t
    second_t_ref[...] = second_t
    for k in range(3):
        columns_ref[k] = columns[k]
    state_t = [state_ref[rows(b), :].T for b in range(blocks)]
    for k, b in enumerate(edge_rows):
        edge_state_ref[:, rows(k)] = state_t[b]

    for copy in copies:
        copy.wait()
    for k, b in enumerate(edge_rows):
        edge_cot_ref[:, rows(k)] = cot_ref[rows(b), :].T
    nothing = jnp.zeros((size, size), BF16)
    for b in [*inner_rows, *edge_rows]:
        for place in range(BAND):
            if place != WIN:
                band_ref[b, place] = nothing
        band_ref[b, WIN] = counts_ref[b, 0].astype(F32).astype(BF16)
        own = col_ref[0, b]
        for t in range(1, tiles):
            band_ref[b, col_ref[t, b] - own + WIN] += counts_ref[b, t].astype(F32).astype(BF16)

    state = state_ref[...]
    wide = joined_lanes([dot(state, w_msg).astype(BF16), state])

    def neighbour_sum(b):
        first, last = max(b - WIN, 0), min(b + WIN, blocks - 1)
        tiles_of = [band_ref[b, block - b + WIN] for block in range(first, last + 1)]
        return dot(joined_lanes(tiles_of), wide[first * size : (last + 1) * size])

    for k, b in enumerate(edge_rows):
        edge_sum_ref[k] = neighbour_sum(b)
    summed = jnp.concatenate([neighbour_sum(b).astype(BF16) for b in inner_rows], axis=0)
    aggregate, summed = summed[:, :features], summed[:, features:]
    updated_t, terms, active_t, d_norm_t, d_hidden_t = node_layer(
        joined_lanes([state_t[b] for b in inner_rows]),
        joined_lanes(blocks_turned(aggregate)),
        joined_lanes([cot_ref[rows(b), :].T for b in inner_rows]),
        first_t,
        second_t,
        w_second,
        columns,
    )
    updated_ref[...] = updated_t
    d_hidden_ref[...] = d_hidden_t
    d_aggregate_t = d_aggregate_of(w_first, d_hidden_t)
    first_sums_ref[...] = first_products(
        d_hidden_t, state_ref[rows(WIN, len(inner_rows)), :], aggregate
    )
    second_sums_ref[...] = second_products(active_t, d_norm_t)
    msg_sums_ref[...] = dot(d_aggregate_t, summed)
    gain_sums_ref[...] = sum(
        terms[:, k * size : (k + 1) * size] for k in range(len(inner_rows))
    )


def outer_kernel(
    grad_scale,
    got_even_ref,
    got_odd_ref,
    state_ref,
    w_msg_ref,
    w_first_ref,
    w_second_ref,
    first_t_ref,
    second_t_ref,
    columns_ref,
    edge_state_ref,
    edge_cot_ref,
    edge_sum_ref,
    band_ref,
    first_sums_ref,
    second_sums_ref,
    msg_sums_ref,
    gain_sums_ref,
    grads_ref,
    updated_ref,
    d_hidden_ref,
):
    blocks, _, size, _ = band_ref.shape
    features = w_msg_ref.shape[0]
    odd = device_is_odd()
    got_even, got_odd = got_even_ref[...], got_odd_ref[...]
    below, above = jnp.where(odd, got_even, got_odd), jnp.where(odd, got_odd, got_even)

    w_msg = w_msg_ref[...]
    below, above = (
        joined_lanes([dot(halo, w_msg).astype(BF16), halo]) for halo in (below, above)
    )
    summed = []
    for k in range(WIN):
        far = joined_lanes([band_ref[k, place] for place in range(WIN - k)])
        summed.append(edge_sum_ref[k] + dot(far, below[k * size :]))
    for k in range(WIN):
        far = [band_ref[blocks - WIN + k, place] for place in range(2 * WIN - k, BAND)]
        summed.append(edge_sum_ref[WIN + k] + dot(joined_lanes(far), above[: (k + 1) * size]))
    summed = jnp.concatenate(summed, axis=0).astype(BF16)
    aggregate, summed = summed[:, :features], summed[:, features:]
    updated_t, terms, active_t, d_norm_t, d_hidden_t = node_layer(
        edge_state_ref[...],
        joined_lanes(blocks_turned(aggregate)),
        edge_cot_ref[...],
        first_t_ref[...],
        second_t_ref[...],
        w_second_ref[...],
        [columns_ref[k] for k in range(3)],
    )
    updated_ref[...] = updated_t
    d_hidden_ref[...] = d_hidden_t
    d_aggregate_t = d_aggregate_of(w_first_ref[...], d_hidden_t)

    width = WIN * size
    ends = [state_ref[pl.ds(0, width), :], state_ref[pl.ds((blocks - WIN) * size, width), :]]
    first_sums = first_sums_ref[...] + first_products(
        d_hidden_t, jnp.concatenate(ends, axis=0), aggregate
    )
    second_sums = second_sums_ref[...] + second_products(active_t, d_norm_t)
    msg_sums = msg_sums_ref[...] + dot(d_aggregate_t, summed)
    gain_sums = gain_sums_ref[...]
    for k in range(2 * WIN):
        gain_sums = gain_sums + terms[:, k * size : (k + 1) * size]

    chunk = grads_ref.shape[1] - BIAS_ROWS
    turned = [first_sums[:, k * size : (k + 1) * size].T for k in range(3)]
    sums = (
        jnp.concatenate([turned[0], turned[1], second_sums[:features], msg_sums.T], axis=0)
        * grad_scale
    ).astype(SENT)
    bias = (
        jnp.concatenate(
            [
                turned[2][:1],
                second_sums[features : features + 1],
                jnp.sum(gain_sums.T, axis=0, keepdims=True),
            ],
            axis=0,
        )
        * grad_scale
    )
    bias_high = bias.astype(SENT)
    bias_low = (bias - bias_high.astype(F32)).astype(SENT)
    bias = jnp.concatenate(
        [bias_high, bias_low, jnp.zeros((BIAS_ROWS - 6, features), SENT)], axis=0
    )
    nothing = jnp.zeros((chunk, features), SENT)
    for k in range(grads_ref.shape[0]):
        block = sums[k * chunk : (k + 1) * chunk] if k * chunk < sums.shape[0] else nothing
        grads_ref[k] = jnp.concatenate([block, bias], axis=0)


def owed_kernel(
    band_ref, w_first_ref, inner_ref, outer_ref, owed_ref, send_even_ref, send_odd_ref
):
    blocks, _, size, _ = band_ref.shape
    odd = device_is_odd()
    w_first = w_first_ref[...]
    inner = d_aggregate_of(w_first, inner_ref[...])
    outer = d_aggregate_of(w_first, outer_ref[...])

    def d_aggregate(b):
        if WIN <= b < blocks - WIN:
            return inner[:, (b - WIN) * size : (b - WIN + 1) * size]
        k = b if b < WIN else b - blocks + 2 * WIN
        return outer[:, k * size : (k + 1) * size]

    def owed(block):
        near = range(max(block - WIN, 0), min(block + WIN, blocks - 1) + 1)
        tiles_of = [band_ref[b, block - b + WIN] for b in near]
        return dot(
            joined_lanes([d_aggregate(b) for b in near]), jnp.concatenate(tiles_of, axis=0)
        )

    for k in range(WIN):
        to_below = owed(k - WIN).astype(BF16)
        to_above = owed(blocks + k).astype(BF16)
        send_even_ref[k] = jnp.where(odd, to_below, to_above)
        send_odd_ref[k] = jnp.where(odd, to_above, to_below)
    for b in range(blocks):
        owed_ref[b] = owed(b)


def sum_kernel(parts_ref, spread_ref, bias_ref):
    total = parts_ref[0].astype(F32)
    for k in range(1, parts_ref.shape[0]):
        total = total + parts_ref[k].astype(F32)
    chunk = spread_ref.shape[1]
    weights = total[:chunk].astype(spread_ref.dtype)
    for k in range(spread_ref.shape[0]):
        spread_ref[k] = weights
    bias_ref[...] = total[chunk:]


def result_kernel(
    even_ref,
    odd_ref,
    cot_hbm,
    w_msg_ref,
    w_first_ref,
    inner_updated_ref,
    outer_updated_ref,
    inner_d_hidden_ref,
    outer_d_hidden_ref,
    owed_ref,
    bias_ref,
    updated_ref,
    grad_state_ref,
    b_first_ref,
    b_second_ref,
    gain_ref,
    cot_ref,
    arrived,
):
    blocks, features, size = owed_ref.shape
    copy = pltpu.make_async_copy(cot_hbm, cot_ref, arrived)
    copy.start()
    odd = device_is_odd()
    even_part, odd_part = even_ref[...].astype(F32), odd_ref[...].astype(F32)
    from_below = jnp.where(odd, even_part, odd_part)
    from_above = jnp.where(odd, odd_part, even_part)
    weights = joined_lanes([w_first_ref[pl.ds(0, features), :], w_msg_ref[...]])
    copy.wait()
    for b in range(blocks):
        owed = owed_ref[b]
        if b < WIN:
            owed = owed + from_below[b]
        elif b >= blocks - WIN:
            owed = owed + from_above[b - blocks + WIN]
        if WIN <= b < blocks - WIN:
            k, updated, d_hidden = b - WIN, inner_updated_ref, inner_d_hidden_ref
        else:
            k = b if b < WIN else b - blocks + 2 * WIN
            updated, d_hidden = outer_updated_ref, outer_d_hidden_ref
        lanes, rows = pl.ds(k * size, size), pl.ds(b * size, size)
        change = dot(weights, jnp.concatenate([d_hidden[:, lanes], owed.astype(BF16)], axis=0))
        grad_state_ref[rows, :] = (cot_ref[rows, :].astype(F32) + change.T).astype(BF16)
        updated_ref[rows, :] = updated[:, lanes].T
    for k, ref in enumerate((b_first_ref, b_second_ref, gain_ref)):
        ref[...] = bias_ref[pl.ds(k, 1), :] + bias_ref[pl.ds(k + 3, 1), :]


def unpack_kernel(rows_ref, msg_ref, first_ref, second_ref):
    place = 0
    for ref in (first_ref, second_ref, msg_ref):
        count = ref.shape[0]
        ref[...] = rows_ref[pl.ds(place, count), :].astype(F32)
        place += count


def swapped(block, parity):
    last = lax.axis_size(AXES) - 1
    lower = range(parity, last, 2)
    return lax.ppermute(block, AXES, [(i, i + 1) for i in lower] + [(i + 1, i) for i in lower])


def call(kernel, name, outs, operands, scratch=(), limit=16, flops=0):
    specs = [pl.BlockSpec(memory_space=space) for _, space in operands]
    arrays = [kept(array, space) for array, space in operands]
    return pl.pallas_call(
        kernel,
        out_shape=tuple(outs),
        in_specs=specs,
        out_specs=tuple(pl.BlockSpec(memory_space=pltpu.VMEM) for _ in outs),
        scratch_shapes=list(scratch),
        compiler_params=pltpu.CompilerParams(vmem_limit_bytes=limit * 1024 * 1024),
        cost_estimate=pl.CostEstimate(
            flops=flops, bytes_accessed=1_000_000, transcendentals=0
        ),
        name=name,
    )(*arrays)


def shards(
    node_state,
    w_msg,
    w_first,
    b_first,
    w_second,
    b_second,
    ln_gain,
    col_index,
    edge_counts,
    cotangent,
):
    nodes, features = node_state.shape
    blocks, tiles, size, _ = edge_counts.shape
    devices = lax.axis_size(AXES)
    grad_scale = 1.0 / math.sqrt(nodes * devices)
    chunk = -(-4 * features // (devices * 8)) * 8
    inner = blocks - 2 * WIN
    edge = 2 * WIN
    vmem, hbm = pltpu.VMEM, pltpu.HBM
    result = jax.ShapeDtypeStruct

    row = lambda vector: vector.reshape(1, features)
    sources = (
        node_state,
        w_msg,
        w_first,
        w_second,
        row(b_first),
        row(b_second),
        row(ln_gain),
    )
    *fetched, even_side, odd_side = call(
        fetch_kernel,
        "fetch",
        [vmem(array.shape, array.dtype) for array in sources]
        + [vmem((WIN * size, features), BF16)] * 2,
        [(array, hbm) for array in sources],
        scratch=(pltpu.SemaphoreType.DMA((len(sources),)),),
    )
    state, w_msg_here, w_first_here, w_second_here, *vectors = fetched
    got_even = swapped(even_side, 0)
    got_odd = swapped(odd_side, 1)

    (
        first_t,
        second_t,
        columns,
        edge_state,
        edge_cot,
        edge_sum,
        band,
        inner_updated,
        inner_d_hidden,
        first_sums,
        second_sums,
        msg_sums,
        gain_sums,
    ) = call(
        inner_kernel,
        "inner_rows",
        (
            vmem((features, 2 * features), BF16),
            vmem((features, features), BF16),
            vmem((3, features, size), F32),
            vmem((features, edge * size), BF16),
            vmem((features, edge * size), BF16),
            vmem((edge, size, 2 * features), F32),
            vmem((blocks, BAND, size, size), BF16),
            vmem((features, inner * size), BF16),
            vmem((features, inner * size), BF16),
            vmem((features, 2 * features + ONES), F32),
            vmem((features + 16, features), F32),
            vmem((features, features), F32),
            vmem((features, size), F32),
        ),
        [(col_index.T, hbm), (edge_counts, hbm), (cotangent, hbm)]
        + [
            (array, vmem)
            for array in (state, w_msg_here, w_first_here, w_second_here, *vectors)
        ],
        scratch=(
            pltpu.SMEM((tiles, blocks), jnp.int32),
            vmem(edge_counts.shape, jnp.int32),
            vmem((nodes, features), BF16),
            pltpu.SemaphoreType.DMA((6,)),
        ),
        limit=32,
        flops=700_000_000,
    )

    grads, outer_updated, outer_d_hidden = call(
        functools.partial(outer_kernel, grad_scale),
        "outer_rows",
        (
            vmem((devices, chunk + BIAS_ROWS, features), SENT),
            vmem((features, edge * size), BF16),
            vmem((features, edge * size), BF16),
        ),
        [
            (array, vmem)
            for array in (
                got_even,
                got_odd,
                state,
                w_msg_here,
                w_first_here,
                w_second_here,
                first_t,
                second_t,
                columns,
                edge_state,
                edge_cot,
                edge_sum,
                band,
                first_sums,
                second_sums,
                msg_sums,
                gain_sums,
            )
        ],
        flops=300_000_000,
    )

    parts = lax.all_to_all(grads, AXES, 0, 0, tiled=True)
    owed, send_even, send_odd = call(
        owed_kernel,
        "owed",
        (
            vmem((blocks, features, size), F32),
            vmem((WIN, features, size), BF16),
            vmem((WIN, features, size), BF16),
        ),
        [(array, vmem) for array in (band, w_first_here, inner_d_hidden, outer_d_hidden)],
        flops=200_000_000,
    )
    owed_even = swapped(send_even, 0)
    owed_odd = swapped(send_odd, 1)
    spread, bias = call(
        sum_kernel,
        "sum",
        (vmem((devices, chunk, features), SENT), vmem((BIAS_ROWS, features), F32)),
        [(parts, vmem)],
        flops=10_000_000_000,
    )
    updated, grad_state, g_b_first, g_b_second, g_gain = call(
        result_kernel,
        "results",
        (
            result((nodes, features), BF16),
            result((nodes, features), BF16),
            result((1, features), F32),
            result((1, features), F32),
            result((1, features), F32),
        ),
        [(owed_even, vmem), (owed_odd, vmem), (cotangent, hbm)]
        + [
            (array, vmem)
            for array in (
                w_msg_here,
                w_first_here,
                inner_updated,
                outer_updated,
                inner_d_hidden,
                outer_d_hidden,
                owed,
                bias,
            )
        ],
        scratch=(vmem((nodes, features), BF16), pltpu.SemaphoreType.DMA),
        flops=50_000_000_000,
    )

    whole = lax.all_to_all(spread, AXES, 0, 0, tiled=True)
    g_msg, g_first, g_second = call(
        unpack_kernel,
        "unpack",
        (
            result((features, features), F32),
            result((2 * features, features), F32),
            result((features, features), F32),
        ),
        [(whole.reshape(devices * chunk, features), vmem)],
    )
    flat = lambda vector: vector.reshape(features)
    return (
        updated,
        grad_state,
        g_msg,
        g_first,
        flat(g_b_first),
        g_second,
        flat(g_b_second),
        flat(g_gain),
    )


def solution(mesh):
    split = P(AXES, None)
    return jax.shard_map(
        shards,
        mesh=mesh,
        in_specs=(split, P(), P(), P(), P(), P(), P(), split, P(AXES, None, None, None), split),
        out_specs=(split, split, P(), P(), P(), P(), P(), P()),
        check_vma=False,
    )
```

```python
import functools
import math

import jax
import jax.numpy as jnp
from jax import lax
from jax.experimental import pallas as pl
from jax.experimental.pallas import tpu as pltpu
from jax.sharding import PartitionSpec as P

WIN = 2
BAND = 2 * WIN + 1
epsilon = 1e-05
AXES = ("dom", "feat")
BF16, F32 = jnp.bfloat16, jnp.float32
SENT = BF16
ONES = 16
BIAS_ROWS = 8

kept = pltpu.with_memory_space_constraint


def dot(left, right):
    return jnp.dot(left, right, preferred_element_type=F32)


def dot_nt(left, right):
    return lax.dot_general(left, right, (((1,), (1,)), ((), ())), preferred_element_type=F32)


def joined_lanes(parts):
    return jnp.concatenate(parts, axis=1)


def device_is_odd():
    index = lax.axis_index("dom") * lax.axis_size("feat") + lax.axis_index("feat")
    return index % 2 == 1


def column(row_ref, width):
    return jnp.broadcast_to(row_ref[...], (width, row_ref.shape[1])).T


def blocks_turned(array):
    size = array.shape[1]
    return [array[k : k + size].T for k in range(0, array.shape[0], size)]


def node_layer(state_t, aggregate_t, cot_t, first_t, second_t, w_second, columns):
    features, width = state_t.shape
    b_first, b_second, gain = (
        joined_lanes([c] * (width // c.shape[1])) for c in columns
    )
    pre_hidden = dot(first_t, jnp.concatenate([state_t, aggregate_t], axis=0)) + b_first
    sigmoid = 0.5 * jnp.tanh(0.5 * pre_hidden) + 0.5
    silu = pre_hidden * sigmoid
    active_t = silu.astype(BF16)
    slope = sigmoid + silu * (1.0 - sigmoid)
    pre_norm = dot(second_t, active_t) + b_second
    centred = pre_norm - jnp.mean(pre_norm, axis=0, keepdims=True)
    inv_std = lax.rsqrt(jnp.mean(centred * centred, axis=0, keepdims=True) + epsilon)
    normed = centred * inv_std
    updated_t = (state_t.astype(F32) + gain * normed).astype(BF16)
    cot = cot_t.astype(F32)
    terms = cot * normed
    q = cot * gain
    mean_q = jnp.mean(q, axis=0, keepdims=True)
    mean_qn = jnp.mean(q * normed, axis=0, keepdims=True)
    d_norm_t = (inv_std * (q - mean_q - normed * mean_qn)).astype(BF16)
    d_hidden_t = (dot(w_second, d_norm_t) * slope).astype(BF16)
    return updated_t, terms, active_t, d_norm_t, d_hidden_t


def d_aggregate_of(w_first, d_hidden_t):
    return dot(w_first[w_first.shape[1] :], d_hidden_t).astype(BF16)


def node_products(parts, right):
    ones = jnp.ones((ONES, right.shape[1]), BF16)
    return dot_nt(jnp.concatenate([*parts, ones], axis=0), right)


def fetch_kernel(*refs):
    count = (len(refs) - 3) // 2
    sources, targets = refs[:count], refs[count : 2 * count]
    even_side_ref, odd_side_ref, arrived = refs[2 * count :]
    copies = [
        pltpu.make_async_copy(source, target, arrived.at[k])
        for k, (source, target) in enumerate(zip(sources, targets))
    ]
    for copy in copies:
        copy.start()
    copies[0].wait()
    state, edge = targets[0], even_side_ref.shape[0]
    odd = device_is_odd()
    head, tail = state[pl.ds(0, edge), :], state[pl.ds(state.shape[0] - edge, edge), :]
    even_side_ref[...] = jnp.where(odd, head, tail)
    odd_side_ref[...] = jnp.where(odd, tail, head)
    for copy in copies[1:]:
        copy.wait()


def inner_kernel(
    col_hbm,
    counts_hbm,
    cot_hbm,
    state_ref,
    w_msg_ref,
    w_first_ref,
    w_second_ref,
    b_first_ref,
    b_second_ref,
    gain_ref,
    first_t_ref,
    second_t_ref,
    columns_ref,
    edge_state_ref,
    edge_cot_ref,
    edge_sum_ref,
    band_ref,
    updated_hbm,
    d_hidden_ref,
    first_sums_ref,
    second_sums_ref,
    msg_sums_ref,
    gain_sums_ref,
    col_ref,
    counts_ref,
    cot_ref,
    updated_ref,
    arrived,
    left,
):
    blocks, tiles, size, _ = counts_ref.shape
    features = state_ref.shape[1]
    edge_rows = [*range(WIN), *range(blocks - WIN, blocks)]
    inner_rows = range(WIN, blocks - WIN)
    part = blocks // 4

    copies = [(col_hbm, col_ref)]
    copies += [
        (counts_hbm.at[pl.ds(b, part)], counts_ref.at[pl.ds(b, part)])
        for b in range(0, blocks, part)
    ]
    copies.append((cot_hbm, cot_ref))
    copies = [
        pltpu.make_async_copy(source, target, arrived.at[k])
        for k, (source, target) in enumerate(copies)
    ]
    for copy in copies:
        copy.start()

    def rows(block, count=1):
        return pl.ds(block * size, count * size)

    w_msg, w_first, w_second = w_msg_ref[...], w_first_ref[...], w_second_ref[...]
    first_t = joined_lanes([w_first[:features].T, w_first[features:].T])
    second_t = w_second.T
    columns = [column(ref, size) for ref in (b_first_ref, b_second_ref, gain_ref)]
    first_t_ref[...] = first_t
    second_t_ref[...] = second_t
    for k in range(3):
        columns_ref[k] = columns[k]
    state_t = [state_ref[rows(b), :].T for b in range(blocks)]
    for k, b in enumerate(edge_rows):
        edge_state_ref[:, rows(k)] = state_t[b]

    nothing = jnp.zeros((size, size), BF16)
    copies[0].wait()
    for b in range(blocks):
        if b % part == 0:
            copies[1 + b // part].wait()
        for place in range(BAND):
            if place != WIN:
                band_ref[b, place] = nothing
        band_ref[b, WIN] = counts_ref[b, 0].astype(F32).astype(BF16)
        own = col_ref[0, b]
        for t in range(1, tiles):
            band_ref[b, col_ref[t, b] - own + WIN] += counts_ref[b, t].astype(F32).astype(BF16)
    copies[-1].wait()
    for k, b in enumerate(edge_rows):
        edge_cot_ref[:, rows(k)] = cot_ref[rows(b), :].T

    state = state_ref[...]
    wide = joined_lanes([dot(state, w_msg).astype(BF16), state])

    def neighbour_sum(b):
        first, last = max(b - WIN, 0), min(b + WIN, blocks - 1)
        tiles_of = [band_ref[b, block - b + WIN] for block in range(first, last + 1)]
        return dot(joined_lanes(tiles_of), wide[first * size : (last + 1) * size])

    for k, b in enumerate(edge_rows):
        edge_sum_ref[k] = neighbour_sum(b)
    summed = jnp.concatenate([neighbour_sum(b).astype(BF16) for b in inner_rows], axis=0)
    aggregate, summed = summed[:, :features], summed[:, features:]
    inner_state_t = joined_lanes([state_t[b] for b in inner_rows])
    aggregate_t = joined_lanes(blocks_turned(aggregate))
    updated_t, terms, active_t, d_norm_t, d_hidden_t = node_layer(
        inner_state_t,
        aggregate_t,
        joined_lanes([cot_ref[rows(b), :].T for b in inner_rows]),
        first_t,
        second_t,
        w_second,
        columns,
    )
    updated_ref[...] = updated_t
    updated_copy = pltpu.make_async_copy(updated_ref, updated_hbm, left)
    updated_copy.start()
    d_hidden_ref[...] = d_hidden_t
    d_aggregate_t = d_aggregate_of(w_first, d_hidden_t)
    first_sums_ref[...] = node_products([inner_state_t, aggregate_t], d_hidden_t)
    second_sums_ref[...] = node_products([active_t], d_norm_t)
    msg_sums_ref[...] = dot(d_aggregate_t, summed)
    gain_sums_ref[...] = sum(
        terms[:, k * size : (k + 1) * size] for k in range(len(inner_rows))
    )
    updated_copy.wait()


def outer_kernel(
    grad_scale,
    got_even_ref,
    got_odd_ref,
    w_msg_ref,
    w_first_ref,
    w_second_ref,
    first_t_ref,
    second_t_ref,
    columns_ref,
    edge_state_ref,
    edge_cot_ref,
    edge_sum_ref,
    band_ref,
    first_sums_ref,
    second_sums_ref,
    msg_sums_ref,
    gain_sums_ref,
    grads_ref,
    updated_hbm,
    d_hidden_ref,
    updated_ref,
    left,
):
    blocks, _, size, _ = band_ref.shape
    features = w_msg_ref.shape[0]
    odd = device_is_odd()
    got_even, got_odd = got_even_ref[...], got_odd_ref[...]
    below, above = jnp.where(odd, got_even, got_odd), jnp.where(odd, got_odd, got_even)

    w_msg = w_msg_ref[...]
    below, above = (
        joined_lanes([dot(halo, w_msg).astype(BF16), halo]) for halo in (below, above)
    )
    summed = []
    for k in range(WIN):
        far = joined_lanes([band_ref[k, place] for place in range(WIN - k)])
        summed.append(edge_sum_ref[k] + dot(far, below[k * size :]))
    for k in range(WIN):
        far = [band_ref[blocks - WIN + k, place] for place in range(2 * WIN - k, BAND)]
        summed.append(edge_sum_ref[WIN + k] + dot(joined_lanes(far), above[: (k + 1) * size]))
    summed = jnp.concatenate(summed, axis=0).astype(BF16)
    aggregate, summed = summed[:, :features], summed[:, features:]
    aggregate_t = joined_lanes(blocks_turned(aggregate))
    updated_t, terms, active_t, d_norm_t, d_hidden_t = node_layer(
        edge_state_ref[...],
        aggregate_t,
        edge_cot_ref[...],
        first_t_ref[...],
        second_t_ref[...],
        w_second_ref[...],
        [columns_ref[k] for k in range(3)],
    )
    updated_ref[...] = updated_t
    updated_copy = pltpu.make_async_copy(updated_ref, updated_hbm, left)
    updated_copy.start()
    d_hidden_ref[...] = d_hidden_t
    d_aggregate_t = d_aggregate_of(w_first_ref[...], d_hidden_t)

    first_sums = first_sums_ref[...] + node_products(
        [edge_state_ref[...], aggregate_t], d_hidden_t
    )
    second_sums = second_sums_ref[...] + node_products([active_t], d_norm_t)
    msg_sums = msg_sums_ref[...] + dot(d_aggregate_t, summed)
    gain_sums = gain_sums_ref[...]
    for k in range(2 * WIN):
        gain_sums = gain_sums + terms[:, k * size : (k + 1) * size]

    chunk = grads_ref.shape[1] - BIAS_ROWS
    sums = (
        jnp.concatenate(
            [first_sums[: 2 * features], second_sums[:features], msg_sums.T], axis=0
        )
        * grad_scale
    ).astype(SENT)
    bias = (
        jnp.concatenate(
            [
                first_sums[2 * features : 2 * features + 1],
                second_sums[features : features + 1],
                jnp.sum(gain_sums.T, axis=0, keepdims=True),
            ],
            axis=0,
        )
        * grad_scale
    )
    bias_high = bias.astype(SENT)
    bias_low = (bias - bias_high.astype(F32)).astype(SENT)
    bias = jnp.concatenate(
        [bias_high, bias_low, jnp.zeros((BIAS_ROWS - 6, features), SENT)], axis=0
    )
    nothing = jnp.zeros((chunk, features), SENT)
    for k in range(grads_ref.shape[0]):
        block = sums[k * chunk : (k + 1) * chunk] if k * chunk < sums.shape[0] else nothing
        grads_ref[k] = jnp.concatenate([block, bias], axis=0)
    updated_copy.wait()


def owed_kernel(
    band_ref, w_first_ref, inner_ref, outer_ref, owed_ref, send_even_ref, send_odd_ref
):
    blocks, _, size, _ = band_ref.shape
    odd = device_is_odd()
    w_first = w_first_ref[...]
    inner = d_aggregate_of(w_first, inner_ref[...])
    outer = d_aggregate_of(w_first, outer_ref[...])

    def d_aggregate(b):
        if WIN <= b < blocks - WIN:
            return inner[:, (b - WIN) * size : (b - WIN + 1) * size]
        k = b if b < WIN else b - blocks + 2 * WIN
        return outer[:, k * size : (k + 1) * size]

    def owed(block):
        near = range(max(block - WIN, 0), min(block + WIN, blocks - 1) + 1)
        tiles_of = [band_ref[b, block - b + WIN] for b in near]
        return dot(
            joined_lanes([d_aggregate(b) for b in near]), jnp.concatenate(tiles_of, axis=0)
        )

    for k in range(WIN):
        to_below = owed(k - WIN).astype(BF16)
        to_above = owed(blocks + k).astype(BF16)
        send_even_ref[k] = jnp.where(odd, to_below, to_above)
        send_odd_ref[k] = jnp.where(odd, to_above, to_below)
    for b in range(blocks):
        owed_ref[b] = owed(b)


def sum_kernel(parts_ref, spread_ref, bias_ref):
    total = parts_ref[0].astype(F32)
    for k in range(1, parts_ref.shape[0]):
        total = total + parts_ref[k].astype(F32)
    chunk = spread_ref.shape[1]
    weights = total[:chunk].astype(spread_ref.dtype)
    for k in range(spread_ref.shape[0]):
        spread_ref[k] = weights
    bias_ref[...] = total[chunk:]


def result_kernel(
    even_ref,
    odd_ref,
    cot_hbm,
    w_msg_ref,
    w_first_ref,
    inner_updated_hbm,
    outer_updated_hbm,
    inner_d_hidden_ref,
    outer_d_hidden_ref,
    owed_ref,
    bias_ref,
    updated_ref,
    grad_state_ref,
    b_first_ref,
    b_second_ref,
    gain_ref,
    cot_ref,
    inner_updated_ref,
    outer_updated_ref,
    arrived,
):
    blocks, features, size = owed_ref.shape
    copies = [
        pltpu.make_async_copy(source, target, arrived.at[k])
        for k, (source, target) in enumerate(
            (
                (cot_hbm, cot_ref),
                (inner_updated_hbm, inner_updated_ref),
                (outer_updated_hbm, outer_updated_ref),
            )
        )
    ]
    for copy in copies:
        copy.start()
    odd = device_is_odd()
    even_part, odd_part = even_ref[...].astype(F32), odd_ref[...].astype(F32)
    from_below = jnp.where(odd, even_part, odd_part)
    from_above = jnp.where(odd, odd_part, even_part)
    weights = joined_lanes([w_first_ref[pl.ds(0, features), :], w_msg_ref[...]])
    for copy in copies:
        copy.wait()
    for b in range(blocks):
        owed = owed_ref[b]
        if b < WIN:
            owed = owed + from_below[b]
        elif b >= blocks - WIN:
            owed = owed + from_above[b - blocks + WIN]
        if WIN <= b < blocks - WIN:
            k, updated, d_hidden = b - WIN, inner_updated_ref, inner_d_hidden_ref
        else:
            k = b if b < WIN else b - blocks + 2 * WIN
            updated, d_hidden = outer_updated_ref, outer_d_hidden_ref
        lanes, rows = pl.ds(k * size, size), pl.ds(b * size, size)
        change = dot(weights, jnp.concatenate([d_hidden[:, lanes], owed.astype(BF16)], axis=0))
        grad_state_ref[rows, :] = (cot_ref[rows, :].astype(F32) + change.T).astype(BF16)
        updated_ref[rows, :] = updated[:, lanes].T
    for k, ref in enumerate((b_first_ref, b_second_ref, gain_ref)):
        ref[...] = bias_ref[pl.ds(k, 1), :] + bias_ref[pl.ds(k + 3, 1), :]


def unpack_kernel(rows_ref, msg_ref, first_ref, second_ref):
    place = 0
    for ref in (first_ref, second_ref, msg_ref):
        count = ref.shape[0]
        ref[...] = rows_ref[pl.ds(place, count), :].astype(F32)
        place += count


def swapped(block, parity):
    last = lax.axis_size(AXES) - 1
    lower = range(parity, last, 2)
    return lax.ppermute(block, AXES, [(i, i + 1) for i in lower] + [(i + 1, i) for i in lower])


def call(kernel, name, outs, operands, scratch=(), limit=16, flops=0):
    specs = [pl.BlockSpec(memory_space=space) for _, space in operands]
    arrays = [kept(array, space) for array, space in operands]
    return pl.pallas_call(
        kernel,
        out_shape=tuple(outs),
        in_specs=specs,
        out_specs=tuple(
            pl.BlockSpec(memory_space=getattr(out, "memory_space", pltpu.VMEM)) for out in outs
        ),
        scratch_shapes=list(scratch),
        compiler_params=pltpu.CompilerParams(vmem_limit_bytes=limit * 1024 * 1024),
        cost_estimate=pl.CostEstimate(
            flops=flops, bytes_accessed=1_000_000, transcendentals=0
        ),
        name=name,
    )(*arrays)


def shards(
    node_state,
    w_msg,
    w_first,
    b_first,
    w_second,
    b_second,
    ln_gain,
    col_index,
    edge_counts,
    cotangent,
):
    nodes, features = node_state.shape
    blocks, tiles, size, _ = edge_counts.shape
    devices = lax.axis_size(AXES)
    grad_scale = 1.0 / math.sqrt(nodes * devices)
    chunk = -(-4 * features // (devices * 8)) * 8
    inner = blocks - 2 * WIN
    edge = 2 * WIN
    vmem, hbm = pltpu.VMEM, pltpu.HBM
    result = jax.ShapeDtypeStruct

    row = lambda vector: vector.reshape(1, features)
    sources = (
        node_state,
        w_msg,
        w_first,
        w_second,
        row(b_first),
        row(b_second),
        row(ln_gain),
    )
    *fetched, even_side, odd_side = call(
        fetch_kernel,
        "fetch",
        [vmem(array.shape, array.dtype) for array in sources]
        + [vmem((WIN * size, features), BF16)] * 2,
        [(array, hbm) for array in sources],
        scratch=(pltpu.SemaphoreType.DMA((len(sources),)),),
    )
    state, w_msg_here, w_first_here, w_second_here, *vectors = fetched
    got_even = swapped(even_side, 0)
    got_odd = swapped(odd_side, 1)

    (
        first_t,
        second_t,
        columns,
        edge_state,
        edge_cot,
        edge_sum,
        band,
        inner_updated,
        inner_d_hidden,
        first_sums,
        second_sums,
        msg_sums,
        gain_sums,
    ) = call(
        inner_kernel,
        "inner_rows",
        (
            vmem((features, 2 * features), BF16),
            vmem((features, features), BF16),
            vmem((3, features, size), F32),
            vmem((features, edge * size), BF16),
            vmem((features, edge * size), BF16),
            vmem((edge, size, 2 * features), F32),
            vmem((blocks, BAND, size, size), BF16),
            hbm((features, inner * size), BF16),
            vmem((features, inner * size), BF16),
            vmem((2 * features + ONES, features), F32),
            vmem((features + ONES, features), F32),
            vmem((features, features), F32),
            vmem((features, size), F32),
        ),
        [(col_index.T, hbm), (edge_counts, hbm), (cotangent, hbm)]
        + [
            (array, vmem)
            for array in (state, w_msg_here, w_first_here, w_second_here, *vectors)
        ],
        scratch=(
            pltpu.SMEM((tiles, blocks), jnp.int32),
            vmem(edge_counts.shape, jnp.int32),
            vmem((nodes, features), BF16),
            vmem((features, inner * size), BF16),
            pltpu.SemaphoreType.DMA((6,)),
            pltpu.SemaphoreType.DMA,
        ),
        limit=32,
        flops=700_000_000,
    )

    grads, outer_updated, outer_d_hidden = call(
        functools.partial(outer_kernel, grad_scale),
        "outer_rows",
        (
            vmem((devices, chunk + BIAS_ROWS, features), SENT),
            hbm((features, edge * size), BF16),
            vmem((features, edge * size), BF16),
        ),
        [
            (array, vmem)
            for array in (
                got_even,
                got_odd,
                w_msg_here,
                w_first_here,
                w_second_here,
                first_t,
                second_t,
                columns,
                edge_state,
                edge_cot,
                edge_sum,
                band,
                first_sums,
                second_sums,
                msg_sums,
                gain_sums,
            )
        ],
        scratch=(vmem((features, edge * size), BF16), pltpu.SemaphoreType.DMA),
        flops=300_000_000,
    )

    parts = lax.all_to_all(grads, AXES, 0, 0, tiled=True)
    owed, send_even, send_odd = call(
        owed_kernel,
        "owed",
        (
            vmem((blocks, features, size), F32),
            vmem((WIN, features, size), BF16),
            vmem((WIN, features, size), BF16),
        ),
        [(array, vmem) for array in (band, w_first_here, inner_d_hidden, outer_d_hidden)],
        flops=200_000_000,
    )
    owed_even = swapped(send_even, 0)
    owed_odd = swapped(send_odd, 1)
    spread, bias = call(
        sum_kernel,
        "sum",
        (vmem((devices, chunk, features), SENT), vmem((BIAS_ROWS, features), F32)),
        [(parts, vmem)],
        flops=10_000_000_000,
    )
    updated, grad_state, g_b_first, g_b_second, g_gain = call(
        result_kernel,
        "results",
        (
            result((nodes, features), BF16),
            result((nodes, features), BF16),
            result((1, features), F32),
            result((1, features), F32),
            result((1, features), F32),
        ),
        [(owed_even, vmem), (owed_odd, vmem), (cotangent, hbm)]
        + [(w_msg_here, vmem), (w_first_here, vmem), (inner_updated, hbm), (outer_updated, hbm)]
        + [(array, vmem) for array in (inner_d_hidden, outer_d_hidden, owed, bias)],
        scratch=(
            vmem((nodes, features), BF16),
            vmem((features, inner * size), BF16),
            vmem((features, edge * size), BF16),
            pltpu.SemaphoreType.DMA((3,)),
        ),
        flops=50_000_000_000,
    )

    whole = lax.all_to_all(spread, AXES, 0, 0, tiled=True)
    g_msg, g_first, g_second = call(
        unpack_kernel,
        "unpack",
        (
            result((features, features), F32),
            result((2 * features, features), F32),
            result((features, features), F32),
        ),
        [(whole.reshape(devices * chunk, features), vmem)],
    )
    flat = lambda vector: vector.reshape(features)
    return (
        updated,
        grad_state,
        g_msg,
        g_first,
        flat(g_b_first),
        g_second,
        flat(g_b_second),
        flat(g_gain),
    )


def solution(mesh):
    split = P(AXES, None)
    return jax.shard_map(
        shards,
        mesh=mesh,
        in_specs=(split, P(), P(), P(), P(), P(), P(), split, P(AXES, None, None, None), split),
        out_specs=(split, split, P(), P(), P(), P(), P(), P()),
        check_vma=False,
    )
```

```python
import functools
import math

import jax
import jax.numpy as jnp
from jax import lax
from jax.experimental import pallas as pl
from jax.experimental.pallas import tpu as pltpu
from jax.sharding import PartitionSpec as P

WIN = 2
BAND = 2 * WIN + 1
epsilon = 1e-05
AXES = ("dom", "feat")
BF16, F32 = jnp.bfloat16, jnp.float32
SENT = BF16
ONES = 128
BIAS_ROWS = 8

kept = pltpu.with_memory_space_constraint


def dot(left, right):
    return jnp.dot(left, right, preferred_element_type=F32)


def dot_nt(left, right):
    return lax.dot_general(left, right, (((1,), (1,)), ((), ())), preferred_element_type=F32)


def joined_lanes(parts):
    return jnp.concatenate(parts, axis=1)


def device_is_odd():
    index = lax.axis_index("dom") * lax.axis_size("feat") + lax.axis_index("feat")
    return index % 2 == 1


def column(row_ref, width):
    return jnp.broadcast_to(row_ref[...], (width, row_ref.shape[1])).T


def blocks_turned(array):
    size = array.shape[1]
    return [array[k : k + size].T for k in range(0, array.shape[0], size)]


def node_layer(state_t, aggregate_t, cot_t, first_t, second_t, w_second, columns):
    features, width = state_t.shape
    b_first, b_second, gain = (
        joined_lanes([c] * (width // c.shape[1])) for c in columns
    )
    pre_hidden = dot(first_t, jnp.concatenate([state_t, aggregate_t], axis=0)) + b_first
    sigmoid = 0.5 * jnp.tanh(0.5 * pre_hidden) + 0.5
    silu = pre_hidden * sigmoid
    active_t = silu.astype(BF16)
    slope = sigmoid + silu * (1.0 - sigmoid)
    pre_norm = dot(second_t, active_t) + b_second
    centred = pre_norm - jnp.mean(pre_norm, axis=0, keepdims=True)
    inv_std = lax.rsqrt(jnp.mean(centred * centred, axis=0, keepdims=True) + epsilon)
    normed = centred * inv_std
    updated_t = (state_t.astype(F32) + gain * normed).astype(BF16)
    cot = cot_t.astype(F32)
    terms = cot * normed
    q = cot * gain
    mean_q = jnp.mean(q, axis=0, keepdims=True)
    mean_qn = jnp.mean(q * normed, axis=0, keepdims=True)
    d_norm_t = (inv_std * (q - mean_q - normed * mean_qn)).astype(BF16)
    d_hidden_t = (dot(w_second, d_norm_t) * slope).astype(BF16)
    return updated_t, terms, active_t, d_norm_t, d_hidden_t


def d_aggregate_of(w_first, d_hidden_t):
    return dot(w_first[w_first.shape[1] :], d_hidden_t).astype(BF16)


def first_products(d_hidden_t, state, aggregate):
    ones = jnp.ones((state.shape[0], ONES), BF16)
    return dot(d_hidden_t, joined_lanes([state, aggregate, ones]))


def second_products(active_t, d_norm_t):
    ones = jnp.ones((16, active_t.shape[1]), BF16)
    return dot_nt(jnp.concatenate([active_t, ones], axis=0), d_norm_t)


def fetch_kernel(*refs):
    count = (len(refs) - 3) // 2
    sources, targets = refs[:count], refs[count : 2 * count]
    even_side_ref, odd_side_ref, arrived = refs[2 * count :]
    copies = [
        pltpu.make_async_copy(source, target, arrived.at[k])
        for k, (source, target) in enumerate(zip(sources, targets))
    ]
    for copy in copies:
        copy.start()
    copies[0].wait()
    state, edge = targets[0], even_side_ref.shape[0]
    odd = device_is_odd()
    head, tail = state[pl.ds(0, edge), :], state[pl.ds(state.shape[0] - edge, edge), :]
    even_side_ref[...] = jnp.where(odd, head, tail)
    odd_side_ref[...] = jnp.where(odd, tail, head)
    for copy in copies[1:]:
        copy.wait()


def inner_kernel(
    col_hbm,
    counts_ref,
    cot_ref,
    state_ref,
    w_msg_ref,
    w_first_ref,
    w_second_ref,
    b_first_ref,
    b_second_ref,
    gain_ref,
    first_t_ref,
    second_t_ref,
    columns_ref,
    edge_state_ref,
    edge_cot_ref,
    edge_sum_ref,
    band_ref,
    updated_hbm,
    d_hidden_ref,
    first_sums_ref,
    second_sums_ref,
    msg_sums_ref,
    gain_sums_ref,
    col_ref,
    updated_ref,
    arrived,
    left,
):
    blocks, tiles, size, _ = counts_ref.shape
    features = state_ref.shape[1]
    edge_rows = [*range(WIN), *range(blocks - WIN, blocks)]
    inner_rows = range(WIN, blocks - WIN)
    col_copy = pltpu.make_async_copy(col_hbm, col_ref, arrived)
    col_copy.start()

    def rows(block, count=1):
        return pl.ds(block * size, count * size)

    w_msg, w_first, w_second = w_msg_ref[...], w_first_ref[...], w_second_ref[...]
    first_t = joined_lanes([w_first[:features].T, w_first[features:].T])
    second_t = w_second.T
    columns = [column(ref, size) for ref in (b_first_ref, b_second_ref, gain_ref)]
    first_t_ref[...] = first_t
    second_t_ref[...] = second_t
    for k in range(3):
        columns_ref[k] = columns[k]
    state_t = [state_ref[rows(b), :].T for b in range(blocks)]
    for k, b in enumerate(edge_rows):
        edge_state_ref[:, rows(k)] = state_t[b]

    nothing = jnp.zeros((size, size), BF16)
    col_copy.wait()
    for b in range(blocks):
        for place in range(BAND):
            if place != WIN:
                band_ref[b, place] = nothing
        band_ref[b, WIN] = counts_ref[b, 0].astype(F32).astype(BF16)
        own = col_ref[0, b]
        for t in range(1, tiles):
            band_ref[b, col_ref[t, b] - own + WIN] += counts_ref[b, t].astype(F32).astype(BF16)
    for k, b in enumerate(edge_rows):
        edge_cot_ref[:, rows(k)] = cot_ref[rows(b), :].T

    state = state_ref[...]
    wide = joined_lanes([dot(state, w_msg).astype(BF16), state])

    def neighbour_sum(b):
        first, last = max(b - WIN, 0), min(b + WIN, blocks - 1)
        tiles_of = [band_ref[b, block - b + WIN] for block in range(first, last + 1)]
        return dot(joined_lanes(tiles_of), wide[first * size : (last + 1) * size])

    for k, b in enumerate(edge_rows):
        edge_sum_ref[k] = neighbour_sum(b)
    summed = jnp.concatenate([neighbour_sum(b).astype(BF16) for b in inner_rows], axis=0)
    aggregate, summed = summed[:, :features], summed[:, features:]
    inner_state_t = joined_lanes([state_t[b] for b in inner_rows])
    aggregate_t = joined_lanes(blocks_turned(aggregate))
    updated_t, terms, active_t, d_norm_t, d_hidden_t = node_layer(
        inner_state_t,
        aggregate_t,
        joined_lanes([cot_ref[rows(b), :].T for b in inner_rows]),
        first_t,
        second_t,
        w_second,
        columns,
    )
    updated_ref[...] = updated_t
    updated_copy = pltpu.make_async_copy(updated_ref, updated_hbm, left)
    updated_copy.start()
    d_hidden_ref[...] = d_hidden_t
    d_aggregate_t = d_aggregate_of(w_first, d_hidden_t)
    first_sums_ref[...] = first_products(
        d_hidden_t, state[WIN * size : (blocks - WIN) * size], aggregate
    )
    second_sums_ref[...] = second_products(active_t, d_norm_t)
    msg_sums_ref[...] = dot(d_aggregate_t, summed)
    gain_sums_ref[...] = sum(
        terms[:, k * size : (k + 1) * size] for k in range(len(inner_rows))
    )
    updated_copy.wait()


def outer_kernel(
    grad_scale,
    got_even_ref,
    got_odd_ref,
    state_ref,
    w_msg_ref,
    w_first_ref,
    w_second_ref,
    first_t_ref,
    second_t_ref,
    columns_ref,
    edge_state_ref,
    edge_cot_ref,
    edge_sum_ref,
    band_ref,
    first_sums_ref,
    second_sums_ref,
    msg_sums_ref,
    gain_sums_ref,
    grads_ref,
    updated_hbm,
    d_hidden_ref,
    updated_ref,
    left,
):
    blocks, _, size, _ = band_ref.shape
    features = w_msg_ref.shape[0]
    odd = device_is_odd()
    got_even, got_odd = got_even_ref[...], got_odd_ref[...]
    below, above = jnp.where(odd, got_even, got_odd), jnp.where(odd, got_odd, got_even)

    w_msg = w_msg_ref[...]
    below, above = (
        joined_lanes([dot(halo, w_msg).astype(BF16), halo]) for halo in (below, above)
    )
    summed = []
    for k in range(WIN):
        far = joined_lanes([band_ref[k, place] for place in range(WIN - k)])
        summed.append(edge_sum_ref[k] + dot(far, below[k * size :]))
    for k in range(WIN):
        far = [band_ref[blocks - WIN + k, place] for place in range(2 * WIN - k, BAND)]
        summed.append(edge_sum_ref[WIN + k] + dot(joined_lanes(far), above[: (k + 1) * size]))
    summed = jnp.concatenate(summed, axis=0).astype(BF16)
    aggregate, summed = summed[:, :features], summed[:, features:]
    aggregate_t = joined_lanes(blocks_turned(aggregate))
    updated_t, terms, active_t, d_norm_t, d_hidden_t = node_layer(
        edge_state_ref[...],
        aggregate_t,
        edge_cot_ref[...],
        first_t_ref[...],
        second_t_ref[...],
        w_second_ref[...],
        [columns_ref[k] for k in range(3)],
    )
    updated_ref[...] = updated_t
    updated_copy = pltpu.make_async_copy(updated_ref, updated_hbm, left)
    updated_copy.start()
    d_hidden_ref[...] = d_hidden_t
    d_aggregate_t = d_aggregate_of(w_first_ref[...], d_hidden_t)

    width = WIN * size
    ends = [state_ref[pl.ds(0, width), :], state_ref[pl.ds((blocks - WIN) * size, width), :]]
    first_sums = first_sums_ref[...] + first_products(
        d_hidden_t, jnp.concatenate(ends, axis=0), aggregate
    )
    second_sums = second_sums_ref[...] + second_products(active_t, d_norm_t)
    msg_sums = msg_sums_ref[...] + dot(d_aggregate_t, summed)
    gain_sums = gain_sums_ref[...]
    for k in range(2 * WIN):
        gain_sums = gain_sums + terms[:, k * size : (k + 1) * size]

    chunk = grads_ref.shape[1] - BIAS_ROWS
    turned = [first_sums[:, k * size : (k + 1) * size].T for k in range(3)]
    sums = (
        jnp.concatenate([turned[0], turned[1], second_sums[:features], msg_sums.T], axis=0)
        * grad_scale
    ).astype(SENT)
    bias = (
        jnp.concatenate(
            [
                turned[2][:1],
                second_sums[features : features + 1],
                jnp.sum(gain_sums.T, axis=0, keepdims=True),
            ],
            axis=0,
        )
        * grad_scale
    )
    bias_high = bias.astype(SENT)
    bias_low = (bias - bias_high.astype(F32)).astype(SENT)
    bias = jnp.concatenate(
        [bias_high, bias_low, jnp.zeros((BIAS_ROWS - 6, features), SENT)], axis=0
    )
    nothing = jnp.zeros((chunk, features), SENT)
    for k in range(grads_ref.shape[0]):
        block = sums[k * chunk : (k + 1) * chunk] if k * chunk < sums.shape[0] else nothing
        grads_ref[k] = jnp.concatenate([block, bias], axis=0)
    updated_copy.wait()


def owed_kernel(
    band_ref, w_first_ref, inner_ref, outer_ref, owed_ref, send_even_ref, send_odd_ref
):
    blocks, _, size, _ = band_ref.shape
    odd = device_is_odd()
    w_first = w_first_ref[...]
    inner = d_aggregate_of(w_first, inner_ref[...])
    outer = d_aggregate_of(w_first, outer_ref[...])

    def d_aggregate(b):
        if WIN <= b < blocks - WIN:
            return inner[:, (b - WIN) * size : (b - WIN + 1) * size]
        k = b if b < WIN else b - blocks + 2 * WIN
        return outer[:, k * size : (k + 1) * size]

    def owed(block):
        near = range(max(block - WIN, 0), min(block + WIN, blocks - 1) + 1)
        tiles_of = [band_ref[b, block - b + WIN] for b in near]
        return dot(
            joined_lanes([d_aggregate(b) for b in near]), jnp.concatenate(tiles_of, axis=0)
        )

    for k in range(WIN):
        to_below = owed(k - WIN).astype(BF16)
        to_above = owed(blocks + k).astype(BF16)
        send_even_ref[k] = jnp.where(odd, to_below, to_above)
        send_odd_ref[k] = jnp.where(odd, to_above, to_below)
    for b in range(blocks):
        owed_ref[b] = owed(b)


def sum_kernel(parts_ref, spread_ref, bias_ref):
    total = parts_ref[0].astype(F32)
    for k in range(1, parts_ref.shape[0]):
        total = total + parts_ref[k].astype(F32)
    chunk = spread_ref.shape[1]
    weights = total[:chunk].astype(spread_ref.dtype)
    for k in range(spread_ref.shape[0]):
        spread_ref[k] = weights
    bias_ref[...] = total[chunk:]


def result_kernel(
    even_ref,
    odd_ref,
    cot_hbm,
    w_msg_ref,
    w_first_ref,
    inner_updated_hbm,
    outer_updated_hbm,
    inner_d_hidden_ref,
    outer_d_hidden_ref,
    owed_ref,
    bias_ref,
    updated_ref,
    grad_state_ref,
    b_first_ref,
    b_second_ref,
    gain_ref,
    cot_ref,
    inner_updated_ref,
    outer_updated_ref,
    arrived,
):
    blocks, features, size = owed_ref.shape
    copies = [
        pltpu.make_async_copy(source, target, arrived.at[k])
        for k, (source, target) in enumerate(
            (
                (cot_hbm, cot_ref),
                (inner_updated_hbm, inner_updated_ref),
                (outer_updated_hbm, outer_updated_ref),
            )
        )
    ]
    for copy in copies:
        copy.start()
    odd = device_is_odd()
    even_part, odd_part = even_ref[...].astype(F32), odd_ref[...].astype(F32)
    from_below = jnp.where(odd, even_part, odd_part)
    from_above = jnp.where(odd, odd_part, even_part)
    weights = joined_lanes([w_first_ref[pl.ds(0, features), :], w_msg_ref[...]])
    for copy in copies:
        copy.wait()
    for b in range(blocks):
        owed = owed_ref[b]
        if b < WIN:
            owed = owed + from_below[b]
        elif b >= blocks - WIN:
            owed = owed + from_above[b - blocks + WIN]
        if WIN <= b < blocks - WIN:
            k, updated, d_hidden = b - WIN, inner_updated_ref, inner_d_hidden_ref
        else:
            k = b if b < WIN else b - blocks + 2 * WIN
            updated, d_hidden = outer_updated_ref, outer_d_hidden_ref
        lanes, rows = pl.ds(k * size, size), pl.ds(b * size, size)
        change = dot(weights, jnp.concatenate([d_hidden[:, lanes], owed.astype(BF16)], axis=0))
        grad_state_ref[rows, :] = (cot_ref[rows, :].astype(F32) + change.T).astype(BF16)
        updated_ref[rows, :] = updated[:, lanes].T
    for k, ref in enumerate((b_first_ref, b_second_ref, gain_ref)):
        ref[...] = bias_ref[pl.ds(k, 1), :] + bias_ref[pl.ds(k + 3, 1), :]


def unpack_kernel(rows_ref, msg_ref, first_ref, second_ref):
    place = 0
    for ref in (first_ref, second_ref, msg_ref):
        count = ref.shape[0]
        ref[...] = rows_ref[pl.ds(place, count), :].astype(F32)
        place += count


def swapped(block, parity):
    last = lax.axis_size(AXES) - 1
    lower = range(parity, last, 2)
    return lax.ppermute(block, AXES, [(i, i + 1) for i in lower] + [(i + 1, i) for i in lower])


def call(kernel, name, outs, operands, scratch=(), limit=16, flops=0):
    specs = [pl.BlockSpec(memory_space=space) for _, space in operands]
    arrays = [kept(array, space) for array, space in operands]
    return pl.pallas_call(
        kernel,
        out_shape=tuple(outs),
        in_specs=specs,
        out_specs=tuple(
            pl.BlockSpec(memory_space=getattr(out, "memory_space", pltpu.VMEM)) for out in outs
        ),
        scratch_shapes=list(scratch),
        compiler_params=pltpu.CompilerParams(vmem_limit_bytes=limit * 1024 * 1024),
        cost_estimate=pl.CostEstimate(
            flops=flops, bytes_accessed=1_000_000, transcendentals=0
        ),
        name=name,
    )(*arrays)


def shards(
    node_state,
    w_msg,
    w_first,
    b_first,
    w_second,
    b_second,
    ln_gain,
    col_index,
    edge_counts,
    cotangent,
):
    nodes, features = node_state.shape
    blocks, tiles, size, _ = edge_counts.shape
    devices = lax.axis_size(AXES)
    grad_scale = 1.0 / math.sqrt(nodes * devices)
    chunk = -(-4 * features // (devices * 8)) * 8
    inner = blocks - 2 * WIN
    edge = 2 * WIN
    vmem, hbm = pltpu.VMEM, pltpu.HBM
    result = jax.ShapeDtypeStruct

    row = lambda vector: vector.reshape(1, features)
    sources = (
        node_state,
        w_msg,
        w_first,
        w_second,
        row(b_first),
        row(b_second),
        row(ln_gain),
    )
    *fetched, even_side, odd_side = call(
        fetch_kernel,
        "fetch",
        [vmem(array.shape, array.dtype) for array in sources]
        + [vmem((WIN * size, features), BF16)] * 2,
        [(array, hbm) for array in sources],
        scratch=(pltpu.SemaphoreType.DMA((len(sources),)),),
        flops=50_000_000_000,
    )
    state, w_msg_here, w_first_here, w_second_here, *vectors = fetched
    got_even = swapped(even_side, 0)
    got_odd = swapped(odd_side, 1)

    (
        first_t,
        second_t,
        columns,
        edge_state,
        edge_cot,
        edge_sum,
        band,
        inner_updated,
        inner_d_hidden,
        first_sums,
        second_sums,
        msg_sums,
        gain_sums,
    ) = call(
        inner_kernel,
        "inner_rows",
        (
            vmem((features, 2 * features), BF16),
            vmem((features, features), BF16),
            vmem((3, features, size), F32),
            vmem((features, edge * size), BF16),
            vmem((features, edge * size), BF16),
            vmem((edge, size, 2 * features), F32),
            vmem((blocks, BAND, size, size), BF16),
            hbm((features, inner * size), BF16),
            vmem((features, inner * size), BF16),
            vmem((features, 2 * features + ONES), F32),
            vmem((features + 16, features), F32),
            vmem((features, features), F32),
            vmem((features, size), F32),
        ),
        [(col_index.T, hbm), (edge_counts, vmem), (cotangent, vmem)]
        + [
            (array, vmem)
            for array in (state, w_msg_here, w_first_here, w_second_here, *vectors)
        ],
        scratch=(
            pltpu.SMEM((tiles, blocks), jnp.int32),
            vmem((features, inner * size), BF16),
            pltpu.SemaphoreType.DMA,
            pltpu.SemaphoreType.DMA,
        ),
        limit=32,
        flops=700_000_000,
    )

    grads, outer_updated, outer_d_hidden = call(
        functools.partial(outer_kernel, grad_scale),
        "outer_rows",
        (
            vmem((devices, chunk + BIAS_ROWS, features), SENT),
            hbm((features, edge * size), BF16),
            vmem((features, edge * size), BF16),
        ),
        [
            (array, vmem)
            for array in (
                got_even,
                got_odd,
                state,
                w_msg_here,
                w_first_here,
                w_second_here,
                first_t,
                second_t,
                columns,
                edge_state,
                edge_cot,
                edge_sum,
                band,
                first_sums,
                second_sums,
                msg_sums,
                gain_sums,
            )
        ],
        scratch=(vmem((features, edge * size), BF16), pltpu.SemaphoreType.DMA),
        flops=300_000_000,
    )

    parts = lax.all_to_all(grads, AXES, 0, 0, tiled=True)
    owed, send_even, send_odd = call(
        owed_kernel,
        "owed",
        (
            vmem((blocks, features, size), F32),
            vmem((WIN, features, size), BF16),
            vmem((WIN, features, size), BF16),
        ),
        [(array, vmem) for array in (band, w_first_here, inner_d_hidden, outer_d_hidden)],
        flops=200_000_000,
    )
    owed_even = swapped(send_even, 0)
    owed_odd = swapped(send_odd, 1)
    spread, bias = call(
        sum_kernel,
        "sum",
        (vmem((devices, chunk, features), SENT), vmem((BIAS_ROWS, features), F32)),
        [(parts, vmem)],
        flops=10_000_000_000,
    )
    updated, grad_state, g_b_first, g_b_second, g_gain = call(
        result_kernel,
        "results",
        (
            result((nodes, features), BF16),
            result((nodes, features), BF16),
            result((1, features), F32),
            result((1, features), F32),
            result((1, features), F32),
        ),
        [(owed_even, vmem), (owed_odd, vmem), (cotangent, hbm)]
        + [(w_msg_here, vmem), (w_first_here, vmem), (inner_updated, hbm), (outer_updated, hbm)]
        + [(array, vmem) for array in (inner_d_hidden, outer_d_hidden, owed, bias)],
        scratch=(
            vmem((nodes, features), BF16),
            vmem((features, inner * size), BF16),
            vmem((features, edge * size), BF16),
            pltpu.SemaphoreType.DMA((3,)),
        ),
        flops=50_000_000_000,
    )

    whole = lax.all_to_all(spread, AXES, 0, 0, tiled=True)
    g_msg, g_first, g_second = call(
        unpack_kernel,
        "unpack",
        (
            result((features, features), F32),
            result((2 * features, features), F32),
            result((features, features), F32),
        ),
        [(whole.reshape(devices * chunk, features), vmem)],
    )
    flat = lambda vector: vector.reshape(features)
    return (
        updated,
        grad_state,
        g_msg,
        g_first,
        flat(g_b_first),
        g_second,
        flat(g_b_second),
        flat(g_gain),
    )


def solution(mesh):
    split = P(AXES, None)
    return jax.shard_map(
        shards,
        mesh=mesh,
        in_specs=(split, P(), P(), P(), P(), P(), P(), split, P(AXES, None, None, None), split),
        out_specs=(split, split, P(), P(), P(), P(), P(), P()),
        check_vma=False,
    )
```

```python
import functools
import math

import jax
import jax.numpy as jnp
from jax import lax
from jax.experimental import pallas as pl
from jax.experimental.pallas import tpu as pltpu
from jax.sharding import PartitionSpec as P

WIN = 2
BAND = 2 * WIN + 1
epsilon = 1e-05
AXES = ("dom", "feat")
BF16, F32 = jnp.bfloat16, jnp.float32
SENT = BF16
ONES = 128
BIAS_ROWS = 8

kept = pltpu.with_memory_space_constraint


def dot(left, right):
    return jnp.dot(left, right, preferred_element_type=F32)


def dot_nt(left, right):
    return lax.dot_general(left, right, (((1,), (1,)), ((), ())), preferred_element_type=F32)


def joined_lanes(parts):
    return jnp.concatenate(parts, axis=1)


def device_is_odd():
    index = lax.axis_index("dom") * lax.axis_size("feat") + lax.axis_index("feat")
    return index % 2 == 1


def column(row_ref, width):
    return jnp.broadcast_to(row_ref[...], (width, row_ref.shape[1])).T


def blocks_turned(array):
    size = array.shape[1]
    return [array[k : k + size].T for k in range(0, array.shape[0], size)]


def node_layer(state_t, aggregate_t, cot_t, first_t, second_t, w_second, columns):
    features, width = state_t.shape
    b_first, b_second, gain = (
        joined_lanes([c] * (width // c.shape[1])) for c in columns
    )
    pre_hidden = dot(first_t, jnp.concatenate([state_t, aggregate_t], axis=0)) + b_first
    sigmoid = 0.5 * jnp.tanh(0.5 * pre_hidden) + 0.5
    silu = pre_hidden * sigmoid
    active_t = silu.astype(BF16)
    slope = sigmoid + silu * (1.0 - sigmoid)
    pre_norm = dot(second_t, active_t) + b_second
    centred = pre_norm - jnp.mean(pre_norm, axis=0, keepdims=True)
    inv_std = lax.rsqrt(jnp.mean(centred * centred, axis=0, keepdims=True) + epsilon)
    normed = centred * inv_std
    updated_t = (state_t.astype(F32) + gain * normed).astype(BF16)
    cot = cot_t.astype(F32)
    terms = cot * normed
    q = cot * gain
    mean_q = jnp.mean(q, axis=0, keepdims=True)
    mean_qn = jnp.mean(q * normed, axis=0, keepdims=True)
    d_norm_t = (inv_std * (q - mean_q - normed * mean_qn)).astype(BF16)
    d_hidden_t = (dot(w_second, d_norm_t) * slope).astype(BF16)
    return updated_t, terms, active_t, d_norm_t, d_hidden_t


def d_aggregate_of(w_first, d_hidden_t):
    return dot(w_first[w_first.shape[1] :], d_hidden_t).astype(BF16)


def first_products(d_hidden_t, state, aggregate):
    ones = jnp.ones((state.shape[0], ONES), BF16)
    return dot(d_hidden_t, joined_lanes([state, aggregate, ones]))


def second_products(active_t, d_norm_t):
    ones = jnp.ones((16, active_t.shape[1]), BF16)
    return dot_nt(jnp.concatenate([active_t, ones], axis=0), d_norm_t)


def fetch_kernel(state_hbm, *refs):
    count = (len(refs) - 3) // 2
    sources, targets = refs[:count], refs[count : 2 * count]
    even_side_ref, odd_side_ref, arrived = refs[2 * count :]
    edge = even_side_ref.shape[0]
    odd = device_is_odd()
    last = state_hbm.shape[0] - edge
    even_start = pl.multiple_of(jnp.where(odd, 0, last), edge)
    odd_start = pl.multiple_of(jnp.where(odd, last, 0), edge)
    pairs = [
        (state_hbm.at[pl.ds(even_start, edge)], even_side_ref),
        (state_hbm.at[pl.ds(odd_start, edge)], odd_side_ref),
        *zip(sources, targets),
    ]
    copies = [
        pltpu.make_async_copy(source, target, arrived.at[k])
        for k, (source, target) in enumerate(pairs)
    ]
    for copy in copies:
        copy.start()
    for copy in copies:
        copy.wait()


def inner_kernel(
    col_hbm,
    counts_ref,
    cot_ref,
    state_ref,
    got_even_ref,
    w_msg_ref,
    w_first_ref,
    w_second_ref,
    b_first_ref,
    b_second_ref,
    gain_ref,
    first_t_ref,
    second_t_ref,
    columns_ref,
    side_state_ref,
    side_state_t_ref,
    side_cot_ref,
    side_sum_ref,
    side_far_ref,
    band_ref,
    updated_hbm,
    d_hidden_ref,
    first_sums_ref,
    second_sums_ref,
    msg_sums_ref,
    gain_sums_ref,
    col_ref,
    updated_ref,
    arrived,
    left,
):
    blocks, tiles, size, _ = counts_ref.shape
    features = state_ref.shape[1]
    inner_rows = range(WIN, blocks - WIN)
    low_rows, high_rows = range(WIN), range(blocks - WIN, blocks)
    odd = device_is_odd()

    def even_side(low, high):
        return jnp.where(odd, low, high)

    def odd_side(low, high):
        return jnp.where(odd, high, low)

    col_copy = pltpu.make_async_copy(col_hbm, col_ref, arrived)
    col_copy.start()

    def rows(block, count=1):
        return pl.ds(block * size, count * size)

    w_msg, w_first, w_second = w_msg_ref[...], w_first_ref[...], w_second_ref[...]
    first_t = joined_lanes([w_first[:features].T, w_first[features:].T])
    second_t = w_second.T
    columns = [column(ref, size) for ref in (b_first_ref, b_second_ref, gain_ref)]
    first_t_ref[...] = first_t
    second_t_ref[...] = second_t
    for k in range(3):
        columns_ref[k] = columns[k]
    state = state_ref[...]
    state_t = [state[b * size : (b + 1) * size].T for b in range(blocks)]
    cot_t = [cot_ref[rows(b), :].T for b in range(blocks)]

    nothing = jnp.zeros((size, size), BF16)
    col_copy.wait()
    for b in range(blocks):
        for place in range(BAND):
            if place != WIN:
                band_ref[b, place] = nothing
        band_ref[b, WIN] = counts_ref[b, 0].astype(F32).astype(BF16)
        own = col_ref[0, b]
        for t in range(1, tiles):
            band_ref[b, col_ref[t, b] - own + WIN] += counts_ref[b, t].astype(F32).astype(BF16)

    wide = joined_lanes([dot(state, w_msg).astype(BF16), state])

    def neighbour_sum(b):
        first, last = max(b - WIN, 0), min(b + WIN, blocks - 1)
        tiles_of = [band_ref[b, block - b + WIN] for block in range(first, last + 1)]
        return dot(joined_lanes(tiles_of), wide[first * size : (last + 1) * size])

    def far(b, first):
        places = [block - b + WIN for block in range(first, first + WIN)]
        return joined_lanes([band_ref[b, p] if 0 <= p < BAND else nothing for p in places])

    def stacked(parts):
        return jnp.concatenate(list(parts), axis=0)

    ends = (stacked(map(neighbour_sum, low_rows)), stacked(map(neighbour_sum, high_rows)))
    fars = (stacked(far(b, -WIN) for b in low_rows), stacked(far(b, blocks) for b in high_rows))
    end_states = (state[: WIN * size], state[(blocks - WIN) * size :])
    end_states_t = (joined_lanes(state_t[:WIN]), joined_lanes(state_t[blocks - WIN :]))
    end_cots_t = (joined_lanes(cot_t[:WIN]), joined_lanes(cot_t[blocks - WIN :]))
    side_sum_ref[...] = odd_side(*ends)
    side_far_ref[...] = odd_side(*fars)
    side_state_ref[...] = odd_side(*end_states)
    side_state_t_ref[...] = odd_side(*end_states_t)
    side_cot_ref[...] = odd_side(*end_cots_t)

    halo = got_even_ref[...]
    wide_halo = joined_lanes([dot(halo, w_msg).astype(BF16), halo])
    end_sum = even_side(*ends) + dot(even_side(*fars), wide_halo)
    summed = stacked([*map(neighbour_sum, inner_rows), end_sum]).astype(BF16)
    aggregate, summed = summed[:, :features], summed[:, features:]
    updated_t, terms, active_t, d_norm_t, d_hidden_t = node_layer(
        joined_lanes([*state_t[WIN : blocks - WIN], even_side(*end_states_t)]),
        joined_lanes(blocks_turned(aggregate)),
        joined_lanes([*cot_t[WIN : blocks - WIN], even_side(*end_cots_t)]),
        first_t,
        second_t,
        w_second,
        columns,
    )
    updated_ref[...] = updated_t
    updated_copy = pltpu.make_async_copy(updated_ref, updated_hbm, left)
    updated_copy.start()
    d_hidden_ref[...] = d_hidden_t
    d_aggregate_t = d_aggregate_of(w_first, d_hidden_t)
    first_sums_ref[...] = first_products(
        d_hidden_t,
        stacked([state[WIN * size : (blocks - WIN) * size], even_side(*end_states)]),
        aggregate,
    )
    second_sums_ref[...] = second_products(active_t, d_norm_t)
    msg_sums_ref[...] = dot(d_aggregate_t, summed)
    gain_sums_ref[...] = sum(
        terms[:, k * size : (k + 1) * size] for k in range(blocks - WIN)
    )
    updated_copy.wait()


def outer_kernel(
    grad_scale,
    got_odd_ref,
    w_msg_ref,
    w_first_ref,
    w_second_ref,
    first_t_ref,
    second_t_ref,
    columns_ref,
    side_state_ref,
    side_state_t_ref,
    side_cot_ref,
    side_sum_ref,
    side_far_ref,
    first_sums_ref,
    second_sums_ref,
    msg_sums_ref,
    gain_sums_ref,
    grads_ref,
    updated_hbm,
    d_hidden_ref,
    updated_ref,
    left,
):
    features, size = w_msg_ref.shape[0], columns_ref.shape[2]
    halo = got_odd_ref[...]
    wide_halo = joined_lanes([dot(halo, w_msg_ref[...]).astype(BF16), halo])
    summed = (side_sum_ref[...] + dot(side_far_ref[...], wide_halo)).astype(BF16)
    aggregate, summed = summed[:, :features], summed[:, features:]
    updated_t, terms, active_t, d_norm_t, d_hidden_t = node_layer(
        side_state_t_ref[...],
        joined_lanes(blocks_turned(aggregate)),
        side_cot_ref[...],
        first_t_ref[...],
        second_t_ref[...],
        w_second_ref[...],
        [columns_ref[k] for k in range(3)],
    )
    updated_ref[...] = updated_t
    updated_copy = pltpu.make_async_copy(updated_ref, updated_hbm, left)
    updated_copy.start()
    d_hidden_ref[...] = d_hidden_t
    d_aggregate_t = d_aggregate_of(w_first_ref[...], d_hidden_t)

    first_sums = first_sums_ref[...] + first_products(d_hidden_t, side_state_ref[...], aggregate)
    second_sums = second_sums_ref[...] + second_products(active_t, d_norm_t)
    msg_sums = msg_sums_ref[...] + dot(d_aggregate_t, summed)
    gain_sums = gain_sums_ref[...]
    for k in range(WIN):
        gain_sums = gain_sums + terms[:, k * size : (k + 1) * size]

    chunk = grads_ref.shape[1] - BIAS_ROWS
    turned = [first_sums[:, k * size : (k + 1) * size].T for k in range(3)]
    sums = (
        jnp.concatenate([turned[0], turned[1], second_sums[:features], msg_sums.T], axis=0)
        * grad_scale
    ).astype(SENT)
    bias = (
        jnp.concatenate(
            [
                turned[2][:1],
                second_sums[features : features + 1],
                jnp.sum(gain_sums.T, axis=0, keepdims=True),
            ],
            axis=0,
        )
        * grad_scale
    )
    bias_high = bias.astype(SENT)
    bias_low = (bias - bias_high.astype(F32)).astype(SENT)
    bias = jnp.concatenate(
        [bias_high, bias_low, jnp.zeros((BIAS_ROWS - 6, features), SENT)], axis=0
    )
    nothing = jnp.zeros((chunk, features), SENT)
    for k in range(grads_ref.shape[0]):
        block = sums[k * chunk : (k + 1) * chunk] if k * chunk < sums.shape[0] else nothing
        grads_ref[k] = jnp.concatenate([block, bias], axis=0)
    updated_copy.wait()


def owed_kernel(
    band_ref, w_first_ref, inner_ref, outer_ref, owed_ref, send_even_ref, send_odd_ref
):
    blocks, _, size, _ = band_ref.shape
    odd = device_is_odd()
    w_first = w_first_ref[...]
    inner = d_aggregate_of(w_first, inner_ref[...])
    outer = d_aggregate_of(w_first, outer_ref[...])

    def d_aggregate(b):
        if WIN <= b < blocks - WIN:
            return inner[:, (b - WIN) * size : (b - WIN + 1) * size]
        k = b if b < WIN else b - blocks + WIN
        even_end = inner[:, (blocks - 2 * WIN + k) * size : (blocks - 2 * WIN + k + 1) * size]
        odd_end = outer[:, k * size : (k + 1) * size]
        return jnp.where(odd == (b < WIN), even_end, odd_end)

    def owed(block):
        near = range(max(block - WIN, 0), min(block + WIN, blocks - 1) + 1)
        tiles_of = [band_ref[b, block - b + WIN] for b in near]
        return dot(
            joined_lanes([d_aggregate(b) for b in near]), jnp.concatenate(tiles_of, axis=0)
        )

    for k in range(WIN):
        to_below = owed(k - WIN).astype(BF16)
        to_above = owed(blocks + k).astype(BF16)
        send_even_ref[k] = jnp.where(odd, to_below, to_above)
        send_odd_ref[k] = jnp.where(odd, to_above, to_below)
    for b in range(blocks):
        owed_ref[b] = owed(b)


def sum_kernel(parts_ref, spread_ref, bias_ref):
    total = parts_ref[0].astype(F32)
    for k in range(1, parts_ref.shape[0]):
        total = total + parts_ref[k].astype(F32)
    chunk = spread_ref.shape[1]
    weights = total[:chunk].astype(spread_ref.dtype)
    for k in range(spread_ref.shape[0]):
        spread_ref[k] = weights
    bias_ref[...] = total[chunk:]


def result_kernel(
    even_ref,
    odd_ref,
    cot_hbm,
    w_msg_ref,
    w_first_ref,
    inner_updated_hbm,
    outer_updated_hbm,
    inner_d_hidden_ref,
    outer_d_hidden_ref,
    owed_ref,
    bias_ref,
    updated_ref,
    grad_state_ref,
    b_first_ref,
    b_second_ref,
    gain_ref,
    cot_ref,
    inner_updated_ref,
    outer_updated_ref,
    arrived,
):
    blocks, features, size = owed_ref.shape
    copies = [
        pltpu.make_async_copy(source, target, arrived.at[k])
        for k, (source, target) in enumerate(
            (
                (cot_hbm, cot_ref),
                (inner_updated_hbm, inner_updated_ref),
                (outer_updated_hbm, outer_updated_ref),
            )
        )
    ]
    for copy in copies:
        copy.start()
    odd = device_is_odd()
    even_part, odd_part = even_ref[...].astype(F32), odd_ref[...].astype(F32)
    from_below = jnp.where(odd, even_part, odd_part)
    from_above = jnp.where(odd, odd_part, even_part)
    weights = joined_lanes([w_first_ref[pl.ds(0, features), :], w_msg_ref[...]])
    for copy in copies:
        copy.wait()
    for b in range(blocks):
        owed = owed_ref[b]
        if b < WIN:
            owed = owed + from_below[b]
        elif b >= blocks - WIN:
            owed = owed + from_above[b - blocks + WIN]
        if WIN <= b < blocks - WIN:
            lanes = pl.ds((b - WIN) * size, size)
            updated, d_hidden = inner_updated_ref[:, lanes], inner_d_hidden_ref[:, lanes]
        else:
            k = b if b < WIN else b - blocks + WIN
            even_end = odd == (b < WIN)
            lanes, outer_lanes = pl.ds((blocks - 2 * WIN + k) * size, size), pl.ds(k * size, size)
            updated = jnp.where(
                even_end, inner_updated_ref[:, lanes], outer_updated_ref[:, outer_lanes]
            )
            d_hidden = jnp.where(
                even_end, inner_d_hidden_ref[:, lanes], outer_d_hidden_ref[:, outer_lanes]
            )
        rows = pl.ds(b * size, size)
        change = dot(weights, jnp.concatenate([d_hidden, owed.astype(BF16)], axis=0))
        grad_state_ref[rows, :] = (cot_ref[rows, :].astype(F32) + change.T).astype(BF16)
        updated_ref[rows, :] = updated.T
    for k, ref in enumerate((b_first_ref, b_second_ref, gain_ref)):
        ref[...] = bias_ref[pl.ds(k, 1), :] + bias_ref[pl.ds(k + 3, 1), :]


def unpack_kernel(rows_ref, msg_ref, first_ref, second_ref):
    place = 0
    for ref in (first_ref, second_ref, msg_ref):
        count = ref.shape[0]
        ref[...] = rows_ref[pl.ds(place, count), :].astype(F32)
        place += count


def swapped(block, parity):
    last = lax.axis_size(AXES) - 1
    lower = range(parity, last, 2)
    return lax.ppermute(block, AXES, [(i, i + 1) for i in lower] + [(i + 1, i) for i in lower])


def call(kernel, name, outs, operands, scratch=(), limit=16, flops=0):
    specs = [pl.BlockSpec(memory_space=space) for _, space in operands]
    arrays = [kept(array, space) for array, space in operands]
    return pl.pallas_call(
        kernel,
        out_shape=tuple(outs),
        in_specs=specs,
        out_specs=tuple(
            pl.BlockSpec(memory_space=getattr(out, "memory_space", pltpu.VMEM)) for out in outs
        ),
        scratch_shapes=list(scratch),
        compiler_params=pltpu.CompilerParams(vmem_limit_bytes=limit * 1024 * 1024),
        cost_estimate=pl.CostEstimate(
            flops=flops, bytes_accessed=1_000_000, transcendentals=0
        ),
        name=name,
    )(*arrays)


def shards(
    node_state,
    w_msg,
    w_first,
    b_first,
    w_second,
    b_second,
    ln_gain,
    col_index,
    edge_counts,
    cotangent,
):
    nodes, features = node_state.shape
    blocks, tiles, size, _ = edge_counts.shape
    devices = lax.axis_size(AXES)
    grad_scale = 1.0 / math.sqrt(nodes * devices)
    chunk = -(-4 * features // (devices * 8)) * 8
    side = WIN * size
    most = nodes - side
    vmem, hbm = pltpu.VMEM, pltpu.HBM
    result = jax.ShapeDtypeStruct

    row = lambda vector: vector.reshape(1, features)
    sources = (w_msg, w_first, w_second, row(b_first), row(b_second), row(ln_gain))
    *fetched, even_side, odd_side = call(
        fetch_kernel,
        "fetch",
        [vmem(array.shape, array.dtype) for array in sources]
        + [vmem((side, features), BF16)] * 2,
        [(array, hbm) for array in (node_state, *sources)],
        scratch=(pltpu.SemaphoreType.DMA((len(sources) + 2,)),),
        flops=50_000_000_000,
    )
    w_msg_here, w_first_here, w_second_here, *vectors = fetched
    got_even = swapped(even_side, 0)
    got_odd = swapped(odd_side, 1)

    *outer_operands, band, inner_updated, inner_d_hidden = (
        lambda *outs: (*outs[:8], *outs[11:], *outs[8:11])
    )(
        *call(
            inner_kernel,
            "inner_rows",
            (
                vmem((features, 2 * features), BF16),
                vmem((features, features), BF16),
                vmem((3, features, size), F32),
                vmem((side, features), BF16),
                vmem((features, side), BF16),
                vmem((features, side), BF16),
                vmem((side, 2 * features), F32),
                vmem((side, side), BF16),
                vmem((blocks, BAND, size, size), BF16),
                hbm((features, most), BF16),
                vmem((features, most), BF16),
                vmem((features, 2 * features + ONES), F32),
                vmem((features + 16, features), F32),
                vmem((features, features), F32),
                vmem((features, size), F32),
            ),
            [(col_index.T, hbm)]
            + [
                (array, vmem)
                for array in (edge_counts, cotangent, node_state, got_even, *fetched)
            ],
            scratch=(
                pltpu.SMEM((tiles, blocks), jnp.int32),
                vmem((features, most), BF16),
                pltpu.SemaphoreType.DMA,
                pltpu.SemaphoreType.DMA,
            ),
            limit=32,
            flops=700_000_000,
        )
    )

    grads, outer_updated, outer_d_hidden = call(
        functools.partial(outer_kernel, grad_scale),
        "outer_rows",
        (
            vmem((devices, chunk + BIAS_ROWS, features), SENT),
            hbm((features, side), BF16),
            vmem((features, side), BF16),
        ),
        [
            (array, vmem)
            for array in (got_odd, w_msg_here, w_first_here, w_second_here, *outer_operands)
        ],
        scratch=(vmem((features, side), BF16), pltpu.SemaphoreType.DMA),
        flops=300_000_000,
    )

    parts = lax.all_to_all(grads, AXES, 0, 0, tiled=True)
    owed, send_even, send_odd = call(
        owed_kernel,
        "owed",
        (
            vmem((blocks, features, size), F32),
            vmem((WIN, features, size), BF16),
            vmem((WIN, features, size), BF16),
        ),
        [(array, vmem) for array in (band, w_first_here, inner_d_hidden, outer_d_hidden)],
        flops=200_000_000,
    )
    owed_even = swapped(send_even, 0)
    owed_odd = swapped(send_odd, 1)
    spread, bias = call(
        sum_kernel,
        "sum",
        (vmem((devices, chunk, features), SENT), vmem((BIAS_ROWS, features), F32)),
        [(parts, vmem)],
        flops=10_000_000_000,
    )
    updated, grad_state, g_b_first, g_b_second, g_gain = call(
        result_kernel,
        "results",
        (
            result((nodes, features), BF16),
            result((nodes, features), BF16),
            result((1, features), F32),
            result((1, features), F32),
            result((1, features), F32),
        ),
        [(owed_even, vmem), (owed_odd, vmem), (cotangent, hbm)]
        + [(w_msg_here, vmem), (w_first_here, vmem), (inner_updated, hbm), (outer_updated, hbm)]
        + [(array, vmem) for array in (inner_d_hidden, outer_d_hidden, owed, bias)],
        scratch=(
            vmem((nodes, features), BF16),
            vmem((features, most), BF16),
            vmem((features, side), BF16),
            pltpu.SemaphoreType.DMA((3,)),
        ),
        flops=50_000_000_000,
    )

    whole = lax.all_to_all(spread, AXES, 0, 0, tiled=True)
    g_msg, g_first, g_second = call(
        unpack_kernel,
        "unpack",
        (
            result((features, features), F32),
            result((2 * features, features), F32),
            result((features, features), F32),
        ),
        [(whole.reshape(devices * chunk, features), vmem)],
    )
    flat = lambda vector: vector.reshape(features)
    return (
        updated,
        grad_state,
        g_msg,
        g_first,
        flat(g_b_first),
        g_second,
        flat(g_b_second),
        flat(g_gain),
    )


def solution(mesh):
    split = P(AXES, None)
    return jax.shard_map(
        shards,
        mesh=mesh,
        in_specs=(split, P(), P(), P(), P(), P(), P(), split, P(AXES, None, None, None), split),
        out_specs=(split, split, P(), P(), P(), P(), P(), P()),
        check_vma=False,
    )
```

```python
import functools
import math

import jax
import jax.numpy as jnp
from jax import lax
from jax.experimental import pallas as pl
from jax.experimental.pallas import tpu as pltpu
from jax.sharding import PartitionSpec as P

WIN = 2
BAND = 2 * WIN + 1
epsilon = 1e-05
AXES = ("dom", "feat")
BF16, F32 = jnp.bfloat16, jnp.float32
SENT = BF16
ONES = 128
BIAS_ROWS = 8

kept = pltpu.with_memory_space_constraint


def dot(left, right):
    return jnp.dot(left, right, preferred_element_type=F32)


def dot_nt(left, right):
    return lax.dot_general(left, right, (((1,), (1,)), ((), ())), preferred_element_type=F32)


def joined_lanes(parts):
    return jnp.concatenate(parts, axis=1)


def device_is_odd():
    index = lax.axis_index("dom") * lax.axis_size("feat") + lax.axis_index("feat")
    return index % 2 == 1


def column(row_ref, width):
    return jnp.broadcast_to(row_ref[...], (width, row_ref.shape[1])).T


def blocks_turned(array):
    size = array.shape[1]
    return [array[k : k + size].T for k in range(0, array.shape[0], size)]


def node_layer(state_t, aggregate_t, cot_t, first_t, second_t, w_second, columns):
    features, width = state_t.shape
    b_first, b_second, gain = (
        joined_lanes([c] * (width // c.shape[1])) for c in columns
    )
    pre_hidden = dot(first_t, jnp.concatenate([state_t, aggregate_t], axis=0)) + b_first
    sigmoid = 0.5 * jnp.tanh(0.5 * pre_hidden) + 0.5
    silu = pre_hidden * sigmoid
    active_t = silu.astype(BF16)
    slope = sigmoid + silu * (1.0 - sigmoid)
    pre_norm = dot(second_t, active_t) + b_second
    centred = pre_norm - jnp.mean(pre_norm, axis=0, keepdims=True)
    inv_std = lax.rsqrt(jnp.mean(centred * centred, axis=0, keepdims=True) + epsilon)
    normed = centred * inv_std
    updated_t = (state_t.astype(F32) + gain * normed).astype(BF16)
    cot = cot_t.astype(F32)
    terms = cot * normed
    q = cot * gain
    mean_q = jnp.mean(q, axis=0, keepdims=True)
    mean_qn = jnp.mean(q * normed, axis=0, keepdims=True)
    d_norm_t = (inv_std * (q - mean_q - normed * mean_qn)).astype(BF16)
    d_hidden_t = (dot(w_second, d_norm_t) * slope).astype(BF16)
    return updated_t, terms, active_t, d_norm_t, d_hidden_t


def d_aggregate_of(w_first, d_hidden_t):
    return dot(w_first[w_first.shape[1] :], d_hidden_t).astype(BF16)


def first_products(d_hidden_t, state, aggregate):
    ones = jnp.ones((state.shape[0], ONES), BF16)
    return dot(d_hidden_t, joined_lanes([state, aggregate, ones]))


def sums_over_nodes(lefts, right):
    ones = jnp.ones((16, right.shape[1]), BF16)
    return dot_nt(jnp.concatenate([*lefts, ones], axis=0), right)


def cut_kernel(state_hbm, even_side_ref, odd_side_ref, arrived):
    side = even_side_ref.shape[0]
    odd = device_is_odd()
    last = state_hbm.shape[0] - side
    even_start = pl.multiple_of(jnp.where(odd, 0, last), side)
    odd_start = pl.multiple_of(jnp.where(odd, last, 0), side)
    copies = [
        pltpu.make_async_copy(state_hbm.at[pl.ds(start, side)], target, arrived.at[k])
        for k, (start, target) in enumerate(
            ((even_start, even_side_ref), (odd_start, odd_side_ref))
        )
    ]
    for copy in copies:
        copy.start()
    for copy in copies:
        copy.wait()


def inner_kernel(
    col_hbm,
    counts_ref,
    cot_ref,
    state_ref,
    got_even_ref,
    w_msg_ref,
    w_first_ref,
    w_second_ref,
    b_first_ref,
    b_second_ref,
    gain_ref,
    w_msg_here_ref,
    w_first_here_ref,
    w_second_here_ref,
    first_t_ref,
    second_t_ref,
    columns_ref,
    side_state_t_ref,
    side_cot_ref,
    side_sum_ref,
    side_far_ref,
    band_ref,
    updated_hbm,
    d_hidden_ref,
    first_sums_ref,
    second_sums_ref,
    msg_sums_ref,
    gain_sums_ref,
    col_ref,
    updated_ref,
    arrived,
    left,
):
    blocks, tiles, size, _ = counts_ref.shape
    features = state_ref.shape[1]
    inner_rows = range(WIN, blocks - WIN)
    low_rows, high_rows = range(WIN), range(blocks - WIN, blocks)
    odd = device_is_odd()

    def even_side(low, high):
        return jnp.where(odd, low, high)

    def odd_side(low, high):
        return jnp.where(odd, high, low)

    col_copy = pltpu.make_async_copy(col_hbm, col_ref, arrived)
    col_copy.start()

    def rows(block, count=1):
        return pl.ds(block * size, count * size)

    w_msg, w_first, w_second = w_msg_ref[...], w_first_ref[...], w_second_ref[...]
    first_t = joined_lanes([w_first[:features].T, w_first[features:].T])
    second_t = w_second.T
    columns = [column(ref, size) for ref in (b_first_ref, b_second_ref, gain_ref)]
    w_msg_here_ref[...] = w_msg
    w_first_here_ref[...] = w_first
    w_second_here_ref[...] = w_second
    first_t_ref[...] = first_t
    second_t_ref[...] = second_t
    for k in range(3):
        columns_ref[k] = columns[k]
    state = state_ref[...]
    state_t = [state[b * size : (b + 1) * size].T for b in range(blocks)]
    cot_t = [cot_ref[rows(b), :].T for b in range(blocks)]

    nothing = jnp.zeros((size, size), BF16)
    col_copy.wait()
    for b in range(blocks):
        for place in range(BAND):
            if place != WIN:
                band_ref[b, place] = nothing
        band_ref[b, WIN] = counts_ref[b, 0].astype(F32).astype(BF16)
        own = col_ref[0, b]
        for t in range(1, tiles):
            band_ref[b, col_ref[t, b] - own + WIN] += counts_ref[b, t].astype(F32).astype(BF16)

    wide = joined_lanes([dot(state, w_msg).astype(BF16), state])

    def neighbour_sum(b):
        first, last = max(b - WIN, 0), min(b + WIN, blocks - 1)
        tiles_of = [band_ref[b, block - b + WIN] for block in range(first, last + 1)]
        return dot(joined_lanes(tiles_of), wide[first * size : (last + 1) * size])

    def far(b, first):
        places = [block - b + WIN for block in range(first, first + WIN)]
        return joined_lanes([band_ref[b, p] if 0 <= p < BAND else nothing for p in places])

    def stacked(parts):
        return jnp.concatenate(list(parts), axis=0)

    ends = (stacked(map(neighbour_sum, low_rows)), stacked(map(neighbour_sum, high_rows)))
    fars = (stacked(far(b, -WIN) for b in low_rows), stacked(far(b, blocks) for b in high_rows))
    end_states = (state[: WIN * size], state[(blocks - WIN) * size :])
    end_states_t = (joined_lanes(state_t[:WIN]), joined_lanes(state_t[blocks - WIN :]))
    end_cots_t = (joined_lanes(cot_t[:WIN]), joined_lanes(cot_t[blocks - WIN :]))
    side_sum_ref[...] = odd_side(*ends)
    side_far_ref[...] = odd_side(*fars)
    side_state_t_ref[...] = odd_side(*end_states_t)
    side_cot_ref[...] = odd_side(*end_cots_t)

    halo = got_even_ref[...]
    wide_halo = joined_lanes([dot(halo, w_msg).astype(BF16), halo])
    end_sum = even_side(*ends) + dot(even_side(*fars), wide_halo)
    summed = stacked([*map(neighbour_sum, inner_rows), end_sum]).astype(BF16)
    aggregate, summed = summed[:, :features], summed[:, features:]
    updated_t, terms, active_t, d_norm_t, d_hidden_t = node_layer(
        joined_lanes([*state_t[WIN : blocks - WIN], even_side(*end_states_t)]),
        joined_lanes(blocks_turned(aggregate)),
        joined_lanes([*cot_t[WIN : blocks - WIN], even_side(*end_cots_t)]),
        first_t,
        second_t,
        w_second,
        columns,
    )
    updated_ref[...] = updated_t
    updated_copy = pltpu.make_async_copy(updated_ref, updated_hbm, left)
    updated_copy.start()
    d_hidden_ref[...] = d_hidden_t
    d_aggregate_t = d_aggregate_of(w_first, d_hidden_t)
    first_sums_ref[...] = first_products(
        d_hidden_t,
        stacked([state[WIN * size : (blocks - WIN) * size], even_side(*end_states)]),
        aggregate,
    )
    second_sums_ref[...] = sums_over_nodes([active_t], d_norm_t)
    msg_sums_ref[...] = dot(d_aggregate_t, summed)
    gain_sums_ref[...] = sum(
        terms[:, k * size : (k + 1) * size] for k in range(blocks - WIN)
    )
    updated_copy.wait()


def outer_kernel(
    grad_scale,
    got_odd_ref,
    w_msg_ref,
    w_first_ref,
    w_second_ref,
    first_t_ref,
    second_t_ref,
    columns_ref,
    side_state_t_ref,
    side_cot_ref,
    side_sum_ref,
    side_far_ref,
    first_sums_ref,
    second_sums_ref,
    msg_sums_ref,
    gain_sums_ref,
    grads_ref,
    updated_hbm,
    d_hidden_ref,
    updated_ref,
    left,
):
    features, size = w_msg_ref.shape[0], columns_ref.shape[2]
    first_before = [first_sums_ref[:, pl.ds(k * size, size)].T for k in range(3)]
    msg_before = msg_sums_ref[...].T
    halo = got_odd_ref[...]
    wide_halo = joined_lanes([dot(halo, w_msg_ref[...]).astype(BF16), halo])
    summed = (side_sum_ref[...] + dot(side_far_ref[...], wide_halo)).astype(BF16)
    aggregate, summed = summed[:, :features], summed[:, features:]
    state_t = side_state_t_ref[...]
    aggregate_t = joined_lanes(blocks_turned(aggregate))
    summed_t = joined_lanes(blocks_turned(summed))
    updated_t, terms, active_t, d_norm_t, d_hidden_t = node_layer(
        state_t,
        aggregate_t,
        side_cot_ref[...],
        first_t_ref[...],
        second_t_ref[...],
        w_second_ref[...],
        [columns_ref[k] for k in range(3)],
    )
    updated_ref[...] = updated_t
    updated_copy = pltpu.make_async_copy(updated_ref, updated_hbm, left)
    updated_copy.start()
    d_hidden_ref[...] = d_hidden_t
    d_aggregate_t = d_aggregate_of(w_first_ref[...], d_hidden_t)

    second_sums = second_sums_ref[...] + sums_over_nodes([active_t], d_norm_t)
    first_sums = sums_over_nodes([state_t, aggregate_t], d_hidden_t)
    msg_sums = msg_before + dot_nt(summed_t, d_aggregate_t)
    gain_sums = gain_sums_ref[...]
    for k in range(WIN):
        gain_sums = gain_sums + terms[:, k * size : (k + 1) * size]

    chunk = grads_ref.shape[1] - BIAS_ROWS
    sums = (
        jnp.concatenate(
            [
                first_before[0] + first_sums[:features],
                first_before[1] + first_sums[features : 2 * features],
                second_sums[:features],
                msg_sums,
            ],
            axis=0,
        )
        * grad_scale
    ).astype(SENT)
    bias = (
        jnp.concatenate(
            [
                first_before[2][:1] + first_sums[2 * features : 2 * features + 1],
                second_sums[features : features + 1],
                jnp.sum(gain_sums.T, axis=0, keepdims=True),
            ],
            axis=0,
        )
        * grad_scale
    )
    bias_high = bias.astype(SENT)
    bias_low = (bias - bias_high.astype(F32)).astype(SENT)
    bias = jnp.concatenate(
        [bias_high, bias_low, jnp.zeros((BIAS_ROWS - 6, features), SENT)], axis=0
    )
    nothing = jnp.zeros((chunk, features), SENT)
    for k in range(grads_ref.shape[0]):
        block = sums[k * chunk : (k + 1) * chunk] if k * chunk < sums.shape[0] else nothing
        grads_ref[k] = jnp.concatenate([block, bias], axis=0)
    updated_copy.wait()


def owed_kernel(
    band_ref, w_first_ref, inner_ref, outer_ref, done_ref, ends_ref, send_even_ref, send_odd_ref
):
    blocks, _, size, _ = band_ref.shape
    odd = device_is_odd()
    w_first = w_first_ref[...]
    inner = d_aggregate_of(w_first, inner_ref[...])
    outer = d_aggregate_of(w_first, outer_ref[...])

    def d_aggregate(b):
        if WIN <= b < blocks - WIN:
            return inner[:, (b - WIN) * size : (b - WIN + 1) * size]
        k = b if b < WIN else b - blocks + WIN
        even_end = inner[:, (blocks - 2 * WIN + k) * size : (blocks - 2 * WIN + k + 1) * size]
        odd_end = outer[:, k * size : (k + 1) * size]
        return jnp.where(odd == (b < WIN), even_end, odd_end)

    def owed(block):
        near = range(max(block - WIN, 0), min(block + WIN, blocks - 1) + 1)
        tiles_of = [band_ref[b, block - b + WIN] for b in near]
        return dot(
            joined_lanes([d_aggregate(b) for b in near]), jnp.concatenate(tiles_of, axis=0)
        )

    for k in range(WIN):
        to_below = owed(k - WIN).astype(BF16)
        to_above = owed(blocks + k).astype(BF16)
        send_even_ref[k] = jnp.where(odd, to_below, to_above)
        send_odd_ref[k] = jnp.where(odd, to_above, to_below)
    for b in range(WIN, blocks - WIN):
        done_ref[b - WIN] = owed(b).astype(BF16)
    for k in range(WIN):
        ends_ref[k] = owed(k)
        ends_ref[WIN + k] = owed(blocks - WIN + k)


def sum_kernel(parts_ref, spread_ref, bias_ref):
    total = parts_ref[0].astype(F32)
    for k in range(1, parts_ref.shape[0]):
        total = total + parts_ref[k].astype(F32)
    chunk = spread_ref.shape[1]
    weights = total[:chunk].astype(spread_ref.dtype)
    for k in range(spread_ref.shape[0]):
        spread_ref[k] = weights
    bias_ref[...] = total[chunk:]


def result_kernel(
    even_ref,
    odd_ref,
    cot_hbm,
    w_msg_ref,
    w_first_ref,
    inner_updated_hbm,
    outer_updated_hbm,
    inner_d_hidden_ref,
    outer_d_hidden_ref,
    owed_ref,
    ends_ref,
    bias_ref,
    updated_ref,
    grad_state_ref,
    b_first_ref,
    b_second_ref,
    gain_ref,
    cot_ref,
    inner_updated_ref,
    outer_updated_ref,
    arrived,
):
    inner, features, size = owed_ref.shape
    blocks = inner + 2 * WIN
    copies = [
        pltpu.make_async_copy(source, target, arrived.at[k])
        for k, (source, target) in enumerate(
            (
                (cot_hbm, cot_ref),
                (inner_updated_hbm, inner_updated_ref),
                (outer_updated_hbm, outer_updated_ref),
            )
        )
    ]
    for copy in copies:
        copy.start()
    odd = device_is_odd()
    even_part, odd_part = even_ref[...].astype(F32), odd_ref[...].astype(F32)
    from_below = jnp.where(odd, even_part, odd_part)
    from_above = jnp.where(odd, odd_part, even_part)
    weights = joined_lanes([w_first_ref[pl.ds(0, features), :], w_msg_ref[...]])
    for copy in copies:
        copy.wait()
    for b in range(blocks):
        if b < WIN:
            owed = (ends_ref[b] + from_below[b]).astype(BF16)
        elif b < blocks - WIN:
            owed = owed_ref[b - WIN]
        else:
            k = b - blocks + WIN
            owed = (ends_ref[WIN + k] + from_above[k]).astype(BF16)
        if WIN <= b < blocks - WIN:
            lanes = pl.ds((b - WIN) * size, size)
            updated, d_hidden = inner_updated_ref[:, lanes], inner_d_hidden_ref[:, lanes]
        else:
            k = b if b < WIN else b - blocks + WIN
            even_end = odd == (b < WIN)
            lanes, outer_lanes = pl.ds((blocks - 2 * WIN + k) * size, size), pl.ds(k * size, size)
            updated = jnp.where(
                even_end, inner_updated_ref[:, lanes], outer_updated_ref[:, outer_lanes]
            )
            d_hidden = jnp.where(
                even_end, inner_d_hidden_ref[:, lanes], outer_d_hidden_ref[:, outer_lanes]
            )
        rows = pl.ds(b * size, size)
        change = dot(weights, jnp.concatenate([d_hidden, owed], axis=0))
        grad_state_ref[rows, :] = (cot_ref[rows, :].astype(F32) + change.T).astype(BF16)
        updated_ref[rows, :] = updated.T
    for k, ref in enumerate((b_first_ref, b_second_ref, gain_ref)):
        ref[...] = bias_ref[pl.ds(k, 1), :] + bias_ref[pl.ds(k + 3, 1), :]


def unpack_kernel(rows_ref, msg_ref, first_ref, second_ref):
    place = 0
    for ref in (first_ref, second_ref, msg_ref):
        count = ref.shape[0]
        ref[...] = rows_ref[pl.ds(place, count), :].astype(F32)
        place += count


def swapped(block, parity):
    last = lax.axis_size(AXES) - 1
    lower = range(parity, last, 2)
    return lax.ppermute(block, AXES, [(i, i + 1) for i in lower] + [(i + 1, i) for i in lower])


def call(kernel, name, outs, operands, scratch=(), limit=16, flops=0):
    specs = [pl.BlockSpec(memory_space=space) for _, space in operands]
    arrays = [kept(array, space) for array, space in operands]
    return pl.pallas_call(
        kernel,
        out_shape=tuple(outs),
        in_specs=specs,
        out_specs=tuple(
            pl.BlockSpec(memory_space=getattr(out, "memory_space", pltpu.VMEM)) for out in outs
        ),
        scratch_shapes=list(scratch),
        compiler_params=pltpu.CompilerParams(vmem_limit_bytes=limit * 1024 * 1024),
        cost_estimate=pl.CostEstimate(
            flops=flops, bytes_accessed=1_000_000, transcendentals=0
        ),
        name=name,
    )(*arrays)


def shards(
    node_state,
    w_msg,
    w_first,
    b_first,
    w_second,
    b_second,
    ln_gain,
    col_index,
    edge_counts,
    cotangent,
):
    nodes, features = node_state.shape
    blocks, tiles, size, _ = edge_counts.shape
    devices = lax.axis_size(AXES)
    grad_scale = 1.0 / math.sqrt(nodes * devices)
    chunk = -(-4 * features // (devices * 8)) * 8
    side = WIN * size
    most = nodes - side
    vmem, hbm = pltpu.VMEM, pltpu.HBM
    result = jax.ShapeDtypeStruct

    row = lambda vector: vector.reshape(1, features)
    even_side, odd_side = call(
        cut_kernel,
        "cut",
        [vmem((side, features), BF16)] * 2,
        [(node_state, hbm)],
        scratch=(pltpu.SemaphoreType.DMA((2,)),),
        flops=50_000_000_000,
    )
    got_even = swapped(even_side, 0)
    got_odd = swapped(odd_side, 1)

    inner_results = call(
            inner_kernel,
            "inner_rows",
            (
                vmem((features, features), BF16),
                vmem((2 * features, features), BF16),
                vmem((features, features), BF16),
                vmem((features, 2 * features), BF16),
                vmem((features, features), BF16),
                vmem((3, features, size), F32),
                vmem((features, side), BF16),
                vmem((features, side), BF16),
                vmem((side, 2 * features), F32),
                vmem((side, side), BF16),
                vmem((blocks, BAND, size, size), BF16),
                hbm((features, most), BF16),
                vmem((features, most), BF16),
                vmem((features, 2 * features + ONES), F32),
                vmem((features + 16, features), F32),
                vmem((features, features), F32),
                vmem((features, size), F32),
            ),
            [(col_index.T, hbm)]
            + [
                (array, vmem)
                for array in (
                    edge_counts,
                    cotangent,
                    node_state,
                    got_even,
                    w_msg,
                    w_first,
                    w_second,
                    row(b_first),
                    row(b_second),
                    row(ln_gain),
                )
            ],
        scratch=(
                pltpu.SMEM((tiles, blocks), jnp.int32),
                vmem((features, most), BF16),
                pltpu.SemaphoreType.DMA,
                pltpu.SemaphoreType.DMA,
            ),
            limit=32,
            flops=700_000_000,
    )
    for_outer, (band, inner_updated, inner_d_hidden), sums = (
        inner_results[:10],
        inner_results[10:13],
        inner_results[13:],
    )
    w_msg_here, w_first_here = inner_results[:2]

    grads, outer_updated, outer_d_hidden = call(
        functools.partial(outer_kernel, grad_scale),
        "outer_rows",
        (
            vmem((devices, chunk + BIAS_ROWS, features), SENT),
            hbm((features, side), BF16),
            vmem((features, side), BF16),
        ),
        [
            (array, vmem)
            for array in (got_odd, *for_outer, *sums)
        ],
        scratch=(vmem((features, side), BF16), pltpu.SemaphoreType.DMA),
        flops=300_000_000,
    )

    parts = lax.all_to_all(grads, AXES, 0, 0, tiled=True)
    owed, owed_ends, send_even, send_odd = call(
        owed_kernel,
        "owed",
        (
            vmem((blocks - 2 * WIN, features, size), BF16),
            vmem((2 * WIN, features, size), F32),
            vmem((WIN, features, size), BF16),
            vmem((WIN, features, size), BF16),
        ),
        [(array, vmem) for array in (band, w_first_here, inner_d_hidden, outer_d_hidden)],
        flops=200_000_000,
    )
    owed_even = swapped(send_even, 0)
    owed_odd = swapped(send_odd, 1)
    spread, bias = call(
        sum_kernel,
        "sum",
        (vmem((devices, chunk, features), SENT), vmem((BIAS_ROWS, features), F32)),
        [(parts, vmem)],
        flops=10_000_000_000,
    )
    updated, grad_state, g_b_first, g_b_second, g_gain = call(
        result_kernel,
        "results",
        (
            result((nodes, features), BF16),
            result((nodes, features), BF16),
            result((1, features), F32),
            result((1, features), F32),
            result((1, features), F32),
        ),
        [(owed_even, vmem), (owed_odd, vmem), (cotangent, hbm)]
        + [(w_msg_here, vmem), (w_first_here, vmem), (inner_updated, hbm), (outer_updated, hbm)]
        + [(array, vmem) for array in (inner_d_hidden, outer_d_hidden, owed, owed_ends, bias)],
        scratch=(
            vmem((nodes, features), BF16),
            vmem((features, most), BF16),
            vmem((features, side), BF16),
            pltpu.SemaphoreType.DMA((3,)),
        ),
        flops=50_000_000_000,
    )

    whole = lax.all_to_all(spread, AXES, 0, 0, tiled=True)
    g_msg, g_first, g_second = call(
        unpack_kernel,
        "unpack",
        (
            result((features, features), F32),
            result((2 * features, features), F32),
            result((features, features), F32),
        ),
        [(whole.reshape(devices * chunk, features), vmem)],
    )
    flat = lambda vector: vector.reshape(features)
    return (
        updated,
        grad_state,
        g_msg,
        g_first,
        flat(g_b_first),
        g_second,
        flat(g_b_second),
        flat(g_gain),
    )


def solution(mesh):
    split = P(AXES, None)
    return jax.shard_map(
        shards,
        mesh=mesh,
        in_specs=(split, P(), P(), P(), P(), P(), P(), split, P(AXES, None, None, None), split),
        out_specs=(split, split, P(), P(), P(), P(), P(), P()),
        check_vma=False,
    )
```

```python
import functools
import math

import jax
import jax.numpy as jnp
from jax import lax
from jax.experimental import pallas as pl
from jax.experimental.pallas import tpu as pltpu
from jax.sharding import PartitionSpec as P

WIN = 2
BAND = 2 * WIN + 1
epsilon = 1e-05
AXES = ("dom", "feat")
BF16, F32 = jnp.bfloat16, jnp.float32
SENT = BF16
ONES = 128
BIAS_ROWS = 8

kept = pltpu.with_memory_space_constraint


def dot(left, right):
    return jnp.dot(left, right, preferred_element_type=F32)


def joined_lanes(parts):
    return jnp.concatenate(parts, axis=1)


def device_is_odd():
    index = lax.axis_index("dom") * lax.axis_size("feat") + lax.axis_index("feat")
    return index % 2 == 1


def column(row_ref, width):
    return jnp.broadcast_to(row_ref[...], (width, row_ref.shape[1])).T


def blocks_turned(array):
    size = array.shape[1]
    return [array[k : k + size].T for k in range(0, array.shape[0], size)]


def rows_of(array_t):
    size = array_t.shape[0]
    turned = [array_t[:, k : k + size].T for k in range(0, array_t.shape[1], size)]
    return jnp.concatenate(turned, axis=0)


def node_layer(state_t, aggregate_t, cot_t, first_t, second_t, w_second, columns):
    features, width = state_t.shape
    b_first, b_second, gain = (
        joined_lanes([c] * (width // c.shape[1])) for c in columns
    )
    pre_hidden = dot(first_t, jnp.concatenate([state_t, aggregate_t], axis=0)) + b_first
    sigmoid = 0.5 * jnp.tanh(0.5 * pre_hidden) + 0.5
    silu = pre_hidden * sigmoid
    active_t = silu.astype(BF16)
    slope = sigmoid + silu * (1.0 - sigmoid)
    pre_norm = dot(second_t, active_t) + b_second
    centred = pre_norm - jnp.mean(pre_norm, axis=0, keepdims=True)
    inv_std = lax.rsqrt(jnp.mean(centred * centred, axis=0, keepdims=True) + epsilon)
    normed = centred * inv_std
    updated_t = (state_t.astype(F32) + gain * normed).astype(BF16)
    cot = cot_t.astype(F32)
    terms = cot * normed
    q = cot * gain
    mean_q = jnp.mean(q, axis=0, keepdims=True)
    mean_qn = jnp.mean(q * normed, axis=0, keepdims=True)
    d_norm_t = (inv_std * (q - mean_q - normed * mean_qn)).astype(BF16)
    d_hidden_t = (dot(w_second, d_norm_t) * slope).astype(BF16)
    return updated_t, terms, active_t, d_norm_t, d_hidden_t


def d_aggregate_of(w_first, d_hidden_t):
    return dot(w_first[w_first.shape[1] :], d_hidden_t).astype(BF16)


def sums_over_nodes(left_t, *rights):
    ones = jnp.ones((rights[0].shape[0], ONES), BF16)
    return dot(left_t, joined_lanes([*rights, ones]))


def cut_kernel(state_hbm, even_side_ref, odd_side_ref, arrived):
    side = even_side_ref.shape[0]
    odd = device_is_odd()
    last = state_hbm.shape[0] - side
    even_start = pl.multiple_of(jnp.where(odd, 0, last), side)
    odd_start = pl.multiple_of(jnp.where(odd, last, 0), side)
    copies = [
        pltpu.make_async_copy(state_hbm.at[pl.ds(start, side)], target, arrived.at[k])
        for k, (start, target) in enumerate(
            ((even_start, even_side_ref), (odd_start, odd_side_ref))
        )
    ]
    for copy in copies:
        copy.start()
    for copy in copies:
        copy.wait()


def inner_kernel(
    col_hbm,
    counts_ref,
    cot_ref,
    state_ref,
    got_even_ref,
    w_msg_ref,
    w_first_ref,
    w_second_ref,
    b_first_ref,
    b_second_ref,
    gain_ref,
    w_msg_here_ref,
    w_first_here_ref,
    w_second_here_ref,
    first_t_ref,
    second_t_ref,
    columns_ref,
    side_state_ref,
    side_state_t_ref,
    side_cot_ref,
    side_sum_ref,
    side_far_ref,
    band_ref,
    updated_hbm,
    d_hidden_ref,
    first_sums_ref,
    second_sums_ref,
    msg_sums_ref,
    gain_sums_ref,
    col_ref,
    updated_ref,
    arrived,
    left,
):
    blocks, tiles, size, _ = counts_ref.shape
    features = state_ref.shape[1]
    inner_rows = range(WIN, blocks - WIN)
    low_rows, high_rows = range(WIN), range(blocks - WIN, blocks)
    odd = device_is_odd()

    def even_side(low, high):
        return jnp.where(odd, low, high)

    def odd_side(low, high):
        return jnp.where(odd, high, low)

    col_copy = pltpu.make_async_copy(col_hbm, col_ref, arrived)
    col_copy.start()

    def rows(block, count=1):
        return pl.ds(block * size, count * size)

    w_msg, w_first, w_second = w_msg_ref[...], w_first_ref[...], w_second_ref[...]
    first_t = joined_lanes([w_first[:features].T, w_first[features:].T])
    second_t = w_second.T
    columns = [column(ref, size) for ref in (b_first_ref, b_second_ref, gain_ref)]
    w_msg_here_ref[...] = w_msg
    w_first_here_ref[...] = w_first
    w_second_here_ref[...] = w_second
    first_t_ref[...] = first_t
    second_t_ref[...] = second_t
    for k in range(3):
        columns_ref[k] = columns[k]
    state = state_ref[...]
    state_t = [state[b * size : (b + 1) * size].T for b in range(blocks)]
    cot_t = [cot_ref[rows(b), :].T for b in range(blocks)]

    nothing = jnp.zeros((size, size), BF16)
    col_copy.wait()
    for b in range(blocks):
        for place in range(BAND):
            if place != WIN:
                band_ref[b, place] = nothing
        band_ref[b, WIN] = counts_ref[b, 0].astype(F32).astype(BF16)
        own = col_ref[0, b]
        for t in range(1, tiles):
            band_ref[b, col_ref[t, b] - own + WIN] += counts_ref[b, t].astype(F32).astype(BF16)

    wide = joined_lanes([dot(state, w_msg).astype(BF16), state])

    def neighbour_sum(b):
        first, last = max(b - WIN, 0), min(b + WIN, blocks - 1)
        tiles_of = [band_ref[b, block - b + WIN] for block in range(first, last + 1)]
        return dot(joined_lanes(tiles_of), wide[first * size : (last + 1) * size])

    def far(b, first):
        places = [block - b + WIN for block in range(first, first + WIN)]
        return joined_lanes([band_ref[b, p] if 0 <= p < BAND else nothing for p in places])

    def stacked(parts):
        return jnp.concatenate(list(parts), axis=0)

    ends = (stacked(map(neighbour_sum, low_rows)), stacked(map(neighbour_sum, high_rows)))
    fars = (stacked(far(b, -WIN) for b in low_rows), stacked(far(b, blocks) for b in high_rows))
    end_states = (state[: WIN * size], state[(blocks - WIN) * size :])
    end_states_t = (joined_lanes(state_t[:WIN]), joined_lanes(state_t[blocks - WIN :]))
    end_cots_t = (joined_lanes(cot_t[:WIN]), joined_lanes(cot_t[blocks - WIN :]))
    side_sum_ref[...] = odd_side(*ends)
    side_far_ref[...] = odd_side(*fars)
    side_state_ref[...] = odd_side(*end_states)
    side_state_t_ref[...] = odd_side(*end_states_t)
    side_cot_ref[...] = odd_side(*end_cots_t)

    halo = got_even_ref[...]
    wide_halo = joined_lanes([dot(halo, w_msg).astype(BF16), halo])
    end_sum = even_side(*ends) + dot(even_side(*fars), wide_halo)
    summed = stacked([*map(neighbour_sum, inner_rows), end_sum]).astype(BF16)
    aggregate, summed = summed[:, :features], summed[:, features:]
    updated_t, terms, active_t, d_norm_t, d_hidden_t = node_layer(
        joined_lanes([*state_t[WIN : blocks - WIN], even_side(*end_states_t)]),
        joined_lanes(blocks_turned(aggregate)),
        joined_lanes([*cot_t[WIN : blocks - WIN], even_side(*end_cots_t)]),
        first_t,
        second_t,
        w_second,
        columns,
    )
    updated_ref[...] = updated_t
    updated_copy = pltpu.make_async_copy(updated_ref, updated_hbm, left)
    updated_copy.start()
    d_hidden_ref[...] = d_hidden_t
    d_aggregate_t = d_aggregate_of(w_first, d_hidden_t)
    first_sums_ref[...] = sums_over_nodes(
        d_hidden_t,
        stacked([state[WIN * size : (blocks - WIN) * size], even_side(*end_states)]),
        aggregate,
    )
    second_sums_ref[...] = sums_over_nodes(d_norm_t, rows_of(active_t))
    msg_sums_ref[...] = dot(d_aggregate_t, summed)
    gain_sums_ref[...] = sum(
        terms[:, k * size : (k + 1) * size] for k in range(blocks - WIN)
    )
    updated_copy.wait()


def outer_kernel(
    grad_scale,
    got_odd_ref,
    w_msg_ref,
    w_first_ref,
    w_second_ref,
    first_t_ref,
    second_t_ref,
    columns_ref,
    side_state_ref,
    side_state_t_ref,
    side_cot_ref,
    side_sum_ref,
    side_far_ref,
    first_sums_ref,
    second_sums_ref,
    msg_sums_ref,
    gain_sums_ref,
    grads_ref,
    updated_hbm,
    d_hidden_ref,
    updated_ref,
    left,
):
    features, size = w_msg_ref.shape[0], columns_ref.shape[2]
    halo = got_odd_ref[...]
    wide_halo = joined_lanes([dot(halo, w_msg_ref[...]).astype(BF16), halo])
    summed = (side_sum_ref[...] + dot(side_far_ref[...], wide_halo)).astype(BF16)
    aggregate, summed = summed[:, :features], summed[:, features:]
    updated_t, terms, active_t, d_norm_t, d_hidden_t = node_layer(
        side_state_t_ref[...],
        joined_lanes(blocks_turned(aggregate)),
        side_cot_ref[...],
        first_t_ref[...],
        second_t_ref[...],
        w_second_ref[...],
        [columns_ref[k] for k in range(3)],
    )
    updated_ref[...] = updated_t
    updated_copy = pltpu.make_async_copy(updated_ref, updated_hbm, left)
    updated_copy.start()
    d_hidden_ref[...] = d_hidden_t
    d_aggregate_t = d_aggregate_of(w_first_ref[...], d_hidden_t)

    second_sums = second_sums_ref[...] + sums_over_nodes(d_norm_t, rows_of(active_t))
    first_sums = first_sums_ref[...] + sums_over_nodes(d_hidden_t, side_state_ref[...], aggregate)
    msg_sums = msg_sums_ref[...] + dot(d_aggregate_t, summed)
    gain_sums = gain_sums_ref[...]
    for k in range(WIN):
        gain_sums = gain_sums + terms[:, k * size : (k + 1) * size]

    chunk = grads_ref.shape[1] - BIAS_ROWS
    first = [first_sums[:, k * size : (k + 1) * size].T for k in range(3)]
    second = [second_sums[:, k * size : (k + 1) * size].T for k in range(2)]
    sums = (
        jnp.concatenate([first[0], first[1], second[0], msg_sums.T], axis=0) * grad_scale
    ).astype(SENT)
    bias = (
        jnp.concatenate(
            [
                first[2][:1],
                second[1][:1],
                jnp.sum(gain_sums.T, axis=0, keepdims=True),
            ],
            axis=0,
        )
        * grad_scale
    )
    bias_high = bias.astype(SENT)
    bias_low = (bias - bias_high.astype(F32)).astype(SENT)
    bias = jnp.concatenate(
        [bias_high, bias_low, jnp.zeros((BIAS_ROWS - 6, features), SENT)], axis=0
    )
    nothing = jnp.zeros((chunk, features), SENT)
    for k in range(grads_ref.shape[0]):
        block = sums[k * chunk : (k + 1) * chunk] if k * chunk < sums.shape[0] else nothing
        grads_ref[k] = jnp.concatenate([block, bias], axis=0)
    updated_copy.wait()


def owed_kernel(
    band_ref, w_first_ref, inner_ref, outer_ref, done_ref, ends_ref, send_even_ref, send_odd_ref
):
    blocks, _, size, _ = band_ref.shape
    odd = device_is_odd()
    w_first = w_first_ref[...]
    inner = d_aggregate_of(w_first, inner_ref[...])
    outer = d_aggregate_of(w_first, outer_ref[...])

    def d_aggregate(b):
        if WIN <= b < blocks - WIN:
            return inner[:, (b - WIN) * size : (b - WIN + 1) * size]
        k = b if b < WIN else b - blocks + WIN
        even_end = inner[:, (blocks - 2 * WIN + k) * size : (blocks - 2 * WIN + k + 1) * size]
        odd_end = outer[:, k * size : (k + 1) * size]
        return jnp.where(odd == (b < WIN), even_end, odd_end)

    def owed(block):
        near = range(max(block - WIN, 0), min(block + WIN, blocks - 1) + 1)
        tiles_of = [band_ref[b, block - b + WIN] for b in near]
        return dot(
            joined_lanes([d_aggregate(b) for b in near]), jnp.concatenate(tiles_of, axis=0)
        )

    for k in range(WIN):
        to_below = owed(k - WIN).astype(BF16)
        to_above = owed(blocks + k).astype(BF16)
        send_even_ref[k] = jnp.where(odd, to_below, to_above)
        send_odd_ref[k] = jnp.where(odd, to_above, to_below)
    for b in range(WIN, blocks - WIN):
        done_ref[b - WIN] = owed(b).astype(BF16)
    for k in range(WIN):
        ends_ref[k] = owed(k)
        ends_ref[WIN + k] = owed(blocks - WIN + k)


def sum_kernel(parts_ref, spread_ref, bias_ref):
    total = parts_ref[0].astype(F32)
    for k in range(1, parts_ref.shape[0]):
        total = total + parts_ref[k].astype(F32)
    chunk = spread_ref.shape[1]
    weights = total[:chunk].astype(spread_ref.dtype)
    for k in range(spread_ref.shape[0]):
        spread_ref[k] = weights
    bias_ref[...] = total[chunk:]


def result_kernel(
    even_ref,
    odd_ref,
    cot_hbm,
    w_msg_ref,
    w_first_ref,
    inner_updated_hbm,
    outer_updated_hbm,
    inner_d_hidden_ref,
    outer_d_hidden_ref,
    owed_ref,
    ends_ref,
    bias_ref,
    updated_ref,
    grad_state_ref,
    b_first_ref,
    b_second_ref,
    gain_ref,
    cot_ref,
    inner_updated_ref,
    outer_updated_ref,
    arrived,
):
    inner, features, size = owed_ref.shape
    blocks = inner + 2 * WIN
    copies = [
        pltpu.make_async_copy(source, target, arrived.at[k])
        for k, (source, target) in enumerate(
            (
                (cot_hbm, cot_ref),
                (inner_updated_hbm, inner_updated_ref),
                (outer_updated_hbm, outer_updated_ref),
            )
        )
    ]
    for copy in copies:
        copy.start()
    odd = device_is_odd()
    even_part, odd_part = even_ref[...].astype(F32), odd_ref[...].astype(F32)
    from_below = jnp.where(odd, even_part, odd_part)
    from_above = jnp.where(odd, odd_part, even_part)
    weights = joined_lanes([w_first_ref[pl.ds(0, features), :], w_msg_ref[...]])
    for copy in copies:
        copy.wait()
    for b in range(blocks):
        if b < WIN:
            owed = (ends_ref[b] + from_below[b]).astype(BF16)
        elif b < blocks - WIN:
            owed = owed_ref[b - WIN]
        else:
            k = b - blocks + WIN
            owed = (ends_ref[WIN + k] + from_above[k]).astype(BF16)
        if WIN <= b < blocks - WIN:
            lanes = pl.ds((b - WIN) * size, size)
            updated, d_hidden = inner_updated_ref[:, lanes], inner_d_hidden_ref[:, lanes]
        else:
            k = b if b < WIN else b - blocks + WIN
            even_end = odd == (b < WIN)
            lanes, outer_lanes = pl.ds((blocks - 2 * WIN + k) * size, size), pl.ds(k * size, size)
            updated = jnp.where(
                even_end, inner_updated_ref[:, lanes], outer_updated_ref[:, outer_lanes]
            )
            d_hidden = jnp.where(
                even_end, inner_d_hidden_ref[:, lanes], outer_d_hidden_ref[:, outer_lanes]
            )
        rows = pl.ds(b * size, size)
        change = dot(weights, jnp.concatenate([d_hidden, owed], axis=0))
        grad_state_ref[rows, :] = (cot_ref[rows, :].astype(F32) + change.T).astype(BF16)
        updated_ref[rows, :] = updated.T
    for k, ref in enumerate((b_first_ref, b_second_ref, gain_ref)):
        ref[...] = bias_ref[pl.ds(k, 1), :] + bias_ref[pl.ds(k + 3, 1), :]


def unpack_kernel(rows_ref, msg_ref, first_ref, second_ref):
    place = 0
    for ref in (first_ref, second_ref, msg_ref):
        count = ref.shape[0]
        ref[...] = rows_ref[pl.ds(place, count), :].astype(F32)
        place += count


def swapped(block, parity):
    last = lax.axis_size(AXES) - 1
    lower = range(parity, last, 2)
    return lax.ppermute(block, AXES, [(i, i + 1) for i in lower] + [(i + 1, i) for i in lower])


def call(kernel, name, outs, operands, scratch=(), limit=16, flops=0):
    specs = [pl.BlockSpec(memory_space=space) for _, space in operands]
    arrays = [kept(array, space) for array, space in operands]
    return pl.pallas_call(
        kernel,
        out_shape=tuple(outs),
        in_specs=specs,
        out_specs=tuple(
            pl.BlockSpec(memory_space=getattr(out, "memory_space", pltpu.VMEM)) for out in outs
        ),
        scratch_shapes=list(scratch),
        compiler_params=pltpu.CompilerParams(vmem_limit_bytes=limit * 1024 * 1024),
        cost_estimate=pl.CostEstimate(
            flops=flops, bytes_accessed=1_000_000, transcendentals=0
        ),
        name=name,
    )(*arrays)


def shards(
    node_state,
    w_msg,
    w_first,
    b_first,
    w_second,
    b_second,
    ln_gain,
    col_index,
    edge_counts,
    cotangent,
):
    nodes, features = node_state.shape
    blocks, tiles, size, _ = edge_counts.shape
    devices = lax.axis_size(AXES)
    grad_scale = 1.0 / math.sqrt(nodes * devices)
    chunk = -(-4 * features // (devices * 8)) * 8
    side = WIN * size
    most = nodes - side
    vmem, hbm = pltpu.VMEM, pltpu.HBM
    result = jax.ShapeDtypeStruct

    row = lambda vector: vector.reshape(1, features)
    even_side, odd_side = call(
        cut_kernel,
        "cut",
        [vmem((side, features), BF16)] * 2,
        [(node_state, hbm)],
        scratch=(pltpu.SemaphoreType.DMA((2,)),),
        flops=50_000_000_000,
    )
    got_even = swapped(even_side, 0)
    got_odd = swapped(odd_side, 1)

    inner_results = call(
            inner_kernel,
            "inner_rows",
            (
                vmem((features, features), BF16),
                vmem((2 * features, features), BF16),
                vmem((features, features), BF16),
                vmem((features, 2 * features), BF16),
                vmem((features, features), BF16),
                vmem((3, features, size), F32),
                vmem((side, features), BF16),
                vmem((features, side), BF16),
                vmem((features, side), BF16),
                vmem((side, 2 * features), F32),
                vmem((side, side), BF16),
                vmem((blocks, BAND, size, size), BF16),
                hbm((features, most), BF16),
                vmem((features, most), BF16),
                vmem((features, 2 * features + ONES), F32),
                vmem((features, features + ONES), F32),
                vmem((features, features), F32),
                vmem((features, size), F32),
            ),
            [(col_index.T, hbm)]
            + [
                (array, vmem)
                for array in (
                    edge_counts,
                    cotangent,
                    node_state,
                    got_even,
                    w_msg,
                    w_first,
                    w_second,
                    row(b_first),
                    row(b_second),
                    row(ln_gain),
                )
            ],
        scratch=(
                pltpu.SMEM((tiles, blocks), jnp.int32),
                vmem((features, most), BF16),
                pltpu.SemaphoreType.DMA,
                pltpu.SemaphoreType.DMA,
            ),
            limit=32,
            flops=700_000_000,
    )
    for_outer, (band, inner_updated, inner_d_hidden), sums = (
        inner_results[:11],
        inner_results[11:14],
        inner_results[14:],
    )
    w_msg_here, w_first_here = inner_results[:2]

    grads, outer_updated, outer_d_hidden = call(
        functools.partial(outer_kernel, grad_scale),
        "outer_rows",
        (
            vmem((devices, chunk + BIAS_ROWS, features), SENT),
            hbm((features, side), BF16),
            vmem((features, side), BF16),
        ),
        [
            (array, vmem)
            for array in (got_odd, *for_outer, *sums)
        ],
        scratch=(vmem((features, side), BF16), pltpu.SemaphoreType.DMA),
        flops=300_000_000,
    )

    parts = lax.all_to_all(grads, AXES, 0, 0, tiled=True)
    owed, owed_ends, send_even, send_odd = call(
        owed_kernel,
        "owed",
        (
            vmem((blocks - 2 * WIN, features, size), BF16),
            vmem((2 * WIN, features, size), F32),
            vmem((WIN, features, size), BF16),
            vmem((WIN, features, size), BF16),
        ),
        [(array, vmem) for array in (band, w_first_here, inner_d_hidden, outer_d_hidden)],
        flops=200_000_000,
    )
    owed_even = swapped(send_even, 0)
    owed_odd = swapped(send_odd, 1)
    spread, bias = call(
        sum_kernel,
        "sum",
        (vmem((devices, chunk, features), SENT), vmem((BIAS_ROWS, features), F32)),
        [(parts, vmem)],
        flops=10_000_000_000,
    )
    updated, grad_state, g_b_first, g_b_second, g_gain = call(
        result_kernel,
        "results",
        (
            result((nodes, features), BF16),
            result((nodes, features), BF16),
            result((1, features), F32),
            result((1, features), F32),
            result((1, features), F32),
        ),
        [(owed_even, vmem), (owed_odd, vmem), (cotangent, hbm)]
        + [(w_msg_here, vmem), (w_first_here, vmem), (inner_updated, hbm), (outer_updated, hbm)]
        + [(array, vmem) for array in (inner_d_hidden, outer_d_hidden, owed, owed_ends, bias)],
        scratch=(
            vmem((nodes, features), BF16),
            vmem((features, most), BF16),
            vmem((features, side), BF16),
            pltpu.SemaphoreType.DMA((3,)),
        ),
        flops=50_000_000_000,
    )

    whole = lax.all_to_all(spread, AXES, 0, 0, tiled=True)
    g_msg, g_first, g_second = call(
        unpack_kernel,
        "unpack",
        (
            result((features, features), F32),
            result((2 * features, features), F32),
            result((features, features), F32),
        ),
        [(whole.reshape(devices * chunk, features), vmem)],
    )
    flat = lambda vector: vector.reshape(features)
    return (
        updated,
        grad_state,
        g_msg,
        g_first,
        flat(g_b_first),
        g_second,
        flat(g_b_second),
        flat(g_gain),
    )


def solution(mesh):
    split = P(AXES, None)
    return jax.shard_map(
        shards,
        mesh=mesh,
        in_specs=(split, P(), P(), P(), P(), P(), P(), split, P(AXES, None, None, None), split),
        out_specs=(split, split, P(), P(), P(), P(), P(), P()),
        check_vma=False,
    )
```

```python
import functools
import math

import jax
import jax.numpy as jnp
from jax import lax
from jax.experimental import pallas as pl
from jax.experimental.pallas import tpu as pltpu
from jax.sharding import PartitionSpec as P

WIN = 2
BAND = 2 * WIN + 1
epsilon = 1e-05
AXES = ("dom", "feat")
BF16, F32 = jnp.bfloat16, jnp.float32
SENT = BF16
ONES = 128
BIAS_ROWS = 8

kept = pltpu.with_memory_space_constraint


def dot(left, right):
    return jnp.dot(left, right, preferred_element_type=F32)


def dot_nt(left, right):
    return lax.dot_general(left, right, (((1,), (1,)), ((), ())), preferred_element_type=F32)


def joined_lanes(parts):
    return jnp.concatenate(parts, axis=1)


def device_is_odd():
    index = lax.axis_index("dom") * lax.axis_size("feat") + lax.axis_index("feat")
    return index % 2 == 1


def column(row_ref):
    features = row_ref.shape[1]
    square = (features, features)
    diagonal = lax.broadcasted_iota(jnp.int32, square, 0) == lax.broadcasted_iota(
        jnp.int32, square, 1
    )
    rest, terms = row_ref[...], []
    for _ in range(3):
        term = rest.astype(BF16).astype(F32)
        terms.append(jnp.where(diagonal, jnp.broadcast_to(term, square), 0.0).astype(BF16))
        rest = rest - term
    return dot(joined_lanes(terms), jnp.ones((3 * features, features), BF16))


def blocks_turned(array):
    size = array.shape[1]
    return [array[k : k + size].T for k in range(0, array.shape[0], size)]


def node_layer(state_t, aggregate_t, cot_t, first_t, second_t, w_second, columns):
    features, width = state_t.shape
    b_first, b_second, gain = (
        joined_lanes([c] * (width // c.shape[1])) for c in columns
    )
    pre_hidden = dot(first_t, jnp.concatenate([state_t, aggregate_t], axis=0)) + b_first
    sigmoid = 0.5 * jnp.tanh(0.5 * pre_hidden) + 0.5
    silu = pre_hidden * sigmoid
    active_t = silu.astype(BF16)
    slope = sigmoid + silu * (1.0 - sigmoid)
    pre_norm = dot(second_t, active_t) + b_second
    centred = pre_norm - jnp.mean(pre_norm, axis=0, keepdims=True)
    inv_std = lax.rsqrt(jnp.mean(centred * centred, axis=0, keepdims=True) + epsilon)
    normed = centred * inv_std
    updated_t = (state_t.astype(F32) + gain * normed).astype(BF16)
    cot = cot_t.astype(F32)
    terms = cot * normed
    q = cot * gain
    mean_q = jnp.mean(q, axis=0, keepdims=True)
    mean_qn = jnp.mean(q * normed, axis=0, keepdims=True)
    d_norm_t = (inv_std * (q - mean_q - normed * mean_qn)).astype(BF16)
    d_hidden_t = (dot(w_second, d_norm_t) * slope).astype(BF16)
    return updated_t, terms, active_t, d_norm_t, d_hidden_t


def d_aggregate_of(w_first, d_hidden_t):
    return dot(w_first[w_first.shape[1] :], d_hidden_t).astype(BF16)


def first_products(d_hidden_t, state, aggregate):
    ones = jnp.ones((state.shape[0], ONES), BF16)
    return dot(d_hidden_t, joined_lanes([state, aggregate, ones]))


def sums_over_nodes(lefts, right):
    ones = jnp.ones((16, right.shape[1]), BF16)
    return dot_nt(jnp.concatenate([*lefts, ones], axis=0), right)


def cut_kernel(state_hbm, even_side_ref, odd_side_ref, arrived):
    side = even_side_ref.shape[0]
    odd = device_is_odd()
    last = state_hbm.shape[0] - side
    even_start = pl.multiple_of(jnp.where(odd, 0, last), side)
    odd_start = pl.multiple_of(jnp.where(odd, last, 0), side)
    copies = [
        pltpu.make_async_copy(state_hbm.at[pl.ds(start, side)], target, arrived.at[k])
        for k, (start, target) in enumerate(
            ((even_start, even_side_ref), (odd_start, odd_side_ref))
        )
    ]
    for copy in copies:
        copy.start()
    for copy in copies:
        copy.wait()


def inner_kernel(
    col_hbm,
    counts_ref,
    cot_ref,
    state_ref,
    got_even_ref,
    w_msg_ref,
    w_first_ref,
    w_second_ref,
    b_first_ref,
    b_second_ref,
    gain_ref,
    w_msg_here_ref,
    w_first_here_ref,
    w_second_here_ref,
    first_t_ref,
    second_t_ref,
    columns_ref,
    side_state_t_ref,
    side_cot_ref,
    side_sum_ref,
    side_far_ref,
    band_ref,
    updated_hbm,
    d_hidden_ref,
    first_sums_ref,
    second_sums_ref,
    msg_sums_ref,
    gain_sums_ref,
    col_ref,
    updated_ref,
    arrived,
    left,
):
    blocks, tiles, size, _ = counts_ref.shape
    features = state_ref.shape[1]
    inner_rows = range(WIN, blocks - WIN)
    low_rows, high_rows = range(WIN), range(blocks - WIN, blocks)
    odd = device_is_odd()

    def even_side(low, high):
        return jnp.where(odd, low, high)

    def odd_side(low, high):
        return jnp.where(odd, high, low)

    col_copy = pltpu.make_async_copy(col_hbm, col_ref, arrived)
    col_copy.start()

    def rows(block, count=1):
        return pl.ds(block * size, count * size)

    w_msg, w_first, w_second = w_msg_ref[...], w_first_ref[...], w_second_ref[...]
    first_t = joined_lanes([w_first[:features].T, w_first[features:].T])
    second_t = w_second.T
    columns = [column(ref) for ref in (b_first_ref, b_second_ref, gain_ref)]
    w_msg_here_ref[...] = w_msg
    w_first_here_ref[...] = w_first
    w_second_here_ref[...] = w_second
    first_t_ref[...] = first_t
    second_t_ref[...] = second_t
    for k in range(3):
        columns_ref[k] = columns[k]
    state = state_ref[...]
    state_t = [state[b * size : (b + 1) * size].T for b in range(blocks)]
    cot_t = [cot_ref[rows(b), :].T for b in range(blocks)]

    nothing = jnp.zeros((size, size), BF16)
    col_copy.wait()
    for b in range(blocks):
        for place in range(BAND):
            if place != WIN:
                band_ref[b, place] = nothing
        band_ref[b, WIN] = counts_ref[b, 0].astype(F32).astype(BF16)
        own = col_ref[0, b]
        for t in range(1, tiles):
            band_ref[b, col_ref[t, b] - own + WIN] += counts_ref[b, t].astype(F32).astype(BF16)

    wide = joined_lanes([dot(state, w_msg).astype(BF16), state])

    def neighbour_sum(b):
        first, last = max(b - WIN, 0), min(b + WIN, blocks - 1)
        tiles_of = [band_ref[b, block - b + WIN] for block in range(first, last + 1)]
        return dot(joined_lanes(tiles_of), wide[first * size : (last + 1) * size])

    def far(b, first):
        places = [block - b + WIN for block in range(first, first + WIN)]
        return joined_lanes([band_ref[b, p] if 0 <= p < BAND else nothing for p in places])

    def stacked(parts):
        return jnp.concatenate(list(parts), axis=0)

    ends = (stacked(map(neighbour_sum, low_rows)), stacked(map(neighbour_sum, high_rows)))
    fars = (stacked(far(b, -WIN) for b in low_rows), stacked(far(b, blocks) for b in high_rows))
    end_states = (state[: WIN * size], state[(blocks - WIN) * size :])
    end_states_t = (joined_lanes(state_t[:WIN]), joined_lanes(state_t[blocks - WIN :]))
    end_cots_t = (joined_lanes(cot_t[:WIN]), joined_lanes(cot_t[blocks - WIN :]))
    side_sum_ref[...] = odd_side(*ends)
    side_far_ref[...] = odd_side(*fars)
    side_state_t_ref[...] = odd_side(*end_states_t)
    side_cot_ref[...] = odd_side(*end_cots_t)

    halo = got_even_ref[...]
    wide_halo = joined_lanes([dot(halo, w_msg).astype(BF16), halo])
    end_sum = even_side(*ends) + dot(even_side(*fars), wide_halo)
    summed = stacked([*map(neighbour_sum, inner_rows), end_sum]).astype(BF16)
    aggregate, summed = summed[:, :features], summed[:, features:]
    updated_t, terms, active_t, d_norm_t, d_hidden_t = node_layer(
        joined_lanes([*state_t[WIN : blocks - WIN], even_side(*end_states_t)]),
        joined_lanes(blocks_turned(aggregate)),
        joined_lanes([*cot_t[WIN : blocks - WIN], even_side(*end_cots_t)]),
        first_t,
        second_t,
        w_second,
        columns,
    )
    updated_ref[...] = updated_t
    updated_copy = pltpu.make_async_copy(updated_ref, updated_hbm, left)
    updated_copy.start()
    d_hidden_ref[...] = d_hidden_t
    d_aggregate_t = d_aggregate_of(w_first, d_hidden_t)
    first_sums = first_products(
        d_hidden_t,
        stacked([state[WIN * size : (blocks - WIN) * size], even_side(*end_states)]),
        aggregate,
    )
    for k in range(2):
        first_sums_ref[rows(k), :] = first_sums[:, k * features : (k + 1) * features].T
    first_sums_ref[pl.ds(2 * features, 16), :] = first_sums[:, 2 * features :].T[:16]
    second_sums_ref[...] = sums_over_nodes([active_t], d_norm_t)
    msg_sums_ref[...] = dot(d_aggregate_t, summed).T
    gain_sums_ref[...] = sum(
        terms[:, k * size : (k + 1) * size] for k in range(blocks - WIN)
    )
    updated_copy.wait()


def outer_kernel(
    grad_scale,
    got_odd_ref,
    w_msg_ref,
    w_first_ref,
    w_second_ref,
    first_t_ref,
    second_t_ref,
    columns_ref,
    side_state_t_ref,
    side_cot_ref,
    side_sum_ref,
    side_far_ref,
    first_sums_ref,
    second_sums_ref,
    msg_sums_ref,
    gain_sums_ref,
    grads_ref,
    updated_hbm,
    d_hidden_ref,
    updated_ref,
    left,
):
    features, size = w_msg_ref.shape[0], columns_ref.shape[2]
    halo = got_odd_ref[...]
    wide_halo = joined_lanes([dot(halo, w_msg_ref[...]).astype(BF16), halo])
    summed = (side_sum_ref[...] + dot(side_far_ref[...], wide_halo)).astype(BF16)
    aggregate, summed = summed[:, :features], summed[:, features:]
    state_t = side_state_t_ref[...]
    aggregate_t = joined_lanes(blocks_turned(aggregate))
    updated_t, terms, active_t, d_norm_t, d_hidden_t = node_layer(
        state_t,
        aggregate_t,
        side_cot_ref[...],
        first_t_ref[...],
        second_t_ref[...],
        w_second_ref[...],
        [columns_ref[k] for k in range(3)],
    )
    updated_ref[...] = updated_t
    updated_copy = pltpu.make_async_copy(updated_ref, updated_hbm, left)
    updated_copy.start()
    d_hidden_ref[...] = d_hidden_t
    d_aggregate_t = d_aggregate_of(w_first_ref[...], d_hidden_t)

    second_sums = second_sums_ref[...] + sums_over_nodes([active_t], d_norm_t)
    first_sums = first_sums_ref[...] + sums_over_nodes([state_t, aggregate_t], d_hidden_t)
    msg_sums = msg_sums_ref[...] + dot(d_aggregate_t, summed).T
    gain_sums = gain_sums_ref[...]
    for k in range(WIN):
        gain_sums = gain_sums + terms[:, k * size : (k + 1) * size]

    chunk = grads_ref.shape[1] - BIAS_ROWS
    sums = (
        jnp.concatenate(
            [
                first_sums[: 2 * features],
                second_sums[:features],
                msg_sums,
            ],
            axis=0,
        )
        * grad_scale
    ).astype(SENT)
    bias = (
        jnp.concatenate(
            [
                first_sums[2 * features : 2 * features + 1],
                second_sums[features : features + 1],
                jnp.sum(gain_sums.T, axis=0, keepdims=True),
            ],
            axis=0,
        )
        * grad_scale
    )
    bias_high = bias.astype(SENT)
    bias_low = (bias - bias_high.astype(F32)).astype(SENT)
    bias = jnp.concatenate(
        [bias_high, bias_low, jnp.zeros((BIAS_ROWS - 6, features), SENT)], axis=0
    )
    nothing = jnp.zeros((chunk, features), SENT)
    for k in range(grads_ref.shape[0]):
        block = sums[k * chunk : (k + 1) * chunk] if k * chunk < sums.shape[0] else nothing
        grads_ref[k] = jnp.concatenate([block, bias], axis=0)
    updated_copy.wait()


def owed_kernel(
    band_ref, w_first_ref, inner_ref, outer_ref, done_ref, ends_ref, send_even_ref, send_odd_ref
):
    blocks, _, size, _ = band_ref.shape
    odd = device_is_odd()
    w_first = w_first_ref[...]
    inner = d_aggregate_of(w_first, inner_ref[...])
    outer = d_aggregate_of(w_first, outer_ref[...])

    def d_aggregate(b):
        if WIN <= b < blocks - WIN:
            return inner[:, (b - WIN) * size : (b - WIN + 1) * size]
        k = b if b < WIN else b - blocks + WIN
        even_end = inner[:, (blocks - 2 * WIN + k) * size : (blocks - 2 * WIN + k + 1) * size]
        odd_end = outer[:, k * size : (k + 1) * size]
        return jnp.where(odd == (b < WIN), even_end, odd_end)

    def owed(block):
        near = range(max(block - WIN, 0), min(block + WIN, blocks - 1) + 1)
        tiles_of = [band_ref[b, block - b + WIN] for b in near]
        return dot(
            joined_lanes([d_aggregate(b) for b in near]), jnp.concatenate(tiles_of, axis=0)
        )

    for k in range(WIN):
        to_below = owed(k - WIN).astype(BF16)
        to_above = owed(blocks + k).astype(BF16)
        send_even_ref[k] = jnp.where(odd, to_below, to_above)
        send_odd_ref[k] = jnp.where(odd, to_above, to_below)
    for b in range(WIN, blocks - WIN):
        done_ref[b - WIN] = owed(b).astype(BF16)
    for k in range(WIN):
        ends_ref[k] = owed(k)
        ends_ref[WIN + k] = owed(blocks - WIN + k)


def sum_kernel(parts_ref, spread_ref, bias_ref):
    total = parts_ref[0].astype(F32)
    for k in range(1, parts_ref.shape[0]):
        total = total + parts_ref[k].astype(F32)
    chunk = spread_ref.shape[1]
    weights = total[:chunk].astype(spread_ref.dtype)
    for k in range(spread_ref.shape[0]):
        spread_ref[k] = weights
    bias_ref[...] = total[chunk:]


def result_kernel(
    even_ref,
    odd_ref,
    cot_hbm,
    w_msg_ref,
    w_first_ref,
    inner_updated_hbm,
    outer_updated_hbm,
    inner_d_hidden_ref,
    outer_d_hidden_ref,
    owed_ref,
    ends_ref,
    bias_ref,
    updated_ref,
    grad_state_ref,
    b_first_ref,
    b_second_ref,
    gain_ref,
    cot_ref,
    inner_updated_ref,
    outer_updated_ref,
    arrived,
):
    inner, features, size = owed_ref.shape
    blocks = inner + 2 * WIN
    copies = [
        pltpu.make_async_copy(source, target, arrived.at[k])
        for k, (source, target) in enumerate(
            (
                (cot_hbm, cot_ref),
                (inner_updated_hbm, inner_updated_ref),
                (outer_updated_hbm, outer_updated_ref),
            )
        )
    ]
    for copy in copies:
        copy.start()
    odd = device_is_odd()
    even_part, odd_part = even_ref[...].astype(F32), odd_ref[...].astype(F32)
    from_below = jnp.where(odd, even_part, odd_part)
    from_above = jnp.where(odd, odd_part, even_part)
    weights = joined_lanes([w_first_ref[pl.ds(0, features), :], w_msg_ref[...]])
    for copy in copies:
        copy.wait()
    for b in range(blocks):
        if b < WIN:
            owed = (ends_ref[b] + from_below[b]).astype(BF16)
        elif b < blocks - WIN:
            owed = owed_ref[b - WIN]
        else:
            k = b - blocks + WIN
            owed = (ends_ref[WIN + k] + from_above[k]).astype(BF16)
        if WIN <= b < blocks - WIN:
            lanes = pl.ds((b - WIN) * size, size)
            updated, d_hidden = inner_updated_ref[:, lanes], inner_d_hidden_ref[:, lanes]
        else:
            k = b if b < WIN else b - blocks + WIN
            even_end = odd == (b < WIN)
            lanes, outer_lanes = pl.ds((blocks - 2 * WIN + k) * size, size), pl.ds(k * size, size)
            updated = jnp.where(
                even_end, inner_updated_ref[:, lanes], outer_updated_ref[:, outer_lanes]
            )
            d_hidden = jnp.where(
                even_end, inner_d_hidden_ref[:, lanes], outer_d_hidden_ref[:, outer_lanes]
            )
        rows = pl.ds(b * size, size)
        change = dot(weights, jnp.concatenate([d_hidden, owed], axis=0))
        grad_state_ref[rows, :] = (cot_ref[rows, :].astype(F32) + change.T).astype(BF16)
        updated_ref[rows, :] = updated.T
    for k, ref in enumerate((b_first_ref, b_second_ref, gain_ref)):
        ref[...] = bias_ref[pl.ds(k, 1), :] + bias_ref[pl.ds(k + 3, 1), :]


def unpack_kernel(rows_ref, msg_ref, first_ref, second_ref):
    place = 0
    for ref in (first_ref, second_ref, msg_ref):
        count = ref.shape[0]
        ref[...] = rows_ref[pl.ds(place, count), :].astype(F32)
        place += count


def swapped(block, parity):
    last = lax.axis_size(AXES) - 1
    lower = range(parity, last, 2)
    return lax.ppermute(block, AXES, [(i, i + 1) for i in lower] + [(i + 1, i) for i in lower])


def call(kernel, name, outs, operands, scratch=(), limit=16, flops=0):
    specs = [pl.BlockSpec(memory_space=space) for _, space in operands]
    arrays = [kept(array, space) for array, space in operands]
    return pl.pallas_call(
        kernel,
        out_shape=tuple(outs),
        in_specs=specs,
        out_specs=tuple(
            pl.BlockSpec(memory_space=getattr(out, "memory_space", pltpu.VMEM)) for out in outs
        ),
        scratch_shapes=list(scratch),
        compiler_params=pltpu.CompilerParams(vmem_limit_bytes=limit * 1024 * 1024),
        cost_estimate=pl.CostEstimate(
            flops=flops, bytes_accessed=1_000_000, transcendentals=0
        ),
        name=name,
    )(*arrays)


def shards(
    node_state,
    w_msg,
    w_first,
    b_first,
    w_second,
    b_second,
    ln_gain,
    col_index,
    edge_counts,
    cotangent,
):
    nodes, features = node_state.shape
    blocks, tiles, size, _ = edge_counts.shape
    devices = lax.axis_size(AXES)
    grad_scale = 1.0 / math.sqrt(nodes * devices)
    chunk = -(-4 * features // (devices * 8)) * 8
    side = WIN * size
    most = nodes - side
    vmem, hbm = pltpu.VMEM, pltpu.HBM
    result = jax.ShapeDtypeStruct

    row = lambda vector: vector.reshape(1, features)
    even_side, odd_side = call(
        cut_kernel,
        "cut",
        [vmem((side, features), BF16)] * 2,
        [(node_state, hbm)],
        scratch=(pltpu.SemaphoreType.DMA((2,)),),
        flops=50_000_000_000,
    )
    got_even = swapped(even_side, 0)
    got_odd = swapped(odd_side, 1)

    inner_results = call(
            inner_kernel,
            "inner_rows",
            (
                vmem((features, features), BF16),
                vmem((2 * features, features), BF16),
                vmem((features, features), BF16),
                vmem((features, 2 * features), BF16),
                vmem((features, features), BF16),
                vmem((3, features, size), F32),
                vmem((features, side), BF16),
                vmem((features, side), BF16),
                vmem((side, 2 * features), F32),
                vmem((side, side), BF16),
                vmem((blocks, BAND, size, size), BF16),
                hbm((features, most), BF16),
                vmem((features, most), BF16),
                vmem((2 * features + 16, features), F32),
                vmem((features + 16, features), F32),
                vmem((features, features), F32),
                vmem((features, size), F32),
            ),
            [(col_index.T, hbm)]
            + [
                (array, vmem)
                for array in (
                    edge_counts,
                    cotangent,
                    node_state,
                    got_even,
                    w_msg,
                    w_first,
                    w_second,
                    row(b_first),
                    row(b_second),
                    row(ln_gain),
                )
            ],
        scratch=(
                pltpu.SMEM((tiles, blocks), jnp.int32),
                vmem((features, most), BF16),
                pltpu.SemaphoreType.DMA,
                pltpu.SemaphoreType.DMA,
            ),
            limit=32,
            flops=700_000_000,
    )
    for_outer, (band, inner_updated, inner_d_hidden), sums = (
        inner_results[:10],
        inner_results[10:13],
        inner_results[13:],
    )
    w_msg_here, w_first_here = inner_results[:2]

    grads, outer_updated, outer_d_hidden = call(
        functools.partial(outer_kernel, grad_scale),
        "outer_rows",
        (
            vmem((devices, chunk + BIAS_ROWS, features), SENT),
            hbm((features, side), BF16),
            vmem((features, side), BF16),
        ),
        [
            (array, vmem)
            for array in (got_odd, *for_outer, *sums)
        ],
        scratch=(vmem((features, side), BF16), pltpu.SemaphoreType.DMA),
        flops=300_000_000,
    )

    parts = lax.all_to_all(grads, AXES, 0, 0, tiled=True)
    owed, owed_ends, send_even, send_odd = call(
        owed_kernel,
        "owed",
        (
            vmem((blocks - 2 * WIN, features, size), BF16),
            vmem((2 * WIN, features, size), F32),
            vmem((WIN, features, size), BF16),
            vmem((WIN, features, size), BF16),
        ),
        [(array, vmem) for array in (band, w_first_here, inner_d_hidden, outer_d_hidden)],
        flops=200_000_000,
    )
    owed_even = swapped(send_even, 0)
    owed_odd = swapped(send_odd, 1)
    spread, bias = call(
        sum_kernel,
        "sum",
        (vmem((devices, chunk, features), SENT), vmem((BIAS_ROWS, features), F32)),
        [(parts, vmem)],
        flops=10_000_000_000,
    )
    updated, grad_state, g_b_first, g_b_second, g_gain = call(
        result_kernel,
        "results",
        (
            result((nodes, features), BF16),
            result((nodes, features), BF16),
            result((1, features), F32),
            result((1, features), F32),
            result((1, features), F32),
        ),
        [(owed_even, vmem), (owed_odd, vmem), (cotangent, hbm)]
        + [(w_msg_here, vmem), (w_first_here, vmem), (inner_updated, hbm), (outer_updated, hbm)]
        + [(array, vmem) for array in (inner_d_hidden, outer_d_hidden, owed, owed_ends, bias)],
        scratch=(
            vmem((nodes, features), BF16),
            vmem((features, most), BF16),
            vmem((features, side), BF16),
            pltpu.SemaphoreType.DMA((3,)),
        ),
        flops=50_000_000_000,
    )

    whole = lax.all_to_all(spread, AXES, 0, 0, tiled=True)
    g_msg, g_first, g_second = call(
        unpack_kernel,
        "unpack",
        (
            result((features, features), F32),
            result((2 * features, features), F32),
            result((features, features), F32),
        ),
        [(whole.reshape(devices * chunk, features), vmem)],
    )
    flat = lambda vector: vector.reshape(features)
    return (
        updated,
        grad_state,
        g_msg,
        g_first,
        flat(g_b_first),
        g_second,
        flat(g_b_second),
        flat(g_gain),
    )


def solution(mesh):
    split = P(AXES, None)
    return jax.shard_map(
        shards,
        mesh=mesh,
        in_specs=(split, P(), P(), P(), P(), P(), P(), split, P(AXES, None, None, None), split),
        out_specs=(split, split, P(), P(), P(), P(), P(), P()),
        check_vma=False,
    )
```

```python
import functools
import math

import jax
import jax.numpy as jnp
from jax import lax
from jax.experimental import pallas as pl
from jax.experimental.pallas import tpu as pltpu
from jax.sharding import PartitionSpec as P

WIN = 2
BAND = 2 * WIN + 1
epsilon = 1e-05
AXES = ("dom", "feat")
BF16, F32 = jnp.bfloat16, jnp.float32
SENT = BF16
ONES = 128
BIAS_ROWS = 8

kept = pltpu.with_memory_space_constraint


def dot(left, right):
    return jnp.dot(left, right, preferred_element_type=F32)


def dot_nt(left, right):
    return lax.dot_general(left, right, (((1,), (1,)), ((), ())), preferred_element_type=F32)


def joined_lanes(parts):
    return jnp.concatenate(parts, axis=1)


def device_is_odd():
    index = lax.axis_index("dom") * lax.axis_size("feat") + lax.axis_index("feat")
    return index % 2 == 1


def column(row_ref, width):
    return jnp.broadcast_to(row_ref[...], (width, row_ref.shape[1])).T


def blocks_turned(array):
    size = array.shape[1]
    return [array[k : k + size].T for k in range(0, array.shape[0], size)]


def node_layer(state_t, aggregate_t, cot_t, first_t, second_t, w_second, columns):
    features, width = state_t.shape
    b_first, b_second, gain = (
        joined_lanes([c] * (width // c.shape[1])) for c in columns
    )
    pre_hidden = dot(first_t, jnp.concatenate([state_t, aggregate_t], axis=0)) + b_first
    sigmoid = 0.5 * jnp.tanh(0.5 * pre_hidden) + 0.5
    silu = pre_hidden * sigmoid
    active_t = silu.astype(BF16)
    slope = sigmoid + silu * (1.0 - sigmoid)
    pre_norm = dot(second_t, active_t) + b_second
    centred = pre_norm - jnp.mean(pre_norm, axis=0, keepdims=True)
    inv_std = lax.rsqrt(jnp.mean(centred * centred, axis=0, keepdims=True) + epsilon)
    normed = centred * inv_std
    updated_t = (state_t.astype(F32) + gain * normed).astype(BF16)
    cot = cot_t.astype(F32)
    terms = cot * normed
    q = cot * gain
    mean_q = jnp.mean(q, axis=0, keepdims=True)
    mean_qn = jnp.mean(q * normed, axis=0, keepdims=True)
    d_norm_t = (inv_std * (q - mean_q - normed * mean_qn)).astype(BF16)
    d_hidden_t = (dot(w_second, d_norm_t) * slope).astype(BF16)
    return updated_t, terms, active_t, d_norm_t, d_hidden_t


def d_aggregate_of(w_first, d_hidden_t):
    return dot(w_first[w_first.shape[1] :], d_hidden_t).astype(BF16)


def first_products(d_hidden_t, state, aggregate):
    ones = jnp.ones((state.shape[0], ONES), BF16)
    return dot(d_hidden_t, joined_lanes([state, aggregate, ones]))


def second_products(active_t, d_norm_t):
    ones = jnp.ones((16, active_t.shape[1]), BF16)
    return dot_nt(jnp.concatenate([active_t, ones], axis=0), d_norm_t)


def fetch_kernel(state_hbm, *refs):
    count = (len(refs) - 3) // 2
    sources, targets = refs[:count], refs[count : 2 * count]
    even_side_ref, odd_side_ref, arrived = refs[2 * count :]
    edge = even_side_ref.shape[0]
    odd = device_is_odd()
    last = state_hbm.shape[0] - edge
    even_start = pl.multiple_of(jnp.where(odd, 0, last), edge)
    odd_start = pl.multiple_of(jnp.where(odd, last, 0), edge)
    pairs = [
        (state_hbm.at[pl.ds(even_start, edge)], even_side_ref),
        (state_hbm.at[pl.ds(odd_start, edge)], odd_side_ref),
        *zip(sources, targets),
    ]
    copies = [
        pltpu.make_async_copy(source, target, arrived.at[k])
        for k, (source, target) in enumerate(pairs)
    ]
    for copy in copies:
        copy.start()
    for copy in copies:
        copy.wait()


def inner_kernel(
    col_hbm,
    counts_ref,
    cot_ref,
    state_ref,
    got_even_ref,
    w_msg_ref,
    w_first_ref,
    w_second_ref,
    b_first_ref,
    b_second_ref,
    gain_ref,
    first_t_ref,
    second_t_ref,
    columns_ref,
    side_state_ref,
    side_state_t_ref,
    side_cot_ref,
    side_sum_ref,
    side_far_ref,
    band_ref,
    updated_hbm,
    d_hidden_ref,
    first_sums_ref,
    second_sums_ref,
    msg_sums_ref,
    gain_sums_ref,
    col_ref,
    updated_ref,
    arrived,
    left,
):
    blocks, tiles, size, _ = counts_ref.shape
    features = state_ref.shape[1]
    inner_rows = range(WIN, blocks - WIN)
    low_rows, high_rows = range(WIN), range(blocks - WIN, blocks)
    odd = device_is_odd()

    def even_side(low, high):
        return jnp.where(odd, low, high)

    def odd_side(low, high):
        return jnp.where(odd, high, low)

    col_copy = pltpu.make_async_copy(col_hbm, col_ref, arrived)
    col_copy.start()

    def rows(block, count=1):
        return pl.ds(block * size, count * size)

    w_msg, w_first, w_second = w_msg_ref[...], w_first_ref[...], w_second_ref[...]
    first_t = joined_lanes([w_first[:features].T, w_first[features:].T])
    second_t = w_second.T
    columns = [column(ref, size) for ref in (b_first_ref, b_second_ref, gain_ref)]
    first_t_ref[...] = first_t
    second_t_ref[...] = second_t
    for k in range(3):
        columns_ref[k] = columns[k]
    state = state_ref[...]
    state_t = [state[b * size : (b + 1) * size].T for b in range(blocks)]
    cot_t = [cot_ref[rows(b), :].T for b in range(blocks)]

    nothing = jnp.zeros((size, size), BF16)
    col_copy.wait()
    for b in range(blocks):
        for place in range(BAND):
            if place != WIN:
                band_ref[b, place] = nothing
        band_ref[b, WIN] = counts_ref[b, 0].astype(F32).astype(BF16)
        own = col_ref[0, b]
        for t in range(1, tiles):
            band_ref[b, col_ref[t, b] - own + WIN] += counts_ref[b, t].astype(F32).astype(BF16)

    wide = joined_lanes([dot(state, w_msg).astype(BF16), state])

    def neighbour_sum(b):
        first, last = max(b - WIN, 0), min(b + WIN, blocks - 1)
        tiles_of = [band_ref[b, block - b + WIN] for block in range(first, last + 1)]
        return dot(joined_lanes(tiles_of), wide[first * size : (last + 1) * size])

    def far(b, first):
        places = [block - b + WIN for block in range(first, first + WIN)]
        return joined_lanes([band_ref[b, p] if 0 <= p < BAND else nothing for p in places])

    def stacked(parts):
        return jnp.concatenate(list(parts), axis=0)

    ends = (stacked(map(neighbour_sum, low_rows)), stacked(map(neighbour_sum, high_rows)))
    fars = (stacked(far(b, -WIN) for b in low_rows), stacked(far(b, blocks) for b in high_rows))
    end_states = (state[: WIN * size], state[(blocks - WIN) * size :])
    end_states_t = (joined_lanes(state_t[:WIN]), joined_lanes(state_t[blocks - WIN :]))
    end_cots_t = (joined_lanes(cot_t[:WIN]), joined_lanes(cot_t[blocks - WIN :]))
    side_sum_ref[...] = odd_side(*ends)
    side_far_ref[...] = odd_side(*fars)
    side_state_ref[...] = odd_side(*end_states)
    side_state_t_ref[...] = odd_side(*end_states_t)
    side_cot_ref[...] = odd_side(*end_cots_t)

    halo = got_even_ref[...]
    wide_halo = joined_lanes([dot(halo, w_msg).astype(BF16), halo])
    end_sum = even_side(*ends) + dot(even_side(*fars), wide_halo)
    summed = stacked([*map(neighbour_sum, inner_rows), end_sum]).astype(BF16)
    aggregate, summed = summed[:, :features], summed[:, features:]
    updated_t, terms, active_t, d_norm_t, d_hidden_t = node_layer(
        joined_lanes([*state_t[WIN : blocks - WIN], even_side(*end_states_t)]),
        joined_lanes(blocks_turned(aggregate)),
        joined_lanes([*cot_t[WIN : blocks - WIN], even_side(*end_cots_t)]),
        first_t,
        second_t,
        w_second,
        columns,
    )
    updated_ref[...] = updated_t
    updated_copy = pltpu.make_async_copy(updated_ref, updated_hbm, left)
    updated_copy.start()
    d_hidden_ref[...] = d_hidden_t
    d_aggregate_t = d_aggregate_of(w_first, d_hidden_t)
    first_sums_ref[...] = first_products(
        d_hidden_t,
        stacked([state[WIN * size : (blocks - WIN) * size], even_side(*end_states)]),
        aggregate,
    )
    second_sums_ref[...] = second_products(active_t, d_norm_t)
    msg_sums_ref[...] = dot(d_aggregate_t, summed)
    gain_sums_ref[...] = sum(
        terms[:, k * size : (k + 1) * size] for k in range(blocks - WIN)
    )
    updated_copy.wait()


def outer_kernel(
    grad_scale,
    got_odd_ref,
    w_msg_ref,
    w_first_ref,
    w_second_ref,
    first_t_ref,
    second_t_ref,
    columns_ref,
    side_state_ref,
    side_state_t_ref,
    side_cot_ref,
    side_sum_ref,
    side_far_ref,
    first_sums_ref,
    second_sums_ref,
    msg_sums_ref,
    gain_sums_ref,
    grads_ref,
    updated_ref,
    d_hidden_ref,
):
    features, size = w_msg_ref.shape[0], columns_ref.shape[2]
    halo = got_odd_ref[...]
    wide_halo = joined_lanes([dot(halo, w_msg_ref[...]).astype(BF16), halo])
    summed = (side_sum_ref[...] + dot(side_far_ref[...], wide_halo)).astype(BF16)
    aggregate, summed = summed[:, :features], summed[:, features:]
    updated_t, terms, active_t, d_norm_t, d_hidden_t = node_layer(
        side_state_t_ref[...],
        joined_lanes(blocks_turned(aggregate)),
        side_cot_ref[...],
        first_t_ref[...],
        second_t_ref[...],
        w_second_ref[...],
        [columns_ref[k] for k in range(3)],
    )
    updated_ref[...] = updated_t
    d_hidden_ref[...] = d_hidden_t
    d_aggregate_t = d_aggregate_of(w_first_ref[...], d_hidden_t)

    first_sums = first_sums_ref[...] + first_products(d_hidden_t, side_state_ref[...], aggregate)
    second_sums = second_sums_ref[...] + second_products(active_t, d_norm_t)
    msg_sums = msg_sums_ref[...] + dot(d_aggregate_t, summed)
    gain_sums = gain_sums_ref[...]
    for k in range(WIN):
        gain_sums = gain_sums + terms[:, k * size : (k + 1) * size]

    chunk = grads_ref.shape[1] - BIAS_ROWS
    turned = [first_sums[:, k * size : (k + 1) * size].T for k in range(3)]
    sums = (
        jnp.concatenate([turned[0], turned[1], second_sums[:features], msg_sums.T], axis=0)
        * grad_scale
    ).astype(SENT)
    bias = (
        jnp.concatenate(
            [
                turned[2][:1],
                second_sums[features : features + 1],
                jnp.sum(gain_sums.T, axis=0, keepdims=True),
            ],
            axis=0,
        )
        * grad_scale
    )
    bias_high = bias.astype(SENT)
    bias_low = (bias - bias_high.astype(F32)).astype(SENT)
    bias = jnp.concatenate(
        [bias_high, bias_low, jnp.zeros((BIAS_ROWS - 6, features), SENT)], axis=0
    )
    nothing = jnp.zeros((chunk, features), SENT)
    for k in range(grads_ref.shape[0]):
        block = sums[k * chunk : (k + 1) * chunk] if k * chunk < sums.shape[0] else nothing
        grads_ref[k] = jnp.concatenate([block, bias], axis=0)


def owed_kernel(
    band_ref, w_first_ref, inner_ref, outer_ref, done_ref, ends_ref, send_even_ref, send_odd_ref
):
    blocks, _, size, _ = band_ref.shape
    odd = device_is_odd()
    w_first = w_first_ref[...]
    inner = d_aggregate_of(w_first, inner_ref[...])
    outer = d_aggregate_of(w_first, outer_ref[...])

    def d_aggregate(b):
        if WIN <= b < blocks - WIN:
            return inner[:, (b - WIN) * size : (b - WIN + 1) * size]
        k = b if b < WIN else b - blocks + WIN
        even_end = inner[:, (blocks - 2 * WIN + k) * size : (blocks - 2 * WIN + k + 1) * size]
        odd_end = outer[:, k * size : (k + 1) * size]
        return jnp.where(odd == (b < WIN), even_end, odd_end)

    def owed(block):
        near = range(max(block - WIN, 0), min(block + WIN, blocks - 1) + 1)
        tiles_of = [band_ref[b, block - b + WIN] for b in near]
        return dot(
            joined_lanes([d_aggregate(b) for b in near]), jnp.concatenate(tiles_of, axis=0)
        )

    for k in range(WIN):
        to_below = owed(k - WIN).astype(BF16)
        to_above = owed(blocks + k).astype(BF16)
        send_even_ref[k] = jnp.where(odd, to_below, to_above)
        send_odd_ref[k] = jnp.where(odd, to_above, to_below)
    for b in range(WIN, blocks - WIN):
        done_ref[b - WIN] = owed(b).astype(BF16)
    for k in range(WIN):
        ends_ref[k] = owed(k)
        ends_ref[WIN + k] = owed(blocks - WIN + k)


def sum_kernel(parts_ref, spread_ref, bias_ref):
    total = parts_ref[0].astype(F32)
    for k in range(1, parts_ref.shape[0]):
        total = total + parts_ref[k].astype(F32)
    chunk = spread_ref.shape[1]
    weights = total[:chunk].astype(spread_ref.dtype)
    for k in range(spread_ref.shape[0]):
        spread_ref[k] = weights
    bias_ref[...] = total[chunk:]


def result_kernel(
    even_ref,
    odd_ref,
    cot_hbm,
    w_msg_ref,
    w_first_ref,
    inner_updated_hbm,
    outer_updated_ref,
    inner_d_hidden_ref,
    outer_d_hidden_ref,
    owed_ref,
    ends_ref,
    bias_ref,
    updated_ref,
    grad_state_ref,
    b_first_ref,
    b_second_ref,
    gain_ref,
    cot_ref,
    inner_updated_ref,
    arrived,
):
    inner, features, size = owed_ref.shape
    blocks = inner + 2 * WIN
    copies = [
        pltpu.make_async_copy(source, target, arrived.at[k])
        for k, (source, target) in enumerate(
            (
                (cot_hbm, cot_ref),
                (inner_updated_hbm, inner_updated_ref),
            )
        )
    ]
    for copy in copies:
        copy.start()
    odd = device_is_odd()
    even_part, odd_part = even_ref[...].astype(F32), odd_ref[...].astype(F32)
    from_below = jnp.where(odd, even_part, odd_part)
    from_above = jnp.where(odd, odd_part, even_part)
    weights = joined_lanes([w_first_ref[pl.ds(0, features), :], w_msg_ref[...]])
    for copy in copies:
        copy.wait()
    for b in range(blocks):
        if b < WIN:
            owed = (ends_ref[b] + from_below[b]).astype(BF16)
        elif b < blocks - WIN:
            owed = owed_ref[b - WIN]
        else:
            k = b - blocks + WIN
            owed = (ends_ref[WIN + k] + from_above[k]).astype(BF16)
        if WIN <= b < blocks - WIN:
            lanes = pl.ds((b - WIN) * size, size)
            updated, d_hidden = inner_updated_ref[:, lanes], inner_d_hidden_ref[:, lanes]
        else:
            k = b if b < WIN else b - blocks + WIN
            even_end = odd == (b < WIN)
            lanes, outer_lanes = pl.ds((blocks - 2 * WIN + k) * size, size), pl.ds(k * size, size)
            updated = jnp.where(
                even_end, inner_updated_ref[:, lanes], outer_updated_ref[:, outer_lanes]
            )
            d_hidden = jnp.where(
                even_end, inner_d_hidden_ref[:, lanes], outer_d_hidden_ref[:, outer_lanes]
            )
        rows = pl.ds(b * size, size)
        change = dot(weights, jnp.concatenate([d_hidden, owed], axis=0))
        grad_state_ref[rows, :] = (cot_ref[rows, :].astype(F32) + change.T).astype(BF16)
        updated_ref[rows, :] = updated.T
    for k, ref in enumerate((b_first_ref, b_second_ref, gain_ref)):
        ref[...] = bias_ref[pl.ds(k, 1), :] + bias_ref[pl.ds(k + 3, 1), :]


def unpack_kernel(rows_ref, msg_ref, first_ref, second_ref):
    place = 0
    for ref in (first_ref, second_ref, msg_ref):
        count = ref.shape[0]
        ref[...] = rows_ref[pl.ds(place, count), :].astype(F32)
        place += count


def swapped(block, parity):
    last = lax.axis_size(AXES) - 1
    lower = range(parity, last, 2)
    return lax.ppermute(block, AXES, [(i, i + 1) for i in lower] + [(i + 1, i) for i in lower])


def call(kernel, name, outs, operands, scratch=(), limit=16, flops=0):
    specs = [pl.BlockSpec(memory_space=space) for _, space in operands]
    arrays = [kept(array, space) for array, space in operands]
    return pl.pallas_call(
        kernel,
        out_shape=tuple(outs),
        in_specs=specs,
        out_specs=tuple(
            pl.BlockSpec(memory_space=getattr(out, "memory_space", pltpu.VMEM)) for out in outs
        ),
        scratch_shapes=list(scratch),
        compiler_params=pltpu.CompilerParams(vmem_limit_bytes=limit * 1024 * 1024),
        cost_estimate=pl.CostEstimate(
            flops=flops, bytes_accessed=1_000_000, transcendentals=0
        ),
        name=name,
    )(*arrays)


def shards(
    node_state,
    w_msg,
    w_first,
    b_first,
    w_second,
    b_second,
    ln_gain,
    col_index,
    edge_counts,
    cotangent,
):
    nodes, features = node_state.shape
    blocks, tiles, size, _ = edge_counts.shape
    devices = lax.axis_size(AXES)
    grad_scale = 1.0 / math.sqrt(nodes * devices)
    chunk = -(-4 * features // (devices * 8)) * 8
    side = WIN * size
    most = nodes - side
    vmem, hbm = pltpu.VMEM, pltpu.HBM
    result = jax.ShapeDtypeStruct

    row = lambda vector: vector.reshape(1, features)
    sources = (w_msg, w_first, w_second, row(b_first), row(b_second), row(ln_gain))
    *fetched, even_side, odd_side = call(
        fetch_kernel,
        "fetch",
        [vmem(array.shape, array.dtype) for array in sources]
        + [vmem((side, features), BF16)] * 2,
        [(array, hbm) for array in (node_state, *sources)],
        scratch=(pltpu.SemaphoreType.DMA((len(sources) + 2,)),),
        flops=50_000_000_000,
    )
    w_msg_here, w_first_here, w_second_here, *vectors = fetched
    got_even = swapped(even_side, 0)
    got_odd = swapped(odd_side, 1)

    inner_results = call(
            inner_kernel,
            "inner_rows",
            (
                vmem((features, 2 * features), BF16),
                vmem((features, features), BF16),
                vmem((3, features, size), F32),
                vmem((side, features), BF16),
                vmem((features, side), BF16),
                vmem((features, side), BF16),
                vmem((side, 2 * features), F32),
                vmem((side, side), BF16),
                vmem((blocks, BAND, size, size), BF16),
                hbm((features, most), BF16),
                vmem((features, most), BF16),
                vmem((features, 2 * features + ONES), F32),
                vmem((features + 16, features), F32),
                vmem((features, features), F32),
                vmem((features, size), F32),
            ),
            [(col_index.T, hbm)]
            + [
                (array, vmem)
                for array in (edge_counts, cotangent, node_state, got_even, *fetched)
            ],
            scratch=(
                pltpu.SMEM((tiles, blocks), jnp.int32),
                vmem((features, most), BF16),
                pltpu.SemaphoreType.DMA,
                pltpu.SemaphoreType.DMA,
            ),
            limit=32,
            flops=700_000_000,
    )
    band, inner_updated, inner_d_hidden = inner_results[8:11]
    outer_operands = inner_results[:8] + inner_results[11:]

    grads, outer_updated, outer_d_hidden = call(
        functools.partial(outer_kernel, grad_scale),
        "outer_rows",
        (
            vmem((devices, chunk + BIAS_ROWS, features), SENT),
            vmem((features, side), BF16),
            vmem((features, side), BF16),
        ),
        [
            (array, vmem)
            for array in (got_odd, w_msg_here, w_first_here, w_second_here, *outer_operands)
        ],
        flops=300_000_000,
    )

    parts = lax.all_to_all(grads, AXES, 0, 0, tiled=True)
    owed, owed_ends, send_even, send_odd = call(
        owed_kernel,
        "owed",
        (
            vmem((blocks - 2 * WIN, features, size), BF16),
            vmem((2 * WIN, features, size), F32),
            vmem((WIN, features, size), BF16),
            vmem((WIN, features, size), BF16),
        ),
        [(array, vmem) for array in (band, w_first_here, inner_d_hidden, outer_d_hidden)],
        flops=200_000_000,
    )
    owed_even = swapped(send_even, 0)
    owed_odd = swapped(send_odd, 1)
    spread, bias = call(
        sum_kernel,
        "sum",
        (vmem((devices, chunk, features), SENT), vmem((BIAS_ROWS, features), F32)),
        [(parts, vmem)],
        flops=10_000_000_000,
    )
    updated, grad_state, g_b_first, g_b_second, g_gain = call(
        result_kernel,
        "results",
        (
            result((nodes, features), BF16),
            result((nodes, features), BF16),
            result((1, features), F32),
            result((1, features), F32),
            result((1, features), F32),
        ),
        [(owed_even, vmem), (owed_odd, vmem), (cotangent, hbm)]
        + [(w_msg_here, vmem), (w_first_here, vmem), (inner_updated, hbm)]
        + [(array, vmem) for array in (outer_updated, inner_d_hidden, outer_d_hidden, owed, owed_ends, bias)],
        scratch=(
            vmem((nodes, features), BF16),
            vmem((features, most), BF16),
            pltpu.SemaphoreType.DMA((2,)),
        ),
        flops=50_000_000_000,
    )

    whole = lax.all_to_all(spread, AXES, 0, 0, tiled=True)
    g_msg, g_first, g_second = call(
        unpack_kernel,
        "unpack",
        (
            result((features, features), F32),
            result((2 * features, features), F32),
            result((features, features), F32),
        ),
        [(whole.reshape(devices * chunk, features), vmem)],
    )
    flat = lambda vector: vector.reshape(features)
    return (
        updated,
        grad_state,
        g_msg,
        g_first,
        flat(g_b_first),
        g_second,
        flat(g_b_second),
        flat(g_gain),
    )


def solution(mesh):
    split = P(AXES, None)
    return jax.shard_map(
        shards,
        mesh=mesh,
        in_specs=(split, P(), P(), P(), P(), P(), P(), split, P(AXES, None, None, None), split),
        out_specs=(split, split, P(), P(), P(), P(), P(), P()),
        check_vma=False,
    )
```

```python
import functools
import math

import jax
import jax.numpy as jnp
from jax import lax
from jax.experimental import pallas as pl
from jax.experimental.pallas import tpu as pltpu
from jax.sharding import PartitionSpec as P

WIN = 2
BAND = 2 * WIN + 1
epsilon = 1e-05
AXES = ("dom", "feat")
BF16, F32 = jnp.bfloat16, jnp.float32
SENT = BF16
ONES = 128
BIAS_ROWS = 8

kept = pltpu.with_memory_space_constraint


def dot(left, right):
    return jnp.dot(left, right, preferred_element_type=F32)


def dot_nt(left, right):
    return lax.dot_general(left, right, (((1,), (1,)), ((), ())), preferred_element_type=F32)


def joined_lanes(parts):
    return jnp.concatenate(parts, axis=1)


def device_is_odd():
    index = lax.axis_index("dom") * lax.axis_size("feat") + lax.axis_index("feat")
    return index % 2 == 1


def column(row_ref, width):
    return jnp.broadcast_to(row_ref[...], (width, row_ref.shape[1])).T


def blocks_turned(array):
    size = array.shape[1]
    return [array[k : k + size].T for k in range(0, array.shape[0], size)]


def node_layer(state_t, aggregate_t, cot_t, first_t, second_t, w_second, columns):
    features, width = state_t.shape
    b_first, b_second, gain = (
        joined_lanes([c] * (width // c.shape[1])) for c in columns
    )
    pre_hidden = dot(first_t, jnp.concatenate([state_t, aggregate_t], axis=0)) + b_first
    sigmoid = 0.5 * jnp.tanh(0.5 * pre_hidden) + 0.5
    silu = pre_hidden * sigmoid
    active_t = silu.astype(BF16)
    slope = sigmoid + silu * (1.0 - sigmoid)
    pre_norm = dot(second_t, active_t) + b_second
    centred = pre_norm - jnp.mean(pre_norm, axis=0, keepdims=True)
    inv_std = lax.rsqrt(jnp.mean(centred * centred, axis=0, keepdims=True) + epsilon)
    normed = centred * inv_std
    updated_t = (state_t.astype(F32) + gain * normed).astype(BF16)
    cot = cot_t.astype(F32)
    terms = cot * normed
    q = cot * gain
    mean_q = jnp.mean(q, axis=0, keepdims=True)
    mean_qn = jnp.mean(q * normed, axis=0, keepdims=True)
    d_norm_t = (inv_std * (q - mean_q - normed * mean_qn)).astype(BF16)
    d_hidden_t = (dot(w_second, d_norm_t) * slope).astype(BF16)
    return updated_t, terms, active_t, d_norm_t, d_hidden_t


def d_aggregate_of(w_first, d_hidden_t):
    return dot(w_first[w_first.shape[1] :], d_hidden_t).astype(BF16)


def first_products(d_hidden_t, state, aggregate):
    ones = jnp.ones((state.shape[0], ONES), BF16)
    return dot(d_hidden_t, joined_lanes([state, aggregate, ones]))


def second_products(active_t, d_norm_t):
    ones = jnp.ones((16, active_t.shape[1]), BF16)
    return dot_nt(jnp.concatenate([active_t, ones], axis=0), d_norm_t)


def fetch_kernel(state_hbm, *refs):
    count = (len(refs) - 3) // 2
    sources, targets = refs[:count], refs[count : 2 * count]
    even_side_ref, odd_side_ref, arrived = refs[2 * count :]
    edge = even_side_ref.shape[0]
    odd = device_is_odd()
    last = state_hbm.shape[0] - edge
    even_start = pl.multiple_of(jnp.where(odd, 0, last), edge)
    odd_start = pl.multiple_of(jnp.where(odd, last, 0), edge)
    pairs = [
        (state_hbm.at[pl.ds(even_start, edge)], even_side_ref),
        (state_hbm.at[pl.ds(odd_start, edge)], odd_side_ref),
        *zip(sources, targets),
    ]
    copies = [
        pltpu.make_async_copy(source, target, arrived.at[k])
        for k, (source, target) in enumerate(pairs)
    ]
    for copy in copies:
        copy.start()
    for copy in copies:
        copy.wait()


def inner_kernel(
    col_hbm,
    counts_ref,
    cot_ref,
    state_ref,
    w_msg_ref,
    w_first_ref,
    w_second_ref,
    b_first_ref,
    b_second_ref,
    gain_ref,
    first_t_ref,
    second_t_ref,
    columns_ref,
    edge_rows_ref,
    edge_state_ref,
    edge_cot_ref,
    edge_sum_ref,
    band_ref,
    updated_hbm,
    d_hidden_ref,
    first_sums_ref,
    second_sums_ref,
    msg_sums_ref,
    gain_sums_ref,
    col_ref,
    updated_ref,
    arrived,
    left,
):
    blocks, tiles, size, _ = counts_ref.shape
    features = state_ref.shape[1]
    edge_rows = [*range(WIN), *range(blocks - WIN, blocks)]
    inner_rows = range(WIN, blocks - WIN)
    col_copy = pltpu.make_async_copy(col_hbm, col_ref, arrived)
    col_copy.start()

    def rows(block, count=1):
        return pl.ds(block * size, count * size)

    w_msg, w_first, w_second = w_msg_ref[...], w_first_ref[...], w_second_ref[...]
    first_t = joined_lanes([w_first[:features].T, w_first[features:].T])
    second_t = w_second.T
    columns = [column(ref, size) for ref in (b_first_ref, b_second_ref, gain_ref)]
    first_t_ref[...] = first_t
    second_t_ref[...] = second_t
    for k in range(3):
        columns_ref[k] = columns[k]
    state_t = [state_ref[rows(b), :].T for b in range(blocks)]
    for k, b in enumerate(edge_rows):
        edge_rows_ref[rows(k), :] = state_ref[rows(b), :]
        edge_state_ref[:, rows(k)] = state_t[b]

    nothing = jnp.zeros((size, size), BF16)
    col_copy.wait()
    for b in range(blocks):
        for place in range(BAND):
            if place != WIN:
                band_ref[b, place] = nothing
        band_ref[b, WIN] = counts_ref[b, 0].astype(F32).astype(BF16)
        own = col_ref[0, b]
        for t in range(1, tiles):
            band_ref[b, col_ref[t, b] - own + WIN] += counts_ref[b, t].astype(F32).astype(BF16)
    for k, b in enumerate(edge_rows):
        edge_cot_ref[:, rows(k)] = cot_ref[rows(b), :].T

    state = state_ref[...]
    wide = joined_lanes([dot(state, w_msg).astype(BF16), state])

    def neighbour_sum(b):
        first, last = max(b - WIN, 0), min(b + WIN, blocks - 1)
        tiles_of = [band_ref[b, block - b + WIN] for block in range(first, last + 1)]
        return dot(joined_lanes(tiles_of), wide[first * size : (last + 1) * size])

    for k, b in enumerate(edge_rows):
        edge_sum_ref[k] = neighbour_sum(b)
    summed = jnp.concatenate([neighbour_sum(b).astype(BF16) for b in inner_rows], axis=0)
    aggregate, summed = summed[:, :features], summed[:, features:]
    inner_state_t = joined_lanes([state_t[b] for b in inner_rows])
    aggregate_t = joined_lanes(blocks_turned(aggregate))
    updated_t, terms, active_t, d_norm_t, d_hidden_t = node_layer(
        inner_state_t,
        aggregate_t,
        joined_lanes([cot_ref[rows(b), :].T for b in inner_rows]),
        first_t,
        second_t,
        w_second,
        columns,
    )
    updated_ref[...] = updated_t
    updated_copy = pltpu.make_async_copy(updated_ref, updated_hbm, left)
    updated_copy.start()
    d_hidden_ref[...] = d_hidden_t
    d_aggregate_t = d_aggregate_of(w_first, d_hidden_t)
    first_sums_ref[...] = first_products(
        d_hidden_t, state[WIN * size : (blocks - WIN) * size], aggregate
    )
    second_sums_ref[...] = second_products(active_t, d_norm_t)
    msg_sums_ref[...] = dot(d_aggregate_t, summed)
    gain_sums_ref[...] = sum(
        terms[:, k * size : (k + 1) * size] for k in range(len(inner_rows))
    )
    updated_copy.wait()


def outer_kernel(
    grad_scale,
    got_odd_ref,
    got_even_ref,
    w_msg_ref,
    w_first_ref,
    w_second_ref,
    first_t_ref,
    second_t_ref,
    columns_ref,
    edge_rows_ref,
    edge_state_ref,
    edge_cot_ref,
    edge_sum_ref,
    band_ref,
    first_sums_ref,
    second_sums_ref,
    msg_sums_ref,
    gain_sums_ref,
    grads_ref,
    updated_ref,
    d_hidden_ref,
):
    blocks, _, size, _ = band_ref.shape
    features = w_msg_ref.shape[0]
    odd = device_is_odd()
    got_even, got_odd = got_even_ref[...], got_odd_ref[...]
    below, above = jnp.where(odd, got_even, got_odd), jnp.where(odd, got_odd, got_even)

    w_msg = w_msg_ref[...]
    below, above = (
        joined_lanes([dot(halo, w_msg).astype(BF16), halo]) for halo in (below, above)
    )
    summed = []
    for k in range(WIN):
        far = joined_lanes([band_ref[k, place] for place in range(WIN - k)])
        summed.append(edge_sum_ref[k] + dot(far, below[k * size :]))
    for k in range(WIN):
        far = [band_ref[blocks - WIN + k, place] for place in range(2 * WIN - k, BAND)]
        summed.append(edge_sum_ref[WIN + k] + dot(joined_lanes(far), above[: (k + 1) * size]))
    summed = jnp.concatenate(summed, axis=0).astype(BF16)
    aggregate, summed = summed[:, :features], summed[:, features:]
    aggregate_t = joined_lanes(blocks_turned(aggregate))
    updated_t, terms, active_t, d_norm_t, d_hidden_t = node_layer(
        edge_state_ref[...],
        aggregate_t,
        edge_cot_ref[...],
        first_t_ref[...],
        second_t_ref[...],
        w_second_ref[...],
        [columns_ref[k] for k in range(3)],
    )
    updated_ref[...] = updated_t
    d_hidden_ref[...] = d_hidden_t
    d_aggregate_t = d_aggregate_of(w_first_ref[...], d_hidden_t)

    first_sums = first_sums_ref[...] + first_products(d_hidden_t, edge_rows_ref[...], aggregate)
    second_sums = second_sums_ref[...] + second_products(active_t, d_norm_t)
    msg_sums = msg_sums_ref[...] + dot(d_aggregate_t, summed)
    gain_sums = gain_sums_ref[...]
    for k in range(2 * WIN):
        gain_sums = gain_sums + terms[:, k * size : (k + 1) * size]

    chunk = grads_ref.shape[1] - BIAS_ROWS
    turned = [first_sums[:, k * size : (k + 1) * size].T for k in range(3)]
    sums = (
        jnp.concatenate([turned[0], turned[1], second_sums[:features], msg_sums.T], axis=0)
        * grad_scale
    ).astype(SENT)
    bias = (
        jnp.concatenate(
            [
                turned[2][:1],
                second_sums[features : features + 1],
                jnp.sum(gain_sums.T, axis=0, keepdims=True),
            ],
            axis=0,
        )
        * grad_scale
    )
    bias_high = bias.astype(SENT)
    bias_low = (bias - bias_high.astype(F32)).astype(SENT)
    bias = jnp.concatenate(
        [bias_high, bias_low, jnp.zeros((BIAS_ROWS - 6, features), SENT)], axis=0
    )
    nothing = jnp.zeros((chunk, features), SENT)
    for k in range(grads_ref.shape[0]):
        block = sums[k * chunk : (k + 1) * chunk] if k * chunk < sums.shape[0] else nothing
        grads_ref[k] = jnp.concatenate([block, bias], axis=0)


def owed_kernel(
    band_ref, w_first_ref, inner_ref, outer_ref, done_ref, ends_ref, send_even_ref, send_odd_ref
):
    blocks, _, size, _ = band_ref.shape
    odd = device_is_odd()
    w_first = w_first_ref[...]
    inner = d_aggregate_of(w_first, inner_ref[...])
    outer = d_aggregate_of(w_first, outer_ref[...])

    def d_aggregate(b):
        if WIN <= b < blocks - WIN:
            return inner[:, (b - WIN) * size : (b - WIN + 1) * size]
        k = b if b < WIN else b - blocks + 2 * WIN
        return outer[:, k * size : (k + 1) * size]

    def owed(block):
        near = range(max(block - WIN, 0), min(block + WIN, blocks - 1) + 1)
        tiles_of = [band_ref[b, block - b + WIN] for b in near]
        return dot(
            joined_lanes([d_aggregate(b) for b in near]), jnp.concatenate(tiles_of, axis=0)
        )

    for k in range(WIN):
        to_below = owed(k - WIN).astype(BF16)
        to_above = owed(blocks + k).astype(BF16)
        send_even_ref[k] = jnp.where(odd, to_below, to_above)
        send_odd_ref[k] = jnp.where(odd, to_above, to_below)
    for b in range(WIN, blocks - WIN):
        done_ref[b - WIN] = owed(b).astype(BF16)
    for k in range(WIN):
        ends_ref[k] = owed(k)
        ends_ref[WIN + k] = owed(blocks - WIN + k)


def sum_kernel(parts_ref, spread_ref, bias_ref):
    total = parts_ref[0].astype(F32)
    for k in range(1, parts_ref.shape[0]):
        total = total + parts_ref[k].astype(F32)
    chunk = spread_ref.shape[1]
    weights = total[:chunk].astype(spread_ref.dtype)
    for k in range(spread_ref.shape[0]):
        spread_ref[k] = weights
    bias_ref[...] = total[chunk:]


def result_kernel(
    even_ref,
    odd_ref,
    cot_hbm,
    w_msg_ref,
    w_first_ref,
    inner_updated_hbm,
    outer_updated_ref,
    inner_d_hidden_ref,
    outer_d_hidden_ref,
    owed_ref,
    ends_ref,
    bias_ref,
    updated_ref,
    grad_state_ref,
    b_first_ref,
    b_second_ref,
    gain_ref,
    cot_ref,
    inner_updated_ref,
    arrived,
):
    inner, features, size = owed_ref.shape
    blocks = inner + 2 * WIN
    copies = [
        pltpu.make_async_copy(source, target, arrived.at[k])
        for k, (source, target) in enumerate(
            (
                (cot_hbm, cot_ref),
                (inner_updated_hbm, inner_updated_ref),
            )
        )
    ]
    for copy in copies:
        copy.start()
    odd = device_is_odd()
    even_part, odd_part = even_ref[...].astype(F32), odd_ref[...].astype(F32)
    from_below = jnp.where(odd, even_part, odd_part)
    from_above = jnp.where(odd, odd_part, even_part)
    weights = joined_lanes([w_first_ref[pl.ds(0, features), :], w_msg_ref[...]])
    for copy in copies:
        copy.wait()
    for b in range(blocks):
        if b < WIN:
            owed = (ends_ref[b] + from_below[b]).astype(BF16)
        elif b < blocks - WIN:
            owed = owed_ref[b - WIN]
        else:
            k = b - blocks + WIN
            owed = (ends_ref[WIN + k] + from_above[k]).astype(BF16)
        if WIN <= b < blocks - WIN:
            k, updated, d_hidden = b - WIN, inner_updated_ref, inner_d_hidden_ref
        else:
            k = b if b < WIN else b - blocks + 2 * WIN
            updated, d_hidden = outer_updated_ref, outer_d_hidden_ref
        lanes, rows = pl.ds(k * size, size), pl.ds(b * size, size)
        change = dot(weights, jnp.concatenate([d_hidden[:, lanes], owed], axis=0))
        grad_state_ref[rows, :] = (cot_ref[rows, :].astype(F32) + change.T).astype(BF16)
        updated_ref[rows, :] = updated[:, lanes].T
    for k, ref in enumerate((b_first_ref, b_second_ref, gain_ref)):
        ref[...] = bias_ref[pl.ds(k, 1), :] + bias_ref[pl.ds(k + 3, 1), :]


def unpack_kernel(rows_ref, msg_ref, first_ref, second_ref):
    place = 0
    for ref in (first_ref, second_ref, msg_ref):
        count = ref.shape[0]
        ref[...] = rows_ref[pl.ds(place, count), :].astype(F32)
        place += count


def swapped(block, parity):
    last = lax.axis_size(AXES) - 1
    lower = range(parity, last, 2)
    return lax.ppermute(block, AXES, [(i, i + 1) for i in lower] + [(i + 1, i) for i in lower])


def call(kernel, name, outs, operands, scratch=(), limit=16, flops=0):
    specs = [pl.BlockSpec(memory_space=space) for _, space in operands]
    arrays = [kept(array, space) for array, space in operands]
    return pl.pallas_call(
        kernel,
        out_shape=tuple(outs),
        in_specs=specs,
        out_specs=tuple(
            pl.BlockSpec(memory_space=getattr(out, "memory_space", pltpu.VMEM)) for out in outs
        ),
        scratch_shapes=list(scratch),
        compiler_params=pltpu.CompilerParams(vmem_limit_bytes=limit * 1024 * 1024),
        cost_estimate=pl.CostEstimate(
            flops=flops, bytes_accessed=1_000_000, transcendentals=0
        ),
        name=name,
    )(*arrays)


def shards(
    node_state,
    w_msg,
    w_first,
    b_first,
    w_second,
    b_second,
    ln_gain,
    col_index,
    edge_counts,
    cotangent,
):
    nodes, features = node_state.shape
    blocks, tiles, size, _ = edge_counts.shape
    devices = lax.axis_size(AXES)
    grad_scale = 1.0 / math.sqrt(nodes * devices)
    chunk = -(-4 * features // (devices * 8)) * 8
    inner = blocks - 2 * WIN
    edge = 2 * WIN
    vmem, hbm = pltpu.VMEM, pltpu.HBM
    result = jax.ShapeDtypeStruct

    row = lambda vector: vector.reshape(1, features)
    side = WIN * size
    sources = (w_msg, w_first, w_second, row(b_first), row(b_second), row(ln_gain))
    *fetched, even_side, odd_side = call(
        fetch_kernel,
        "fetch",
        [vmem(array.shape, array.dtype) for array in sources]
        + [vmem((side, features), BF16)] * 2,
        [(array, hbm) for array in (node_state, *sources)],
        scratch=(pltpu.SemaphoreType.DMA((len(sources) + 2,)),),
        flops=50_000_000_000,
    )
    w_msg_here, w_first_here, w_second_here, *vectors = fetched
    got_odd = swapped(odd_side, 1)
    got_even = swapped(even_side, 0)

    (
        first_t,
        second_t,
        columns,
        edge_rows,
        edge_state,
        edge_cot,
        edge_sum,
        band,
        inner_updated,
        inner_d_hidden,
        first_sums,
        second_sums,
        msg_sums,
        gain_sums,
    ) = call(
        inner_kernel,
        "inner_rows",
        (
            vmem((features, 2 * features), BF16),
            vmem((features, features), BF16),
            vmem((3, features, size), F32),
            vmem((edge * size, features), BF16),
            vmem((features, edge * size), BF16),
            vmem((features, edge * size), BF16),
            vmem((edge, size, 2 * features), F32),
            vmem((blocks, BAND, size, size), BF16),
            hbm((features, inner * size), BF16),
            vmem((features, inner * size), BF16),
            vmem((features, 2 * features + ONES), F32),
            vmem((features + 16, features), F32),
            vmem((features, features), F32),
            vmem((features, size), F32),
        ),
        [(col_index.T, hbm), (edge_counts, vmem), (cotangent, vmem)]
        + [
            (array, vmem)
            for array in (node_state, w_msg_here, w_first_here, w_second_here, *vectors)
        ],
        scratch=(
            pltpu.SMEM((tiles, blocks), jnp.int32),
            vmem((features, inner * size), BF16),
            pltpu.SemaphoreType.DMA,
            pltpu.SemaphoreType.DMA,
        ),
        limit=32,
        flops=700_000_000,
    )

    grads, outer_updated, outer_d_hidden = call(
        functools.partial(outer_kernel, grad_scale),
        "outer_rows",
        (
            vmem((devices, chunk + BIAS_ROWS, features), SENT),
            vmem((features, edge * size), BF16),
            vmem((features, edge * size), BF16),
        ),
        [
            (array, vmem)
            for array in (
                got_odd,
                got_even,
                w_msg_here,
                w_first_here,
                w_second_here,
                first_t,
                second_t,
                columns,
                edge_rows,
                edge_state,
                edge_cot,
                edge_sum,
                band,
                first_sums,
                second_sums,
                msg_sums,
                gain_sums,
            )
        ],
        flops=300_000_000,
    )

    parts = lax.all_to_all(grads, AXES, 0, 0, tiled=True)
    owed, owed_ends, send_even, send_odd = call(
        owed_kernel,
        "owed",
        (
            vmem((blocks - 2 * WIN, features, size), BF16),
            vmem((2 * WIN, features, size), F32),
            vmem((WIN, features, size), BF16),
            vmem((WIN, features, size), BF16),
        ),
        [(array, vmem) for array in (band, w_first_here, inner_d_hidden, outer_d_hidden)],
        flops=200_000_000,
    )
    owed_even = swapped(send_even, 0)
    owed_odd = swapped(send_odd, 1)
    spread, bias = call(
        sum_kernel,
        "sum",
        (vmem((devices, chunk, features), SENT), vmem((BIAS_ROWS, features), F32)),
        [(parts, vmem)],
        flops=10_000_000_000,
    )
    updated, grad_state, g_b_first, g_b_second, g_gain = call(
        result_kernel,
        "results",
        (
            result((nodes, features), BF16),
            result((nodes, features), BF16),
            result((1, features), F32),
            result((1, features), F32),
            result((1, features), F32),
        ),
        [(owed_even, vmem), (owed_odd, vmem), (cotangent, hbm)]
        + [(w_msg_here, vmem), (w_first_here, vmem), (inner_updated, hbm)]
        + [(array, vmem) for array in (outer_updated, inner_d_hidden, outer_d_hidden, owed, owed_ends, bias)],
        scratch=(
            vmem((nodes, features), BF16),
            vmem((features, inner * size), BF16),
            pltpu.SemaphoreType.DMA((2,)),
        ),
        flops=50_000_000_000,
    )

    whole = lax.all_to_all(spread, AXES, 0, 0, tiled=True)
    g_msg, g_first, g_second = call(
        unpack_kernel,
        "unpack",
        (
            result((features, features), F32),
            result((2 * features, features), F32),
            result((features, features), F32),
        ),
        [(whole.reshape(devices * chunk, features), vmem)],
    )
    flat = lambda vector: vector.reshape(features)
    return (
        updated,
        grad_state,
        g_msg,
        g_first,
        flat(g_b_first),
        g_second,
        flat(g_b_second),
        flat(g_gain),
    )


def solution(mesh):
    split = P(AXES, None)
    return jax.shard_map(
        shards,
        mesh=mesh,
        in_specs=(split, P(), P(), P(), P(), P(), P(), split, P(AXES, None, None, None), split),
        out_specs=(split, split, P(), P(), P(), P(), P(), P()),
        check_vma=False,
    )
```

```python
import functools
import math

import jax
import jax.numpy as jnp
from jax import lax
from jax.experimental import pallas as pl
from jax.experimental.pallas import tpu as pltpu
from jax.sharding import PartitionSpec as P

WIN = 2
BAND = 2 * WIN + 1
epsilon = 1e-05
AXES = ("dom", "feat_hi", "feat_lo")
GATHERED = ("dom", "feat_lo")
BF16, F32 = jnp.bfloat16, jnp.float32
SENT = BF16
ONES = 128
BIAS_ROWS = 8

kept = pltpu.with_memory_space_constraint


def dot(left, right):
    return jnp.dot(left, right, preferred_element_type=F32)


def dot_nt(left, right):
    return lax.dot_general(left, right, (((1,), (1,)), ((), ())), preferred_element_type=F32)


def joined_lanes(parts):
    return jnp.concatenate(parts, axis=1)


def device_is_odd():
    index = 0
    for axis in AXES:
        index = index * lax.axis_size(axis) + lax.axis_index(axis)
    return index % 2 == 1


def column(row_ref, width):
    return jnp.broadcast_to(row_ref[...], (width, row_ref.shape[1])).T


def blocks_turned(array):
    size = array.shape[1]
    return [array[k : k + size].T for k in range(0, array.shape[0], size)]


def node_layer(state_t, aggregate_t, cot_t, first_t, second_t, w_second, columns):
    features, width = state_t.shape
    b_first, b_second, gain = (
        joined_lanes([c] * (width // c.shape[1])) for c in columns
    )
    pre_hidden = dot(first_t, jnp.concatenate([state_t, aggregate_t], axis=0)) + b_first
    sigmoid = 0.5 * jnp.tanh(0.5 * pre_hidden) + 0.5
    silu = pre_hidden * sigmoid
    active_t = silu.astype(BF16)
    slope = sigmoid + silu * (1.0 - sigmoid)
    pre_norm = dot(second_t, active_t) + b_second
    centred = pre_norm - jnp.mean(pre_norm, axis=0, keepdims=True)
    inv_std = lax.rsqrt(jnp.mean(centred * centred, axis=0, keepdims=True) + epsilon)
    normed = centred * inv_std
    updated_t = (state_t.astype(F32) + gain * normed).astype(BF16)
    cot = cot_t.astype(F32)
    terms = cot * normed
    q = cot * gain
    mean_q = jnp.mean(q, axis=0, keepdims=True)
    mean_qn = jnp.mean(q * normed, axis=0, keepdims=True)
    d_norm_t = (inv_std * (q - mean_q - normed * mean_qn)).astype(BF16)
    d_hidden_t = (dot(w_second, d_norm_t) * slope).astype(BF16)
    return updated_t, terms, active_t, d_norm_t, d_hidden_t


def d_aggregate_of(w_first, d_hidden_t):
    return dot(w_first[w_first.shape[1] :], d_hidden_t).astype(BF16)


def first_products(d_hidden_t, state, aggregate):
    ones = jnp.ones((state.shape[0], ONES), BF16)
    return dot(d_hidden_t, joined_lanes([state, aggregate, ones]))


def second_products(active_t, d_norm_t):
    ones = jnp.ones((16, active_t.shape[1]), BF16)
    return dot_nt(jnp.concatenate([active_t, ones], axis=0), d_norm_t)


def fetch_kernel(state_hbm, *refs):
    count = (len(refs) - 3) // 2
    sources, targets = refs[:count], refs[count : 2 * count]
    even_side_ref, odd_side_ref, arrived = refs[2 * count :]
    edge = even_side_ref.shape[0]
    odd = device_is_odd()
    last = state_hbm.shape[0] - edge
    even_start = pl.multiple_of(jnp.where(odd, 0, last), edge)
    odd_start = pl.multiple_of(jnp.where(odd, last, 0), edge)
    pairs = [
        (state_hbm.at[pl.ds(even_start, edge)], even_side_ref),
        (state_hbm.at[pl.ds(odd_start, edge)], odd_side_ref),
        *zip(sources, targets),
    ]
    copies = [
        pltpu.make_async_copy(source, target, arrived.at[k])
        for k, (source, target) in enumerate(pairs)
    ]
    for copy in copies:
        copy.start()
    for copy in copies:
        copy.wait()


def inner_kernel(
    col_hbm,
    counts_ref,
    cot_ref,
    state_ref,
    got_even_ref,
    w_msg_ref,
    w_first_ref,
    w_second_ref,
    b_first_ref,
    b_second_ref,
    gain_ref,
    first_t_ref,
    second_t_ref,
    columns_ref,
    side_state_ref,
    side_state_t_ref,
    side_cot_ref,
    side_sum_ref,
    side_far_ref,
    band_ref,
    updated_hbm,
    d_hidden_ref,
    first_sums_ref,
    second_sums_ref,
    msg_sums_ref,
    gain_sums_ref,
    col_ref,
    updated_ref,
    arrived,
    left,
):
    blocks, tiles, size, _ = counts_ref.shape
    features = state_ref.shape[1]
    inner_rows = range(WIN, blocks - WIN)
    low_rows, high_rows = range(WIN), range(blocks - WIN, blocks)
    odd = device_is_odd()

    def even_side(low, high):
        return jnp.where(odd, low, high)

    def odd_side(low, high):
        return jnp.where(odd, high, low)

    col_copy = pltpu.make_async_copy(col_hbm, col_ref, arrived)
    col_copy.start()

    def rows(block, count=1):
        return pl.ds(block * size, count * size)

    w_msg, w_first, w_second = w_msg_ref[...], w_first_ref[...], w_second_ref[...]
    first_t = joined_lanes([w_first[:features].T, w_first[features:].T])
    second_t = w_second.T
    columns = [column(ref, size) for ref in (b_first_ref, b_second_ref, gain_ref)]
    first_t_ref[...] = first_t
    second_t_ref[...] = second_t
    for k in range(3):
        columns_ref[k] = columns[k]
    state = state_ref[...]
    state_t = [state[b * size : (b + 1) * size].T for b in range(blocks)]
    cot_t = [cot_ref[rows(b), :].T for b in range(blocks)]

    nothing = jnp.zeros((size, size), BF16)
    col_copy.wait()
    for b in range(blocks):
        for place in range(BAND):
            if place != WIN:
                band_ref[b, place] = nothing
        band_ref[b, WIN] = counts_ref[b, 0].astype(F32).astype(BF16)
        own = col_ref[0, b]
        for t in range(1, tiles):
            band_ref[b, col_ref[t, b] - own + WIN] += counts_ref[b, t].astype(F32).astype(BF16)

    wide = joined_lanes([dot(state, w_msg).astype(BF16), state])

    def neighbour_sum(b):
        first, last = max(b - WIN, 0), min(b + WIN, blocks - 1)
        tiles_of = [band_ref[b, block - b + WIN] for block in range(first, last + 1)]
        return dot(joined_lanes(tiles_of), wide[first * size : (last + 1) * size])

    def far(b, first):
        places = [block - b + WIN for block in range(first, first + WIN)]
        return joined_lanes([band_ref[b, p] if 0 <= p < BAND else nothing for p in places])

    def stacked(parts):
        return jnp.concatenate(list(parts), axis=0)

    ends = (stacked(map(neighbour_sum, low_rows)), stacked(map(neighbour_sum, high_rows)))
    fars = (stacked(far(b, -WIN) for b in low_rows), stacked(far(b, blocks) for b in high_rows))
    end_states = (state[: WIN * size], state[(blocks - WIN) * size :])
    end_states_t = (joined_lanes(state_t[:WIN]), joined_lanes(state_t[blocks - WIN :]))
    end_cots_t = (joined_lanes(cot_t[:WIN]), joined_lanes(cot_t[blocks - WIN :]))
    side_sum_ref[...] = odd_side(*ends)
    side_far_ref[...] = odd_side(*fars)
    side_state_ref[...] = odd_side(*end_states)
    side_state_t_ref[...] = odd_side(*end_states_t)
    side_cot_ref[...] = odd_side(*end_cots_t)

    halo = got_even_ref[...]
    wide_halo = joined_lanes([dot(halo, w_msg).astype(BF16), halo])
    end_sum = even_side(*ends) + dot(even_side(*fars), wide_halo)
    summed = stacked([*map(neighbour_sum, inner_rows), end_sum]).astype(BF16)
    aggregate, summed = summed[:, :features], summed[:, features:]
    updated_t, terms, active_t, d_norm_t, d_hidden_t = node_layer(
        joined_lanes([*state_t[WIN : blocks - WIN], even_side(*end_states_t)]),
        joined_lanes(blocks_turned(aggregate)),
        joined_lanes([*cot_t[WIN : blocks - WIN], even_side(*end_cots_t)]),
        first_t,
        second_t,
        w_second,
        columns,
    )
    updated_ref[...] = updated_t
    updated_copy = pltpu.make_async_copy(updated_ref, updated_hbm, left)
    updated_copy.start()
    d_hidden_ref[...] = d_hidden_t
    d_aggregate_t = d_aggregate_of(w_first, d_hidden_t)
    first_sums_ref[...] = first_products(
        d_hidden_t,
        stacked([state[WIN * size : (blocks - WIN) * size], even_side(*end_states)]),
        aggregate,
    )
    second_sums_ref[...] = second_products(active_t, d_norm_t)
    msg_sums_ref[...] = dot(d_aggregate_t, summed)
    gain_sums_ref[...] = sum(
        terms[:, k * size : (k + 1) * size] for k in range(blocks - WIN)
    )
    updated_copy.wait()


def outer_kernel(
    grad_scale,
    copies,
    got_odd_ref,
    w_msg_ref,
    w_first_ref,
    w_second_ref,
    first_t_ref,
    second_t_ref,
    columns_ref,
    side_state_ref,
    side_state_t_ref,
    side_cot_ref,
    side_sum_ref,
    side_far_ref,
    first_sums_ref,
    second_sums_ref,
    msg_sums_ref,
    gain_sums_ref,
    grads_ref,
    updated_ref,
    d_hidden_ref,
):
    features, size = w_msg_ref.shape[0], columns_ref.shape[2]
    halo = got_odd_ref[...]
    wide_halo = joined_lanes([dot(halo, w_msg_ref[...]).astype(BF16), halo])
    summed = (side_sum_ref[...] + dot(side_far_ref[...], wide_halo)).astype(BF16)
    aggregate, summed = summed[:, :features], summed[:, features:]
    updated_t, terms, active_t, d_norm_t, d_hidden_t = node_layer(
        side_state_t_ref[...],
        joined_lanes(blocks_turned(aggregate)),
        side_cot_ref[...],
        first_t_ref[...],
        second_t_ref[...],
        w_second_ref[...],
        [columns_ref[k] for k in range(3)],
    )
    updated_ref[...] = updated_t
    d_hidden_ref[...] = d_hidden_t
    d_aggregate_t = d_aggregate_of(w_first_ref[...], d_hidden_t)

    first_sums = first_sums_ref[...] + first_products(d_hidden_t, side_state_ref[...], aggregate)
    second_sums = second_sums_ref[...] + second_products(active_t, d_norm_t)
    msg_sums = msg_sums_ref[...] + dot(d_aggregate_t, summed)
    gain_sums = gain_sums_ref[...]
    for k in range(WIN):
        gain_sums = gain_sums + terms[:, k * size : (k + 1) * size]

    chunk = grads_ref.shape[1] - BIAS_ROWS
    turned = [first_sums[:, k * size : (k + 1) * size].T for k in range(3)]
    sums = (
        jnp.concatenate([turned[0], turned[1], second_sums[:features], msg_sums.T], axis=0)
        * grad_scale
    ).astype(SENT)
    bias = (
        jnp.concatenate(
            [
                turned[2][:1],
                second_sums[features : features + 1],
                jnp.sum(gain_sums.T, axis=0, keepdims=True),
            ],
            axis=0,
        )
        * grad_scale
    )
    bias_high = bias.astype(SENT)
    bias_low = (bias - bias_high.astype(F32)).astype(SENT)
    bias = jnp.concatenate(
        [bias_high, bias_low, jnp.zeros((BIAS_ROWS - 6, features), SENT)], axis=0
    )
    nothing = jnp.zeros((chunk, features), SENT)
    low = lax.axis_size("feat_lo")
    for k in range(grads_ref.shape[0] // copies):
        block = sums[k * chunk : (k + 1) * chunk] if k * chunk < sums.shape[0] else nothing
        block = jnp.concatenate([block, bias], axis=0)
        for copy in range(copies):
            grads_ref[(k // low * copies + copy) * low + k % low] = block


def owed_kernel(
    band_ref, w_first_ref, inner_ref, outer_ref, done_ref, ends_ref, send_even_ref, send_odd_ref
):
    blocks, _, size, _ = band_ref.shape
    odd = device_is_odd()
    w_first = w_first_ref[...]
    inner = d_aggregate_of(w_first, inner_ref[...])
    outer = d_aggregate_of(w_first, outer_ref[...])

    def d_aggregate(b):
        if WIN <= b < blocks - WIN:
            return inner[:, (b - WIN) * size : (b - WIN + 1) * size]
        k = b if b < WIN else b - blocks + WIN
        even_end = inner[:, (blocks - 2 * WIN + k) * size : (blocks - 2 * WIN + k + 1) * size]
        odd_end = outer[:, k * size : (k + 1) * size]
        return jnp.where(odd == (b < WIN), even_end, odd_end)

    def owed(block):
        near = range(max(block - WIN, 0), min(block + WIN, blocks - 1) + 1)
        tiles_of = [band_ref[b, block - b + WIN] for b in near]
        return dot(
            joined_lanes([d_aggregate(b) for b in near]), jnp.concatenate(tiles_of, axis=0)
        )

    for k in range(WIN):
        to_below = owed(k - WIN).astype(BF16)
        to_above = owed(blocks + k).astype(BF16)
        send_even_ref[k] = jnp.where(odd, to_below, to_above)
        send_odd_ref[k] = jnp.where(odd, to_above, to_below)
    for b in range(WIN, blocks - WIN):
        done_ref[b - WIN] = owed(b).astype(BF16)
    for k in range(WIN):
        ends_ref[k] = owed(k)
        ends_ref[WIN + k] = owed(blocks - WIN + k)


def sum_kernel(parts_ref, spread_ref, bias_ref):
    total = parts_ref[0].astype(F32)
    for k in range(1, parts_ref.shape[0]):
        total = total + parts_ref[k].astype(F32)
    chunk = spread_ref.shape[1]
    weights = total[:chunk].astype(spread_ref.dtype)
    for k in range(spread_ref.shape[0]):
        spread_ref[k] = weights
    bias_ref[...] = total[chunk:]


def result_kernel(
    even_ref,
    odd_ref,
    cot_hbm,
    w_msg_ref,
    w_first_ref,
    inner_updated_hbm,
    outer_updated_ref,
    inner_d_hidden_ref,
    outer_d_hidden_ref,
    owed_ref,
    ends_ref,
    bias_ref,
    updated_ref,
    grad_state_ref,
    b_first_ref,
    b_second_ref,
    gain_ref,
    cot_ref,
    inner_updated_ref,
    arrived,
):
    inner, features, size = owed_ref.shape
    blocks = inner + 2 * WIN
    copies = [
        pltpu.make_async_copy(source, target, arrived.at[k])
        for k, (source, target) in enumerate(
            (
                (cot_hbm, cot_ref),
                (inner_updated_hbm, inner_updated_ref),
            )
        )
    ]
    for copy in copies:
        copy.start()
    odd = device_is_odd()
    even_part, odd_part = even_ref[...].astype(F32), odd_ref[...].astype(F32)
    from_below = jnp.where(odd, even_part, odd_part)
    from_above = jnp.where(odd, odd_part, even_part)
    weights = joined_lanes([w_first_ref[pl.ds(0, features), :], w_msg_ref[...]])
    for copy in copies:
        copy.wait()
    for b in range(blocks):
        if b < WIN:
            owed = (ends_ref[b] + from_below[b]).astype(BF16)
        elif b < blocks - WIN:
            owed = owed_ref[b - WIN]
        else:
            k = b - blocks + WIN
            owed = (ends_ref[WIN + k] + from_above[k]).astype(BF16)
        if WIN <= b < blocks - WIN:
            lanes = pl.ds((b - WIN) * size, size)
            updated, d_hidden = inner_updated_ref[:, lanes], inner_d_hidden_ref[:, lanes]
        else:
            k = b if b < WIN else b - blocks + WIN
            even_end = odd == (b < WIN)
            lanes, outer_lanes = pl.ds((blocks - 2 * WIN + k) * size, size), pl.ds(k * size, size)
            updated = jnp.where(
                even_end, inner_updated_ref[:, lanes], outer_updated_ref[:, outer_lanes]
            )
            d_hidden = jnp.where(
                even_end, inner_d_hidden_ref[:, lanes], outer_d_hidden_ref[:, outer_lanes]
            )
        rows = pl.ds(b * size, size)
        change = dot(weights, jnp.concatenate([d_hidden, owed], axis=0))
        grad_state_ref[rows, :] = (cot_ref[rows, :].astype(F32) + change.T).astype(BF16)
        updated_ref[rows, :] = updated.T
    for k, ref in enumerate((b_first_ref, b_second_ref, gain_ref)):
        ref[...] = bias_ref[pl.ds(k, 1), :] + bias_ref[pl.ds(k + 3, 1), :]


def unpack_kernel(rows_ref, msg_ref, first_ref, second_ref):
    place = 0
    for ref in (first_ref, second_ref, msg_ref):
        count = ref.shape[0]
        ref[...] = rows_ref[pl.ds(place, count), :].astype(F32)
        place += count


def swapped(block, parity):
    last = lax.axis_size(AXES) - 1
    lower = range(parity, last, 2)
    return lax.ppermute(block, AXES, [(i, i + 1) for i in lower] + [(i + 1, i) for i in lower])


def call(kernel, name, outs, operands, scratch=(), limit=16, flops=0):
    specs = [pl.BlockSpec(memory_space=space) for _, space in operands]
    arrays = [kept(array, space) for array, space in operands]
    return pl.pallas_call(
        kernel,
        out_shape=tuple(outs),
        in_specs=specs,
        out_specs=tuple(
            pl.BlockSpec(memory_space=getattr(out, "memory_space", pltpu.VMEM)) for out in outs
        ),
        scratch_shapes=list(scratch),
        compiler_params=pltpu.CompilerParams(vmem_limit_bytes=limit * 1024 * 1024),
        cost_estimate=pl.CostEstimate(
            flops=flops, bytes_accessed=1_000_000, transcendentals=0
        ),
        name=name,
    )(*arrays)


def shards(
    node_state,
    w_msg,
    w_first,
    b_first,
    w_second,
    b_second,
    ln_gain,
    col_index,
    edge_counts,
    cotangent,
):
    nodes, features = node_state.shape
    blocks, tiles, size, _ = edge_counts.shape
    devices = lax.axis_size(AXES)
    grad_scale = 1.0 / math.sqrt(nodes * devices)
    gathered = lax.axis_size(GATHERED)
    chunk = -(-4 * features // (gathered * 8)) * 8
    side = WIN * size
    most = nodes - side
    vmem, hbm = pltpu.VMEM, pltpu.HBM
    result = jax.ShapeDtypeStruct

    row = lambda vector: vector.reshape(1, features)
    sources = (w_msg, w_first, w_second, row(b_first), row(b_second), row(ln_gain))
    *fetched, even_side, odd_side = call(
        fetch_kernel,
        "fetch",
        [vmem(array.shape, array.dtype) for array in sources]
        + [vmem((side, features), BF16)] * 2,
        [(array, hbm) for array in (node_state, *sources)],
        scratch=(pltpu.SemaphoreType.DMA((len(sources) + 2,)),),
        flops=50_000_000_000,
    )
    w_msg_here, w_first_here, w_second_here, *vectors = fetched
    got_even = swapped(even_side, 0)
    got_odd = swapped(odd_side, 1)

    inner_results = call(
            inner_kernel,
            "inner_rows",
            (
                vmem((features, 2 * features), BF16),
                vmem((features, features), BF16),
                vmem((3, features, size), F32),
                vmem((side, features), BF16),
                vmem((features, side), BF16),
                vmem((features, side), BF16),
                vmem((side, 2 * features), F32),
                vmem((side, side), BF16),
                vmem((blocks, BAND, size, size), BF16),
                hbm((features, most), BF16),
                vmem((features, most), BF16),
                vmem((features, 2 * features + ONES), F32),
                vmem((features + 16, features), F32),
                vmem((features, features), F32),
                vmem((features, size), F32),
            ),
            [(col_index.T, hbm)]
            + [
                (array, vmem)
                for array in (edge_counts, cotangent, node_state, got_even, *fetched)
            ],
            scratch=(
                pltpu.SMEM((tiles, blocks), jnp.int32),
                vmem((features, most), BF16),
                pltpu.SemaphoreType.DMA,
                pltpu.SemaphoreType.DMA,
            ),
            limit=32,
            flops=700_000_000,
    )
    band, inner_updated, inner_d_hidden = inner_results[8:11]
    outer_operands = inner_results[:8] + inner_results[11:]

    grads, outer_updated, outer_d_hidden = call(
        functools.partial(outer_kernel, grad_scale, devices // gathered),
        "outer_rows",
        (
            vmem((devices, chunk + BIAS_ROWS, features), SENT),
            vmem((features, side), BF16),
            vmem((features, side), BF16),
        ),
        [
            (array, vmem)
            for array in (got_odd, w_msg_here, w_first_here, w_second_here, *outer_operands)
        ],
        flops=300_000_000,
    )

    parts = lax.all_to_all(grads, AXES, 0, 0, tiled=True)
    owed, owed_ends, send_even, send_odd = call(
        owed_kernel,
        "owed",
        (
            vmem((blocks - 2 * WIN, features, size), BF16),
            vmem((2 * WIN, features, size), F32),
            vmem((WIN, features, size), BF16),
            vmem((WIN, features, size), BF16),
        ),
        [(array, vmem) for array in (band, w_first_here, inner_d_hidden, outer_d_hidden)],
        flops=200_000_000,
    )
    owed_even = swapped(send_even, 0)
    owed_odd = swapped(send_odd, 1)
    spread, bias = call(
        sum_kernel,
        "sum",
        (vmem((gathered, chunk, features), SENT), vmem((BIAS_ROWS, features), F32)),
        [(parts, vmem)],
        flops=10_000_000_000,
    )
    updated, grad_state, g_b_first, g_b_second, g_gain = call(
        result_kernel,
        "results",
        (
            result((nodes, features), BF16),
            result((nodes, features), BF16),
            result((1, features), F32),
            result((1, features), F32),
            result((1, features), F32),
        ),
        [(owed_even, vmem), (owed_odd, vmem), (cotangent, hbm)]
        + [(w_msg_here, vmem), (w_first_here, vmem), (inner_updated, hbm)]
        + [(array, vmem) for array in (outer_updated, inner_d_hidden, outer_d_hidden, owed, owed_ends, bias)],
        scratch=(
            vmem((nodes, features), BF16),
            vmem((features, most), BF16),
            pltpu.SemaphoreType.DMA((2,)),
        ),
        flops=50_000_000_000,
    )

    whole = lax.all_to_all(spread, GATHERED, 0, 0, tiled=True)
    g_msg, g_first, g_second = call(
        unpack_kernel,
        "unpack",
        (
            result((features, features), F32),
            result((2 * features, features), F32),
            result((features, features), F32),
        ),
        [(whole.reshape(gathered * chunk, features), vmem)],
    )
    flat = lambda vector: vector.reshape(features)
    return (
        updated,
        grad_state,
        g_msg,
        g_first,
        flat(g_b_first),
        g_second,
        flat(g_b_second),
        flat(g_gain),
    )


def solution(mesh):
    dom, feat = mesh.devices.shape
    low = 2 - feat % 2
    mesh = jax.sharding.Mesh(mesh.devices.reshape(dom, feat // low, low), AXES)
    split = P(AXES, None)
    return jax.shard_map(
        shards,
        mesh=mesh,
        in_specs=(split, P(), P(), P(), P(), P(), P(), split, P(AXES, None, None, None), split),
        out_specs=(split, split, P(), P(), P(), P(), P(), P()),
        check_vma=False,
    )
```

```python
import functools
import math

import jax
import jax.numpy as jnp
from jax import lax
from jax.experimental import pallas as pl
from jax.experimental.pallas import tpu as pltpu
from jax.sharding import PartitionSpec as P

WIN = 2
BAND = 2 * WIN + 1
epsilon = 1e-05
AXES = ("dom", "feat")
BF16, F32 = jnp.bfloat16, jnp.float32
SENT = BF16
ONES = 128
SLAB = 4

kept = pltpu.with_memory_space_constraint


def dot(left, right):
    return jnp.dot(left, right, preferred_element_type=F32)


def dot_nt(left, right):
    return lax.dot_general(left, right, (((1,), (1,)), ((), ())), preferred_element_type=F32)


def joined_lanes(parts):
    return jnp.concatenate(parts, axis=1)


def device_is_odd():
    index = lax.axis_index("dom") * lax.axis_size("feat") + lax.axis_index("feat")
    return index % 2 == 1


def column(row_ref, width):
    return jnp.broadcast_to(row_ref[...], (width, row_ref.shape[1])).T


def blocks_turned(array):
    size = array.shape[1]
    return [array[k : k + size].T for k in range(0, array.shape[0], size)]


def node_layer(state_t, aggregate_t, cot_t, first_t, second_t, w_second, columns):
    features, width = state_t.shape
    b_first, b_second, gain = (
        joined_lanes([c] * (width // c.shape[1])) for c in columns
    )
    pre_hidden = dot(first_t, jnp.concatenate([state_t, aggregate_t], axis=0)) + b_first
    sigmoid = 0.5 * jnp.tanh(0.5 * pre_hidden) + 0.5
    silu = pre_hidden * sigmoid
    active_t = silu.astype(BF16)
    slope = sigmoid + silu * (1.0 - sigmoid)
    pre_norm = dot(second_t, active_t) + b_second
    centred = pre_norm - jnp.mean(pre_norm, axis=0, keepdims=True)
    inv_std = lax.rsqrt(jnp.mean(centred * centred, axis=0, keepdims=True) + epsilon)
    normed = centred * inv_std
    updated_t = (state_t.astype(F32) + gain * normed).astype(BF16)
    cot = cot_t.astype(F32)
    terms = cot * normed
    q = cot * gain
    mean_q = jnp.mean(q, axis=0, keepdims=True)
    mean_qn = jnp.mean(q * normed, axis=0, keepdims=True)
    d_norm_t = (inv_std * (q - mean_q - normed * mean_qn)).astype(BF16)
    d_hidden_t = (dot(w_second, d_norm_t) * slope).astype(BF16)
    return updated_t, terms, active_t, d_norm_t, d_hidden_t


def d_aggregate_of(w_first, d_hidden_t):
    return dot(w_first[w_first.shape[1] :], d_hidden_t).astype(BF16)


def first_products(d_hidden_t, state, aggregate):
    ones = jnp.ones((state.shape[0], ONES), BF16)
    return dot(d_hidden_t, joined_lanes([state, aggregate, ones]))


def second_products(active_t, d_norm_t):
    ones = jnp.ones((16, active_t.shape[1]), BF16)
    return dot_nt(jnp.concatenate([active_t, ones], axis=0), d_norm_t)


def fetch_kernel(state_hbm, *refs):
    count = (len(refs) - 3) // 2
    sources, targets = refs[:count], refs[count : 2 * count]
    even_side_ref, odd_side_ref, arrived = refs[2 * count :]
    edge = even_side_ref.shape[0]
    odd = device_is_odd()
    last = state_hbm.shape[0] - edge
    even_start = pl.multiple_of(jnp.where(odd, 0, last), edge)
    odd_start = pl.multiple_of(jnp.where(odd, last, 0), edge)
    pairs = [
        (state_hbm.at[pl.ds(even_start, edge)], even_side_ref),
        (state_hbm.at[pl.ds(odd_start, edge)], odd_side_ref),
        *zip(sources, targets),
    ]
    copies = [
        pltpu.make_async_copy(source, target, arrived.at[k])
        for k, (source, target) in enumerate(pairs)
    ]
    for copy in copies:
        copy.start()
    for copy in copies:
        copy.wait()


def inner_kernel(
    col_hbm,
    counts_ref,
    cot_ref,
    state_ref,
    got_even_ref,
    w_msg_ref,
    w_first_ref,
    w_second_ref,
    b_first_ref,
    b_second_ref,
    gain_ref,
    first_t_ref,
    second_t_ref,
    columns_ref,
    side_state_ref,
    side_state_t_ref,
    side_cot_ref,
    side_sum_ref,
    side_far_ref,
    band_ref,
    updated_hbm,
    d_hidden_ref,
    first_sums_ref,
    second_sums_ref,
    msg_sums_ref,
    gain_sums_ref,
    col_ref,
    updated_ref,
    arrived,
    left,
):
    blocks, tiles, size, _ = counts_ref.shape
    features = state_ref.shape[1]
    inner_rows = range(WIN, blocks - WIN)
    low_rows, high_rows = range(WIN), range(blocks - WIN, blocks)
    odd = device_is_odd()

    def even_side(low, high):
        return jnp.where(odd, low, high)

    def odd_side(low, high):
        return jnp.where(odd, high, low)

    col_copy = pltpu.make_async_copy(col_hbm, col_ref, arrived)
    col_copy.start()

    def rows(block, count=1):
        return pl.ds(block * size, count * size)

    w_msg, w_first, w_second = w_msg_ref[...], w_first_ref[...], w_second_ref[...]
    first_t = joined_lanes([w_first[:features].T, w_first[features:].T])
    second_t = w_second.T
    columns = [column(ref, size) for ref in (b_first_ref, b_second_ref, gain_ref)]
    first_t_ref[...] = first_t
    second_t_ref[...] = second_t
    for k in range(3):
        columns_ref[k] = columns[k]
    state = state_ref[...]
    state_t = [state[b * size : (b + 1) * size].T for b in range(blocks)]
    cot_t = [cot_ref[rows(b), :].T for b in range(blocks)]

    nothing = jnp.zeros((size, size), BF16)
    col_copy.wait()
    for b in range(blocks):
        for place in range(BAND):
            if place != WIN:
                band_ref[b, place] = nothing
        band_ref[b, WIN] = counts_ref[b, 0].astype(F32).astype(BF16)
        own = col_ref[0, b]
        for t in range(1, tiles):
            band_ref[b, col_ref[t, b] - own + WIN] += counts_ref[b, t].astype(F32).astype(BF16)

    wide = joined_lanes([dot(state, w_msg).astype(BF16), state])

    def neighbour_sum(b):
        first, last = max(b - WIN, 0), min(b + WIN, blocks - 1)
        tiles_of = [band_ref[b, block - b + WIN] for block in range(first, last + 1)]
        return dot(joined_lanes(tiles_of), wide[first * size : (last + 1) * size])

    def far(b, first):
        places = [block - b + WIN for block in range(first, first + WIN)]
        return joined_lanes([band_ref[b, p] if 0 <= p < BAND else nothing for p in places])

    def stacked(parts):
        return jnp.concatenate(list(parts), axis=0)

    ends = (stacked(map(neighbour_sum, low_rows)), stacked(map(neighbour_sum, high_rows)))
    fars = (stacked(far(b, -WIN) for b in low_rows), stacked(far(b, blocks) for b in high_rows))
    end_states = (state[: WIN * size], state[(blocks - WIN) * size :])
    end_states_t = (joined_lanes(state_t[:WIN]), joined_lanes(state_t[blocks - WIN :]))
    end_cots_t = (joined_lanes(cot_t[:WIN]), joined_lanes(cot_t[blocks - WIN :]))
    side_sum_ref[...] = odd_side(*ends)
    side_far_ref[...] = odd_side(*fars)
    side_state_ref[...] = odd_side(*end_states)
    side_state_t_ref[...] = odd_side(*end_states_t)
    side_cot_ref[...] = odd_side(*end_cots_t)

    halo = got_even_ref[...]
    wide_halo = joined_lanes([dot(halo, w_msg).astype(BF16), halo])
    end_sum = even_side(*ends) + dot(even_side(*fars), wide_halo)
    summed = stacked([*map(neighbour_sum, inner_rows), end_sum]).astype(BF16)
    aggregate, summed = summed[:, :features], summed[:, features:]
    updated_t, terms, active_t, d_norm_t, d_hidden_t = node_layer(
        joined_lanes([*state_t[WIN : blocks - WIN], even_side(*end_states_t)]),
        joined_lanes(blocks_turned(aggregate)),
        joined_lanes([*cot_t[WIN : blocks - WIN], even_side(*end_cots_t)]),
        first_t,
        second_t,
        w_second,
        columns,
    )
    updated_ref[...] = updated_t
    updated_copy = pltpu.make_async_copy(updated_ref, updated_hbm, left)
    updated_copy.start()
    d_hidden_ref[...] = d_hidden_t
    d_aggregate_t = d_aggregate_of(w_first, d_hidden_t)
    first_sums_ref[...] = first_products(
        d_hidden_t,
        stacked([state[WIN * size : (blocks - WIN) * size], even_side(*end_states)]),
        aggregate,
    )
    second_sums_ref[...] = second_products(active_t, d_norm_t)
    msg_sums_ref[...] = dot(d_aggregate_t, summed)
    gain_sums_ref[...] = sum(
        terms[:, k * size : (k + 1) * size] for k in range(blocks - WIN)
    )
    updated_copy.wait()


def outer_kernel(
    grad_scale,
    got_odd_ref,
    w_msg_ref,
    w_first_ref,
    w_second_ref,
    first_t_ref,
    second_t_ref,
    columns_ref,
    side_state_ref,
    side_state_t_ref,
    side_cot_ref,
    side_sum_ref,
    side_far_ref,
    first_sums_ref,
    second_sums_ref,
    msg_sums_ref,
    gain_sums_ref,
    grads_ref,
    updated_ref,
    d_hidden_ref,
):
    features, size = w_msg_ref.shape[0], columns_ref.shape[2]
    halo = got_odd_ref[...]
    wide_halo = joined_lanes([dot(halo, w_msg_ref[...]).astype(BF16), halo])
    summed = (side_sum_ref[...] + dot(side_far_ref[...], wide_halo)).astype(BF16)
    aggregate, summed = summed[:, :features], summed[:, features:]
    updated_t, terms, active_t, d_norm_t, d_hidden_t = node_layer(
        side_state_t_ref[...],
        joined_lanes(blocks_turned(aggregate)),
        side_cot_ref[...],
        first_t_ref[...],
        second_t_ref[...],
        w_second_ref[...],
        [columns_ref[k] for k in range(3)],
    )
    updated_ref[...] = updated_t
    d_hidden_ref[...] = d_hidden_t
    d_aggregate_t = d_aggregate_of(w_first_ref[...], d_hidden_t)

    first_sums = first_sums_ref[...] + first_products(d_hidden_t, side_state_ref[...], aggregate)
    second_sums = second_sums_ref[...] + second_products(active_t, d_norm_t)
    msg_sums = msg_sums_ref[...] + dot(d_aggregate_t, summed)
    gain_sums = gain_sums_ref[...]
    for k in range(WIN):
        gain_sums = gain_sums + terms[:, k * size : (k + 1) * size]

    slabs = grads_ref.shape[1] - 1
    turned = [first_sums[:, k * size : (k + 1) * size].T for k in range(3)]
    sums = (
        jnp.concatenate([turned[0], turned[1], second_sums[:features], msg_sums.T], axis=0)
        * grad_scale
    ).astype(SENT)
    bias = (
        jnp.concatenate(
            [
                turned[2][:1],
                second_sums[features : features + 1],
                jnp.sum(gain_sums.T, axis=0, keepdims=True),
            ],
            axis=0,
        )
        * grad_scale
    )
    bias = jnp.concatenate([bias, jnp.zeros((SLAB - 3, features), F32)], axis=0).astype(SENT)
    nothing = jnp.zeros((SLAB, features), SENT)
    for k in range(grads_ref.shape[0]):
        for slab in range(slabs):
            row = (k * slabs + slab) * SLAB
            grads_ref[k, slab] = sums[row : row + SLAB] if row < sums.shape[0] else nothing
        grads_ref[k, slabs] = bias


def owed_kernel(
    band_ref, w_first_ref, inner_ref, outer_ref, done_ref, ends_ref, send_even_ref, send_odd_ref
):
    blocks, _, size, _ = band_ref.shape
    odd = device_is_odd()
    w_first = w_first_ref[...]
    inner = d_aggregate_of(w_first, inner_ref[...])
    outer = d_aggregate_of(w_first, outer_ref[...])

    def d_aggregate(b):
        if WIN <= b < blocks - WIN:
            return inner[:, (b - WIN) * size : (b - WIN + 1) * size]
        k = b if b < WIN else b - blocks + WIN
        even_end = inner[:, (blocks - 2 * WIN + k) * size : (blocks - 2 * WIN + k + 1) * size]
        odd_end = outer[:, k * size : (k + 1) * size]
        return jnp.where(odd == (b < WIN), even_end, odd_end)

    def owed(block):
        near = range(max(block - WIN, 0), min(block + WIN, blocks - 1) + 1)
        tiles_of = [band_ref[b, block - b + WIN] for b in near]
        return dot(
            joined_lanes([d_aggregate(b) for b in near]), jnp.concatenate(tiles_of, axis=0)
        )

    for k in range(WIN):
        to_below = owed(k - WIN).astype(BF16)
        to_above = owed(blocks + k).astype(BF16)
        send_even_ref[k] = jnp.where(odd, to_below, to_above)
        send_odd_ref[k] = jnp.where(odd, to_above, to_below)
    for b in range(WIN, blocks - WIN):
        done_ref[b - WIN] = owed(b).astype(BF16)
    for k in range(WIN):
        ends_ref[k] = owed(k)
        ends_ref[WIN + k] = owed(blocks - WIN + k)


def sum_kernel(parts_ref, spread_ref, bias_ref):
    def total(slab):
        result = parts_ref[0, slab].astype(F32)
        for k in range(1, parts_ref.shape[0]):
            result = result + parts_ref[k, slab].astype(F32)
        return result

    slabs = parts_ref.shape[1] - 1
    weights = jnp.concatenate([total(slab) for slab in range(slabs)], axis=0)
    weights = weights.astype(spread_ref.dtype)
    for k in range(spread_ref.shape[0]):
        spread_ref[k] = weights
    bias_ref[...] = total(slabs)


def result_kernel(
    even_ref,
    odd_ref,
    cot_hbm,
    w_msg_ref,
    w_first_ref,
    inner_updated_hbm,
    outer_updated_ref,
    inner_d_hidden_ref,
    outer_d_hidden_ref,
    owed_ref,
    ends_ref,
    bias_ref,
    updated_ref,
    grad_state_ref,
    b_first_ref,
    b_second_ref,
    gain_ref,
    cot_ref,
    inner_updated_ref,
    arrived,
):
    inner, features, size = owed_ref.shape
    blocks = inner + 2 * WIN
    copies = [
        pltpu.make_async_copy(source, target, arrived.at[k])
        for k, (source, target) in enumerate(
            (
                (cot_hbm, cot_ref),
                (inner_updated_hbm, inner_updated_ref),
            )
        )
    ]
    for copy in copies:
        copy.start()
    odd = device_is_odd()
    even_part, odd_part = even_ref[...].astype(F32), odd_ref[...].astype(F32)
    from_below = jnp.where(odd, even_part, odd_part)
    from_above = jnp.where(odd, odd_part, even_part)
    weights = joined_lanes([w_first_ref[pl.ds(0, features), :], w_msg_ref[...]])
    for copy in copies:
        copy.wait()
    for b in range(blocks):
        if b < WIN:
            owed = (ends_ref[b] + from_below[b]).astype(BF16)
        elif b < blocks - WIN:
            owed = owed_ref[b - WIN]
        else:
            k = b - blocks + WIN
            owed = (ends_ref[WIN + k] + from_above[k]).astype(BF16)
        if WIN <= b < blocks - WIN:
            lanes = pl.ds((b - WIN) * size, size)
            updated, d_hidden = inner_updated_ref[:, lanes], inner_d_hidden_ref[:, lanes]
        else:
            k = b if b < WIN else b - blocks + WIN
            even_end = odd == (b < WIN)
            lanes, outer_lanes = pl.ds((blocks - 2 * WIN + k) * size, size), pl.ds(k * size, size)
            updated = jnp.where(
                even_end, inner_updated_ref[:, lanes], outer_updated_ref[:, outer_lanes]
            )
            d_hidden = jnp.where(
                even_end, inner_d_hidden_ref[:, lanes], outer_d_hidden_ref[:, outer_lanes]
            )
        rows = pl.ds(b * size, size)
        change = dot(weights, jnp.concatenate([d_hidden, owed], axis=0))
        grad_state_ref[rows, :] = (cot_ref[rows, :].astype(F32) + change.T).astype(BF16)
        updated_ref[rows, :] = updated.T
    for k, ref in enumerate((b_first_ref, b_second_ref, gain_ref)):
        ref[...] = bias_ref[pl.ds(k, 1), :]


def unpack_kernel(rows_ref, msg_ref, first_ref, second_ref):
    place = 0
    for ref in (first_ref, second_ref, msg_ref):
        count = ref.shape[0]
        ref[...] = rows_ref[pl.ds(place, count), :].astype(F32)
        place += count


def swapped(block, parity):
    last = lax.axis_size(AXES) - 1
    lower = range(parity, last, 2)
    return lax.ppermute(block, AXES, [(i, i + 1) for i in lower] + [(i + 1, i) for i in lower])


def call(kernel, name, outs, operands, scratch=(), limit=16, flops=0):
    specs = [pl.BlockSpec(memory_space=space) for _, space in operands]
    arrays = [kept(array, space) for array, space in operands]
    return pl.pallas_call(
        kernel,
        out_shape=tuple(outs),
        in_specs=specs,
        out_specs=tuple(
            pl.BlockSpec(memory_space=getattr(out, "memory_space", pltpu.VMEM)) for out in outs
        ),
        scratch_shapes=list(scratch),
        compiler_params=pltpu.CompilerParams(vmem_limit_bytes=limit * 1024 * 1024),
        cost_estimate=pl.CostEstimate(
            flops=flops, bytes_accessed=1_000_000, transcendentals=0
        ),
        name=name,
    )(*arrays)


def shards(
    node_state,
    w_msg,
    w_first,
    b_first,
    w_second,
    b_second,
    ln_gain,
    col_index,
    edge_counts,
    cotangent,
):
    nodes, features = node_state.shape
    blocks, tiles, size, _ = edge_counts.shape
    devices = lax.axis_size(AXES)
    grad_scale = 1.0 / math.sqrt(nodes * devices)
    chunk = -(-4 * features // (devices * 8)) * 8
    side = WIN * size
    most = nodes - side
    vmem, hbm = pltpu.VMEM, pltpu.HBM
    result = jax.ShapeDtypeStruct

    row = lambda vector: vector.reshape(1, features)
    sources = (w_msg, w_first, w_second, row(b_first), row(b_second), row(ln_gain))
    *fetched, even_side, odd_side = call(
        fetch_kernel,
        "fetch",
        [vmem(array.shape, array.dtype) for array in sources]
        + [vmem((side, features), BF16)] * 2,
        [(array, hbm) for array in (node_state, *sources)],
        scratch=(pltpu.SemaphoreType.DMA((len(sources) + 2,)),),
        flops=50_000_000_000,
    )
    w_msg_here, w_first_here, w_second_here, *vectors = fetched
    got_even = swapped(even_side, 0)
    got_odd = swapped(odd_side, 1)

    inner_results = call(
            inner_kernel,
            "inner_rows",
            (
                vmem((features, 2 * features), BF16),
                vmem((features, features), BF16),
                vmem((3, features, size), F32),
                vmem((side, features), BF16),
                vmem((features, side), BF16),
                vmem((features, side), BF16),
                vmem((side, 2 * features), F32),
                vmem((side, side), BF16),
                vmem((blocks, BAND, size, size), BF16),
                hbm((features, most), BF16),
                vmem((features, most), BF16),
                vmem((features, 2 * features + ONES), F32),
                vmem((features + 16, features), F32),
                vmem((features, features), F32),
                vmem((features, size), F32),
            ),
            [(col_index.T, hbm)]
            + [
                (array, vmem)
                for array in (edge_counts, cotangent, node_state, got_even, *fetched)
            ],
            scratch=(
                pltpu.SMEM((tiles, blocks), jnp.int32),
                vmem((features, most), BF16),
                pltpu.SemaphoreType.DMA,
                pltpu.SemaphoreType.DMA,
            ),
            limit=32,
            flops=700_000_000,
    )
    band, inner_updated, inner_d_hidden = inner_results[8:11]
    outer_operands = inner_results[:8] + inner_results[11:]

    grads, outer_updated, outer_d_hidden = call(
        functools.partial(outer_kernel, grad_scale),
        "outer_rows",
        (
            vmem((devices, chunk // SLAB + 1, SLAB, features), SENT),
            vmem((features, side), BF16),
            vmem((features, side), BF16),
        ),
        [
            (array, vmem)
            for array in (got_odd, w_msg_here, w_first_here, w_second_here, *outer_operands)
        ],
        flops=300_000_000,
    )

    parts = lax.all_to_all(grads, AXES, 0, 0, tiled=True)
    owed, owed_ends, send_even, send_odd = call(
        owed_kernel,
        "owed",
        (
            vmem((blocks - 2 * WIN, features, size), BF16),
            vmem((2 * WIN, features, size), F32),
            vmem((WIN, features, size), BF16),
            vmem((WIN, features, size), BF16),
        ),
        [(array, vmem) for array in (band, w_first_here, inner_d_hidden, outer_d_hidden)],
        flops=200_000_000,
    )
    owed_even = swapped(send_even, 0)
    owed_odd = swapped(send_odd, 1)
    spread, bias = call(
        sum_kernel,
        "sum",
        (vmem((devices, chunk, features), SENT), vmem((SLAB, features), F32)),
        [(parts, vmem)],
        flops=10_000_000_000,
    )
    updated, grad_state, g_b_first, g_b_second, g_gain = call(
        result_kernel,
        "results",
        (
            result((nodes, features), BF16),
            result((nodes, features), BF16),
            result((1, features), F32),
            result((1, features), F32),
            result((1, features), F32),
        ),
        [(owed_even, vmem), (owed_odd, vmem), (cotangent, hbm)]
        + [(w_msg_here, vmem), (w_first_here, vmem), (inner_updated, hbm)]
        + [(array, vmem) for array in (outer_updated, inner_d_hidden, outer_d_hidden, owed, owed_ends, bias)],
        scratch=(
            vmem((nodes, features), BF16),
            vmem((features, most), BF16),
            pltpu.SemaphoreType.DMA((2,)),
        ),
        flops=50_000_000_000,
    )

    whole = lax.all_to_all(spread, AXES, 0, 0, tiled=True)
    g_msg, g_first, g_second = call(
        unpack_kernel,
        "unpack",
        (
            result((features, features), F32),
            result((2 * features, features), F32),
            result((features, features), F32),
        ),
        [(whole.reshape(devices * chunk, features), vmem)],
    )
    flat = lambda vector: vector.reshape(features)
    return (
        updated,
        grad_state,
        g_msg,
        g_first,
        flat(g_b_first),
        g_second,
        flat(g_b_second),
        flat(g_gain),
    )


def solution(mesh):
    split = P(AXES, None)
    return jax.shard_map(
        shards,
        mesh=mesh,
        in_specs=(split, P(), P(), P(), P(), P(), P(), split, P(AXES, None, None, None), split),
        out_specs=(split, split, P(), P(), P(), P(), P(), P()),
        check_vma=False,
    )
```

```python
import functools
import math

import jax
import jax.numpy as jnp
from jax import lax
from jax.experimental import pallas as pl
from jax.experimental.pallas import tpu as pltpu
from jax.sharding import PartitionSpec as P

WIN = 2
BAND = 2 * WIN + 1
epsilon = 1e-05
AXES = ("dom", "feat")
BF16, F32 = jnp.bfloat16, jnp.float32
SENT = BF16
ONES = 128
SLAB = 4

kept = pltpu.with_memory_space_constraint


def dot(left, right):
    return jnp.dot(left, right, preferred_element_type=F32)


def dot_nt(left, right):
    return lax.dot_general(left, right, (((1,), (1,)), ((), ())), preferred_element_type=F32)


def joined_lanes(parts):
    return jnp.concatenate(parts, axis=1)


def device_is_odd():
    index = lax.axis_index("dom") * lax.axis_size("feat") + lax.axis_index("feat")
    return index % 2 == 1


def column(row_ref, width):
    return jnp.broadcast_to(row_ref[...], (width, row_ref.shape[1])).T


def blocks_turned(array):
    size = array.shape[1]
    return [array[k : k + size].T for k in range(0, array.shape[0], size)]


def widened(square, width):
    return joined_lanes([square] * (width // square.shape[1]))


def node_layer(pre_hidden, state_t, cot_t, second_t, w_second, b_second, gain):
    width = state_t.shape[1]
    b_second, gain = widened(b_second, width), widened(gain, width)
    sigmoid = 0.5 * jnp.tanh(0.5 * pre_hidden) + 0.5
    silu = pre_hidden * sigmoid
    active_t = silu.astype(BF16)
    slope = sigmoid + silu * (1.0 - sigmoid)
    pre_norm = dot(second_t, active_t) + b_second
    centred = pre_norm - jnp.mean(pre_norm, axis=0, keepdims=True)
    cot = cot_t.astype(F32)
    q = cot * gain
    mean_q = jnp.mean(q, axis=0, keepdims=True)
    mean_qc = jnp.mean(q * centred, axis=0, keepdims=True)
    inv_std = lax.rsqrt(jnp.mean(centred * centred, axis=0, keepdims=True) + epsilon)
    share = inv_std * (inv_std * mean_qc)
    d_norm_t = (inv_std * ((q - mean_q) - centred * share)).astype(BF16)
    normed = centred * inv_std
    updated_t = (state_t.astype(F32) + gain * normed).astype(BF16)
    terms = cot * normed
    d_hidden_t = (dot(w_second, d_norm_t) * slope).astype(BF16)
    return updated_t, terms, active_t, d_norm_t, d_hidden_t


def d_aggregate_of(w_first, d_hidden_t):
    return dot(w_first[w_first.shape[1] :], d_hidden_t).astype(BF16)


def first_products(d_hidden_t, state, aggregate):
    ones = jnp.ones((state.shape[0], ONES), BF16)
    return dot(d_hidden_t, joined_lanes([state, aggregate, ones]))


def second_products(active_t, d_norm_t):
    ones = jnp.ones((16, active_t.shape[1]), BF16)
    return dot_nt(jnp.concatenate([active_t, ones], axis=0), d_norm_t)


def fetch_kernel(state_hbm, *refs):
    count = (len(refs) - 3) // 2
    sources, targets = refs[:count], refs[count : 2 * count]
    even_side_ref, odd_side_ref, arrived = refs[2 * count :]
    edge = even_side_ref.shape[0]
    odd = device_is_odd()
    last = state_hbm.shape[0] - edge
    even_start = pl.multiple_of(jnp.where(odd, 0, last), edge)
    odd_start = pl.multiple_of(jnp.where(odd, last, 0), edge)
    pairs = [
        (state_hbm.at[pl.ds(even_start, edge)], even_side_ref),
        (state_hbm.at[pl.ds(odd_start, edge)], odd_side_ref),
        *zip(sources, targets),
    ]
    copies = [
        pltpu.make_async_copy(source, target, arrived.at[k])
        for k, (source, target) in enumerate(pairs)
    ]
    for copy in copies:
        copy.start()
    for copy in copies:
        copy.wait()


def inner_kernel(
    col_hbm,
    counts_ref,
    cot_ref,
    state_ref,
    got_even_ref,
    w_msg_ref,
    w_first_ref,
    w_second_ref,
    b_first_ref,
    b_second_ref,
    gain_ref,
    first_t_ref,
    second_t_ref,
    columns_ref,
    side_hidden_ref,
    side_state_ref,
    side_state_t_ref,
    side_cot_ref,
    side_sum_ref,
    side_far_ref,
    band_ref,
    updated_hbm,
    d_hidden_ref,
    first_sums_ref,
    second_sums_ref,
    msg_sums_ref,
    gain_sums_ref,
    col_ref,
    updated_ref,
    arrived,
    left,
):
    blocks, tiles, size, _ = counts_ref.shape
    features = state_ref.shape[1]
    inner_rows = range(WIN, blocks - WIN)
    low_rows, high_rows = range(WIN), range(blocks - WIN, blocks)
    odd = device_is_odd()

    def even_side(low, high):
        return jnp.where(odd, low, high)

    def odd_side(low, high):
        return jnp.where(odd, high, low)

    col_copy = pltpu.make_async_copy(col_hbm, col_ref, arrived)
    col_copy.start()

    def rows(block, count=1):
        return pl.ds(block * size, count * size)

    w_msg, w_first, w_second = w_msg_ref[...], w_first_ref[...], w_second_ref[...]
    first_t = joined_lanes([w_first[:features].T, w_first[features:].T])
    second_t = w_second.T
    b_first, b_second, gain = (
        column(ref, size) for ref in (b_first_ref, b_second_ref, gain_ref)
    )
    first_t_ref[...] = first_t
    second_t_ref[...] = second_t
    columns_ref[0] = b_second
    columns_ref[1] = gain
    state = state_ref[...]
    state_t = [state[b * size : (b + 1) * size].T for b in range(blocks)]
    cot_t = [cot_ref[rows(b), :].T for b in range(blocks)]

    nothing = jnp.zeros((size, size), BF16)
    col_copy.wait()
    for b in range(blocks):
        for place in range(BAND):
            if place != WIN:
                band_ref[b, place] = nothing
        band_ref[b, WIN] = counts_ref[b, 0].astype(F32).astype(BF16)
        own = col_ref[0, b]
        for t in range(1, tiles):
            band_ref[b, col_ref[t, b] - own + WIN] += counts_ref[b, t].astype(F32).astype(BF16)

    wide = joined_lanes([dot(state, w_msg).astype(BF16), state])

    def neighbour_sum(b):
        first, last = max(b - WIN, 0), min(b + WIN, blocks - 1)
        tiles_of = [band_ref[b, block - b + WIN] for block in range(first, last + 1)]
        return dot(joined_lanes(tiles_of), wide[first * size : (last + 1) * size])

    def far(b, first):
        places = [block - b + WIN for block in range(first, first + WIN)]
        return joined_lanes([band_ref[b, p] if 0 <= p < BAND else nothing for p in places])

    def stacked(parts):
        return jnp.concatenate(list(parts), axis=0)

    ends = (stacked(map(neighbour_sum, low_rows)), stacked(map(neighbour_sum, high_rows)))
    fars = (stacked(far(b, -WIN) for b in low_rows), stacked(far(b, blocks) for b in high_rows))
    end_states = (state[: WIN * size], state[(blocks - WIN) * size :])
    end_states_t = (joined_lanes(state_t[:WIN]), joined_lanes(state_t[blocks - WIN :]))
    end_cots_t = (joined_lanes(cot_t[:WIN]), joined_lanes(cot_t[blocks - WIN :]))
    side_sum_ref[...] = odd_side(*ends)
    side_far_ref[...] = odd_side(*fars)
    side_state_ref[...] = odd_side(*end_states)
    side_state_t = odd_side(*end_states_t)
    side_state_t_ref[...] = side_state_t
    side_hidden_ref[...] = dot(first_t[:, :features], side_state_t) + widened(
        b_first, WIN * size
    )
    side_cot_ref[...] = odd_side(*end_cots_t)

    halo = got_even_ref[...]
    wide_halo = joined_lanes([dot(halo, w_msg).astype(BF16), halo])
    end_sum = even_side(*ends) + dot(even_side(*fars), wide_halo)
    summed = stacked([*map(neighbour_sum, inner_rows), end_sum]).astype(BF16)
    aggregate, summed = summed[:, :features], summed[:, features:]
    these_states_t = joined_lanes([*state_t[WIN : blocks - WIN], even_side(*end_states_t)])
    joined_t = stacked([these_states_t, joined_lanes(blocks_turned(aggregate))])
    updated_t, terms, active_t, d_norm_t, d_hidden_t = node_layer(
        dot(first_t, joined_t) + widened(b_first, joined_t.shape[1]),
        these_states_t,
        joined_lanes([*cot_t[WIN : blocks - WIN], even_side(*end_cots_t)]),
        second_t,
        w_second,
        b_second,
        gain,
    )
    updated_ref[...] = updated_t
    updated_copy = pltpu.make_async_copy(updated_ref, updated_hbm, left)
    updated_copy.start()
    d_hidden_ref[...] = d_hidden_t
    d_aggregate_t = d_aggregate_of(w_first, d_hidden_t)
    first_sums_ref[...] = first_products(
        d_hidden_t,
        stacked([state[WIN * size : (blocks - WIN) * size], even_side(*end_states)]),
        aggregate,
    )
    second_sums_ref[...] = second_products(active_t, d_norm_t)
    msg_sums_ref[...] = dot(d_aggregate_t, summed)
    gain_sums_ref[...] = sum(
        terms[:, k * size : (k + 1) * size] for k in range(blocks - WIN)
    )
    updated_copy.wait()


def outer_kernel(
    grad_scale,
    got_odd_ref,
    w_msg_ref,
    w_first_ref,
    w_second_ref,
    first_t_ref,
    second_t_ref,
    columns_ref,
    side_hidden_ref,
    side_state_ref,
    side_state_t_ref,
    side_cot_ref,
    side_sum_ref,
    side_far_ref,
    first_sums_ref,
    second_sums_ref,
    msg_sums_ref,
    gain_sums_ref,
    grads_ref,
    updated_ref,
    d_hidden_ref,
):
    features, size = w_msg_ref.shape[0], columns_ref.shape[2]
    halo = got_odd_ref[...]
    wide_halo = joined_lanes([dot(halo, w_msg_ref[...]).astype(BF16), halo])
    summed = (side_sum_ref[...] + dot(side_far_ref[...], wide_halo)).astype(BF16)
    aggregate, summed = summed[:, :features], summed[:, features:]
    aggregate_t = joined_lanes(blocks_turned(aggregate))
    updated_t, terms, active_t, d_norm_t, d_hidden_t = node_layer(
        side_hidden_ref[...] + dot(first_t_ref[:, pl.ds(features, features)], aggregate_t),
        side_state_t_ref[...],
        side_cot_ref[...],
        second_t_ref[...],
        w_second_ref[...],
        columns_ref[0],
        columns_ref[1],
    )
    updated_ref[...] = updated_t
    d_hidden_ref[...] = d_hidden_t
    d_aggregate_t = d_aggregate_of(w_first_ref[...], d_hidden_t)

    first_sums = first_sums_ref[...] + first_products(d_hidden_t, side_state_ref[...], aggregate)
    second_sums = second_sums_ref[...] + second_products(active_t, d_norm_t)
    msg_sums = msg_sums_ref[...] + dot(d_aggregate_t, summed)
    gain_sums = gain_sums_ref[...]
    for k in range(WIN):
        gain_sums = gain_sums + terms[:, k * size : (k + 1) * size]

    slabs = grads_ref.shape[1] - 1
    turned = [first_sums[:, k * size : (k + 1) * size].T for k in range(3)]
    sums = (
        jnp.concatenate([turned[0], turned[1], second_sums[:features], msg_sums.T], axis=0)
        * grad_scale
    ).astype(SENT)
    bias = (
        jnp.concatenate(
            [
                turned[2][:1],
                second_sums[features : features + 1],
                jnp.sum(gain_sums.T, axis=0, keepdims=True),
            ],
            axis=0,
        )
        * grad_scale
    )
    bias = jnp.concatenate([bias, jnp.zeros((SLAB - 3, features), F32)], axis=0).astype(SENT)
    nothing = jnp.zeros((SLAB, features), SENT)
    for k in range(grads_ref.shape[0]):
        for slab in range(slabs):
            row = (k * slabs + slab) * SLAB
            grads_ref[k, slab] = sums[row : row + SLAB] if row < sums.shape[0] else nothing
        grads_ref[k, slabs] = bias


def owed_kernel(
    band_ref, w_first_ref, inner_ref, outer_ref, done_ref, ends_ref, send_even_ref, send_odd_ref
):
    blocks, _, size, _ = band_ref.shape
    odd = device_is_odd()
    w_first = w_first_ref[...]
    inner = d_aggregate_of(w_first, inner_ref[...])
    outer = d_aggregate_of(w_first, outer_ref[...])

    def d_aggregate(b):
        if WIN <= b < blocks - WIN:
            return inner[:, (b - WIN) * size : (b - WIN + 1) * size]
        k = b if b < WIN else b - blocks + WIN
        even_end = inner[:, (blocks - 2 * WIN + k) * size : (blocks - 2 * WIN + k + 1) * size]
        odd_end = outer[:, k * size : (k + 1) * size]
        return jnp.where(odd == (b < WIN), even_end, odd_end)

    def owed(block):
        near = range(max(block - WIN, 0), min(block + WIN, blocks - 1) + 1)
        tiles_of = [band_ref[b, block - b + WIN] for b in near]
        return dot(
            joined_lanes([d_aggregate(b) for b in near]), jnp.concatenate(tiles_of, axis=0)
        )

    for k in range(WIN):
        to_below = owed(k - WIN).astype(BF16)
        to_above = owed(blocks + k).astype(BF16)
        send_even_ref[k] = jnp.where(odd, to_below, to_above)
        send_odd_ref[k] = jnp.where(odd, to_above, to_below)
    for b in range(WIN, blocks - WIN):
        done_ref[b - WIN] = owed(b).astype(BF16)
    for k in range(WIN):
        ends_ref[k] = owed(k)
        ends_ref[WIN + k] = owed(blocks - WIN + k)


def sum_kernel(parts_ref, spread_ref, bias_ref):
    def total(slab):
        result = parts_ref[0, slab].astype(F32)
        for k in range(1, parts_ref.shape[0]):
            result = result + parts_ref[k, slab].astype(F32)
        return result

    slabs = parts_ref.shape[1] - 1
    weights = jnp.concatenate([total(slab) for slab in range(slabs)], axis=0)
    weights = weights.astype(spread_ref.dtype)
    for k in range(spread_ref.shape[0]):
        spread_ref[k] = weights
    bias_ref[...] = total(slabs)


def result_kernel(
    even_ref,
    odd_ref,
    cot_hbm,
    w_msg_ref,
    w_first_ref,
    inner_updated_hbm,
    outer_updated_ref,
    inner_d_hidden_ref,
    outer_d_hidden_ref,
    owed_ref,
    ends_ref,
    bias_ref,
    updated_ref,
    grad_state_ref,
    b_first_ref,
    b_second_ref,
    gain_ref,
    cot_ref,
    inner_updated_ref,
    arrived,
):
    inner, features, size = owed_ref.shape
    blocks = inner + 2 * WIN
    copies = [
        pltpu.make_async_copy(source, target, arrived.at[k])
        for k, (source, target) in enumerate(
            (
                (cot_hbm, cot_ref),
                (inner_updated_hbm, inner_updated_ref),
            )
        )
    ]
    for copy in copies:
        copy.start()
    odd = device_is_odd()
    even_part, odd_part = even_ref[...].astype(F32), odd_ref[...].astype(F32)
    from_below = jnp.where(odd, even_part, odd_part)
    from_above = jnp.where(odd, odd_part, even_part)
    weights = joined_lanes([w_first_ref[pl.ds(0, features), :], w_msg_ref[...]])
    for copy in copies:
        copy.wait()
    for b in range(blocks):
        if b < WIN:
            owed = (ends_ref[b] + from_below[b]).astype(BF16)
        elif b < blocks - WIN:
            owed = owed_ref[b - WIN]
        else:
            k = b - blocks + WIN
            owed = (ends_ref[WIN + k] + from_above[k]).astype(BF16)
        if WIN <= b < blocks - WIN:
            lanes = pl.ds((b - WIN) * size, size)
            updated, d_hidden = inner_updated_ref[:, lanes], inner_d_hidden_ref[:, lanes]
        else:
            k = b if b < WIN else b - blocks + WIN
            even_end = odd == (b < WIN)
            lanes, outer_lanes = pl.ds((blocks - 2 * WIN + k) * size, size), pl.ds(k * size, size)
            updated = jnp.where(
                even_end, inner_updated_ref[:, lanes], outer_updated_ref[:, outer_lanes]
            )
            d_hidden = jnp.where(
                even_end, inner_d_hidden_ref[:, lanes], outer_d_hidden_ref[:, outer_lanes]
            )
        rows = pl.ds(b * size, size)
        change = dot(weights, jnp.concatenate([d_hidden, owed], axis=0))
        grad_state_ref[rows, :] = (cot_ref[rows, :].astype(F32) + change.T).astype(BF16)
        updated_ref[rows, :] = updated.T
    for k, ref in enumerate((b_first_ref, b_second_ref, gain_ref)):
        ref[...] = bias_ref[pl.ds(k, 1), :]


def unpack_kernel(rows_ref, msg_ref, first_ref, second_ref):
    place = 0
    for ref in (first_ref, second_ref, msg_ref):
        count = ref.shape[0]
        ref[...] = rows_ref[pl.ds(place, count), :].astype(F32)
        place += count


def swapped(block, parity):
    last = lax.axis_size(AXES) - 1
    lower = range(parity, last, 2)
    return lax.ppermute(block, AXES, [(i, i + 1) for i in lower] + [(i + 1, i) for i in lower])


def call(kernel, name, outs, operands, scratch=(), limit=16, flops=0):
    specs = [pl.BlockSpec(memory_space=space) for _, space in operands]
    arrays = [kept(array, space) for array, space in operands]
    return pl.pallas_call(
        kernel,
        out_shape=tuple(outs),
        in_specs=specs,
        out_specs=tuple(
            pl.BlockSpec(memory_space=getattr(out, "memory_space", pltpu.VMEM)) for out in outs
        ),
        scratch_shapes=list(scratch),
        compiler_params=pltpu.CompilerParams(vmem_limit_bytes=limit * 1024 * 1024),
        cost_estimate=pl.CostEstimate(
            flops=flops, bytes_accessed=1_000_000, transcendentals=0
        ),
        name=name,
    )(*arrays)


def shards(
    node_state,
    w_msg,
    w_first,
    b_first,
    w_second,
    b_second,
    ln_gain,
    col_index,
    edge_counts,
    cotangent,
):
    nodes, features = node_state.shape
    blocks, tiles, size, _ = edge_counts.shape
    devices = lax.axis_size(AXES)
    grad_scale = 1.0 / math.sqrt(nodes * devices)
    chunk = -(-4 * features // (devices * 8)) * 8
    side = WIN * size
    most = nodes - side
    vmem, hbm = pltpu.VMEM, pltpu.HBM
    result = jax.ShapeDtypeStruct

    row = lambda vector: vector.reshape(1, features)
    sources = (w_msg, w_first, w_second, row(b_first), row(b_second), row(ln_gain))
    *fetched, even_side, odd_side = call(
        fetch_kernel,
        "fetch",
        [vmem(array.shape, array.dtype) for array in sources]
        + [vmem((side, features), BF16)] * 2,
        [(array, hbm) for array in (node_state, *sources)],
        scratch=(pltpu.SemaphoreType.DMA((len(sources) + 2,)),),
        flops=50_000_000_000,
    )
    w_msg_here, w_first_here, w_second_here, *vectors = fetched
    got_even = swapped(even_side, 0)
    got_odd = swapped(odd_side, 1)

    inner_results = call(
            inner_kernel,
            "inner_rows",
            (
                vmem((features, 2 * features), BF16),
                vmem((features, features), BF16),
                vmem((2, features, size), F32),
                vmem((features, side), F32),
                vmem((side, features), BF16),
                vmem((features, side), BF16),
                vmem((features, side), BF16),
                vmem((side, 2 * features), F32),
                vmem((side, side), BF16),
                vmem((blocks, BAND, size, size), BF16),
                hbm((features, most), BF16),
                vmem((features, most), BF16),
                vmem((features, 2 * features + ONES), F32),
                vmem((features + 16, features), F32),
                vmem((features, features), F32),
                vmem((features, size), F32),
            ),
            [(col_index.T, hbm)]
            + [
                (array, vmem)
                for array in (edge_counts, cotangent, node_state, got_even, *fetched)
            ],
            scratch=(
                pltpu.SMEM((tiles, blocks), jnp.int32),
                vmem((features, most), BF16),
                pltpu.SemaphoreType.DMA,
                pltpu.SemaphoreType.DMA,
            ),
            limit=32,
            flops=700_000_000,
    )
    band, inner_updated, inner_d_hidden = inner_results[9:12]
    outer_operands = inner_results[:9] + inner_results[12:]

    grads, outer_updated, outer_d_hidden = call(
        functools.partial(outer_kernel, grad_scale),
        "outer_rows",
        (
            vmem((devices, chunk // SLAB + 1, SLAB, features), SENT),
            vmem((features, side), BF16),
            vmem((features, side), BF16),
        ),
        [
            (array, vmem)
            for array in (got_odd, w_msg_here, w_first_here, w_second_here, *outer_operands)
        ],
        flops=300_000_000,
    )

    parts = lax.all_to_all(grads, AXES, 0, 0, tiled=True)
    owed, owed_ends, send_even, send_odd = call(
        owed_kernel,
        "owed",
        (
            vmem((blocks - 2 * WIN, features, size), BF16),
            vmem((2 * WIN, features, size), F32),
            vmem((WIN, features, size), BF16),
            vmem((WIN, features, size), BF16),
        ),
        [(array, vmem) for array in (band, w_first_here, inner_d_hidden, outer_d_hidden)],
        flops=200_000_000,
    )
    owed_even = swapped(send_even, 0)
    owed_odd = swapped(send_odd, 1)
    spread, bias = call(
        sum_kernel,
        "sum",
        (vmem((devices, chunk, features), SENT), vmem((SLAB, features), F32)),
        [(parts, vmem)],
        flops=10_000_000_000,
    )
    updated, grad_state, g_b_first, g_b_second, g_gain = call(
        result_kernel,
        "results",
        (
            result((nodes, features), BF16),
            result((nodes, features), BF16),
            result((1, features), F32),
            result((1, features), F32),
            result((1, features), F32),
        ),
        [(owed_even, vmem), (owed_odd, vmem), (cotangent, hbm)]
        + [(w_msg_here, vmem), (w_first_here, vmem), (inner_updated, hbm)]
        + [(array, vmem) for array in (outer_updated, inner_d_hidden, outer_d_hidden, owed, owed_ends, bias)],
        scratch=(
            vmem((nodes, features), BF16),
            vmem((features, most), BF16),
            pltpu.SemaphoreType.DMA((2,)),
        ),
        flops=50_000_000_000,
    )

    whole = lax.all_to_all(spread, AXES, 0, 0, tiled=True)
    g_msg, g_first, g_second = call(
        unpack_kernel,
        "unpack",
        (
            result((features, features), F32),
            result((2 * features, features), F32),
            result((features, features), F32),
        ),
        [(whole.reshape(devices * chunk, features), vmem)],
    )
    flat = lambda vector: vector.reshape(features)
    return (
        updated,
        grad_state,
        g_msg,
        g_first,
        flat(g_b_first),
        g_second,
        flat(g_b_second),
        flat(g_gain),
    )


def solution(mesh):
    split = P(AXES, None)
    return jax.shard_map(
        shards,
        mesh=mesh,
        in_specs=(split, P(), P(), P(), P(), P(), P(), split, P(AXES, None, None, None), split),
        out_specs=(split, split, P(), P(), P(), P(), P(), P()),
        check_vma=False,
    )
```

```python
import functools
import math

import jax
import jax.numpy as jnp
from jax import lax
from jax.experimental import pallas as pl
from jax.experimental.pallas import tpu as pltpu
from jax.sharding import PartitionSpec as P

WIN = 2
BAND = 2 * WIN + 1
epsilon = 1e-05
AXES = ("dom", "feat")
PARTNERS = ("feat", "dom")
BF16, F32 = jnp.bfloat16, jnp.float32
SENT = BF16
ONES = 128
SLAB = 4

kept = pltpu.with_memory_space_constraint


def dot(left, right):
    return jnp.dot(left, right, preferred_element_type=F32)


def dot_nt(left, right):
    return lax.dot_general(left, right, (((1,), (1,)), ((), ())), preferred_element_type=F32)


def joined_lanes(parts):
    return jnp.concatenate(parts, axis=1)


def device_is_odd():
    index = lax.axis_index("dom") * lax.axis_size("feat") + lax.axis_index("feat")
    return index % 2 == 1


def column(row_ref, width):
    return jnp.broadcast_to(row_ref[...], (width, row_ref.shape[1])).T


def blocks_turned(array):
    size = array.shape[1]
    return [array[k : k + size].T for k in range(0, array.shape[0], size)]


def node_layer(state_t, aggregate_t, cot_t, first_t, second_t, w_second, columns):
    features, width = state_t.shape
    b_first, b_second, gain = (
        joined_lanes([c] * (width // c.shape[1])) for c in columns
    )
    pre_hidden = dot(first_t, jnp.concatenate([state_t, aggregate_t], axis=0)) + b_first
    sigmoid = 0.5 * jnp.tanh(0.5 * pre_hidden) + 0.5
    silu = pre_hidden * sigmoid
    active_t = silu.astype(BF16)
    slope = sigmoid + silu * (1.0 - sigmoid)
    pre_norm = dot(second_t, active_t) + b_second
    centred = pre_norm - jnp.mean(pre_norm, axis=0, keepdims=True)
    inv_std = lax.rsqrt(jnp.mean(centred * centred, axis=0, keepdims=True) + epsilon)
    normed = centred * inv_std
    updated_t = (state_t.astype(F32) + gain * normed).astype(BF16)
    cot = cot_t.astype(F32)
    terms = cot * normed
    q = cot * gain
    mean_q = jnp.mean(q, axis=0, keepdims=True)
    mean_qn = jnp.mean(q * normed, axis=0, keepdims=True)
    d_norm_t = (inv_std * (q - mean_q - normed * mean_qn)).astype(BF16)
    d_hidden_t = (dot(w_second, d_norm_t) * slope).astype(BF16)
    return updated_t, terms, active_t, d_norm_t, d_hidden_t


def d_aggregate_of(w_first, d_hidden_t):
    return dot(w_first[w_first.shape[1] :], d_hidden_t).astype(BF16)


def first_products(d_hidden_t, state, aggregate):
    ones = jnp.ones((state.shape[0], ONES), BF16)
    return dot(d_hidden_t, joined_lanes([state, aggregate, ones]))


def second_products(active_t, d_norm_t):
    ones = jnp.ones((16, active_t.shape[1]), BF16)
    return dot_nt(jnp.concatenate([active_t, ones], axis=0), d_norm_t)


def fetch_kernel(state_hbm, *refs):
    count = (len(refs) - 3) // 2
    sources, targets = refs[:count], refs[count : 2 * count]
    even_side_ref, odd_side_ref, arrived = refs[2 * count :]
    edge = even_side_ref.shape[0]
    odd = device_is_odd()
    last = state_hbm.shape[0] - edge
    even_start = pl.multiple_of(jnp.where(odd, 0, last), edge)
    odd_start = pl.multiple_of(jnp.where(odd, last, 0), edge)
    pairs = [
        (state_hbm.at[pl.ds(even_start, edge)], even_side_ref),
        (state_hbm.at[pl.ds(odd_start, edge)], odd_side_ref),
        *zip(sources, targets),
    ]
    copies = [
        pltpu.make_async_copy(source, target, arrived.at[k])
        for k, (source, target) in enumerate(pairs)
    ]
    for copy in copies:
        copy.start()
    for copy in copies:
        copy.wait()


def inner_kernel(
    col_hbm,
    counts_ref,
    cot_ref,
    state_ref,
    got_even_ref,
    w_msg_ref,
    w_first_ref,
    w_second_ref,
    b_first_ref,
    b_second_ref,
    gain_ref,
    first_t_ref,
    second_t_ref,
    columns_ref,
    side_state_ref,
    side_state_t_ref,
    side_cot_ref,
    side_sum_ref,
    side_far_ref,
    band_ref,
    updated_hbm,
    d_hidden_ref,
    first_sums_ref,
    second_sums_ref,
    msg_sums_ref,
    gain_sums_ref,
    col_ref,
    updated_ref,
    arrived,
    left,
):
    blocks, tiles, size, _ = counts_ref.shape
    features = state_ref.shape[1]
    inner_rows = range(WIN, blocks - WIN)
    low_rows, high_rows = range(WIN), range(blocks - WIN, blocks)
    odd = device_is_odd()

    def even_side(low, high):
        return jnp.where(odd, low, high)

    def odd_side(low, high):
        return jnp.where(odd, high, low)

    col_copy = pltpu.make_async_copy(col_hbm, col_ref, arrived)
    col_copy.start()

    def rows(block, count=1):
        return pl.ds(block * size, count * size)

    w_msg, w_first, w_second = w_msg_ref[...], w_first_ref[...], w_second_ref[...]
    first_t = joined_lanes([w_first[:features].T, w_first[features:].T])
    second_t = w_second.T
    columns = [column(ref, size) for ref in (b_first_ref, b_second_ref, gain_ref)]
    first_t_ref[...] = first_t
    second_t_ref[...] = second_t
    for k in range(3):
        columns_ref[k] = columns[k]
    state = state_ref[...]
    state_t = [state[b * size : (b + 1) * size].T for b in range(blocks)]
    cot_t = [cot_ref[rows(b), :].T for b in range(blocks)]

    nothing = jnp.zeros((size, size), BF16)
    col_copy.wait()
    for b in range(blocks):
        for place in range(BAND):
            if place != WIN:
                band_ref[b, place] = nothing
        band_ref[b, WIN] = counts_ref[b, 0].astype(F32).astype(BF16)
        own = col_ref[0, b]
        for t in range(1, tiles):
            band_ref[b, col_ref[t, b] - own + WIN] += counts_ref[b, t].astype(F32).astype(BF16)

    wide = joined_lanes([dot(state, w_msg).astype(BF16), state])

    def neighbour_sum(b):
        first, last = max(b - WIN, 0), min(b + WIN, blocks - 1)
        tiles_of = [band_ref[b, block - b + WIN] for block in range(first, last + 1)]
        return dot(joined_lanes(tiles_of), wide[first * size : (last + 1) * size])

    def far(b, first):
        places = [block - b + WIN for block in range(first, first + WIN)]
        return joined_lanes([band_ref[b, p] if 0 <= p < BAND else nothing for p in places])

    def stacked(parts):
        return jnp.concatenate(list(parts), axis=0)

    ends = (stacked(map(neighbour_sum, low_rows)), stacked(map(neighbour_sum, high_rows)))
    fars = (stacked(far(b, -WIN) for b in low_rows), stacked(far(b, blocks) for b in high_rows))
    end_states = (state[: WIN * size], state[(blocks - WIN) * size :])
    end_states_t = (joined_lanes(state_t[:WIN]), joined_lanes(state_t[blocks - WIN :]))
    end_cots_t = (joined_lanes(cot_t[:WIN]), joined_lanes(cot_t[blocks - WIN :]))
    side_sum_ref[...] = odd_side(*ends)
    side_far_ref[...] = odd_side(*fars)
    side_state_ref[...] = odd_side(*end_states)
    side_state_t_ref[...] = odd_side(*end_states_t)
    side_cot_ref[...] = odd_side(*end_cots_t)

    halo = got_even_ref[...]
    wide_halo = joined_lanes([dot(halo, w_msg).astype(BF16), halo])
    end_sum = even_side(*ends) + dot(even_side(*fars), wide_halo)
    summed = stacked([*map(neighbour_sum, inner_rows), end_sum]).astype(BF16)
    aggregate, summed = summed[:, :features], summed[:, features:]
    updated_t, terms, active_t, d_norm_t, d_hidden_t = node_layer(
        joined_lanes([*state_t[WIN : blocks - WIN], even_side(*end_states_t)]),
        joined_lanes(blocks_turned(aggregate)),
        joined_lanes([*cot_t[WIN : blocks - WIN], even_side(*end_cots_t)]),
        first_t,
        second_t,
        w_second,
        columns,
    )
    updated_ref[...] = updated_t
    updated_copy = pltpu.make_async_copy(updated_ref, updated_hbm, left)
    updated_copy.start()
    d_hidden_ref[...] = d_hidden_t
    d_aggregate_t = d_aggregate_of(w_first, d_hidden_t)
    first_sums_ref[...] = first_products(
        d_hidden_t,
        stacked([state[WIN * size : (blocks - WIN) * size], even_side(*end_states)]),
        aggregate,
    )
    second_sums_ref[...] = second_products(active_t, d_norm_t)
    msg_sums_ref[...] = dot(d_aggregate_t, summed)
    gain_sums_ref[...] = sum(
        terms[:, k * size : (k + 1) * size] for k in range(blocks - WIN)
    )
    updated_copy.wait()


def outer_kernel(
    grad_scale,
    got_odd_ref,
    w_msg_ref,
    w_first_ref,
    w_second_ref,
    first_t_ref,
    second_t_ref,
    columns_ref,
    side_state_ref,
    side_state_t_ref,
    side_cot_ref,
    side_sum_ref,
    side_far_ref,
    first_sums_ref,
    second_sums_ref,
    msg_sums_ref,
    gain_sums_ref,
    grads_ref,
    updated_ref,
    d_hidden_ref,
):
    features, size = w_msg_ref.shape[0], columns_ref.shape[2]
    halo = got_odd_ref[...]
    wide_halo = joined_lanes([dot(halo, w_msg_ref[...]).astype(BF16), halo])
    summed = (side_sum_ref[...] + dot(side_far_ref[...], wide_halo)).astype(BF16)
    aggregate, summed = summed[:, :features], summed[:, features:]
    updated_t, terms, active_t, d_norm_t, d_hidden_t = node_layer(
        side_state_t_ref[...],
        joined_lanes(blocks_turned(aggregate)),
        side_cot_ref[...],
        first_t_ref[...],
        second_t_ref[...],
        w_second_ref[...],
        [columns_ref[k] for k in range(3)],
    )
    updated_ref[...] = updated_t
    d_hidden_ref[...] = d_hidden_t
    d_aggregate_t = d_aggregate_of(w_first_ref[...], d_hidden_t)

    first_sums = first_sums_ref[...] + first_products(d_hidden_t, side_state_ref[...], aggregate)
    second_sums = second_sums_ref[...] + second_products(active_t, d_norm_t)
    msg_sums = msg_sums_ref[...] + dot(d_aggregate_t, summed)
    gain_sums = gain_sums_ref[...]
    for k in range(WIN):
        gain_sums = gain_sums + terms[:, k * size : (k + 1) * size]

    slabs = grads_ref.shape[1] - 1
    turned = [first_sums[:, k * size : (k + 1) * size].T for k in range(3)]
    sums = (
        jnp.concatenate([turned[0], turned[1], second_sums[:features], msg_sums.T], axis=0)
        * grad_scale
    ).astype(SENT)
    bias = (
        jnp.concatenate(
            [
                turned[2][:1],
                second_sums[features : features + 1],
                jnp.sum(gain_sums.T, axis=0, keepdims=True),
            ],
            axis=0,
        )
        * grad_scale
    )
    bias = jnp.concatenate([bias, jnp.zeros((SLAB - 3, features), F32)], axis=0).astype(SENT)
    nothing = jnp.zeros((SLAB, features), SENT)
    for k in range(grads_ref.shape[0]):
        for slab in range(slabs):
            row = (k * slabs + slab) * SLAB
            grads_ref[k, slab] = sums[row : row + SLAB] if row < sums.shape[0] else nothing
        grads_ref[k, slabs] = bias


def owed_kernel(
    band_ref, w_first_ref, inner_ref, outer_ref, done_ref, ends_ref, send_even_ref, send_odd_ref
):
    blocks, _, size, _ = band_ref.shape
    odd = device_is_odd()
    w_first = w_first_ref[...]
    inner = d_aggregate_of(w_first, inner_ref[...])
    outer = d_aggregate_of(w_first, outer_ref[...])

    def d_aggregate(b):
        if WIN <= b < blocks - WIN:
            return inner[:, (b - WIN) * size : (b - WIN + 1) * size]
        k = b if b < WIN else b - blocks + WIN
        even_end = inner[:, (blocks - 2 * WIN + k) * size : (blocks - 2 * WIN + k + 1) * size]
        odd_end = outer[:, k * size : (k + 1) * size]
        return jnp.where(odd == (b < WIN), even_end, odd_end)

    def owed(block):
        near = range(max(block - WIN, 0), min(block + WIN, blocks - 1) + 1)
        tiles_of = [band_ref[b, block - b + WIN] for b in near]
        return dot(
            joined_lanes([d_aggregate(b) for b in near]), jnp.concatenate(tiles_of, axis=0)
        )

    for k in range(WIN):
        to_below = owed(k - WIN).astype(BF16)
        to_above = owed(blocks + k).astype(BF16)
        send_even_ref[k] = jnp.where(odd, to_below, to_above)
        send_odd_ref[k] = jnp.where(odd, to_above, to_below)
    for b in range(WIN, blocks - WIN):
        done_ref[b - WIN] = owed(b).astype(BF16)
    for k in range(WIN):
        ends_ref[k] = owed(k)
        ends_ref[WIN + k] = owed(blocks - WIN + k)


def sum_kernel(parts_ref, spread_ref, bias_ref):
    def total(slab):
        result = parts_ref[0, slab].astype(F32)
        for k in range(1, parts_ref.shape[0]):
            result = result + parts_ref[k, slab].astype(F32)
        return result

    slabs = parts_ref.shape[1] - 1
    weights = jnp.concatenate([total(slab) for slab in range(slabs)], axis=0)
    weights = weights.astype(spread_ref.dtype)
    for k in range(spread_ref.shape[0]):
        spread_ref[k] = weights
    bias_ref[...] = total(slabs)


def result_kernel(
    even_ref,
    odd_ref,
    cot_hbm,
    w_msg_ref,
    w_first_ref,
    inner_updated_hbm,
    outer_updated_ref,
    inner_d_hidden_ref,
    outer_d_hidden_ref,
    owed_ref,
    ends_ref,
    bias_ref,
    updated_ref,
    grad_state_ref,
    b_first_ref,
    b_second_ref,
    gain_ref,
    cot_ref,
    inner_updated_ref,
    arrived,
):
    inner, features, size = owed_ref.shape
    blocks = inner + 2 * WIN
    copies = [
        pltpu.make_async_copy(source, target, arrived.at[k])
        for k, (source, target) in enumerate(
            (
                (cot_hbm, cot_ref),
                (inner_updated_hbm, inner_updated_ref),
            )
        )
    ]
    for copy in copies:
        copy.start()
    odd = device_is_odd()
    even_part, odd_part = even_ref[...].astype(F32), odd_ref[...].astype(F32)
    from_below = jnp.where(odd, even_part, odd_part)
    from_above = jnp.where(odd, odd_part, even_part)
    weights = joined_lanes([w_first_ref[pl.ds(0, features), :], w_msg_ref[...]])
    for copy in copies:
        copy.wait()
    for b in range(blocks):
        if b < WIN:
            owed = (ends_ref[b] + from_below[b]).astype(BF16)
        elif b < blocks - WIN:
            owed = owed_ref[b - WIN]
        else:
            k = b - blocks + WIN
            owed = (ends_ref[WIN + k] + from_above[k]).astype(BF16)
        if WIN <= b < blocks - WIN:
            lanes = pl.ds((b - WIN) * size, size)
            updated, d_hidden = inner_updated_ref[:, lanes], inner_d_hidden_ref[:, lanes]
        else:
            k = b if b < WIN else b - blocks + WIN
            even_end = odd == (b < WIN)
            lanes, outer_lanes = pl.ds((blocks - 2 * WIN + k) * size, size), pl.ds(k * size, size)
            updated = jnp.where(
                even_end, inner_updated_ref[:, lanes], outer_updated_ref[:, outer_lanes]
            )
            d_hidden = jnp.where(
                even_end, inner_d_hidden_ref[:, lanes], outer_d_hidden_ref[:, outer_lanes]
            )
        rows = pl.ds(b * size, size)
        change = dot(weights, jnp.concatenate([d_hidden, owed], axis=0))
        grad_state_ref[rows, :] = (cot_ref[rows, :].astype(F32) + change.T).astype(BF16)
        updated_ref[rows, :] = updated.T
    for k, ref in enumerate((b_first_ref, b_second_ref, gain_ref)):
        ref[...] = bias_ref[pl.ds(k, 1), :]


def unpack_kernel(rows_ref, msg_ref, first_ref, second_ref):
    place = 0
    for ref in (first_ref, second_ref, msg_ref):
        count = ref.shape[0]
        ref[...] = rows_ref[pl.ds(place, count), :].astype(F32)
        place += count


def swapped(block, parity):
    last = lax.axis_size(AXES) - 1
    lower = range(parity, last, 2)
    return lax.ppermute(block, AXES, [(i, i + 1) for i in lower] + [(i + 1, i) for i in lower])


def call(kernel, name, outs, operands, scratch=(), limit=16, flops=0):
    specs = [pl.BlockSpec(memory_space=space) for _, space in operands]
    arrays = [kept(array, space) for array, space in operands]
    return pl.pallas_call(
        kernel,
        out_shape=tuple(outs),
        in_specs=specs,
        out_specs=tuple(
            pl.BlockSpec(memory_space=getattr(out, "memory_space", pltpu.VMEM)) for out in outs
        ),
        scratch_shapes=list(scratch),
        compiler_params=pltpu.CompilerParams(vmem_limit_bytes=limit * 1024 * 1024),
        cost_estimate=pl.CostEstimate(
            flops=flops, bytes_accessed=1_000_000, transcendentals=0
        ),
        name=name,
    )(*arrays)


def shards(
    node_state,
    w_msg,
    w_first,
    b_first,
    w_second,
    b_second,
    ln_gain,
    col_index,
    edge_counts,
    cotangent,
):
    nodes, features = node_state.shape
    blocks, tiles, size, _ = edge_counts.shape
    devices = lax.axis_size(AXES)
    grad_scale = 1.0 / math.sqrt(nodes * devices)
    chunk = -(-4 * features // (devices * 8)) * 8
    side = WIN * size
    most = nodes - side
    vmem, hbm = pltpu.VMEM, pltpu.HBM
    result = jax.ShapeDtypeStruct

    row = lambda vector: vector.reshape(1, features)
    sources = (w_msg, w_first, w_second, row(b_first), row(b_second), row(ln_gain))
    *fetched, even_side, odd_side = call(
        fetch_kernel,
        "fetch",
        [vmem(array.shape, array.dtype) for array in sources]
        + [vmem((side, features), BF16)] * 2,
        [(array, hbm) for array in (node_state, *sources)],
        scratch=(pltpu.SemaphoreType.DMA((len(sources) + 2,)),),
        flops=50_000_000_000,
    )
    w_msg_here, w_first_here, w_second_here, *vectors = fetched
    got_even = swapped(even_side, 0)
    got_odd = swapped(odd_side, 1)

    inner_results = call(
            inner_kernel,
            "inner_rows",
            (
                vmem((features, 2 * features), BF16),
                vmem((features, features), BF16),
                vmem((3, features, size), F32),
                vmem((side, features), BF16),
                vmem((features, side), BF16),
                vmem((features, side), BF16),
                vmem((side, 2 * features), F32),
                vmem((side, side), BF16),
                vmem((blocks, BAND, size, size), BF16),
                hbm((features, most), BF16),
                vmem((features, most), BF16),
                vmem((features, 2 * features + ONES), F32),
                vmem((features + 16, features), F32),
                vmem((features, features), F32),
                vmem((features, size), F32),
            ),
            [(col_index.T, hbm)]
            + [
                (array, vmem)
                for array in (edge_counts, cotangent, node_state, got_even, *fetched)
            ],
            scratch=(
                pltpu.SMEM((tiles, blocks), jnp.int32),
                vmem((features, most), BF16),
                pltpu.SemaphoreType.DMA,
                pltpu.SemaphoreType.DMA,
            ),
            limit=32,
            flops=700_000_000,
    )
    band, inner_updated, inner_d_hidden = inner_results[8:11]
    outer_operands = inner_results[:8] + inner_results[11:]

    grads, outer_updated, outer_d_hidden = call(
        functools.partial(outer_kernel, grad_scale),
        "outer_rows",
        (
            vmem((devices, chunk // SLAB + 1, SLAB, features), SENT),
            vmem((features, side), BF16),
            vmem((features, side), BF16),
        ),
        [
            (array, vmem)
            for array in (got_odd, w_msg_here, w_first_here, w_second_here, *outer_operands)
        ],
        flops=300_000_000,
    )

    parts = lax.all_to_all(grads, PARTNERS, 0, 0, tiled=True)
    owed, owed_ends, send_even, send_odd = call(
        owed_kernel,
        "owed",
        (
            vmem((blocks - 2 * WIN, features, size), BF16),
            vmem((2 * WIN, features, size), F32),
            vmem((WIN, features, size), BF16),
            vmem((WIN, features, size), BF16),
        ),
        [(array, vmem) for array in (band, w_first_here, inner_d_hidden, outer_d_hidden)],
        flops=200_000_000,
    )
    owed_even = swapped(send_even, 0)
    owed_odd = swapped(send_odd, 1)
    spread, bias = call(
        sum_kernel,
        "sum",
        (vmem((devices, chunk, features), SENT), vmem((SLAB, features), F32)),
        [(parts, vmem)],
        flops=10_000_000_000,
    )
    updated, grad_state, g_b_first, g_b_second, g_gain = call(
        result_kernel,
        "results",
        (
            result((nodes, features), BF16),
            result((nodes, features), BF16),
            result((1, features), F32),
            result((1, features), F32),
            result((1, features), F32),
        ),
        [(owed_even, vmem), (owed_odd, vmem), (cotangent, hbm)]
        + [(w_msg_here, vmem), (w_first_here, vmem), (inner_updated, hbm)]
        + [(array, vmem) for array in (outer_updated, inner_d_hidden, outer_d_hidden, owed, owed_ends, bias)],
        scratch=(
            vmem((nodes, features), BF16),
            vmem((features, most), BF16),
            pltpu.SemaphoreType.DMA((2,)),
        ),
        flops=50_000_000_000,
    )

    whole = lax.all_to_all(spread, PARTNERS, 0, 0, tiled=True)
    g_msg, g_first, g_second = call(
        unpack_kernel,
        "unpack",
        (
            result((features, features), F32),
            result((2 * features, features), F32),
            result((features, features), F32),
        ),
        [(whole.reshape(devices * chunk, features), vmem)],
    )
    flat = lambda vector: vector.reshape(features)
    return (
        updated,
        grad_state,
        g_msg,
        g_first,
        flat(g_b_first),
        g_second,
        flat(g_b_second),
        flat(g_gain),
    )


def solution(mesh):
    split = P(AXES, None)
    return jax.shard_map(
        shards,
        mesh=mesh,
        in_specs=(split, P(), P(), P(), P(), P(), P(), split, P(AXES, None, None, None), split),
        out_specs=(split, split, P(), P(), P(), P(), P(), P()),
        check_vma=False,
    )
```

```python
import functools
import math

import jax
import jax.numpy as jnp
from jax import lax
from jax.experimental import pallas as pl
from jax.experimental.pallas import tpu as pltpu
from jax.sharding import PartitionSpec as P

WIN = 2
BAND = 2 * WIN + 1
epsilon = 1e-05
AXES = ("dom_hi", "dom_lo", "feat")
PARTNERS = ("feat", "dom_lo", "dom_hi")
BF16, F32 = jnp.bfloat16, jnp.float32
SENT = BF16
ONES = 128
SLAB = 4

kept = pltpu.with_memory_space_constraint


def dot(left, right):
    return jnp.dot(left, right, preferred_element_type=F32)


def dot_nt(left, right):
    return lax.dot_general(left, right, (((1,), (1,)), ((), ())), preferred_element_type=F32)


def joined_lanes(parts):
    return jnp.concatenate(parts, axis=1)


def device_is_odd():
    index = 0
    for axis in AXES:
        index = index * lax.axis_size(axis) + lax.axis_index(axis)
    return index % 2 == 1


def column(row_ref, width):
    return jnp.broadcast_to(row_ref[...], (width, row_ref.shape[1])).T


def blocks_turned(array):
    size = array.shape[1]
    return [array[k : k + size].T for k in range(0, array.shape[0], size)]


def node_layer(state_t, aggregate_t, cot_t, first_t, second_t, w_second, columns):
    features, width = state_t.shape
    b_first, b_second, gain = (
        joined_lanes([c] * (width // c.shape[1])) for c in columns
    )
    pre_hidden = dot(first_t, jnp.concatenate([state_t, aggregate_t], axis=0)) + b_first
    sigmoid = 0.5 * jnp.tanh(0.5 * pre_hidden) + 0.5
    silu = pre_hidden * sigmoid
    active_t = silu.astype(BF16)
    slope = sigmoid + silu * (1.0 - sigmoid)
    pre_norm = dot(second_t, active_t) + b_second
    centred = pre_norm - jnp.mean(pre_norm, axis=0, keepdims=True)
    inv_std = lax.rsqrt(jnp.mean(centred * centred, axis=0, keepdims=True) + epsilon)
    normed = centred * inv_std
    updated_t = (state_t.astype(F32) + gain * normed).astype(BF16)
    cot = cot_t.astype(F32)
    terms = cot * normed
    q = cot * gain
    mean_q = jnp.mean(q, axis=0, keepdims=True)
    mean_qn = jnp.mean(q * normed, axis=0, keepdims=True)
    d_norm_t = (inv_std * (q - mean_q - normed * mean_qn)).astype(BF16)
    d_hidden_t = (dot(w_second, d_norm_t) * slope).astype(BF16)
    return updated_t, terms, active_t, d_norm_t, d_hidden_t


def d_aggregate_of(w_first, d_hidden_t):
    return dot(w_first[w_first.shape[1] :], d_hidden_t).astype(BF16)


def first_products(d_hidden_t, state, aggregate):
    ones = jnp.ones((state.shape[0], ONES), BF16)
    return dot(d_hidden_t, joined_lanes([state, aggregate, ones]))


def second_products(active_t, d_norm_t):
    ones = jnp.ones((16, active_t.shape[1]), BF16)
    return dot_nt(jnp.concatenate([active_t, ones], axis=0), d_norm_t)


def fetch_kernel(state_hbm, *refs):
    count = (len(refs) - 3) // 2
    sources, targets = refs[:count], refs[count : 2 * count]
    even_side_ref, odd_side_ref, arrived = refs[2 * count :]
    edge = even_side_ref.shape[0]
    odd = device_is_odd()
    last = state_hbm.shape[0] - edge
    even_start = pl.multiple_of(jnp.where(odd, 0, last), edge)
    odd_start = pl.multiple_of(jnp.where(odd, last, 0), edge)
    pairs = [
        (state_hbm.at[pl.ds(even_start, edge)], even_side_ref),
        (state_hbm.at[pl.ds(odd_start, edge)], odd_side_ref),
        *zip(sources, targets),
    ]
    copies = [
        pltpu.make_async_copy(source, target, arrived.at[k])
        for k, (source, target) in enumerate(pairs)
    ]
    for copy in copies:
        copy.start()
    for copy in copies:
        copy.wait()


def inner_kernel(
    col_hbm,
    counts_ref,
    cot_ref,
    state_ref,
    got_even_ref,
    w_msg_ref,
    w_first_ref,
    w_second_ref,
    b_first_ref,
    b_second_ref,
    gain_ref,
    first_t_ref,
    second_t_ref,
    columns_ref,
    side_state_ref,
    side_state_t_ref,
    side_cot_ref,
    side_sum_ref,
    side_far_ref,
    band_ref,
    updated_hbm,
    d_hidden_ref,
    first_sums_ref,
    second_sums_ref,
    msg_sums_ref,
    gain_sums_ref,
    col_ref,
    updated_ref,
    arrived,
    left,
):
    blocks, tiles, size, _ = counts_ref.shape
    features = state_ref.shape[1]
    inner_rows = range(WIN, blocks - WIN)
    low_rows, high_rows = range(WIN), range(blocks - WIN, blocks)
    odd = device_is_odd()

    def even_side(low, high):
        return jnp.where(odd, low, high)

    def odd_side(low, high):
        return jnp.where(odd, high, low)

    col_copy = pltpu.make_async_copy(col_hbm, col_ref, arrived)
    col_copy.start()

    def rows(block, count=1):
        return pl.ds(block * size, count * size)

    w_msg, w_first, w_second = w_msg_ref[...], w_first_ref[...], w_second_ref[...]
    first_t = joined_lanes([w_first[:features].T, w_first[features:].T])
    second_t = w_second.T
    columns = [column(ref, size) for ref in (b_first_ref, b_second_ref, gain_ref)]
    first_t_ref[...] = first_t
    second_t_ref[...] = second_t
    for k in range(3):
        columns_ref[k] = columns[k]
    state = state_ref[...]
    state_t = [state[b * size : (b + 1) * size].T for b in range(blocks)]
    cot_t = [cot_ref[rows(b), :].T for b in range(blocks)]

    nothing = jnp.zeros((size, size), BF16)
    col_copy.wait()
    for b in range(blocks):
        for place in range(BAND):
            if place != WIN:
                band_ref[b, place] = nothing
        band_ref[b, WIN] = counts_ref[b, 0].astype(F32).astype(BF16)
        own = col_ref[0, b]
        for t in range(1, tiles):
            band_ref[b, col_ref[t, b] - own + WIN] += counts_ref[b, t].astype(F32).astype(BF16)

    wide = joined_lanes([dot(state, w_msg).astype(BF16), state])

    def neighbour_sum(b):
        first, last = max(b - WIN, 0), min(b + WIN, blocks - 1)
        tiles_of = [band_ref[b, block - b + WIN] for block in range(first, last + 1)]
        return dot(joined_lanes(tiles_of), wide[first * size : (last + 1) * size])

    def far(b, first):
        places = [block - b + WIN for block in range(first, first + WIN)]
        return joined_lanes([band_ref[b, p] if 0 <= p < BAND else nothing for p in places])

    def stacked(parts):
        return jnp.concatenate(list(parts), axis=0)

    ends = (stacked(map(neighbour_sum, low_rows)), stacked(map(neighbour_sum, high_rows)))
    fars = (stacked(far(b, -WIN) for b in low_rows), stacked(far(b, blocks) for b in high_rows))
    end_states = (state[: WIN * size], state[(blocks - WIN) * size :])
    end_states_t = (joined_lanes(state_t[:WIN]), joined_lanes(state_t[blocks - WIN :]))
    end_cots_t = (joined_lanes(cot_t[:WIN]), joined_lanes(cot_t[blocks - WIN :]))
    side_sum_ref[...] = odd_side(*ends)
    side_far_ref[...] = odd_side(*fars)
    side_state_ref[...] = odd_side(*end_states)
    side_state_t_ref[...] = odd_side(*end_states_t)
    side_cot_ref[...] = odd_side(*end_cots_t)

    halo = got_even_ref[...]
    wide_halo = joined_lanes([dot(halo, w_msg).astype(BF16), halo])
    end_sum = even_side(*ends) + dot(even_side(*fars), wide_halo)
    summed = stacked([*map(neighbour_sum, inner_rows), end_sum]).astype(BF16)
    aggregate, summed = summed[:, :features], summed[:, features:]
    updated_t, terms, active_t, d_norm_t, d_hidden_t = node_layer(
        joined_lanes([*state_t[WIN : blocks - WIN], even_side(*end_states_t)]),
        joined_lanes(blocks_turned(aggregate)),
        joined_lanes([*cot_t[WIN : blocks - WIN], even_side(*end_cots_t)]),
        first_t,
        second_t,
        w_second,
        columns,
    )
    updated_ref[...] = updated_t
    updated_copy = pltpu.make_async_copy(updated_ref, updated_hbm, left)
    updated_copy.start()
    d_hidden_ref[...] = d_hidden_t
    d_aggregate_t = d_aggregate_of(w_first, d_hidden_t)
    first_sums_ref[...] = first_products(
        d_hidden_t,
        stacked([state[WIN * size : (blocks - WIN) * size], even_side(*end_states)]),
        aggregate,
    )
    second_sums_ref[...] = second_products(active_t, d_norm_t)
    msg_sums_ref[...] = dot(d_aggregate_t, summed)
    gain_sums_ref[...] = sum(
        terms[:, k * size : (k + 1) * size] for k in range(blocks - WIN)
    )
    updated_copy.wait()


def outer_kernel(
    grad_scale,
    got_odd_ref,
    w_msg_ref,
    w_first_ref,
    w_second_ref,
    first_t_ref,
    second_t_ref,
    columns_ref,
    side_state_ref,
    side_state_t_ref,
    side_cot_ref,
    side_sum_ref,
    side_far_ref,
    first_sums_ref,
    second_sums_ref,
    msg_sums_ref,
    gain_sums_ref,
    grads_ref,
    updated_ref,
    d_hidden_ref,
):
    features, size = w_msg_ref.shape[0], columns_ref.shape[2]
    halo = got_odd_ref[...]
    wide_halo = joined_lanes([dot(halo, w_msg_ref[...]).astype(BF16), halo])
    summed = (side_sum_ref[...] + dot(side_far_ref[...], wide_halo)).astype(BF16)
    aggregate, summed = summed[:, :features], summed[:, features:]
    updated_t, terms, active_t, d_norm_t, d_hidden_t = node_layer(
        side_state_t_ref[...],
        joined_lanes(blocks_turned(aggregate)),
        side_cot_ref[...],
        first_t_ref[...],
        second_t_ref[...],
        w_second_ref[...],
        [columns_ref[k] for k in range(3)],
    )
    updated_ref[...] = updated_t
    d_hidden_ref[...] = d_hidden_t
    d_aggregate_t = d_aggregate_of(w_first_ref[...], d_hidden_t)

    first_sums = first_sums_ref[...] + first_products(d_hidden_t, side_state_ref[...], aggregate)
    second_sums = second_sums_ref[...] + second_products(active_t, d_norm_t)
    msg_sums = msg_sums_ref[...] + dot(d_aggregate_t, summed)
    gain_sums = gain_sums_ref[...]
    for k in range(WIN):
        gain_sums = gain_sums + terms[:, k * size : (k + 1) * size]

    slabs = grads_ref.shape[1] - 1
    turned = [first_sums[:, k * size : (k + 1) * size].T for k in range(3)]
    sums = (
        jnp.concatenate([turned[0], turned[1], second_sums[:features], msg_sums.T], axis=0)
        * grad_scale
    ).astype(SENT)
    bias = (
        jnp.concatenate(
            [
                turned[2][:1],
                second_sums[features : features + 1],
                jnp.sum(gain_sums.T, axis=0, keepdims=True),
            ],
            axis=0,
        )
        * grad_scale
    )
    bias = jnp.concatenate([bias, jnp.zeros((SLAB - 3, features), F32)], axis=0).astype(SENT)
    nothing = jnp.zeros((SLAB, features), SENT)
    for k in range(grads_ref.shape[0]):
        for slab in range(slabs):
            row = (k * slabs + slab) * SLAB
            grads_ref[k, slab] = sums[row : row + SLAB] if row < sums.shape[0] else nothing
        grads_ref[k, slabs] = bias


def owed_kernel(
    band_ref, w_first_ref, inner_ref, outer_ref, done_ref, ends_ref, send_even_ref, send_odd_ref
):
    blocks, _, size, _ = band_ref.shape
    odd = device_is_odd()
    w_first = w_first_ref[...]
    inner = d_aggregate_of(w_first, inner_ref[...])
    outer = d_aggregate_of(w_first, outer_ref[...])

    def d_aggregate(b):
        if WIN <= b < blocks - WIN:
            return inner[:, (b - WIN) * size : (b - WIN + 1) * size]
        k = b if b < WIN else b - blocks + WIN
        even_end = inner[:, (blocks - 2 * WIN + k) * size : (blocks - 2 * WIN + k + 1) * size]
        odd_end = outer[:, k * size : (k + 1) * size]
        return jnp.where(odd == (b < WIN), even_end, odd_end)

    def owed(block):
        near = range(max(block - WIN, 0), min(block + WIN, blocks - 1) + 1)
        tiles_of = [band_ref[b, block - b + WIN] for b in near]
        return dot(
            joined_lanes([d_aggregate(b) for b in near]), jnp.concatenate(tiles_of, axis=0)
        )

    for k in range(WIN):
        to_below = owed(k - WIN).astype(BF16)
        to_above = owed(blocks + k).astype(BF16)
        send_even_ref[k] = jnp.where(odd, to_below, to_above)
        send_odd_ref[k] = jnp.where(odd, to_above, to_below)
    for b in range(WIN, blocks - WIN):
        done_ref[b - WIN] = owed(b).astype(BF16)
    for k in range(WIN):
        ends_ref[k] = owed(k)
        ends_ref[WIN + k] = owed(blocks - WIN + k)


def sum_kernel(parts_ref, spread_ref, bias_ref):
    def total(slab):
        result = parts_ref[0, slab].astype(F32)
        for k in range(1, parts_ref.shape[0]):
            result = result + parts_ref[k, slab].astype(F32)
        return result

    slabs = parts_ref.shape[1] - 1
    weights = jnp.concatenate([total(slab) for slab in range(slabs)], axis=0)
    weights = weights.astype(spread_ref.dtype)
    for k in range(spread_ref.shape[0]):
        spread_ref[k] = weights
    bias_ref[...] = total(slabs)


def result_kernel(
    even_ref,
    odd_ref,
    cot_hbm,
    w_msg_ref,
    w_first_ref,
    inner_updated_hbm,
    outer_updated_ref,
    inner_d_hidden_ref,
    outer_d_hidden_ref,
    owed_ref,
    ends_ref,
    bias_ref,
    updated_ref,
    grad_state_ref,
    b_first_ref,
    b_second_ref,
    gain_ref,
    cot_ref,
    inner_updated_ref,
    arrived,
):
    inner, features, size = owed_ref.shape
    blocks = inner + 2 * WIN
    copies = [
        pltpu.make_async_copy(source, target, arrived.at[k])
        for k, (source, target) in enumerate(
            (
                (cot_hbm, cot_ref),
                (inner_updated_hbm, inner_updated_ref),
            )
        )
    ]
    for copy in copies:
        copy.start()
    odd = device_is_odd()
    even_part, odd_part = even_ref[...].astype(F32), odd_ref[...].astype(F32)
    from_below = jnp.where(odd, even_part, odd_part)
    from_above = jnp.where(odd, odd_part, even_part)
    weights = joined_lanes([w_first_ref[pl.ds(0, features), :], w_msg_ref[...]])
    for copy in copies:
        copy.wait()
    for b in range(blocks):
        if b < WIN:
            owed = (ends_ref[b] + from_below[b]).astype(BF16)
        elif b < blocks - WIN:
            owed = owed_ref[b - WIN]
        else:
            k = b - blocks + WIN
            owed = (ends_ref[WIN + k] + from_above[k]).astype(BF16)
        if WIN <= b < blocks - WIN:
            lanes = pl.ds((b - WIN) * size, size)
            updated, d_hidden = inner_updated_ref[:, lanes], inner_d_hidden_ref[:, lanes]
        else:
            k = b if b < WIN else b - blocks + WIN
            even_end = odd == (b < WIN)
            lanes, outer_lanes = pl.ds((blocks - 2 * WIN + k) * size, size), pl.ds(k * size, size)
            updated = jnp.where(
                even_end, inner_updated_ref[:, lanes], outer_updated_ref[:, outer_lanes]
            )
            d_hidden = jnp.where(
                even_end, inner_d_hidden_ref[:, lanes], outer_d_hidden_ref[:, outer_lanes]
            )
        rows = pl.ds(b * size, size)
        change = dot(weights, jnp.concatenate([d_hidden, owed], axis=0))
        grad_state_ref[rows, :] = (cot_ref[rows, :].astype(F32) + change.T).astype(BF16)
        updated_ref[rows, :] = updated.T
    for k, ref in enumerate((b_first_ref, b_second_ref, gain_ref)):
        ref[...] = bias_ref[pl.ds(k, 1), :]


def unpack_kernel(rows_ref, msg_ref, first_ref, second_ref):
    place = 0
    for ref in (first_ref, second_ref, msg_ref):
        count = ref.shape[0]
        ref[...] = rows_ref[pl.ds(place, count), :].astype(F32)
        place += count


def swapped(block, parity):
    last = lax.axis_size(AXES) - 1
    lower = range(parity, last, 2)
    return lax.ppermute(block, AXES, [(i, i + 1) for i in lower] + [(i + 1, i) for i in lower])


def call(kernel, name, outs, operands, scratch=(), limit=16, flops=0):
    specs = [pl.BlockSpec(memory_space=space) for _, space in operands]
    arrays = [kept(array, space) for array, space in operands]
    return pl.pallas_call(
        kernel,
        out_shape=tuple(outs),
        in_specs=specs,
        out_specs=tuple(
            pl.BlockSpec(memory_space=getattr(out, "memory_space", pltpu.VMEM)) for out in outs
        ),
        scratch_shapes=list(scratch),
        compiler_params=pltpu.CompilerParams(vmem_limit_bytes=limit * 1024 * 1024),
        cost_estimate=pl.CostEstimate(
            flops=flops, bytes_accessed=1_000_000, transcendentals=0
        ),
        name=name,
    )(*arrays)


def shards(
    node_state,
    w_msg,
    w_first,
    b_first,
    w_second,
    b_second,
    ln_gain,
    col_index,
    edge_counts,
    cotangent,
):
    nodes, features = node_state.shape
    blocks, tiles, size, _ = edge_counts.shape
    devices = lax.axis_size(AXES)
    grad_scale = 1.0 / math.sqrt(nodes * devices)
    chunk = -(-4 * features // (devices * 8)) * 8
    side = WIN * size
    most = nodes - side
    vmem, hbm = pltpu.VMEM, pltpu.HBM
    result = jax.ShapeDtypeStruct

    row = lambda vector: vector.reshape(1, features)
    sources = (w_msg, w_first, w_second, row(b_first), row(b_second), row(ln_gain))
    *fetched, even_side, odd_side = call(
        fetch_kernel,
        "fetch",
        [vmem(array.shape, array.dtype) for array in sources]
        + [vmem((side, features), BF16)] * 2,
        [(array, hbm) for array in (node_state, *sources)],
        scratch=(pltpu.SemaphoreType.DMA((len(sources) + 2,)),),
        flops=50_000_000_000,
    )
    w_msg_here, w_first_here, w_second_here, *vectors = fetched
    got_even = swapped(even_side, 0)
    got_odd = swapped(odd_side, 1)

    inner_results = call(
            inner_kernel,
            "inner_rows",
            (
                vmem((features, 2 * features), BF16),
                vmem((features, features), BF16),
                vmem((3, features, size), F32),
                vmem((side, features), BF16),
                vmem((features, side), BF16),
                vmem((features, side), BF16),
                vmem((side, 2 * features), F32),
                vmem((side, side), BF16),
                vmem((blocks, BAND, size, size), BF16),
                hbm((features, most), BF16),
                vmem((features, most), BF16),
                vmem((features, 2 * features + ONES), F32),
                vmem((features + 16, features), F32),
                vmem((features, features), F32),
                vmem((features, size), F32),
            ),
            [(col_index.T, hbm)]
            + [
                (array, vmem)
                for array in (edge_counts, cotangent, node_state, got_even, *fetched)
            ],
            scratch=(
                pltpu.SMEM((tiles, blocks), jnp.int32),
                vmem((features, most), BF16),
                pltpu.SemaphoreType.DMA,
                pltpu.SemaphoreType.DMA,
            ),
            limit=32,
            flops=700_000_000,
    )
    band, inner_updated, inner_d_hidden = inner_results[8:11]
    outer_operands = inner_results[:8] + inner_results[11:]

    grads, outer_updated, outer_d_hidden = call(
        functools.partial(outer_kernel, grad_scale),
        "outer_rows",
        (
            vmem((devices, chunk // SLAB + 1, SLAB, features), SENT),
            vmem((features, side), BF16),
            vmem((features, side), BF16),
        ),
        [
            (array, vmem)
            for array in (got_odd, w_msg_here, w_first_here, w_second_here, *outer_operands)
        ],
        flops=300_000_000,
    )

    parts = lax.all_to_all(grads, PARTNERS, 0, 0, tiled=True)
    owed, owed_ends, send_even, send_odd = call(
        owed_kernel,
        "owed",
        (
            vmem((blocks - 2 * WIN, features, size), BF16),
            vmem((2 * WIN, features, size), F32),
            vmem((WIN, features, size), BF16),
            vmem((WIN, features, size), BF16),
        ),
        [(array, vmem) for array in (band, w_first_here, inner_d_hidden, outer_d_hidden)],
        flops=200_000_000,
    )
    owed_even = swapped(send_even, 0)
    owed_odd = swapped(send_odd, 1)
    spread, bias = call(
        sum_kernel,
        "sum",
        (vmem((devices, chunk, features), SENT), vmem((SLAB, features), F32)),
        [(parts, vmem)],
        flops=10_000_000_000,
    )
    updated, grad_state, g_b_first, g_b_second, g_gain = call(
        result_kernel,
        "results",
        (
            result((nodes, features), BF16),
            result((nodes, features), BF16),
            result((1, features), F32),
            result((1, features), F32),
            result((1, features), F32),
        ),
        [(owed_even, vmem), (owed_odd, vmem), (cotangent, hbm)]
        + [(w_msg_here, vmem), (w_first_here, vmem), (inner_updated, hbm)]
        + [(array, vmem) for array in (outer_updated, inner_d_hidden, outer_d_hidden, owed, owed_ends, bias)],
        scratch=(
            vmem((nodes, features), BF16),
            vmem((features, most), BF16),
            pltpu.SemaphoreType.DMA((2,)),
        ),
        flops=50_000_000_000,
    )

    whole = lax.all_to_all(spread, PARTNERS, 0, 0, tiled=True)
    g_msg, g_first, g_second = call(
        unpack_kernel,
        "unpack",
        (
            result((features, features), F32),
            result((2 * features, features), F32),
            result((features, features), F32),
        ),
        [(whole.reshape(devices * chunk, features), vmem)],
    )
    flat = lambda vector: vector.reshape(features)
    return (
        updated,
        grad_state,
        g_msg,
        g_first,
        flat(g_b_first),
        g_second,
        flat(g_b_second),
        flat(g_gain),
    )


def solution(mesh):
    dom, feat = mesh.devices.shape
    low = 2 - dom % 2
    mesh = jax.sharding.Mesh(mesh.devices.reshape(dom // low, low, feat), AXES)
    split = P(AXES, None)
    return jax.shard_map(
        shards,
        mesh=mesh,
        in_specs=(split, P(), P(), P(), P(), P(), P(), split, P(AXES, None, None, None), split),
        out_specs=(split, split, P(), P(), P(), P(), P(), P()),
        check_vma=False,
    )
```

```python
import functools
import math

import jax
import jax.numpy as jnp
from jax import lax
from jax.experimental import pallas as pl
from jax.experimental.pallas import tpu as pltpu
from jax.sharding import PartitionSpec as P

WIN = 2
BAND = 2 * WIN + 1
epsilon = 1e-05
AXES = ("dom", "feat")
PARTNERS = ("feat", "dom")
BF16, F32 = jnp.bfloat16, jnp.float32
SENT = BF16
ONES = 128
SLAB = 4

kept = pltpu.with_memory_space_constraint


def dot(left, right):
    return jnp.dot(left, right, preferred_element_type=F32)


def dot_nt(left, right):
    return lax.dot_general(left, right, (((1,), (1,)), ((), ())), preferred_element_type=F32)


def joined_lanes(parts):
    return jnp.concatenate(parts, axis=1)


def device_is_odd():
    index = lax.axis_index("dom") * lax.axis_size("feat") + lax.axis_index("feat")
    return index % 2 == 1


def column(row_ref, width):
    return jnp.broadcast_to(row_ref[...], (width, row_ref.shape[1])).T


def blocks_turned(array):
    size = array.shape[1]
    return [array[k : k + size].T for k in range(0, array.shape[0], size)]


def node_layer(state_t, aggregate_t, cot_t, first_t, second_t, w_second, columns):
    features, width = state_t.shape
    b_first, b_second, gain = (
        joined_lanes([c] * (width // c.shape[1])) for c in columns
    )
    pre_hidden = dot(first_t, jnp.concatenate([state_t, aggregate_t], axis=0)) + b_first
    sigmoid = 0.5 * jnp.tanh(0.5 * pre_hidden) + 0.5
    silu = pre_hidden * sigmoid
    active_t = silu.astype(BF16)
    slope = sigmoid + silu * (1.0 - sigmoid)
    pre_norm = dot(second_t, active_t) + b_second
    centred = pre_norm - jnp.mean(pre_norm, axis=0, keepdims=True)
    inv_std = lax.rsqrt(jnp.mean(centred * centred, axis=0, keepdims=True) + epsilon)
    normed = centred * inv_std
    updated_t = (state_t.astype(F32) + gain * normed).astype(BF16)
    cot = cot_t.astype(F32)
    terms = cot * normed
    q = cot * gain
    mean_q = jnp.mean(q, axis=0, keepdims=True)
    mean_qn = jnp.mean(q * normed, axis=0, keepdims=True)
    d_norm_t = (inv_std * (q - mean_q - normed * mean_qn)).astype(BF16)
    d_hidden_t = (dot(w_second, d_norm_t) * slope).astype(BF16)
    return updated_t, terms, active_t, d_norm_t, d_hidden_t


def d_aggregate_of(w_first, d_hidden_t):
    return dot(w_first[w_first.shape[1] :], d_hidden_t).astype(BF16)


def first_products(d_hidden_t, state, aggregate):
    ones = jnp.ones((state.shape[0], ONES), BF16)
    return dot(d_hidden_t, joined_lanes([state, aggregate, ones]))


def second_products(active_t, d_norm_t):
    ones = jnp.ones((16, active_t.shape[1]), BF16)
    return dot_nt(jnp.concatenate([active_t, ones], axis=0), d_norm_t)


def fetch_kernel(state_hbm, *refs):
    count = (len(refs) - 3) // 2
    sources, targets = refs[:count], refs[count : 2 * count]
    even_side_ref, odd_side_ref, arrived = refs[2 * count :]
    edge = even_side_ref.shape[0]
    odd = device_is_odd()
    last = state_hbm.shape[0] - edge
    even_start = pl.multiple_of(jnp.where(odd, 0, last), edge)
    odd_start = pl.multiple_of(jnp.where(odd, last, 0), edge)
    pairs = [
        (state_hbm.at[pl.ds(even_start, edge)], even_side_ref),
        (state_hbm.at[pl.ds(odd_start, edge)], odd_side_ref),
        *zip(sources, targets),
    ]
    copies = [
        pltpu.make_async_copy(source, target, arrived.at[k])
        for k, (source, target) in enumerate(pairs)
    ]
    for copy in copies:
        copy.start()
    for copy in copies:
        copy.wait()


def inner_kernel(
    col_hbm,
    counts_ref,
    cot_ref,
    state_ref,
    got_even_ref,
    w_msg_ref,
    w_first_ref,
    w_second_ref,
    b_first_ref,
    b_second_ref,
    gain_ref,
    first_t_ref,
    second_t_ref,
    columns_ref,
    side_state_ref,
    side_state_t_ref,
    side_cot_ref,
    side_sum_ref,
    side_far_ref,
    band_ref,
    updated_hbm,
    d_hidden_ref,
    first_sums_ref,
    second_sums_ref,
    msg_sums_ref,
    gain_sums_ref,
    col_ref,
    updated_ref,
    arrived,
    left,
):
    blocks, tiles, size, _ = counts_ref.shape
    features = state_ref.shape[1]
    inner_rows = range(WIN, blocks - WIN)
    low_rows, high_rows = range(WIN), range(blocks - WIN, blocks)
    odd = device_is_odd()

    def even_side(low, high):
        return jnp.where(odd, low, high)

    def odd_side(low, high):
        return jnp.where(odd, high, low)

    col_copy = pltpu.make_async_copy(col_hbm, col_ref, arrived)
    col_copy.start()

    def rows(block, count=1):
        return pl.ds(block * size, count * size)

    w_msg, w_first, w_second = w_msg_ref[...], w_first_ref[...], w_second_ref[...]
    first_t = joined_lanes([w_first[:features].T, w_first[features:].T])
    second_t = w_second.T
    columns = [column(ref, size) for ref in (b_first_ref, b_second_ref, gain_ref)]
    first_t_ref[...] = first_t
    second_t_ref[...] = second_t
    for k in range(3):
        columns_ref[k] = columns[k]
    state = state_ref[...]
    state_t = [state[b * size : (b + 1) * size].T for b in range(blocks)]
    cot_t = [cot_ref[rows(b), :].T for b in range(blocks)]

    nothing = jnp.zeros((size, size), BF16)
    col_copy.wait()
    for b in range(blocks):
        for place in range(BAND):
            if place != WIN:
                band_ref[b, place] = nothing
        band_ref[b, WIN] = counts_ref[b, 0].astype(F32).astype(BF16)
        own = col_ref[0, b]
        for t in range(1, tiles):
            band_ref[b, col_ref[t, b] - own + WIN] += counts_ref[b, t].astype(F32).astype(BF16)

    wide = joined_lanes([dot(state, w_msg).astype(BF16), state])

    def neighbour_sum(b):
        first, last = max(b - WIN, 0), min(b + WIN, blocks - 1)
        tiles_of = [band_ref[b, block - b + WIN] for block in range(first, last + 1)]
        return dot(joined_lanes(tiles_of), wide[first * size : (last + 1) * size])

    def far(b, first):
        places = [block - b + WIN for block in range(first, first + WIN)]
        return joined_lanes([band_ref[b, p] if 0 <= p < BAND else nothing for p in places])

    def stacked(parts):
        return jnp.concatenate(list(parts), axis=0)

    ends = (stacked(map(neighbour_sum, low_rows)), stacked(map(neighbour_sum, high_rows)))
    fars = (stacked(far(b, -WIN) for b in low_rows), stacked(far(b, blocks) for b in high_rows))
    end_states = (state[: WIN * size], state[(blocks - WIN) * size :])
    end_states_t = (joined_lanes(state_t[:WIN]), joined_lanes(state_t[blocks - WIN :]))
    end_cots_t = (joined_lanes(cot_t[:WIN]), joined_lanes(cot_t[blocks - WIN :]))
    side_sum_ref[...] = odd_side(*ends)
    side_far_ref[...] = odd_side(*fars)
    side_state_ref[...] = odd_side(*end_states)
    side_state_t_ref[...] = odd_side(*end_states_t)
    side_cot_ref[...] = odd_side(*end_cots_t)

    halo = got_even_ref[...]
    wide_halo = joined_lanes([dot(halo, w_msg).astype(BF16), halo])
    end_sum = even_side(*ends) + dot(even_side(*fars), wide_halo)
    summed = stacked([*map(neighbour_sum, inner_rows), end_sum]).astype(BF16)
    aggregate, summed = summed[:, :features], summed[:, features:]
    updated_t, terms, active_t, d_norm_t, d_hidden_t = node_layer(
        joined_lanes([*state_t[WIN : blocks - WIN], even_side(*end_states_t)]),
        joined_lanes(blocks_turned(aggregate)),
        joined_lanes([*cot_t[WIN : blocks - WIN], even_side(*end_cots_t)]),
        first_t,
        second_t,
        w_second,
        columns,
    )
    updated_ref[...] = updated_t
    updated_copy = pltpu.make_async_copy(updated_ref, updated_hbm, left)
    updated_copy.start()
    d_hidden_ref[...] = d_hidden_t
    d_aggregate_t = d_aggregate_of(w_first, d_hidden_t)
    first_sums_ref[...] = first_products(
        d_hidden_t,
        stacked([state[WIN * size : (blocks - WIN) * size], even_side(*end_states)]),
        aggregate,
    )
    second_sums_ref[...] = second_products(active_t, d_norm_t)
    msg_sums_ref[...] = dot(d_aggregate_t, summed)
    gain_sums_ref[...] = sum(
        terms[:, k * size : (k + 1) * size] for k in range(blocks - WIN)
    )
    updated_copy.wait()


def outer_kernel(
    grad_scale,
    got_odd_ref,
    w_msg_ref,
    w_first_ref,
    w_second_ref,
    first_t_ref,
    second_t_ref,
    columns_ref,
    side_state_ref,
    side_state_t_ref,
    side_cot_ref,
    side_sum_ref,
    side_far_ref,
    first_sums_ref,
    second_sums_ref,
    msg_sums_ref,
    gain_sums_ref,
    grads_ref,
    updated_ref,
    d_hidden_ref,
):
    features, size = w_msg_ref.shape[0], columns_ref.shape[2]
    halo = got_odd_ref[...]
    wide_halo = joined_lanes([dot(halo, w_msg_ref[...]).astype(BF16), halo])
    summed = (side_sum_ref[...] + dot(side_far_ref[...], wide_halo)).astype(BF16)
    aggregate, summed = summed[:, :features], summed[:, features:]
    updated_t, terms, active_t, d_norm_t, d_hidden_t = node_layer(
        side_state_t_ref[...],
        joined_lanes(blocks_turned(aggregate)),
        side_cot_ref[...],
        first_t_ref[...],
        second_t_ref[...],
        w_second_ref[...],
        [columns_ref[k] for k in range(3)],
    )
    updated_ref[...] = updated_t
    d_hidden_ref[...] = d_hidden_t
    d_aggregate_t = d_aggregate_of(w_first_ref[...], d_hidden_t)

    first_sums = first_sums_ref[...] + first_products(d_hidden_t, side_state_ref[...], aggregate)
    second_sums = second_sums_ref[...] + second_products(active_t, d_norm_t)
    msg_sums = msg_sums_ref[...] + dot(d_aggregate_t, summed)
    gain_sums = gain_sums_ref[...]
    for k in range(WIN):
        gain_sums = gain_sums + terms[:, k * size : (k + 1) * size]

    slabs = grads_ref.shape[1] - 1
    turned = [first_sums[:, k * size : (k + 1) * size].T for k in range(3)]
    sums = (
        jnp.concatenate([turned[0], turned[1], second_sums[:features], msg_sums.T], axis=0)
        * grad_scale
    ).astype(SENT)
    bias = (
        jnp.concatenate(
            [
                turned[2][:1],
                second_sums[features : features + 1],
                jnp.sum(gain_sums.T, axis=0, keepdims=True),
            ],
            axis=0,
        )
        * grad_scale
    )
    bias = jnp.concatenate([bias, jnp.zeros((SLAB - 3, features), F32)], axis=0).astype(SENT)
    nothing = jnp.zeros((SLAB, features), SENT)
    for k in range(grads_ref.shape[0]):
        for slab in range(slabs):
            row = (k * slabs + slab) * SLAB
            grads_ref[k, slab] = sums[row : row + SLAB] if row < sums.shape[0] else nothing
        grads_ref[k, slabs] = bias


def owed_kernel(
    band_ref, w_first_ref, inner_ref, outer_ref, done_ref, ends_ref, send_even_ref, send_odd_ref
):
    blocks, _, size, _ = band_ref.shape
    odd = device_is_odd()
    w_first = w_first_ref[...]
    inner = d_aggregate_of(w_first, inner_ref[...])
    outer = d_aggregate_of(w_first, outer_ref[...])

    def d_aggregate(b):
        if WIN <= b < blocks - WIN:
            return inner[:, (b - WIN) * size : (b - WIN + 1) * size]
        k = b if b < WIN else b - blocks + WIN
        even_end = inner[:, (blocks - 2 * WIN + k) * size : (blocks - 2 * WIN + k + 1) * size]
        odd_end = outer[:, k * size : (k + 1) * size]
        return jnp.where(odd == (b < WIN), even_end, odd_end)

    def owed(block):
        near = range(max(block - WIN, 0), min(block + WIN, blocks - 1) + 1)
        tiles_of = [band_ref[b, block - b + WIN] for b in near]
        return dot(
            joined_lanes([d_aggregate(b) for b in near]), jnp.concatenate(tiles_of, axis=0)
        )

    for k in range(WIN):
        to_below = owed(k - WIN).astype(BF16)
        to_above = owed(blocks + k).astype(BF16)
        send_even_ref[k] = jnp.where(odd, to_below, to_above)
        send_odd_ref[k] = jnp.where(odd, to_above, to_below)
    for b in range(WIN, blocks - WIN):
        done_ref[b - WIN] = owed(b).astype(BF16)
    for k in range(WIN):
        ends_ref[k] = owed(k)
        ends_ref[WIN + k] = owed(blocks - WIN + k)


def sum_kernel(parts_ref, spread_ref, bias_ref):
    def total(slab):
        result = parts_ref[0, slab].astype(F32)
        for k in range(1, parts_ref.shape[0]):
            result = result + parts_ref[k, slab].astype(F32)
        return result

    slabs = parts_ref.shape[1] - 1
    weights = jnp.concatenate([total(slab) for slab in range(slabs)], axis=0)
    weights = weights.astype(spread_ref.dtype)
    for k in range(spread_ref.shape[0]):
        spread_ref[k] = weights
    bias_ref[...] = total(slabs)


def result_kernel(
    odd_ref,
    even_ref,
    cot_hbm,
    w_msg_ref,
    w_first_ref,
    inner_updated_hbm,
    outer_updated_ref,
    inner_d_hidden_ref,
    outer_d_hidden_ref,
    owed_ref,
    ends_ref,
    bias_ref,
    updated_ref,
    grad_state_ref,
    b_first_ref,
    b_second_ref,
    gain_ref,
    cot_ref,
    inner_updated_ref,
    arrived,
):
    inner, features, size = owed_ref.shape
    blocks = inner + 2 * WIN
    copies = [
        pltpu.make_async_copy(source, target, arrived.at[k])
        for k, (source, target) in enumerate(
            (
                (cot_hbm, cot_ref),
                (inner_updated_hbm, inner_updated_ref),
            )
        )
    ]
    for copy in copies:
        copy.start()
    odd = device_is_odd()
    even_part, odd_part = even_ref[...].astype(F32), odd_ref[...].astype(F32)
    from_below = jnp.where(odd, even_part, odd_part)
    from_above = jnp.where(odd, odd_part, even_part)
    weights = joined_lanes([w_first_ref[pl.ds(0, features), :], w_msg_ref[...]])
    for copy in copies:
        copy.wait()
    for b in range(blocks):
        if b < WIN:
            owed = (ends_ref[b] + from_below[b]).astype(BF16)
        elif b < blocks - WIN:
            owed = owed_ref[b - WIN]
        else:
            k = b - blocks + WIN
            owed = (ends_ref[WIN + k] + from_above[k]).astype(BF16)
        if WIN <= b < blocks - WIN:
            lanes = pl.ds((b - WIN) * size, size)
            updated, d_hidden = inner_updated_ref[:, lanes], inner_d_hidden_ref[:, lanes]
        else:
            k = b if b < WIN else b - blocks + WIN
            even_end = odd == (b < WIN)
            lanes, outer_lanes = pl.ds((blocks - 2 * WIN + k) * size, size), pl.ds(k * size, size)
            updated = jnp.where(
                even_end, inner_updated_ref[:, lanes], outer_updated_ref[:, outer_lanes]
            )
            d_hidden = jnp.where(
                even_end, inner_d_hidden_ref[:, lanes], outer_d_hidden_ref[:, outer_lanes]
            )
        rows = pl.ds(b * size, size)
        change = dot(weights, jnp.concatenate([d_hidden, owed], axis=0))
        grad_state_ref[rows, :] = (cot_ref[rows, :].astype(F32) + change.T).astype(BF16)
        updated_ref[rows, :] = updated.T
    for k, ref in enumerate((b_first_ref, b_second_ref, gain_ref)):
        ref[...] = bias_ref[pl.ds(k, 1), :]


def unpack_kernel(rows_ref, msg_ref, first_ref, second_ref):
    place = 0
    for ref in (first_ref, second_ref, msg_ref):
        count = ref.shape[0]
        ref[...] = rows_ref[pl.ds(place, count), :].astype(F32)
        place += count


def swapped(block, parity):
    last = lax.axis_size(AXES) - 1
    lower = range(parity, last, 2)
    return lax.ppermute(block, AXES, [(i, i + 1) for i in lower] + [(i + 1, i) for i in lower])


def call(kernel, name, outs, operands, scratch=(), limit=16, flops=0):
    specs = [pl.BlockSpec(memory_space=space) for _, space in operands]
    arrays = [kept(array, space) for array, space in operands]
    return pl.pallas_call(
        kernel,
        out_shape=tuple(outs),
        in_specs=specs,
        out_specs=tuple(
            pl.BlockSpec(memory_space=getattr(out, "memory_space", pltpu.VMEM)) for out in outs
        ),
        scratch_shapes=list(scratch),
        compiler_params=pltpu.CompilerParams(vmem_limit_bytes=limit * 1024 * 1024),
        cost_estimate=pl.CostEstimate(
            flops=flops, bytes_accessed=1_000_000, transcendentals=0
        ),
        name=name,
    )(*arrays)


def shards(
    node_state,
    w_msg,
    w_first,
    b_first,
    w_second,
    b_second,
    ln_gain,
    col_index,
    edge_counts,
    cotangent,
):
    nodes, features = node_state.shape
    blocks, tiles, size, _ = edge_counts.shape
    devices = lax.axis_size(AXES)
    grad_scale = 1.0 / math.sqrt(nodes * devices)
    chunk = -(-4 * features // (devices * 8)) * 8
    side = WIN * size
    most = nodes - side
    vmem, hbm = pltpu.VMEM, pltpu.HBM
    result = jax.ShapeDtypeStruct

    row = lambda vector: vector.reshape(1, features)
    sources = (w_msg, w_first, w_second, row(b_first), row(b_second), row(ln_gain))
    *fetched, even_side, odd_side = call(
        fetch_kernel,
        "fetch",
        [vmem(array.shape, array.dtype) for array in sources]
        + [vmem((side, features), BF16)] * 2,
        [(array, hbm) for array in (node_state, *sources)],
        scratch=(pltpu.SemaphoreType.DMA((len(sources) + 2,)),),
        flops=50_000_000_000,
    )
    w_msg_here, w_first_here, w_second_here, *vectors = fetched
    got_even = swapped(even_side, 0)
    got_odd = swapped(odd_side, 1)

    inner_results = call(
            inner_kernel,
            "inner_rows",
            (
                vmem((features, 2 * features), BF16),
                vmem((features, features), BF16),
                vmem((3, features, size), F32),
                vmem((side, features), BF16),
                vmem((features, side), BF16),
                vmem((features, side), BF16),
                vmem((side, 2 * features), F32),
                vmem((side, side), BF16),
                vmem((blocks, BAND, size, size), BF16),
                hbm((features, most), BF16),
                vmem((features, most), BF16),
                vmem((features, 2 * features + ONES), F32),
                vmem((features + 16, features), F32),
                vmem((features, features), F32),
                vmem((features, size), F32),
            ),
            [(col_index.T, hbm)]
            + [
                (array, vmem)
                for array in (edge_counts, cotangent, node_state, got_even, *fetched)
            ],
            scratch=(
                pltpu.SMEM((tiles, blocks), jnp.int32),
                vmem((features, most), BF16),
                pltpu.SemaphoreType.DMA,
                pltpu.SemaphoreType.DMA,
            ),
            limit=32,
            flops=700_000_000,
    )
    band, inner_updated, inner_d_hidden = inner_results[8:11]
    outer_operands = inner_results[:8] + inner_results[11:]

    grads, outer_updated, outer_d_hidden = call(
        functools.partial(outer_kernel, grad_scale),
        "outer_rows",
        (
            vmem((devices, chunk // SLAB + 1, SLAB, features), SENT),
            vmem((features, side), BF16),
            vmem((features, side), BF16),
        ),
        [
            (array, vmem)
            for array in (got_odd, w_msg_here, w_first_here, w_second_here, *outer_operands)
        ],
        flops=300_000_000,
    )

    parts = lax.all_to_all(grads, PARTNERS, 0, 0, tiled=True)
    owed, owed_ends, send_even, send_odd = call(
        owed_kernel,
        "owed",
        (
            vmem((blocks - 2 * WIN, features, size), BF16),
            vmem((2 * WIN, features, size), F32),
            vmem((WIN, features, size), BF16),
            vmem((WIN, features, size), BF16),
        ),
        [(array, vmem) for array in (band, w_first_here, inner_d_hidden, outer_d_hidden)],
        flops=200_000_000,
    )
    owed_even = swapped(send_even, 0)
    owed_odd = swapped(send_odd, 1)
    spread, bias = call(
        sum_kernel,
        "sum",
        (vmem((devices, chunk, features), SENT), vmem((SLAB, features), F32)),
        [(parts, vmem)],
        flops=10_000_000_000,
    )
    updated, grad_state, g_b_first, g_b_second, g_gain = call(
        result_kernel,
        "results",
        (
            result((nodes, features), BF16),
            result((nodes, features), BF16),
            result((1, features), F32),
            result((1, features), F32),
            result((1, features), F32),
        ),
        [(owed_odd, vmem), (owed_even, vmem), (cotangent, hbm)]
        + [(w_msg_here, vmem), (w_first_here, vmem), (inner_updated, hbm)]
        + [(array, vmem) for array in (outer_updated, inner_d_hidden, outer_d_hidden, owed, owed_ends, bias)],
        scratch=(
            vmem((nodes, features), BF16),
            vmem((features, most), BF16),
            pltpu.SemaphoreType.DMA((2,)),
        ),
        flops=50_000_000_000,
    )

    whole = lax.all_to_all(spread, PARTNERS, 0, 0, tiled=True)
    g_msg, g_first, g_second = call(
        unpack_kernel,
        "unpack",
        (
            result((features, features), F32),
            result((2 * features, features), F32),
            result((features, features), F32),
        ),
        [(whole.reshape(devices * chunk, features), vmem)],
    )
    flat = lambda vector: vector.reshape(features)
    return (
        updated,
        grad_state,
        g_msg,
        g_first,
        flat(g_b_first),
        g_second,
        flat(g_b_second),
        flat(g_gain),
    )


def solution(mesh):
    split = P(AXES, None)
    return jax.shard_map(
        shards,
        mesh=mesh,
        in_specs=(split, P(), P(), P(), P(), P(), P(), split, P(AXES, None, None, None), split),
        out_specs=(split, split, P(), P(), P(), P(), P(), P()),
        check_vma=False,
    )
```

```python
import functools
import math

import jax
import jax.numpy as jnp
from jax import lax
from jax.experimental import pallas as pl
from jax.experimental.pallas import tpu as pltpu
from jax.sharding import PartitionSpec as P

WIN = 2
BAND = 2 * WIN + 1
epsilon = 1e-05
AXES = ("dom", "feat")
PARTNERS = ("feat", "dom")
BF16, F32 = jnp.bfloat16, jnp.float32
SENT = BF16
ONES = 128
SLAB = 4

kept = pltpu.with_memory_space_constraint


def dot(left, right):
    return jnp.dot(left, right, preferred_element_type=F32)


def dot_nt(left, right):
    return lax.dot_general(left, right, (((1,), (1,)), ((), ())), preferred_element_type=F32)


def joined_lanes(parts):
    return jnp.concatenate(parts, axis=1)


def device_is_odd():
    index = lax.axis_index("dom") * lax.axis_size("feat") + lax.axis_index("feat")
    return index % 2 == 1


def column(row_ref, width):
    return jnp.broadcast_to(row_ref[...], (width, row_ref.shape[1])).T


def blocks_turned(array):
    size = array.shape[1]
    return [array[k : k + size].T for k in range(0, array.shape[0], size)]


def node_layer(state_t, aggregate_t, cot_t, first_t, second_t, w_second, columns):
    features, width = state_t.shape
    b_first, b_second, gain = (
        joined_lanes([c] * (width // c.shape[1])) for c in columns
    )
    pre_hidden = dot(first_t, jnp.concatenate([state_t, aggregate_t], axis=0)) + b_first
    sigmoid = 0.5 * jnp.tanh(0.5 * pre_hidden) + 0.5
    silu = pre_hidden * sigmoid
    active_t = silu.astype(BF16)
    slope = sigmoid + silu * (1.0 - sigmoid)
    pre_norm = dot(second_t, active_t) + b_second
    centred = pre_norm - jnp.mean(pre_norm, axis=0, keepdims=True)
    inv_std = lax.rsqrt(jnp.mean(centred * centred, axis=0, keepdims=True) + epsilon)
    normed = centred * inv_std
    updated_t = (state_t.astype(F32) + gain * normed).astype(BF16)
    cot = cot_t.astype(F32)
    terms = cot * normed
    q = cot * gain
    mean_q = jnp.mean(q, axis=0, keepdims=True)
    mean_qn = jnp.mean(q * normed, axis=0, keepdims=True)
    d_norm_t = (inv_std * (q - mean_q - normed * mean_qn)).astype(BF16)
    d_hidden_t = (dot(w_second, d_norm_t) * slope).astype(BF16)
    return updated_t, terms, active_t, d_norm_t, d_hidden_t


def d_aggregate_of(w_first, d_hidden_t):
    return dot(w_first[w_first.shape[1] :], d_hidden_t).astype(BF16)


def first_products(d_hidden_t, state, aggregate):
    ones = jnp.ones((state.shape[0], ONES), BF16)
    return dot(d_hidden_t, joined_lanes([state, aggregate, ones]))


def second_products(active_t, d_norm_t):
    ones = jnp.ones((16, active_t.shape[1]), BF16)
    return dot_nt(jnp.concatenate([active_t, ones], axis=0), d_norm_t)


def fetch_kernel(state_hbm, *refs):
    count = (len(refs) - 3) // 2
    sources, targets = refs[:count], refs[count : 2 * count]
    even_side_ref, odd_side_ref, arrived = refs[2 * count :]
    edge = even_side_ref.shape[0]
    odd = device_is_odd()
    last = state_hbm.shape[0] - edge
    even_start = pl.multiple_of(jnp.where(odd, 0, last), edge)
    odd_start = pl.multiple_of(jnp.where(odd, last, 0), edge)
    pairs = [
        (state_hbm.at[pl.ds(even_start, edge)], even_side_ref),
        (state_hbm.at[pl.ds(odd_start, edge)], odd_side_ref),
        *zip(sources, targets),
    ]
    copies = [
        pltpu.make_async_copy(source, target, arrived.at[k])
        for k, (source, target) in enumerate(pairs)
    ]
    for copy in copies:
        copy.start()
    for copy in copies:
        copy.wait()


def inner_kernel(
    col_hbm,
    counts_ref,
    cot_ref,
    state_ref,
    got_even_ref,
    w_msg_ref,
    w_first_ref,
    w_second_ref,
    b_first_ref,
    b_second_ref,
    gain_ref,
    first_t_ref,
    second_t_ref,
    columns_ref,
    side_state_ref,
    side_state_t_ref,
    side_cot_ref,
    side_sum_ref,
    side_far_ref,
    band_ref,
    updated_hbm,
    d_hidden_ref,
    first_sums_ref,
    second_sums_ref,
    msg_sums_ref,
    gain_sums_ref,
    col_ref,
    updated_ref,
    arrived,
    left,
):
    blocks, tiles, size, _ = counts_ref.shape
    features = state_ref.shape[1]
    inner_rows = range(WIN, blocks - WIN)
    low_rows, high_rows = range(WIN), range(blocks - WIN, blocks)
    odd = device_is_odd()

    def even_side(low, high):
        return jnp.where(odd, low, high)

    def odd_side(low, high):
        return jnp.where(odd, high, low)

    col_copy = pltpu.make_async_copy(col_hbm, col_ref, arrived)
    col_copy.start()

    def rows(block, count=1):
        return pl.ds(block * size, count * size)

    w_msg, w_first, w_second = w_msg_ref[...], w_first_ref[...], w_second_ref[...]
    first_t = joined_lanes([w_first[:features].T, w_first[features:].T])
    second_t = w_second.T
    columns = [column(ref, size) for ref in (b_first_ref, b_second_ref, gain_ref)]
    first_t_ref[...] = first_t
    second_t_ref[...] = second_t
    for k in range(3):
        columns_ref[k] = columns[k]
    state = state_ref[...]
    state_t = [state[b * size : (b + 1) * size].T for b in range(blocks)]
    cot_t = [cot_ref[rows(b), :].T for b in range(blocks)]

    nothing = jnp.zeros((size, size), BF16)
    col_copy.wait()
    for b in range(blocks):
        for place in range(BAND):
            if place != WIN:
                band_ref[b, place] = nothing
        band_ref[b, WIN] = counts_ref[b, 0].astype(F32).astype(BF16)
        own = col_ref[0, b]
        for t in range(1, tiles):
            band_ref[b, col_ref[t, b] - own + WIN] += counts_ref[b, t].astype(F32).astype(BF16)

    wide = joined_lanes([dot(state, w_msg).astype(BF16), state])

    def neighbour_sum(b):
        first, last = max(b - WIN, 0), min(b + WIN, blocks - 1)
        tiles_of = [band_ref[b, block - b + WIN] for block in range(first, last + 1)]
        return dot(joined_lanes(tiles_of), wide[first * size : (last + 1) * size])

    def far(b, first):
        places = [block - b + WIN for block in range(first, first + WIN)]
        return joined_lanes([band_ref[b, p] if 0 <= p < BAND else nothing for p in places])

    def stacked(parts):
        return jnp.concatenate(list(parts), axis=0)

    ends = (stacked(map(neighbour_sum, low_rows)), stacked(map(neighbour_sum, high_rows)))
    fars = (stacked(far(b, -WIN) for b in low_rows), stacked(far(b, blocks) for b in high_rows))
    end_states = (state[: WIN * size], state[(blocks - WIN) * size :])
    end_states_t = (joined_lanes(state_t[:WIN]), joined_lanes(state_t[blocks - WIN :]))
    end_cots_t = (joined_lanes(cot_t[:WIN]), joined_lanes(cot_t[blocks - WIN :]))
    side_sum_ref[...] = odd_side(*ends)
    side_far_ref[...] = odd_side(*fars)
    side_state_ref[...] = odd_side(*end_states)
    side_state_t_ref[...] = odd_side(*end_states_t)
    side_cot_ref[...] = odd_side(*end_cots_t)

    halo = got_even_ref[...]
    wide_halo = joined_lanes([dot(halo, w_msg).astype(BF16), halo])
    end_sum = even_side(*ends) + dot(even_side(*fars), wide_halo)
    summed = stacked([*map(neighbour_sum, inner_rows), end_sum]).astype(BF16)
    aggregate, summed = summed[:, :features], summed[:, features:]
    updated_t, terms, active_t, d_norm_t, d_hidden_t = node_layer(
        joined_lanes([*state_t[WIN : blocks - WIN], even_side(*end_states_t)]),
        joined_lanes(blocks_turned(aggregate)),
        joined_lanes([*cot_t[WIN : blocks - WIN], even_side(*end_cots_t)]),
        first_t,
        second_t,
        w_second,
        columns,
    )
    updated_ref[...] = updated_t
    updated_copy = pltpu.make_async_copy(updated_ref, updated_hbm, left)
    updated_copy.start()
    d_hidden_ref[...] = d_hidden_t
    d_aggregate_t = d_aggregate_of(w_first, d_hidden_t)
    first_sums_ref[...] = first_products(
        d_hidden_t,
        stacked([state[WIN * size : (blocks - WIN) * size], even_side(*end_states)]),
        aggregate,
    )
    second_sums_ref[...] = second_products(active_t, d_norm_t)
    msg_sums_ref[...] = dot(d_aggregate_t, summed)
    gain_sums_ref[...] = sum(
        terms[:, k * size : (k + 1) * size] for k in range(blocks - WIN)
    )
    updated_copy.wait()


def outer_kernel(
    grad_scale,
    got_odd_ref,
    w_msg_ref,
    w_first_ref,
    w_second_ref,
    first_t_ref,
    second_t_ref,
    columns_ref,
    side_state_ref,
    side_state_t_ref,
    side_cot_ref,
    side_sum_ref,
    side_far_ref,
    first_sums_ref,
    second_sums_ref,
    msg_sums_ref,
    gain_sums_ref,
    grads_ref,
    updated_ref,
    d_hidden_ref,
):
    features, size = w_msg_ref.shape[0], columns_ref.shape[2]
    halo = got_odd_ref[...]
    wide_halo = joined_lanes([dot(halo, w_msg_ref[...]).astype(BF16), halo])
    summed = (side_sum_ref[...] + dot(side_far_ref[...], wide_halo)).astype(BF16)
    aggregate, summed = summed[:, :features], summed[:, features:]
    updated_t, terms, active_t, d_norm_t, d_hidden_t = node_layer(
        side_state_t_ref[...],
        joined_lanes(blocks_turned(aggregate)),
        side_cot_ref[...],
        first_t_ref[...],
        second_t_ref[...],
        w_second_ref[...],
        [columns_ref[k] for k in range(3)],
    )
    updated_ref[...] = updated_t
    d_hidden_ref[...] = d_hidden_t
    d_aggregate_t = d_aggregate_of(w_first_ref[...], d_hidden_t)

    first_sums = first_sums_ref[...] + first_products(d_hidden_t, side_state_ref[...], aggregate)
    second_sums = second_sums_ref[...] + second_products(active_t, d_norm_t)
    msg_sums = msg_sums_ref[...] + dot(d_aggregate_t, summed)
    gain_sums = gain_sums_ref[...]
    for k in range(WIN):
        gain_sums = gain_sums + terms[:, k * size : (k + 1) * size]

    slabs = grads_ref.shape[1] - 1
    turned = [first_sums[:, k * size : (k + 1) * size].T for k in range(3)]
    sums = (
        jnp.concatenate([turned[0], turned[1], second_sums[:features], msg_sums.T], axis=0)
        * grad_scale
    ).astype(SENT)
    bias = (
        jnp.concatenate(
            [
                turned[2][:1],
                second_sums[features : features + 1],
                jnp.sum(gain_sums.T, axis=0, keepdims=True),
            ],
            axis=0,
        )
        * grad_scale
    )
    bias = jnp.concatenate([bias, jnp.zeros((SLAB - 3, features), F32)], axis=0).astype(SENT)
    nothing = jnp.zeros((SLAB, features), SENT)
    for k in range(grads_ref.shape[0]):
        for slab in range(slabs):
            row = (k * slabs + slab) * SLAB
            grads_ref[k, slab] = sums[row : row + SLAB] if row < sums.shape[0] else nothing
        grads_ref[k, slabs] = bias


def owed_kernel(
    band_ref, w_first_ref, inner_ref, outer_ref, done_ref, ends_ref, send_even_ref, send_odd_ref
):
    blocks, _, size, _ = band_ref.shape
    odd = device_is_odd()
    w_first = w_first_ref[...]
    inner = d_aggregate_of(w_first, inner_ref[...])
    outer = d_aggregate_of(w_first, outer_ref[...])

    def d_aggregate(b):
        if WIN <= b < blocks - WIN:
            return inner[:, (b - WIN) * size : (b - WIN + 1) * size]
        k = b if b < WIN else b - blocks + WIN
        even_end = inner[:, (blocks - 2 * WIN + k) * size : (blocks - 2 * WIN + k + 1) * size]
        odd_end = outer[:, k * size : (k + 1) * size]
        return jnp.where(odd == (b < WIN), even_end, odd_end)

    def owed(block):
        near = range(max(block - WIN, 0), min(block + WIN, blocks - 1) + 1)
        tiles_of = [band_ref[b, block - b + WIN] for b in near]
        return dot(
            joined_lanes([d_aggregate(b) for b in near]), jnp.concatenate(tiles_of, axis=0)
        )

    for k in range(WIN):
        to_below = owed(k - WIN).astype(BF16)
        to_above = owed(blocks + k).astype(BF16)
        send_even_ref[k] = jnp.where(odd, to_below, to_above)
        send_odd_ref[k] = jnp.where(odd, to_above, to_below)
    for b in range(WIN, blocks - WIN):
        done_ref[b - WIN] = owed(b).astype(BF16)
    for k in range(WIN):
        ends_ref[k] = owed(k)
        ends_ref[WIN + k] = owed(blocks - WIN + k)


def sum_kernel(parts_ref, spread_ref, bias_ref):
    def total(slab):
        result = parts_ref[0, slab].astype(F32)
        for k in range(1, parts_ref.shape[0]):
            result = result + parts_ref[k, slab].astype(F32)
        return result

    slabs = parts_ref.shape[1] - 1
    weights = jnp.concatenate([total(slab) for slab in range(slabs)], axis=0)
    weights = weights.astype(spread_ref.dtype)
    for k in range(spread_ref.shape[0]):
        spread_ref[k] = weights
    bias_ref[...] = total(slabs)


def result_kernel(
    odd_ref,
    even_ref,
    cot_hbm,
    w_msg_ref,
    w_first_ref,
    inner_updated_hbm,
    outer_updated_ref,
    inner_d_hidden_ref,
    outer_d_hidden_ref,
    owed_ref,
    ends_ref,
    bias_ref,
    updated_ref,
    grad_state_ref,
    b_first_ref,
    b_second_ref,
    gain_ref,
    cot_ref,
    inner_updated_ref,
    arrived,
):
    inner, features, size = owed_ref.shape
    blocks = inner + 2 * WIN
    copies = [
        pltpu.make_async_copy(source, target, arrived.at[k])
        for k, (source, target) in enumerate(
            (
                (cot_hbm, cot_ref),
                (inner_updated_hbm, inner_updated_ref),
            )
        )
    ]
    for copy in copies:
        copy.start()
    odd = device_is_odd()
    even_part, odd_part = even_ref[...].astype(F32), odd_ref[...].astype(F32)
    from_below = jnp.where(odd, even_part, odd_part)
    from_above = jnp.where(odd, odd_part, even_part)
    weights = joined_lanes([w_first_ref[pl.ds(0, features), :], w_msg_ref[...]])
    for copy in copies:
        copy.wait()
    for b in range(blocks):
        if b < WIN:
            owed = (ends_ref[b] + from_below[b]).astype(BF16)
        elif b < blocks - WIN:
            owed = owed_ref[b - WIN]
        else:
            k = b - blocks + WIN
            owed = (ends_ref[WIN + k] + from_above[k]).astype(BF16)
        if WIN <= b < blocks - WIN:
            lanes = pl.ds((b - WIN) * size, size)
            updated, d_hidden = inner_updated_ref[:, lanes], inner_d_hidden_ref[:, lanes]
        else:
            k = b if b < WIN else b - blocks + WIN
            even_end = odd == (b < WIN)
            lanes, outer_lanes = pl.ds((blocks - 2 * WIN + k) * size, size), pl.ds(k * size, size)
            updated = jnp.where(
                even_end, inner_updated_ref[:, lanes], outer_updated_ref[:, outer_lanes]
            )
            d_hidden = jnp.where(
                even_end, inner_d_hidden_ref[:, lanes], outer_d_hidden_ref[:, outer_lanes]
            )
        rows = pl.ds(b * size, size)
        change = dot(weights, jnp.concatenate([d_hidden, owed], axis=0))
        grad_state_ref[rows, :] = (cot_ref[rows, :].astype(F32) + change.T).astype(BF16)
        updated_ref[rows, :] = updated.T
    for k, ref in enumerate((b_first_ref, b_second_ref, gain_ref)):
        ref[...] = bias_ref[pl.ds(k, 1), :]


def unpack_kernel(rows_ref, msg_hbm, first_hbm, second_hbm, wide_ref, left):
    place, copies = 0, []
    for k, target in enumerate((first_hbm, second_hbm, msg_hbm)):
        here = pl.ds(place, target.shape[0])
        wide_ref[here, :] = rows_ref[here, :].astype(F32)
        copies.append(pltpu.make_async_copy(wide_ref.at[here], target, left.at[k]))
        copies[-1].start()
        place += target.shape[0]
    for copy in copies:
        copy.wait()


def swapped(block, parity):
    last = lax.axis_size(AXES) - 1
    lower = range(parity, last, 2)
    return lax.ppermute(block, AXES, [(i, i + 1) for i in lower] + [(i + 1, i) for i in lower])


def call(kernel, name, outs, operands, scratch=(), limit=16, flops=0):
    specs = [pl.BlockSpec(memory_space=space) for _, space in operands]
    arrays = [kept(array, space) for array, space in operands]
    return pl.pallas_call(
        kernel,
        out_shape=tuple(outs),
        in_specs=specs,
        out_specs=tuple(
            pl.BlockSpec(memory_space=getattr(out, "memory_space", pltpu.VMEM)) for out in outs
        ),
        scratch_shapes=list(scratch),
        compiler_params=pltpu.CompilerParams(vmem_limit_bytes=limit * 1024 * 1024),
        cost_estimate=pl.CostEstimate(
            flops=flops, bytes_accessed=1_000_000, transcendentals=0
        ),
        name=name,
    )(*arrays)


def shards(
    node_state,
    w_msg,
    w_first,
    b_first,
    w_second,
    b_second,
    ln_gain,
    col_index,
    edge_counts,
    cotangent,
):
    nodes, features = node_state.shape
    blocks, tiles, size, _ = edge_counts.shape
    devices = lax.axis_size(AXES)
    grad_scale = 1.0 / math.sqrt(nodes * devices)
    chunk = -(-4 * features // (devices * 8)) * 8
    side = WIN * size
    most = nodes - side
    vmem, hbm = pltpu.VMEM, pltpu.HBM
    result = jax.ShapeDtypeStruct

    row = lambda vector: vector.reshape(1, features)
    sources = (w_msg, w_first, w_second, row(b_first), row(b_second), row(ln_gain))
    *fetched, even_side, odd_side = call(
        fetch_kernel,
        "fetch",
        [vmem(array.shape, array.dtype) for array in sources]
        + [vmem((side, features), BF16)] * 2,
        [(array, hbm) for array in (node_state, *sources)],
        scratch=(pltpu.SemaphoreType.DMA((len(sources) + 2,)),),
        flops=50_000_000_000,
    )
    w_msg_here, w_first_here, w_second_here, *vectors = fetched
    got_even = swapped(even_side, 0)
    got_odd = swapped(odd_side, 1)

    inner_results = call(
            inner_kernel,
            "inner_rows",
            (
                vmem((features, 2 * features), BF16),
                vmem((features, features), BF16),
                vmem((3, features, size), F32),
                vmem((side, features), BF16),
                vmem((features, side), BF16),
                vmem((features, side), BF16),
                vmem((side, 2 * features), F32),
                vmem((side, side), BF16),
                vmem((blocks, BAND, size, size), BF16),
                hbm((features, most), BF16),
                vmem((features, most), BF16),
                vmem((features, 2 * features + ONES), F32),
                vmem((features + 16, features), F32),
                vmem((features, features), F32),
                vmem((features, size), F32),
            ),
            [(col_index.T, hbm)]
            + [
                (array, vmem)
                for array in (edge_counts, cotangent, node_state, got_even, *fetched)
            ],
            scratch=(
                pltpu.SMEM((tiles, blocks), jnp.int32),
                vmem((features, most), BF16),
                pltpu.SemaphoreType.DMA,
                pltpu.SemaphoreType.DMA,
            ),
            limit=32,
            flops=700_000_000,
    )
    band, inner_updated, inner_d_hidden = inner_results[8:11]
    outer_operands = inner_results[:8] + inner_results[11:]

    grads, outer_updated, outer_d_hidden = call(
        functools.partial(outer_kernel, grad_scale),
        "outer_rows",
        (
            vmem((devices, chunk // SLAB + 1, SLAB, features), SENT),
            vmem((features, side), BF16),
            vmem((features, side), BF16),
        ),
        [
            (array, vmem)
            for array in (got_odd, w_msg_here, w_first_here, w_second_here, *outer_operands)
        ],
        flops=300_000_000,
    )

    parts = lax.all_to_all(grads, PARTNERS, 0, 0, tiled=True)
    owed, owed_ends, send_even, send_odd = call(
        owed_kernel,
        "owed",
        (
            vmem((blocks - 2 * WIN, features, size), BF16),
            vmem((2 * WIN, features, size), F32),
            vmem((WIN, features, size), BF16),
            vmem((WIN, features, size), BF16),
        ),
        [(array, vmem) for array in (band, w_first_here, inner_d_hidden, outer_d_hidden)],
        flops=200_000_000,
    )
    owed_even = swapped(send_even, 0)
    owed_odd = swapped(send_odd, 1)
    spread, bias = call(
        sum_kernel,
        "sum",
        (vmem((devices, chunk, features), SENT), vmem((SLAB, features), F32)),
        [(parts, vmem)],
        flops=10_000_000_000,
    )
    updated, grad_state, g_b_first, g_b_second, g_gain = call(
        result_kernel,
        "results",
        (
            result((nodes, features), BF16),
            result((nodes, features), BF16),
            result((1, features), F32),
            result((1, features), F32),
            result((1, features), F32),
        ),
        [(owed_odd, vmem), (owed_even, vmem), (cotangent, hbm)]
        + [(w_msg_here, vmem), (w_first_here, vmem), (inner_updated, hbm)]
        + [(array, vmem) for array in (outer_updated, inner_d_hidden, outer_d_hidden, owed, owed_ends, bias)],
        scratch=(
            vmem((nodes, features), BF16),
            vmem((features, most), BF16),
            pltpu.SemaphoreType.DMA((2,)),
        ),
        flops=50_000_000_000,
    )

    whole = lax.all_to_all(spread, PARTNERS, 0, 0, tiled=True)
    g_msg, g_first, g_second = call(
        unpack_kernel,
        "unpack",
        (
            hbm((features, features), F32),
            hbm((2 * features, features), F32),
            hbm((features, features), F32),
        ),
        [(whole.reshape(devices * chunk, features), vmem)],
        scratch=(vmem((4 * features, features), F32), pltpu.SemaphoreType.DMA((3,))),
    )
    flat = lambda vector: vector.reshape(features)
    return (
        updated,
        grad_state,
        g_msg,
        g_first,
        flat(g_b_first),
        g_second,
        flat(g_b_second),
        flat(g_gain),
    )


def solution(mesh):
    split = P(AXES, None)
    return jax.shard_map(
        shards,
        mesh=mesh,
        in_specs=(split, P(), P(), P(), P(), P(), P(), split, P(AXES, None, None, None), split),
        out_specs=(split, split, P(), P(), P(), P(), P(), P()),
        check_vma=False,
    )
```
